32 devices in a mesh: seq: 8 (over z, x), head: 4 (over y, core).
Axes of the slice: x: 2, y: 2, z: 4, core: 2. Of those that a mesh axis runs over, the one named last changes fastest.
Arguments:
- tokens: bfloat16 [4096, 2048], P('seq'), may hold values from -6 to 6
- gain_attn: float32 [2048], replicated, may hold values from 0.1 to 1.9
- gain_mlp: float32 [2048], replicated, may hold values from 0.1 to 1.9
- w_query: bfloat16 [2048, 2048], P(None, 'head'), may hold values from -0.125 to 0.125
- w_key: bfloat16 [2048, 2048], P(None, 'head'), may hold values from -0.125 to 0.125
- w_value: bfloat16 [2048, 2048], P(None, 'head'), may hold values from -0.125 to 0.125
- w_out: bfloat16 [2048, 2048], P(None, 'head'), may hold values from -1.5 to 1.5
- w_gate: bfloat16 [2048, 5504], P(None, 'head'), may hold values from -0.125 to 0.125
- w_up: bfloat16 [2048, 5504], P(None, 'head'), may hold values from -0.125 to 0.125
- w_down: bfloat16 [2048, 5504], P(None, 'head'), may hold values from -0.078125 to 0.078125
- prev_keys: bfloat16 [2048, 2048], P(None, 'head'), may hold values from -6 to 6
- prev_values: bfloat16 [2048, 2048], P(None, 'head'), may hold values from -6 to 6
- lengths: int32 [4], replicated, may hold values from 1 to 3648, as said below
- out_grad: bfloat16 [4096, 2048], P('seq'), may hold values from -6 to 6
Outputs:
- block_out: bfloat16 [4096, 2048], P('seq')
- tokens_grad: bfloat16 [4096, 2048], P('seq')
- gain_attn_grad: float32 [2048], P('seq')
- gain_mlp_grad: float32 [2048], P('seq')
- w_query_grad: float32 [2048, 2048], P('seq', 'head')
- w_key_grad: float32 [2048, 2048], P('seq', 'head')
- w_value_grad: float32 [2048, 2048], P('seq', 'head')
- w_out_grad: float32 [2048, 2048], P('seq', 'head')
- w_gate_grad: float32 [2048, 5504], P('seq', 'head')
- w_up_grad: float32 [2048, 5504], P('seq', 'head')
- w_down_grad: float32 [2048, 5504], P('seq', 'head')
The draws below stay inside these ranges and needn't reach their ends.
Inputs may be any that keep to these rules, and one draw needn't show every extreme that they name: The lengths rounded up to multiples of 64 add up to exactly 4096.
All inputs are finite; a program needn't handle non-finite values.
Results may differ from the reference program's by a relative error of at most 0.02.
Values may be sent and summed in bfloat16 or wider, within the bound.
A program may use at most 320 MiB of HBM per device.

```python
import math
import jax
import jax.numpy as jnp
from jax import lax

D = 2048
HEADS = 16
HEAD_DIM = 128
FF = 5504
WINDOW = 2048
PAD = 64
NSEQ = 4
HD_ALL = 2048
TOKENS = 4096
QB = 512
OTHER_BLOCKS = 7


def draw_lengths(key, part):
    key = jax.random.fold_in(key, 7)
    pick_key, spread_key, trim_key = jax.random.split(key, 3)
    long_slot = jax.random.randint(pick_key, (), 0, NSEQ)
    spare = OTHER_BLOCKS - (NSEQ - 1)
    picks = jax.random.randint(spread_key, (spare,), 0, NSEQ - 1)
    shorts = 1 + jnp.sum((picks[:, None] == jnp.arange(NSEQ - 1)[None, :]).astype(jnp.int32), axis=0)
    slots = jnp.arange(NSEQ)
    other_slot = jnp.clip(slots - (slots > long_slot).astype(jnp.int32), 0, NSEQ - 2)
    blocks = jnp.where(slots == long_slot, TOKENS // PAD - OTHER_BLOCKS, shorts[other_slot])
    trims = jax.random.randint(trim_key, (NSEQ,), 0, PAD)
    trims = jnp.where(slots == long_slot, 0, trims)
    return (blocks * PAD - trims).astype(jnp.int32)


def spiked(array, own_key, source, target, parts, factor):
    def block_of(axis_at):
        return (jnp.arange(array.shape[axis_at]) // (array.shape[axis_at] // parts)).reshape((-1,) + (1,) * (array.ndim - 1 - axis_at))

    near = jax.random.permutation(own_key, parts)[block_of(target)]
    far = (block_of(target) + parts // 2) % parts
    return jnp.where((block_of(source) == near) | (block_of(source) == far), factor * array, array)


def block_levels(rng, extent, cuts, smallest, top_value):
    gain = 1.0
    for dim, shards_of in cuts:
        heights = jax.random.uniform(jax.random.fold_in(jax.random.fold_in(rng, 6), dim), (shards_of,), jnp.float32, smallest / len(cuts), top_value / len(cuts))
        gain = gain * jnp.repeat(jnp.exp(heights), extent[dim] // shards_of).reshape((-1,) + (1,) * (len(extent) - 1 - dim))
    return gain


def centred(stream_key, extent, scale, reach, cuts=(), held_as=jnp.bfloat16):
    level = block_levels(stream_key, extent, cuts, -0.22, 0.18) if cuts else 1.0
    array = jax.random.normal(stream_key, extent, jnp.float32) * scale * level
    return jnp.minimum(jnp.maximum(array, -reach), reach).astype(held_as)


def noise_with(key, dims, spread, limit, cuts, heavy, kind=jnp.bfloat16):
    entries = spread * jax.random.normal(key, dims, jnp.float32)
    if cuts:
        entries = entries * block_levels(key, dims, cuts, -0.22, 0.18)
    return jnp.clip(spiked(entries, jax.random.fold_in(key, 3), *heavy), -limit, limit).astype(kind)


def setup_inputs(seed: int = 0) -> dict:
    arg_keys = jax.random.split(jax.random.key(seed), 15)
    return {
        "tokens": centred(arg_keys[0], (TOKENS, D), 1.0, 6.0, ((0, 8),)),
        "gain_attn": jnp.clip(1.0 + 0.18 * jax.random.normal(arg_keys[1], (D,), jnp.float32), 0.1, 1.9),
        "gain_mlp": jnp.clip(1.0 + 0.18 * jax.random.normal(arg_keys[2], (D,), jnp.float32), 0.1, 1.9),
        "w_query": centred(arg_keys[3], (D, HD_ALL), D ** -0.5, 0.125, ((1, 4),)),
        "w_key": centred(arg_keys[4], (D, HD_ALL), D ** -0.5, 0.125, ((1, 4),)),
        "w_value": centred(arg_keys[5], (D, HD_ALL), D ** -0.5, 0.125, ((1, 4),)),
        "w_out": centred(arg_keys[6], (D, HD_ALL), 16 ** -0.5, 1.5, ((1, 4),)),
        "w_gate": centred(arg_keys[7], (D, FF), D ** -0.5, 0.125, ((1, 4),)),
        "w_up": centred(arg_keys[8], (D, FF), D ** -0.5, 0.125, ((1, 4),)),
        "w_down": centred(arg_keys[9], (D, FF), FF ** -0.5, 0.078125, ((1, 4),)),
        "prev_keys": centred(arg_keys[10], (WINDOW, HD_ALL), 1.0, 6.0, ((1, 4),)),
        "prev_values": centred(arg_keys[11], (WINDOW, HD_ALL), 1.0, 6.0, ((1, 4),)),
        "lengths": draw_lengths(jax.random.fold_in(arg_keys[14], 71), 0),
        "out_grad": noise_with(arg_keys[13], (TOKENS, D), 1.0, 6.0, ((0, 8),), (0, 1, 8, 2.0)),
    }


EPS = 1e-06
MASKED = -1e+30
HIGH = lax.Precision.HIGHEST

@jax.custom_vjp
def low(v):
    return lax.optimization_barrier(v.astype(jnp.bfloat16)).astype(jnp.float32)

@jax.custom_vjp
def low_back(v):
    return v

def low_keep(v):
    return (low(v), None)

def low_pass(kept, grad):
    return (grad,)

def back_keep(v):
    return (v, None)

def back_low(kept, grad):
    return (low(grad),)
low.defvjp(low_keep, low_pass)
low_back.defvjp(back_keep, back_low)

def token_meta(global_rows, lengths):
    padded = ((lengths + PAD - 1) // PAD * PAD).astype(jnp.int32)
    starts = (jnp.cumsum(padded) - padded).astype(jnp.int32)
    member = lax.optimization_barrier(jnp.sum((global_rows[:, None] >= starts[None, :]).astype(jnp.int32), axis=1)).astype(jnp.int32) - 1
    member = jnp.maximum(member, 0)
    one_hot = member[:, None] == jnp.arange(NSEQ, dtype=jnp.int32)[None, :]
    start_row = lax.optimization_barrier(jnp.sum(jnp.where(one_hot, starts[None, :], 0), axis=1)).astype(jnp.int32)
    length_row = lax.optimization_barrier(jnp.sum(jnp.where(one_hot, lengths[None, :], 0), axis=1)).astype(jnp.int32)
    position = global_rows - start_row
    return (member, position, position < length_row)

def rope_tables(position):
    half_dim = HEAD_DIM // 2
    freq = jnp.exp(-math.log(10000.0) * (2.0 * jnp.arange(half_dim, dtype=jnp.float32) / HEAD_DIM))
    angle = position.astype(jnp.float32)[:, None] * freq[None, :]
    return (jnp.cos(angle)[:, None, :], jnp.sin(angle)[:, None, :])

def rotate(values, cosine, sine):
    half_dim = values.shape[-1] // 2
    front_half = values[..., :half_dim]
    back_half = values[..., half_dim:]
    return jnp.concatenate([front_half * cosine - back_half * sine, back_half * cosine + front_half * sine], axis=-1)

def forward(inputs, gain_attn, gain_mlp, w_query, w_key, w_value, w_out, w_gate, w_up, w_down, cached_keys, cached_values, query_meta, key_meta):
    member_q, position_q, valid_q = query_meta
    member_k, position_k, valid_k = key_meta
    scale_one = lax.rsqrt(lax.optimization_barrier(jnp.mean(inputs * inputs, axis=-1, keepdims=True)) + EPS)
    normed_one = low(inputs * scale_one * gain_attn)
    cosine, sine = rope_tables(position_q)
    query_raw = low_back(jnp.dot(normed_one, w_query, precision=HIGH)).reshape(TOKENS, HEADS, HEAD_DIM)
    key_raw = low_back(jnp.dot(normed_one, w_key, precision=HIGH)).reshape(TOKENS, HEADS, HEAD_DIM)
    value_raw = low_back(jnp.dot(normed_one, w_value, precision=HIGH)).reshape(TOKENS, HEADS, HEAD_DIM)
    queries = low(rotate(query_raw, cosine, sine))
    keys_all = jnp.concatenate([cached_keys, low(rotate(key_raw, cosine, sine))], axis=0)
    values_all = jnp.concatenate([cached_values, low(value_raw)], axis=0)
    scale = HEAD_DIM ** (-0.5)

    def one_block(block_num):
        block_start = block_num * QB
        query_blk = lax.dynamic_slice_in_dim(queries, block_start, QB, 0)
        key_blk = lax.dynamic_slice_in_dim(keys_all, block_start, WINDOW + QB, 0)
        value_blk = lax.dynamic_slice_in_dim(values_all, block_start, WINDOW + QB, 0)
        mem_q = lax.dynamic_slice_in_dim(member_q, block_start, QB, 0)
        pos_q = lax.dynamic_slice_in_dim(position_q, block_start, QB, 0)
        val_q = lax.dynamic_slice_in_dim(valid_q, block_start, QB, 0)
        mem_k = lax.dynamic_slice_in_dim(member_k, block_start, WINDOW + QB, 0)
        pos_k = lax.dynamic_slice_in_dim(position_k, block_start, WINDOW + QB, 0)
        val_k = lax.dynamic_slice_in_dim(valid_k, block_start, WINDOW + QB, 0)
        distance = pos_q[:, None] - pos_k[None, :]
        key_mask = (mem_q[:, None] == mem_k[None, :]) & (distance >= 0) & (distance < WINDOW) & val_k[None, :] & val_q[:, None]
        scores = low_back(jnp.einsum('qhd,khd->hqk', query_blk, key_blk, precision=HIGH) * scale)
        scores = jnp.where(key_mask[None], scores, MASKED)
        row_top = lax.optimization_barrier(jnp.max(scores, axis=-1, keepdims=True))
        exp_scores = jnp.exp(scores - row_top)
        probs = exp_scores / lax.optimization_barrier(jnp.sum(exp_scores, axis=-1, keepdims=True))
        mixed = jnp.einsum('hqk,khd->qhd', low(probs), value_blk, precision=HIGH)
        return mixed * val_q[:, None, None].astype(mixed.dtype)
    attended = lax.map(jax.checkpoint(one_block), jnp.arange(TOKENS // QB, dtype=jnp.int32))
    attended = low(low_back(attended.reshape(TOKENS, HD_ALL)))
    mid = inputs + low_back(jnp.dot(attended, w_out.T, precision=HIGH))
    scale_two = lax.rsqrt(lax.optimization_barrier(jnp.mean(mid * mid, axis=-1, keepdims=True)) + EPS)
    normed_two = low(mid * scale_two * gain_mlp)
    gate = low_back(jnp.dot(normed_two, w_gate, precision=HIGH))
    up_proj = low_back(jnp.dot(normed_two, w_up, precision=HIGH))
    act = low(jax.nn.silu(gate) * up_proj)
    return mid + low_back(jnp.dot(act, w_down.T, precision=HIGH))

def reference(tokens, gain_attn, gain_mlp, w_query, w_key, w_value, w_out, w_gate, w_up, w_down, prev_keys, prev_values, lengths, out_grad):
    query_meta = token_meta(jnp.arange(TOKENS, dtype=jnp.int32), lengths)
    key_meta = token_meta(jnp.arange(TOKENS + WINDOW, dtype=jnp.int32) - WINDOW, lengths)
    cached_keys = prev_keys.astype(jnp.float32).reshape(WINDOW, HEADS, HEAD_DIM)
    cached_values = prev_values.astype(jnp.float32).reshape(WINDOW, HEADS, HEAD_DIM)

    def layer(inputs, gain_one, gain_two, query_w, key_w, value_w, out_w, gate_w, up_w, down_w):
        return forward(inputs, gain_one, gain_two, query_w, key_w, value_w, out_w, gate_w, up_w, down_w, cached_keys, cached_values, query_meta, key_meta)
    result, pull = jax.vjp(layer, tokens.astype(jnp.float32), gain_attn, gain_mlp, w_query.astype(jnp.float32), w_key.astype(jnp.float32), w_value.astype(jnp.float32), w_out.astype(jnp.float32), w_gate.astype(jnp.float32), w_up.astype(jnp.float32), w_down.astype(jnp.float32))
    grads = pull(out_grad.astype(jnp.float32))
    return (result.astype(jnp.bfloat16), grads[0].astype(jnp.bfloat16), grads[1], grads[2], grads[3], grads[4], grads[5], grads[6], grads[7], grads[8], grads[9])
```

```python
import functools
import math

import jax
import jax.numpy as jnp
from jax import lax
from jax.experimental import pallas as pl
from jax.experimental.pallas import tpu as pltpu
from jax.sharding import PartitionSpec as P

HEAD_DIM = 128
WINDOW = 2048
PAD = 64
NSEQ = 4
EPS = 1e-06
MASKED = -1e30
LOG2E = 1.4426950408889634
BIG = 1 << 28
F32 = jnp.float32
BF16 = jnp.bfloat16


def swap(block, axis, bit):
    return lax.ppermute(block, axis, [(i, i ^ bit) for i in range(lax.axis_size(axis))])


def shifted(block, distance):
    n = lax.axis_size("seq")
    return lax.ppermute(
        block, "seq", [(i, i + distance) for i in range(n) if 0 <= i + distance < n]
    )


def head_sum(partial):
    core = lax.axis_index("head") & 1
    rows, width = partial.shape
    halves = partial.reshape(rows, 2, width // 2)
    low, high = halves[:, 0], halves[:, 1]
    keep = jnp.where(core == 0, low, high)
    give = jnp.where(core == 0, high, low).astype(BF16)
    chip = (keep + swap(give, "head", 1).astype(F32)).astype(BF16)
    total = (chip.astype(F32) + swap(chip, "head", 2).astype(F32)).astype(BF16)
    other = swap(total, "head", 1)
    return jnp.concatenate(
        [jnp.where(core == 0, total, other), jnp.where(core == 0, other, total)], axis=1
    ).astype(F32)


def pair_rows(left):
    n = lax.axis_size("seq")
    bit = lax.axis_index("seq") & 1
    rows, width = left.shape
    parts = left.reshape(rows, n // 2, 2, width // n)
    keep = lax.dynamic_index_in_dim(parts, bit, 2, keepdims=False).reshape(rows, width // 2)
    give = lax.dynamic_index_in_dim(parts, 1 - bit, 2, keepdims=False).reshape(rows, width // 2)
    return jnp.concatenate([keep, swap(give, "seq", 1)], axis=0)


def pair_tokens(right):
    return jnp.concatenate([right, swap(right, "seq", 1)], axis=0)


def scatter_sum(grad):
    n = lax.axis_size("seq")
    index = lax.axis_index("seq")
    rows, cols = grad.shape
    shares = n // 2
    part = grad
    bit = 2
    while bit < n:
        shares //= 2
        mine = (index // bit) & 1
        view = part.reshape(shares, 2, rows // (n // 2), cols)
        keep = lax.dynamic_index_in_dim(view, mine, 1, keepdims=False)
        give = lax.dynamic_index_in_dim(view, 1 - mine, 1, keepdims=False)
        total = keep.astype(F32) + swap(give, "seq", bit).astype(F32)
        bit *= 2
        part = total.astype(BF16) if bit < n else total
    return part.reshape(rows // (n // 2), cols).astype(F32)


def gain_sum(part):
    n = lax.axis_size("seq")
    total = part
    bit = 1
    while bit < n:
        total = total + swap(total, "seq", bit)
        bit *= 2
    width = part.shape[0] // n
    return lax.dynamic_slice_in_dim(total, lax.axis_index("seq") * width, width, 0)


def fwd_kernel(lo_ref, valid_ref, q_ref, *refs):
    rows = q_ref.shape[0]
    n_parts = (len(refs) - 3) // 2
    k_refs, v_refs = refs[:n_parts], refs[n_parts : 2 * n_parts]
    out_ref, lse_ref, s_ref = refs[2 * n_parts :]
    sub = s_ref.shape[0]
    scale = HEAD_DIM ** (-0.5) * LOG2E
    for start in range(0, rows, sub):
        q = q_ref[start : start + sub, :]
        lo = lo_ref[start : start + sub, :]
        top = None
        for d in range(n_parts):
            s = lax.dot_general(
                q, k_refs[d][...], (((1,), (1,)), ((), ())), preferred_element_type=F32
            )
            u = lax.broadcasted_iota(jnp.int32, s.shape, 1) - d * rows
            seen = u >= lo
            if d == 0:
                t = lax.broadcasted_iota(jnp.int32, s.shape, 0) + start
                seen = seen & (u <= t)
            s = jnp.where(seen, s * scale, MASKED)
            s_ref[:, d * rows : (d + 1) * rows] = s
            part_top = jnp.max(s, axis=1, keepdims=True)
            top = part_top if top is None else jnp.maximum(top, part_top)
        total = jnp.zeros_like(top)
        acc = jnp.zeros((sub, HEAD_DIM), F32)
        for d in range(n_parts):
            p = jnp.exp2(s_ref[:, d * rows : (d + 1) * rows] - top)
            total = total + jnp.sum(p, axis=1, keepdims=True)
            acc = acc + jnp.dot(p.astype(BF16), v_refs[d][...], preferred_element_type=F32)
        out = jnp.where(valid_ref[start : start + sub, :] > 0, acc / total, 0.0)
        out_ref[start : start + sub, :] = out.astype(BF16)
        lse_ref[0, start : start + sub, :] = top + jnp.log2(total)


def attention_fwd(lo, valid, queries, keys, values):
    rows, width = queries.shape
    heads = width // HEAD_DIM
    n_parts = len(keys)
    column = pl.BlockSpec((rows, HEAD_DIM), lambda h: (0, h))
    whole = pl.BlockSpec((rows, 1), lambda h: (0, 0))
    flops = 4 * rows * rows * n_parts * width
    return pl.pallas_call(
        fwd_kernel,
        grid=(heads,),
        in_specs=[whole, whole] + [column] * (1 + 2 * n_parts),
        out_specs=[column, pl.BlockSpec((1, rows, 1), lambda h: (h, 0, 0))],
        out_shape=[
            jax.ShapeDtypeStruct((rows, width), BF16),
            jax.ShapeDtypeStruct((heads, rows, 1), F32),
        ],
        scratch_shapes=[pltpu.VMEM((rows // 2, n_parts * rows), F32)],
        compiler_params=pltpu.CompilerParams(vmem_limit_bytes=48 << 20),
        cost_estimate=pl.CostEstimate(
            flops=flops, bytes_accessed=12 * rows * width * 2, transcendentals=flops // 512
        ),
        name="attention_fwd",
    )(lo, valid, queries, *keys, *values)


def dq_kernel(lo_ref, q_ref, do_ref, lse_ref, delta_ref, *refs):
    rows = q_ref.shape[0]
    n_parts = (len(refs) - 1) // 2
    k_refs, v_refs = refs[:n_parts], refs[n_parts : 2 * n_parts]
    out_ref = refs[-1]
    scale = HEAD_DIM ** (-0.5) * LOG2E
    sub = rows // 2
    for start in range(0, rows, sub):
        rs = slice(start, start + sub)
        q, do, lo = q_ref[rs, :], do_ref[rs, :], lo_ref[rs, :]
        lse, delta = lse_ref[0, rs, :], delta_ref[0, rs, :]
        acc = jnp.zeros((sub, HEAD_DIM), F32)
        for d in range(n_parts):
            k = k_refs[d][...]
            s = lax.dot_general(q, k, (((1,), (1,)), ((), ())), preferred_element_type=F32)
            u = lax.broadcasted_iota(jnp.int32, s.shape, 1) - d * rows
            seen = u >= lo
            if d == 0:
                t = lax.broadcasted_iota(jnp.int32, s.shape, 0) + start
                seen = seen & (u <= t)
            p = jnp.exp2(jnp.where(seen, s * scale, MASKED) - lse)
            dp = lax.dot_general(
                do, v_refs[d][...], (((1,), (1,)), ((), ())), preferred_element_type=F32
            )
            ds = (p * (dp - delta)).astype(BF16)
            acc = acc + jnp.dot(ds, k, preferred_element_type=F32)
        out_ref[rs, :] = acc * HEAD_DIM ** (-0.5)


def attention_dq(lo, queries, grad_att, lse, delta, keys, values):
    rows, width = queries.shape
    heads = width // HEAD_DIM
    n_parts = len(keys)
    column = pl.BlockSpec((rows, HEAD_DIM), lambda h: (0, h))
    stat = pl.BlockSpec((1, rows, 1), lambda h: (h, 0, 0))
    flops = 6 * rows * rows * n_parts * width
    return pl.pallas_call(
        dq_kernel,
        grid=(heads,),
        in_specs=[pl.BlockSpec((rows, 1), lambda h: (0, 0)), column, column, stat, stat]
        + [column] * (2 * n_parts),
        out_specs=column,
        out_shape=jax.ShapeDtypeStruct((rows, width), F32),
        compiler_params=pltpu.CompilerParams(vmem_limit_bytes=48 << 20),
        cost_estimate=pl.CostEstimate(
            flops=flops, bytes_accessed=14 * rows * width * 2, transcendentals=flops // 768
        ),
        name="attention_dq",
    )(lo, queries, grad_att, lse, delta, *keys, *values)


def dkv_kernel(lo_ref, k_ref, v_ref, *refs):
    rows = k_ref.shape[0]
    n_parts = (len(refs) - 2) // 3
    q_refs, do_refs, st_refs = (
        refs[:n_parts],
        refs[n_parts : 2 * n_parts],
        refs[2 * n_parts : 3 * n_parts],
    )
    dk_ref, dv_ref = refs[-2:]
    scale = HEAD_DIM ** (-0.5) * LOG2E
    sub = rows // 2
    for start in range(0, rows, sub):
        rs = slice(start, start + sub)
        k, v = k_ref[rs, :], v_ref[rs, :]
        dk = jnp.zeros((sub, HEAD_DIM), F32)
        dv = jnp.zeros((sub, HEAD_DIM), F32)
        for d in range(n_parts):
            q, do = q_refs[d][...], do_refs[d][...]
            s = lax.dot_general(k, q, (((1,), (1,)), ((), ())), preferred_element_type=F32)
            u = lax.broadcasted_iota(jnp.int32, s.shape, 0) + start
            seen = u >= lo_ref[:, d * rows : (d + 1) * rows]
            if d == 0:
                seen = seen & (u <= lax.broadcasted_iota(jnp.int32, s.shape, 1))
            lse, delta = st_refs[d][0, 0:1, :], st_refs[d][0, 1:2, :]
            p = jnp.exp2(jnp.where(seen, s * scale - lse, MASKED))
            dv = dv + jnp.dot(p.astype(BF16), do, preferred_element_type=F32)
            dp = lax.dot_general(v, do, (((1,), (1,)), ((), ())), preferred_element_type=F32)
            ds = (p * (dp - delta)).astype(BF16)
            dk = dk + jnp.dot(ds, q, preferred_element_type=F32)
        dk_ref[rs, :] = dk * HEAD_DIM ** (-0.5)
        dv_ref[rs, :] = dv


def attention_dkv(lo_row, keys, values, queries, grad_atts, stats):
    rows, width = keys.shape
    heads = width // HEAD_DIM
    n_parts = len(queries)
    column = pl.BlockSpec((rows, HEAD_DIM), lambda h: (0, h))
    stat = pl.BlockSpec((1, 2, rows), lambda h: (h, 0, 0))
    flops = 8 * rows * rows * n_parts * width
    return pl.pallas_call(
        dkv_kernel,
        grid=(heads,),
        in_specs=[pl.BlockSpec((1, n_parts * rows), lambda h: (0, 0)), column, column]
        + [column] * (2 * n_parts)
        + [stat] * n_parts,
        out_specs=[column, column],
        out_shape=[jax.ShapeDtypeStruct((rows, width), F32)] * 2,
        compiler_params=pltpu.CompilerParams(vmem_limit_bytes=48 << 20),
        cost_estimate=pl.CostEstimate(
            flops=flops, bytes_accessed=16 * rows * width * 2, transcendentals=flops // 1024
        ),
        name="attention_dkv",
    )(lo_row, keys, values, *queries, *grad_atts, *stats)


def first_key(rows, lengths, total):
    padded = (lengths + PAD - 1) // PAD * PAD
    starts = jnp.cumsum(padded) - padded
    start_row = jnp.zeros_like(rows)
    length_row = jnp.full_like(rows, 0) + lengths[0]
    low_row = jnp.full_like(rows, -BIG)
    for r in range(1, NSEQ):
        inside = rows >= starts[r]
        start_row = jnp.where(inside, starts[r], start_row)
        low_row = jnp.where(inside, starts[r], low_row)
        length_row = jnp.where(inside, lengths[r], length_row)
    position = rows - start_row
    valid = position < length_row
    low = jnp.where(valid, jnp.maximum(low_row, rows - (WINDOW - 1)), rows)
    low = jnp.where(rows < total, low, BIG)
    return low, valid, position


def outer_sum(left, right):
    return lax.dot_general(left, right, (((0,), (0,)), ((), ())), preferred_element_type=F32)


def times_transpose(left, right):
    return lax.dot_general(left, right, (((1,), (1,)), ((), ())), preferred_element_type=F32)


def turned(values):
    half = HEAD_DIM // 2
    out = []
    for start in range(0, values.shape[1], HEAD_DIM):
        out += [values[:, start + half : start + HEAD_DIM], values[:, start : start + half]]
    return jnp.concatenate(out, axis=1)


def norm_back(grad_normed, inputs, scale_rows, gain):
    unit = inputs * scale_rows
    grad_unit = grad_normed * gain
    gain_part = jnp.sum(grad_normed * unit, axis=0)
    grad_inputs = scale_rows * (
        grad_unit - unit * jnp.mean(grad_unit * unit, axis=-1, keepdims=True)
    )
    return (grad_inputs, gain_part)


def on_device(
    tokens,
    gain_attn,
    gain_mlp,
    w_query,
    w_key,
    w_value,
    w_out,
    w_gate,
    w_up,
    w_down,
    prev_keys,
    prev_values,
    lengths,
    out_grad,
):
    rows = tokens.shape[0]
    width = w_query.shape[1]
    heads = width // HEAD_DIM
    devices = lax.axis_size("seq")
    index = lax.axis_index("seq")
    odd = (index & 1) == 1
    first_row = index * rows
    far = WINDOW // rows
    low, valid, position = first_key(
        first_row + jnp.arange((far + 1) * rows, dtype=jnp.int32), lengths, devices * rows
    )
    low = low - first_row
    low_col = low[:rows, None]
    low_row = low[None, :]
    valid_col = valid[:rows, None]
    valid_int = valid_col.astype(jnp.int32)
    half = HEAD_DIM // 2
    freq = jnp.exp(-math.log(10000.0) * (2.0 * jnp.arange(half, dtype=F32) / HEAD_DIM))
    angle = position[:rows].astype(F32)[:, None] * freq[None, :]
    cos_one, sin_one = jnp.cos(angle), jnp.sin(angle)
    cosine = jnp.tile(jnp.concatenate([cos_one, cos_one], axis=1), (1, heads))
    sine = jnp.tile(jnp.concatenate([-sin_one, sin_one], axis=1), (1, heads))

    inputs = tokens.astype(F32)
    scale_one = lax.rsqrt(jnp.mean(inputs * inputs, axis=-1, keepdims=True) + EPS)
    normed_one = (inputs * scale_one * gain_attn).astype(BF16)
    key_raw = jnp.dot(normed_one, w_key, preferred_element_type=F32)
    keys_own = (key_raw * cosine + turned(key_raw) * sine).astype(BF16)
    values_own = jnp.dot(normed_one, w_value, preferred_element_type=F32).astype(BF16)

    def borrowed(own, prev):
        def cached(distance):
            at = jnp.clip((index - distance) * rows + WINDOW, 0, WINDOW - rows)
            return lax.dynamic_slice_in_dim(prev, at, rows, 0)

        two = jnp.where(index >= 2, shifted(own, 2), cached(2))
        one = swap(jnp.where(odd, two, own), "seq", 1)
        four = jnp.where(index >= 2, shifted(two, 2), cached(4))
        three = swap(jnp.where(odd, four, two), "seq", 1)
        return [own, one, two, three, four]

    def lent(own):
        two = shifted(own, -2)
        one = swap(jnp.where(odd, own, two), "seq", 1)
        four = shifted(two, -2)
        three = swap(jnp.where(odd, two, four), "seq", 1)
        return [own, one, two, three, four]

    keys = borrowed(keys_own, prev_keys)
    values = borrowed(values_own, prev_values)
    query_raw = jnp.dot(normed_one, w_query, preferred_element_type=F32)
    queries = (query_raw * cosine + turned(query_raw) * sine).astype(BF16)
    queries_lent = lent(queries)
    grad_branch = out_grad
    grad_act = jnp.dot(grad_branch, w_down, preferred_element_type=F32)

    attended, lse = attention_fwd(low_col, valid_int, queries, keys, values)
    mid = inputs + head_sum(times_transpose(attended, w_out))
    scale_two = lax.rsqrt(jnp.mean(mid * mid, axis=-1, keepdims=True) + EPS)
    normed_two = (mid * scale_two * gain_mlp).astype(BF16)
    gate = jnp.dot(normed_two, w_gate, preferred_element_type=F32)
    up_proj = jnp.dot(normed_two, w_up, preferred_element_type=F32)
    sigmoid_gate = jax.nn.sigmoid(gate)
    silu_gate = gate * sigmoid_gate
    act = (silu_gate * up_proj).astype(BF16)
    grad_gate = (grad_act * up_proj * sigmoid_gate * (1.0 + gate * (1.0 - sigmoid_gate))).astype(
        BF16
    )
    grad_up = (grad_act * silu_gate).astype(BF16)

    grad_norm_two = head_sum(times_transpose(grad_gate, w_gate) + times_transpose(grad_up, w_up))

    w_down_grad = scatter_sum(outer_sum(pair_rows(grad_branch), pair_tokens(act)).astype(BF16))
    normed_two_pair = pair_rows(normed_two)
    w_gate_grad = scatter_sum(outer_sum(normed_two_pair, pair_tokens(grad_gate)).astype(BF16))
    w_up_grad = scatter_sum(outer_sum(normed_two_pair, pair_tokens(grad_up)).astype(BF16))

    block_out = (mid + head_sum(times_transpose(act, w_down))).astype(BF16)

    grad_out = out_grad.astype(F32)
    grad_mid_norm, gain_mlp_part = norm_back(grad_norm_two, mid, scale_two, gain_mlp)
    grad_mid = grad_out + grad_mid_norm
    gain_mlp_grad = gain_sum(gain_mlp_part)
    grad_attn_branch = grad_mid.astype(BF16)
    grad_att = jnp.dot(grad_attn_branch, w_out, preferred_element_type=F32).astype(BF16)
    grad_att = jnp.where(valid_col, grad_att, jnp.zeros_like(grad_att))
    grad_atts = lent(grad_att)
    delta = jnp.sum(
        (grad_att.astype(F32) * attended.astype(F32)).reshape(rows, heads, HEAD_DIM), axis=-1
    )
    stats = lent(jnp.stack([lse[:, :, 0], delta.T], axis=1))
    grad_queries = attention_dq(
        low_col, queries, grad_att, lse, delta.T[:, :, None], keys, values
    )
    grad_keys, grad_values = attention_dkv(
        low_row, keys_own, values_own, queries_lent, grad_atts, stats
    )
    grad_query_raw = (grad_queries * cosine - turned(grad_queries) * sine).astype(BF16)
    grad_key_raw = (grad_keys * cosine - turned(grad_keys) * sine).astype(BF16)
    grad_value_raw = grad_values.astype(BF16)

    w_out_grad = scatter_sum(
        outer_sum(pair_rows(grad_attn_branch), pair_tokens(attended)).astype(BF16)
    )
    normed_one_pair = pair_rows(normed_one)
    w_query_grad = scatter_sum(outer_sum(normed_one_pair, pair_tokens(grad_query_raw)).astype(BF16))
    w_key_grad = scatter_sum(outer_sum(normed_one_pair, pair_tokens(grad_key_raw)).astype(BF16))
    w_value_grad = scatter_sum(outer_sum(normed_one_pair, pair_tokens(grad_value_raw)).astype(BF16))
    grad_norm_one = head_sum(
        times_transpose(grad_query_raw, w_query)
        + times_transpose(grad_key_raw, w_key)
        + times_transpose(grad_value_raw, w_value)
    )
    grad_in_norm, gain_attn_part = norm_back(grad_norm_one, inputs, scale_one, gain_attn)
    tokens_grad = (grad_mid + grad_in_norm).astype(BF16)
    gain_attn_grad = gain_sum(gain_attn_part)
    return (
        block_out,
        tokens_grad,
        gain_attn_grad,
        gain_mlp_grad,
        w_query_grad,
        w_key_grad,
        w_value_grad,
        w_out_grad,
        w_gate_grad,
        w_up_grad,
        w_down_grad,
    )


def solution(mesh):
    by_head = P(None, "head")
    both = P("seq", "head")
    placed = (P("seq", None), P(), P()) + (by_head,) * 9 + (P(), P("seq", None))
    return jax.shard_map(
        on_device,
        mesh=mesh,
        in_specs=placed,
        out_specs=(P("seq", None), P("seq", None), P("seq"), P("seq")) + (both,) * 7,
        check_vma=False,
    )
```

```python
import functools
import math

import jax
import jax.numpy as jnp
from jax import lax
from jax.experimental import pallas as pl
from jax.experimental.pallas import tpu as pltpu
from jax.sharding import PartitionSpec as P

HEAD_DIM = 128
WINDOW = 2048
PAD = 64
NSEQ = 4
EPS = 1e-06
MASKED = -1e30
LOG2E = 1.4426950408889634
BIG = 1 << 28
F32 = jnp.float32
BF16 = jnp.bfloat16


def swap(block, axis, bit):
    return lax.ppermute(block, axis, [(i, i ^ bit) for i in range(lax.axis_size(axis))])


def shifted(block, distance):
    n = lax.axis_size("seq")
    return lax.ppermute(
        block, "seq", [(i, i + distance) for i in range(n) if 0 <= i + distance < n]
    )


BIG_VMEM = pltpu.CompilerParams(vmem_limit_bytes=48 << 20)


def cost(flops, moved):
    return pl.CostEstimate(flops=int(flops), bytes_accessed=int(moved), transcendentals=0)


def dot_nt(left, right):
    return lax.dot_general(left, right, (((1,), (1,)), ((), ())), preferred_element_type=F32)


def split_columns(mine, values, keep_ref, give_ref, flip):
    pairs = keep_ref.shape[0]
    depth = values.shape[1] // (2 * pairs)
    if flip:
        values = values.T
    for j in range(pairs):
        even = slice(2 * j * depth, (2 * j + 1) * depth)
        odd = slice((2 * j + 1) * depth, (2 * j + 2) * depth)
        even, odd = (values[even, :], values[odd, :]) if flip else (values[:, even], values[:, odd])
        keep_ref[j] = jnp.where(mine, even, odd)
        give_ref[j] = jnp.where(mine, odd, even)


def row_blocks(width, step):
    return pl.BlockSpec((step, width), lambda i, bits: (i, 0))


def prep_kernel(bits_ref, x_ref, gain_ref, out_ref, keep_ref, give_ref):
    x = x_ref[...].astype(F32)
    scale = lax.rsqrt(jnp.mean(x * x, axis=-1, keepdims=True) + EPS)
    normed = (x * scale * gain_ref[...]).astype(BF16)
    out_ref[...] = normed
    split_columns(bits_ref[0] == 0, normed, keep_ref, give_ref, True)


def split_kernel(bits_ref, x_ref, keep_ref, give_ref):
    split_columns(bits_ref[0] == 0, x_ref[...], keep_ref, give_ref, False)


def joined(bits_ref, own_ref, other_ref):
    low = bits_ref[1] == 0
    own, other = own_ref[...].astype(F32), other_ref[...].astype(F32)
    return jnp.concatenate([jnp.where(low, own, other), jnp.where(low, other, own)], axis=1)


def mid_kernel(
    bits_ref, x_ref, own_ref, other_ref, gain_ref, mid_ref, out_ref, keep_ref, give_ref
):
    mid = x_ref[...].astype(F32) + joined(bits_ref, own_ref, other_ref)
    mid_ref[...] = mid
    scale = lax.rsqrt(jnp.mean(mid * mid, axis=-1, keepdims=True) + EPS)
    normed = (mid * scale * gain_ref[...]).astype(BF16)
    out_ref[...] = normed
    split_columns(bits_ref[0] == 0, normed, keep_ref, give_ref, False)


def back_kernel(
    bits_ref, x_ref, own_ref, other_ref, gain_ref, add_ref, out_ref, part_ref, *more
):
    x = x_ref[...].astype(F32)
    scale = lax.rsqrt(jnp.mean(x * x, axis=-1, keepdims=True) + EPS)
    grad = joined(bits_ref, own_ref, other_ref)
    unit = x * scale
    grad_unit = grad * gain_ref[...]
    total = add_ref[...].astype(F32) + scale * (
        grad_unit - unit * jnp.mean(grad_unit * unit, axis=-1, keepdims=True)
    )
    out_ref[...] = total.astype(out_ref.dtype)
    part = jnp.sum(grad * unit, axis=0, keepdims=True)

    @pl.when(pl.program_id(0) == 0)
    def _():
        part_ref[...] = part

    @pl.when(pl.program_id(0) > 0)
    def _():
        part_ref[...] += part

    if more:
        low_ref, keep_ref, give_ref = more
        low = total.astype(BF16)
        low_ref[...] = low
        split_columns(bits_ref[0] == 0, low, keep_ref, give_ref, True)


def by_rows(kernel, bits, arrays, gains_at, outs, split, name, part=None):
    rows, width = arrays[0].shape
    step = rows // 4
    shards = lax.axis_size("seq")
    in_specs = [
        pl.BlockSpec((1, width), lambda i, bits: (0, 0))
        if k == gains_at
        else row_blocks(a.shape[1], step)
        for k, a in enumerate(arrays)
    ]
    out_specs, out_shape = [], []
    for k, dtype in enumerate(outs):
        if k == part:
            out_specs.append(pl.BlockSpec((1, width), lambda i, bits: (0, 0)))
            out_shape.append(jax.ShapeDtypeStruct((1, width), F32))
        else:
            out_specs.append(row_blocks(width, step))
            out_shape.append(jax.ShapeDtypeStruct((rows, width), dtype))
    depth = width // shards
    for _ in range(2 if split else 0):
        if split == "flip":
            out_specs.append(pl.BlockSpec((shards // 2, depth, step), lambda i, bits: (0, 0, i)))
            out_shape.append(jax.ShapeDtypeStruct((shards // 2, depth, rows), BF16))
        else:
            out_specs.append(pl.BlockSpec((shards // 2, step, depth), lambda i, bits: (0, i, 0)))
            out_shape.append(jax.ShapeDtypeStruct((shards // 2, rows, depth), BF16))
    return pl.pallas_call(
        kernel,
        grid_spec=pltpu.PrefetchScalarGridSpec(
            num_scalar_prefetch=1, grid=(rows // step,), in_specs=in_specs, out_specs=out_specs
        ),
        out_shape=out_shape,
        compiler_params=BIG_VMEM,
        cost_estimate=cost(rows * width * 10, rows * width * 2 * (len(arrays) + len(out_shape))),
        name=name,
    )(bits, *arrays)


def project_kernel(x_ref, w_ref, cos_ref, sin_ref, out_ref):
    raw = jnp.dot(x_ref[...], w_ref[...], preferred_element_type=F32)
    for start in range(0, raw.shape[1], HEAD_DIM):
        u = raw[:, start : start + HEAD_DIM]
        u = u * cos_ref[...] + pltpu.roll(u, HEAD_DIM // 2, 1) * sin_ref[...]
        out_ref[:, start : start + HEAD_DIM] = u.astype(BF16)


def plain_kernel(x_ref, w_ref, out_ref):
    out_ref[...] = jnp.dot(x_ref[...], w_ref[...], preferred_element_type=F32).astype(BF16)


def project(x, weight, tables, name):
    rows, depth = x.shape
    width = weight.shape[1]
    step = 2 * HEAD_DIM
    table = pl.BlockSpec((rows, HEAD_DIM), lambda i: (0, 0))
    return pl.pallas_call(
        project_kernel if tables else plain_kernel,
        grid=(width // step,),
        in_specs=[
            pl.BlockSpec((rows, depth), lambda i: (0, 0)),
            pl.BlockSpec((depth, step), lambda i: (0, i)),
        ]
        + [table] * len(tables),
        out_specs=pl.BlockSpec((rows, step), lambda i: (0, i)),
        out_shape=jax.ShapeDtypeStruct((rows, width), BF16),
        compiler_params=BIG_VMEM,
        cost_estimate=cost(2 * rows * depth * width, 2 * (rows + width) * depth),
        name=name,
    )(x, weight, *tables)


def half_kernel(pairs, flip, added, bits_ref, *refs):
    total = refs[2 * pairs][...].astype(F32) if added else None
    for k in range(pairs):
        term = dot_nt(refs[k][...], refs[pairs + k][...])
        total = term if total is None else total + term
    refs[-1][...] = total.astype(BF16)


def half_product(bits, lefts, rights, flip, added, name):
    rows = lefts[0].shape[0]
    width = rights[0].shape[0] // 2
    step = min(width, 512)
    steps = width // step

    def at(i, bits):
        return ((bits[1] ^ flip) * steps + i, 0)

    specs = [pl.BlockSpec(a.shape, lambda i, bits: (0, 0)) for a in lefts]
    specs += [pl.BlockSpec((step, a.shape[1]), at) for a in rights]
    extra = []
    if added is not None:
        extra = [added]
        specs.append(pl.BlockSpec((rows, step), lambda i, bits: (0, i)))
    depth = sum(a.shape[1] for a in lefts)
    return pl.pallas_call(
        functools.partial(half_kernel, len(lefts), flip, added is not None),
        grid_spec=pltpu.PrefetchScalarGridSpec(
            num_scalar_prefetch=1,
            grid=(steps,),
            in_specs=specs,
            out_specs=pl.BlockSpec((rows, step), lambda i, bits: (0, i)),
        ),
        out_shape=jax.ShapeDtypeStruct((rows, width), BF16),
        compiler_params=BIG_VMEM,
        cost_estimate=cost(2 * rows * depth * width, 2 * (rows + width) * depth),
        name=name,
    )(bits, *lefts, *rights, *extra)


def head_sum(bits, lefts, rights, name):
    give = half_product(bits, lefts, rights, 1, None, name + "_give")
    chip = half_product(bits, lefts, rights, 0, swap(give, "head", 1), name + "_keep")
    total = (chip.astype(F32) + swap(chip, "head", 2).astype(F32)).astype(BF16)
    return total, swap(total, "head", 1)


def head_sum_of(give, keep):
    chip = (keep.astype(F32) + swap(give, "head", 1).astype(F32)).astype(BF16)
    total = (chip.astype(F32) + swap(chip, "head", 2).astype(F32)).astype(BF16)
    return total, swap(total, "head", 1)


def dot_tn(left, right):
    return lax.dot_general(left, right, (((0,), (0,)), ((), ())), preferred_element_type=F32)


def mlp_kernel(
    bits_ref,
    x_ref,
    g_ref,
    wg_ref,
    wu_ref,
    wd_ref,
    act_ref,
    gg_ref,
    gu_ref,
    norm_keep_ref,
    norm_give_ref,
    out_keep_ref,
    out_give_ref,
    norm_ref,
    branch_ref,
):
    step = pl.program_id(0)
    x, g = x_ref[...], g_ref[...]
    gate = dot_nt(wg_ref[...], x)
    up = dot_nt(wu_ref[...], x)
    grad = dot_nt(wd_ref[...], g)
    sig = 1.0 / (1.0 + jnp.exp(-gate))
    silu = gate * sig
    act = (silu * up).astype(BF16)
    grad_gate = (grad * up * sig * (1.0 + gate * (1.0 - sig))).astype(BF16)
    grad_up = (grad * silu).astype(BF16)
    act_ref[...] = act
    gg_ref[...] = grad_gate
    gu_ref[...] = grad_up

    @pl.when(step == 0)
    def _():
        norm_ref[...] = jnp.zeros_like(norm_ref)
        branch_ref[...] = jnp.zeros_like(branch_ref)

    norm_ref[...] += jnp.dot(grad_gate.T, wg_ref[...], preferred_element_type=F32)
    norm_ref[...] += jnp.dot(grad_up.T, wu_ref[...], preferred_element_type=F32)
    branch_ref[...] += jnp.dot(act.T, wd_ref[...], preferred_element_type=F32)

    @pl.when(step == pl.num_programs(0) - 1)
    def _():
        half = norm_ref.shape[1] // 2
        low = bits_ref[1] == 0
        for total, keep_ref, give_ref in (
            (norm_ref, norm_keep_ref, norm_give_ref),
            (branch_ref, out_keep_ref, out_give_ref),
        ):
            first, second = total[:, :half], total[:, half:]
            keep_ref[...] = jnp.where(low, first, second).astype(BF16)
            give_ref[...] = jnp.where(low, second, first).astype(BF16)


def mlp(bits, x, grad, w_gate, w_up, w_down):
    rows, depth = x.shape
    width = w_gate.shape[0]
    step = width // 2
    whole = pl.BlockSpec((rows, depth), lambda i, bits: (0, 0))
    half = pl.BlockSpec((rows, depth // 2), lambda i, bits: (0, 0))
    block = pl.BlockSpec((step, depth), lambda i, bits: (i, 0))
    return pl.pallas_call(
        mlp_kernel,
        grid_spec=pltpu.PrefetchScalarGridSpec(
            num_scalar_prefetch=1,
            grid=(width // step,),
            in_specs=[whole, whole, block, block, block],
            out_specs=[pl.BlockSpec((step, rows), lambda i, bits: (i, 0))] * 3 + [half] * 4,
            scratch_shapes=[pltpu.VMEM((rows, depth), F32)] * 2,
        ),
        out_shape=[jax.ShapeDtypeStruct((width, rows), BF16)] * 3
        + [jax.ShapeDtypeStruct((rows, depth // 2), BF16)] * 4,
        compiler_params=pltpu.CompilerParams(vmem_limit_bytes=56 << 20),
        cost_estimate=cost(12 * rows * depth * width, 6 * depth * width),
        name="mlp",
    )(bits, x, grad, w_gate, w_up, w_down)


def blocks_kernel(order_ref, flip, xa_ref, xb_ref, ga_ref, gb_ref, *refs):
    if flip:
        total = jnp.dot(ga_ref[...], xa_ref[0], preferred_element_type=F32)
        total = total + jnp.dot(gb_ref[...], xb_ref[0], preferred_element_type=F32)
    else:
        total = jnp.dot(xa_ref[0], ga_ref[...], preferred_element_type=F32)
        total = total + jnp.dot(xb_ref[0], gb_ref[...], preferred_element_type=F32)
    if len(refs) == 2:
        total = total + refs[0][0].astype(F32)
    refs[-1][0] = total.astype(BF16)


def grad_blocks(order, x_own, x_got, g_own, g_got, added, flip, name):
    count = order.shape[0]
    if flip:
        _, rows, depth = x_own.shape
        cols = g_own.shape[0]
        shape = (cols, depth)
    else:
        _, depth, rows = x_own.shape
        cols = g_own.shape[1]
        shape = (depth, cols)
    x_spec = pl.BlockSpec((1,) + x_own.shape[1:], lambda i, order: (order[i], 0, 0))
    g_spec = pl.BlockSpec(g_own.shape, lambda i, order: (0, 0))
    out_spec = pl.BlockSpec((1,) + shape, lambda i, order: (i, 0, 0))
    extra = [] if added is None else [added]

    def kernel(order_ref, *refs):
        blocks_kernel(order_ref, flip, *refs)

    return pl.pallas_call(
        kernel,
        grid_spec=pltpu.PrefetchScalarGridSpec(
            num_scalar_prefetch=1,
            grid=(count,),
            in_specs=[x_spec, x_spec, g_spec, g_spec] + [out_spec] * len(extra),
            out_specs=out_spec,
        ),
        out_shape=jax.ShapeDtypeStruct((count,) + shape, BF16),
        compiler_params=BIG_VMEM,
        cost_estimate=cost(
            4 * count * depth * rows * cols, 2 * count * depth * cols + 4 * rows * cols
        ),
        name=name,
    )(order, x_own, x_got, g_own, g_got, *extra)


def weight_grad(x_pair, g_own, name, flip=False):
    n = lax.axis_size("seq")
    x_own, x_got = x_pair
    g_got = swap(g_own, "seq", 1)
    mine = lax.axis_index("seq") // 2
    bits = (n // 2).bit_length() - 1
    relative = [
        sum(((p >> k) & 1) << (bits - 1 - k) for k in range(bits)) for p in range(n // 2)
    ]
    order = mine ^ jnp.array(relative, jnp.int32)
    count = n // 4
    give = grad_blocks(order[count:], x_own, x_got, g_own, g_got, None, flip, name + "_give")
    part = grad_blocks(
        order[:count], x_own, x_got, g_own, g_got, swap(give, "seq", 2), flip, name + "_keep"
    )
    bit = 4
    while bit < n:
        count //= 2
        total = part[:count].astype(F32) + swap(part[count:], "seq", bit).astype(F32)
        bit *= 2
        part = total.astype(BF16) if bit < n else total
    return part[0].astype(F32).T if flip else part[0].astype(F32)


def gain_sum(part):
    n = lax.axis_size("seq")
    total = part
    bit = 1
    while bit < n:
        total = total + swap(total, "seq", bit)
        bit *= 2
    width = part.shape[-1] // n
    return lax.dynamic_slice_in_dim(total, lax.axis_index("seq") * width, width, total.ndim - 1)


def out_back_kernel(valid_ref, g_ref, w_ref, att_ref, do_ref, delta_ref, row_ref):
    rows = g_ref.shape[0]
    do = jnp.dot(g_ref[...], w_ref[...], preferred_element_type=F32).astype(BF16)
    do = jnp.where(valid_ref[...] > 0, do.astype(F32), 0.0)
    do_ref[...] = do.astype(BF16)
    product = do * att_ref[...].astype(F32)
    for k in range(do.shape[1] // HEAD_DIM):
        delta = jnp.sum(product[:, k * HEAD_DIM : (k + 1) * HEAD_DIM], axis=1, keepdims=True)
        delta_ref[k] = delta
        row_ref[k] = jnp.broadcast_to(delta, (rows, HEAD_DIM)).T[0:1, :]


def out_back(valid, grad, w_out, attended):
    rows, depth = grad.shape
    width = w_out.shape[1]
    heads = width // HEAD_DIM
    step = 2 * HEAD_DIM
    column = pl.BlockSpec((rows, step), lambda i: (0, i))
    return pl.pallas_call(
        out_back_kernel,
        grid=(width // step,),
        in_specs=[
            pl.BlockSpec((rows, 1), lambda i: (0, 0)),
            pl.BlockSpec((rows, depth), lambda i: (0, 0)),
            pl.BlockSpec((depth, step), lambda i: (0, i)),
            column,
        ],
        out_specs=[
            column,
            pl.BlockSpec((2, rows, 1), lambda i: (i, 0, 0)),
            pl.BlockSpec((2, 1, rows), lambda i: (i, 0, 0)),
        ],
        out_shape=[
            jax.ShapeDtypeStruct((rows, width), BF16),
            jax.ShapeDtypeStruct((heads, rows, 1), F32),
            jax.ShapeDtypeStruct((heads, 1, rows), F32),
        ],
        compiler_params=BIG_VMEM,
        cost_estimate=cost(2 * rows * depth * width, 2 * (rows + width) * depth),
        name="out_back",
    )(valid, grad, w_out, attended)


def turned_back(grad, cosine, sine):
    return (grad * cosine - pltpu.roll(grad, HEAD_DIM // 2, 1) * sine).astype(BF16)


def dq_kernel(lo_ref, cos_ref, sin_ref, q_ref, do_ref, lse_ref, delta_ref, k_refs, v_refs, out_ref):
    rows = q_ref.shape[1]
    n_parts = k_refs.shape[0]
    scale = HEAD_DIM ** (-0.5) * LOG2E
    sub = rows // 2
    for start in range(0, rows, sub):
        rs = slice(start, start + sub)
        q, do, lo = q_ref[0, rs, :], do_ref[rs, :], lo_ref[rs, :]
        lse, delta = lse_ref[0, rs, :], delta_ref[0, rs, :]
        acc = jnp.zeros((sub, HEAD_DIM), F32)
        for d in range(n_parts):
            k = k_refs[d]
            s = lax.dot_general(q, k, (((1,), (1,)), ((), ())), preferred_element_type=F32)
            u = lax.broadcasted_iota(jnp.int32, s.shape, 1) - d * rows
            seen = u >= lo
            if d == 0:
                t = lax.broadcasted_iota(jnp.int32, s.shape, 0) + start
                seen = seen & (u <= t)
            p = jnp.exp2(jnp.where(seen, s * scale, MASKED) - lse)
            dp = lax.dot_general(
                do, v_refs[d], (((1,), (1,)), ((), ())), preferred_element_type=F32
            )
            ds = (p * (dp - delta)).astype(BF16)
            acc = acc + jnp.dot(ds, k, preferred_element_type=F32)
        out_ref[rs, :] = turned_back(acc * HEAD_DIM ** (-0.5), cos_ref[rs, :], sin_ref[rs, :])


def attention_dq(lo, tables, queries, grad_att, lse, delta, keys, values):
    n_parts, rows, width = queries.shape
    heads = width // HEAD_DIM
    stack = pl.BlockSpec((n_parts, rows, HEAD_DIM), lambda h: (0, 0, h))
    first = pl.BlockSpec((1, rows, HEAD_DIM), lambda h: (0, 0, h))
    column = pl.BlockSpec((rows, HEAD_DIM), lambda h: (0, h))
    stat = pl.BlockSpec((1, rows, 1), lambda h: (h, 0, 0))
    table = pl.BlockSpec((rows, HEAD_DIM), lambda h: (0, 0))
    flops = 6 * rows * rows * n_parts * width
    return pl.pallas_call(
        dq_kernel,
        grid=(heads,),
        in_specs=[pl.BlockSpec((rows, 1), lambda h: (0, 0)), table, table]
        + [first, column, stat, stat, stack, stack],
        out_specs=column,
        out_shape=jax.ShapeDtypeStruct((rows, width), BF16),
        compiler_params=pltpu.CompilerParams(vmem_limit_bytes=48 << 20),
        cost_estimate=pl.CostEstimate(
            flops=flops, bytes_accessed=14 * rows * width * 2, transcendentals=flops // 768
        ),
        name="attention_dq",
    )(lo, *tables, queries, grad_att, lse, delta, keys, values)


def dkv_kernel(lo_ref, cos_ref, sin_ref, k_ref, v_ref, *refs):
    rows = k_ref.shape[1]
    q_refs, refs = refs[0], refs[1:]
    n_parts = q_refs.shape[0]
    do_refs, lse_refs, delta_refs = (refs[k * n_parts : (k + 1) * n_parts] for k in range(3))
    dk_ref, dv_ref = refs[-2:]
    scale = HEAD_DIM ** (-0.5) * LOG2E
    sub = rows // 2
    for start in range(0, rows, sub):
        rs = slice(start, start + sub)
        k, v = k_ref[0, rs, :], v_ref[0, rs, :]
        dk = jnp.zeros((sub, HEAD_DIM), F32)
        dv = jnp.zeros((sub, HEAD_DIM), F32)
        for d in range(n_parts):
            q, do = q_refs[d], do_refs[d][...]
            s = lax.dot_general(k, q, (((1,), (1,)), ((), ())), preferred_element_type=F32)
            u = lax.broadcasted_iota(jnp.int32, s.shape, 0) + start
            seen = u >= lo_ref[:, d * rows : (d + 1) * rows]
            if d == 0:
                seen = seen & (u <= lax.broadcasted_iota(jnp.int32, s.shape, 1))
            lse, delta = lse_refs[d][0], delta_refs[d][0]
            p = jnp.exp2(jnp.where(seen, s * scale - lse, MASKED))
            dv = dv + jnp.dot(p.astype(BF16), do, preferred_element_type=F32)
            dp = lax.dot_general(v, do, (((1,), (1,)), ((), ())), preferred_element_type=F32)
            ds = (p * (dp - delta)).astype(BF16)
            dk = dk + jnp.dot(ds, q, preferred_element_type=F32)
        dk_ref[rs, :] = turned_back(dk * HEAD_DIM ** (-0.5), cos_ref[rs, :], sin_ref[rs, :])
        dv_ref[rs, :] = dv.astype(BF16)


def attention_dkv(lo_row, tables, keys, values, queries, grad_atts, lses, deltas):
    n_parts, rows, width = keys.shape
    heads = width // HEAD_DIM
    stack = pl.BlockSpec((n_parts, rows, HEAD_DIM), lambda h: (0, 0, h))
    first = pl.BlockSpec((1, rows, HEAD_DIM), lambda h: (0, 0, h))
    column = pl.BlockSpec((rows, HEAD_DIM), lambda h: (0, h))
    stat = pl.BlockSpec((1, 1, rows), lambda h: (h, 0, 0))
    table = pl.BlockSpec((rows, HEAD_DIM), lambda h: (0, 0))
    flops = 8 * rows * rows * n_parts * width
    return pl.pallas_call(
        dkv_kernel,
        grid=(heads,),
        in_specs=[pl.BlockSpec((1, n_parts * rows), lambda h: (0, 0)), table, table]
        + [first, first, stack]
        + [column] * n_parts
        + [stat] * (2 * n_parts),
        out_specs=[column, column],
        out_shape=[jax.ShapeDtypeStruct((rows, width), BF16)] * 2,
        compiler_params=pltpu.CompilerParams(vmem_limit_bytes=48 << 20),
        cost_estimate=pl.CostEstimate(
            flops=flops, bytes_accessed=16 * rows * width * 2, transcendentals=flops // 1024
        ),
        name="attention_dkv",
    )(lo_row, *tables, keys, values, queries, *grad_atts, *lses, *deltas)


def forward_kernel(
    devices,
    cores,
    x_ref,
    gain_one_ref,
    gain_two_ref,
    cos_ref,
    sin_ref,
    lo_ref,
    valid_ref,
    wk_hbm,
    wv_hbm,
    wq_hbm,
    wo_hbm,
    prev_k_hbm,
    prev_v_hbm,
    k_out,
    v_out,
    q_out,
    one_keep_out,
    one_give_out,
    mid_out,
    two_out,
    two_keep_out,
    two_give_out,
    att_out,
    lse_out,
    row_out,
    kx,
    vx,
    qx,
    wk,
    wv,
    wq,
    wo,
    normed,
    flipped,
    tops,
    totals,
    acc,
    core_send,
    core_got,
    chip,
    y_got,
    own_half,
    other_half,
    mid,
    two_blocks,
    load_sem,
    store_sem,
    k_send,
    k_recv,
    v_send,
    v_recv,
    q_send,
    q_recv,
    sum_send,
    sum_recv,
):
    rows, width = x_ref.shape
    heads = kx.shape[2] // HEAD_DIM
    s, h = lax.axis_index("seq"), lax.axis_index("head")
    odd, core = lax.rem(s, 2), lax.rem(h, 2)
    pair = s + 1 - 2 * odd
    mate = h + 1 - 2 * core
    across = lax.rem(h + cores // 2, cores)
    has_left, has_right = s >= 2, s < devices - 2
    scale = HEAD_DIM ** (-0.5) * LOG2E

    def remote(src, dst, send, recv, seq, head):
        return pltpu.make_async_remote_copy(
            src_ref=src,
            dst_ref=dst,
            send_sem=send,
            recv_sem=recv,
            device_id=(seq, head),
            device_id_type=pl.DeviceIdType.MESH,
        )

    loads = [
        pltpu.make_async_copy(src, dst, load_sem.at[i])
        for i, (src, dst) in enumerate(((wk_hbm, wk), (wv_hbm, wv), (wq_hbm, wq), (wo_hbm, wo)))
    ]
    for load in loads:
        load.start()

    barrier = pltpu.get_barrier_semaphore()

    def greet(seq, head):
        pl.semaphore_signal(
            barrier, inc=1, device_id=(seq, head), device_id_type=pl.DeviceIdType.MESH
        )

    greet(pair, h)
    greet(s, mate)
    greet(s, across)

    @pl.when(has_left)
    def _():
        greet(s - 2, h)

    @pl.when(has_right)
    def _():
        greet(s + 2, h)

    step = rows // 4

    def normalize(i, _):
        at = pl.ds(pl.multiple_of(i * step, step), step)
        x = x_ref[at, :].astype(F32)
        root = lax.rsqrt(jnp.mean(x * x, axis=-1, keepdims=True) + EPS)
        normed[at, :] = (x * root * gain_one_ref[...]).astype(BF16)
        return 0

    lax.fori_loop(0, 4, normalize, 0)

    def turn_into(weight, out):
        raw = jnp.dot(normed[...], weight[...], preferred_element_type=F32)
        for k in range(heads):
            u = raw[:, k * HEAD_DIM : (k + 1) * HEAD_DIM]
            u = u * cos_ref[...] + pltpu.roll(u, HEAD_DIM // 2, 1) * sin_ref[...]
            out[0, :, k * HEAD_DIM : (k + 1) * HEAD_DIM] = u.astype(BF16)

    loads[0].wait()
    turn_into(wk, kx)

    inner = has_left & has_right

    @pl.when(inner)
    def _():
        pl.semaphore_wait(barrier, 5)

    @pl.when(jnp.logical_not(inner))
    def _():
        pl.semaphore_wait(barrier, 4)

    def hop(buf, send, recv, slot, seq, src, dst):
        return remote(buf.at[src], buf.at[dst], send.at[slot], recv.at[slot], seq, h)

    chains = {
        "k": (kx, k_send, k_recv, s + 2, has_right, has_left, 0),
        "v": (vx, v_send, v_recv, s + 2, has_right, has_left, 0),
        "q": (qx, q_send, q_recv, s - 2, has_left, has_right, 1),
    }

    def first_hops(name):
        buf, send, recv, seq, sends, gets, early = chains[name]

        @pl.when(sends)
        def _():
            hop(buf, send, recv, 0, seq, 0, 2).start()

        @pl.when(odd == early)
        def _():
            hop(buf, send, recv, 2, pair, 0, 1).start()

    def second_hops(name):
        buf, send, recv, seq, sends, gets, early = chains[name]

        @pl.when(gets)
        def _():
            hop(buf, send, recv, 0, seq, 0, 2).wait_recv()

        @pl.when(sends)
        def _():
            hop(buf, send, recv, 1, seq, 2, 4).start()

        @pl.when(odd == early)
        def _():
            hop(buf, send, recv, 3, pair, 2, 3).start()

        @pl.when(odd != early)
        def _():
            hop(buf, send, recv, 2, pair, 2, 1).start()

    def third_hops(name):
        buf, send, recv, seq, sends, gets, early = chains[name]

        @pl.when(gets)
        def _():
            hop(buf, send, recv, 1, seq, 2, 4).wait_recv()

        @pl.when(odd != early)
        def _():
            hop(buf, send, recv, 3, pair, 4, 3).start()

    def pair_arrived(name, slot):
        buf, send, recv, seq, sends, gets, early = chains[name]
        hop(buf, send, recv, slot, pair, 0, 1 if slot == 2 else 3).wait_recv()

    def all_sent(name):
        buf, send, recv, seq, sends, gets, early = chains[name]

        @pl.when(sends)
        def _():
            hop(buf, send, recv, 0, seq, 0, 2).wait_send()
            hop(buf, send, recv, 1, seq, 2, 4).wait_send()

        hop(buf, send, recv, 2, pair, 0, 1).wait_send()
        hop(buf, send, recv, 3, pair, 0, 3).wait_send()

    first_hops("k")
    loads[1].wait()
    vx[0] = jnp.dot(normed[...], wv[...], preferred_element_type=F32).astype(BF16)
    first_hops("v")

    @pl.when(jnp.logical_not(has_left))
    def _():
        copies = []
        for i, (src, dst) in enumerate(((prev_k_hbm, kx), (prev_v_hbm, vx))):
            for j, d in enumerate((2, 4)):
                at = pl.multiple_of((s - d) * rows + WINDOW, rows)
                copies.append(
                    pltpu.make_async_copy(
                        src.at[pl.ds(at, rows), :], dst.at[d], load_sem.at[4 + 2 * i + j]
                    )
                )
        for copy in copies:
            copy.start()
        for copy in copies:
            copy.wait()

    @pl.when(jnp.logical_not(has_right))
    def _():
        qx[2] = jnp.zeros_like(qx[2])
        qx[4] = jnp.zeros_like(qx[4])

    loads[2].wait()
    turn_into(wq, qx)
    first_hops("q")

    for i in range(4):
        flip_at = slice(i * step, (i + 1) * step)
        flipped[:, :, flip_at] = normed[flip_at, :].T.reshape(devices, width // devices, step)
    split = flipped.reshape(devices // 2, 2, width // devices, rows)
    stores = [
        pltpu.make_async_copy(split.at[:, odd], one_keep_out, store_sem.at[0]),
        pltpu.make_async_copy(split.at[:, 1 - odd], one_give_out, store_sem.at[1]),
    ]
    stores[0].start()
    stores[1].start()

    sub = rows // 2

    def attend(d):
        def body(i, _):
            k = i // 2
            at = pl.ds(pl.multiple_of((i % 2) * sub, sub), sub)
            lanes = pl.ds(pl.multiple_of(k * HEAD_DIM, HEAD_DIM), HEAD_DIM)
            scores = dot_nt(qx[0, at, lanes], kx[d, :, lanes])
            u = lax.broadcasted_iota(jnp.int32, scores.shape, 1) - d * rows
            seen = u >= lo_ref[at, :]
            if d == 0:
                t = lax.broadcasted_iota(jnp.int32, scores.shape, 0) + (i % 2) * sub
                seen = seen & (u <= t)
            scores = jnp.where(seen, scores * scale, MASKED)
            top = jnp.max(scores, axis=1, keepdims=True)
            if d > 0:
                old = tops[k, at, :]
                top = jnp.maximum(top, old)
            p = jnp.exp2(scores - top)
            total = jnp.sum(p, axis=1, keepdims=True)
            mixed = jnp.dot(p.astype(BF16), vx[d, :, lanes], preferred_element_type=F32)
            if d > 0:
                fade = jnp.exp2(old - top)
                total = total + totals[k, at, :] * fade
                mixed = mixed + acc[at, lanes] * fade
            tops[k, at, :] = top
            totals[k, at, :] = total
            acc[at, lanes] = mixed
            return 0

        lax.fori_loop(0, 2 * heads, body, 0)

    attend(0)
    second_hops("k")
    second_hops("v")
    attend(2)
    pair_arrived("k", 2)
    pair_arrived("v", 2)
    attend(1)
    third_hops("k")
    third_hops("v")
    attend(4)
    second_hops("q")
    pair_arrived("k", 3)
    pair_arrived("v", 3)
    attend(3)
    stores.append(pltpu.make_async_copy(kx, k_out, store_sem.at[2]))
    stores.append(pltpu.make_async_copy(vx, v_out, store_sem.at[3]))
    stores[2].start()
    stores[3].start()

    for k in range(heads):
        lanes = slice(k * HEAD_DIM, (k + 1) * HEAD_DIM)
        out = jnp.where(valid_ref[...] > 0, acc[:, lanes] / totals[k], 0.0)
        att_out[:, lanes] = out.astype(BF16)
        lse = tops[k] + jnp.log2(totals[k])
        lse_out[k] = lse
        row_out[k] = jnp.broadcast_to(lse, (rows, HEAD_DIM)).T[0:1, :]

    half = width // 2
    loads[3].wait()
    mine = pl.ds(pl.multiple_of(core * half, half), half)
    theirs = pl.ds(pl.multiple_of((1 - core) * half, half), half)

    def to_mate(i):
        return remote(core_send.at[i], core_got.at[i], sum_send.at[i], sum_recv.at[i], s, mate)

    def over(i):
        return remote(chip.at[i], y_got.at[i], sum_send.at[4 + i], sum_recv.at[4 + i], s, across)

    def back(i):
        return remote(
            own_half.at[i], other_half.at[i], sum_send.at[8 + i], sum_recv.at[8 + i], s, mate
        )

    for i in range(4):
        part = dot_nt(att_out[i * step : (i + 1) * step, :], wo[theirs, :])
        core_send[i] = part.astype(BF16)
        to_mate(i).start()
    for i in range(4):
        part = dot_nt(att_out[i * step : (i + 1) * step, :], wo[mine, :])
        to_mate(i).wait_recv()
        chip[i] = (part + core_got[i].astype(F32)).astype(BF16)
        over(i).start()
    third_hops("q")

    def finish(i):
        at = slice(i * step, (i + 1) * step)
        back(i).wait_recv()
        own, other = own_half[i].astype(F32), other_half[i].astype(F32)
        low = core == 0
        branch = jnp.concatenate([jnp.where(low, own, other), jnp.where(low, other, own)], axis=1)
        total = x_ref[at, :].astype(F32) + branch
        mid[at, :] = total
        root = lax.rsqrt(jnp.mean(total * total, axis=-1, keepdims=True) + EPS)
        two = (total * root * gain_two_ref[...]).astype(BF16)
        normed[at, :] = two
        depth = width // devices
        for j in range(devices):
            two_blocks[j, at, :] = two[:, j * depth : (j + 1) * depth]

    for i in range(4):
        over(i).wait_recv()
        own_half[i] = (chip[i].astype(F32) + y_got[i].astype(F32)).astype(BF16)
        back(i).start()
        if i > 0:
            finish(i - 1)
    finish(3)
    blocks = two_blocks.reshape(devices // 2, 2, rows, width // devices)
    for src, dst in (
        (mid, mid_out),
        (normed, two_out),
        (blocks.at[:, odd], two_keep_out),
        (blocks.at[:, 1 - odd], two_give_out),
    ):
        stores.append(pltpu.make_async_copy(src, dst, store_sem.at[len(stores)]))
        stores[-1].start()
    pair_arrived("q", 2)
    pair_arrived("q", 3)
    stores.append(pltpu.make_async_copy(qx, q_out, store_sem.at[len(stores)]))
    stores[-1].start()
    for name in chains:
        all_sent(name)
    for i in range(4):
        to_mate(i).wait_send()
        over(i).wait_send()
        back(i).wait_send()
    for store in stores:
        store.wait()


def forward(devices, cores, x, gains, tables, low, valid, weights, w_out, prevs):
    rows, width = x.shape
    cols = weights[0].shape[1]
    heads = cols // HEAD_DIM
    depth = width // devices
    parts = WINDOW // rows + 1
    step = rows // 4
    vmem = pl.BlockSpec(memory_space=pltpu.VMEM)
    hbm = pl.BlockSpec(memory_space=pl.ANY)

    def shape(*dims, dtype=BF16):
        return jax.ShapeDtypeStruct(dims, dtype)

    blocks = pltpu.VMEM((4, step, width // 2), BF16)
    dma = pltpu.SemaphoreType.DMA
    return pl.pallas_call(
        functools.partial(forward_kernel, devices, cores),
        in_specs=[vmem] * 7 + [hbm] * 6,
        out_specs=[hbm] * 9 + [vmem] * 3,
        out_shape=[
            shape(parts, rows, cols),
            shape(parts, rows, cols),
            shape(parts, rows, cols),
            shape(devices // 2, depth, rows),
            shape(devices // 2, depth, rows),
            shape(rows, width, dtype=F32),
            shape(rows, width),
            shape(devices // 2, rows, depth),
            shape(devices // 2, rows, depth),
            shape(rows, cols),
            shape(heads, rows, 1, dtype=F32),
            shape(heads, 1, rows, dtype=F32),
        ],
        scratch_shapes=[pltpu.VMEM((parts, rows, cols), BF16)] * 3
        + [pltpu.VMEM((width, cols), BF16)] * 4
        + [
            pltpu.VMEM((rows, width), BF16),
            pltpu.VMEM((devices, depth, rows), BF16),
            pltpu.VMEM((heads, rows, 1), F32),
            pltpu.VMEM((heads, rows, 1), F32),
            pltpu.VMEM((rows, cols), F32),
        ]
        + [blocks] * 6
        + [
            pltpu.VMEM((rows, width), F32),
            pltpu.VMEM((devices, rows, depth), BF16),
            dma((8,)),
            dma((9,)),
        ]
        + [dma((4,))] * 6
        + [dma((12,))] * 2,
        compiler_params=pltpu.CompilerParams(
            collective_id=0, has_side_effects=True, vmem_limit_bytes=56 << 20
        ),
        cost_estimate=cost(10 * rows * width * cols, 40 << 20),
        name="forward",
    )(x, *gains, *tables, low, valid, *weights, w_out, *prevs)


def first_key(rows, lengths, total):
    padded = (lengths + PAD - 1) // PAD * PAD
    starts = jnp.cumsum(padded) - padded
    start_row = jnp.zeros_like(rows)
    length_row = jnp.full_like(rows, 0) + lengths[0]
    low_row = jnp.full_like(rows, -BIG)
    for r in range(1, NSEQ):
        inside = rows >= starts[r]
        start_row = jnp.where(inside, starts[r], start_row)
        low_row = jnp.where(inside, starts[r], low_row)
        length_row = jnp.where(inside, lengths[r], length_row)
    position = rows - start_row
    valid = position < length_row
    low = jnp.where(valid, jnp.maximum(low_row, rows - (WINDOW - 1)), rows)
    low = jnp.where(rows < total, low, BIG)
    return low, valid, position


def on_device(
    tokens,
    gain_attn,
    gain_mlp,
    w_query,
    w_key,
    w_value,
    w_out,
    w_gate,
    w_up,
    w_down,
    prev_keys,
    prev_values,
    lengths,
    out_grad,
):
    rows = tokens.shape[0]
    width = w_query.shape[1]
    heads = width // HEAD_DIM
    devices = lax.axis_size("seq")
    index = lax.axis_index("seq")
    odd = (index & 1) == 1
    first_row = index * rows
    far = WINDOW // rows
    low, valid, position = first_key(
        first_row + jnp.arange((far + 1) * rows, dtype=jnp.int32), lengths, devices * rows
    )
    low = low - first_row
    low_col = low[:rows, None]
    low_row = low[None, :]
    valid_col = valid[:rows, None]
    valid_int = valid_col.astype(jnp.int32)
    half = HEAD_DIM // 2
    freq = jnp.exp(-math.log(10000.0) * (2.0 * jnp.arange(half, dtype=F32) / HEAD_DIM))
    angle = position[:rows].astype(F32)[:, None] * freq[None, :]
    cos_one, sin_one = jnp.cos(angle), jnp.sin(angle)
    tables = (
        jnp.concatenate([cos_one, cos_one], axis=1),
        jnp.concatenate([-sin_one, sin_one], axis=1),
    )
    bits = jnp.stack([index & 1, lax.axis_index("head") & 1]).astype(jnp.int32)
    gain_one, gain_two = gain_attn[None, :], gain_mlp[None, :]

    (
        keys,
        values,
        queries,
        one_keep,
        one_give,
        mid,
        normed_two,
        two_keep,
        two_give,
        attended,
        lse,
        lse_row,
    ) = forward(
        devices,
        lax.axis_size("head"),
        tokens,
        (gain_one, gain_two),
        tables,
        low_col,
        valid_int,
        (w_key, w_value, w_query),
        w_out,
        (prev_keys, prev_values),
    )

    def lent(own):
        two = shifted(own, -2)
        one = swap(jnp.where(odd, own, two), "seq", 1)
        four = shifted(two, -2)
        three = swap(jnp.where(odd, two, four), "seq", 1)
        return [own, one, two, three, four]

    one_pair = (one_keep, swap(one_give, "seq", 1))
    out_keep, out_give = by_rows(split_kernel, bits, (out_grad,), -1, (), "split", "split")
    out_pair = (out_keep, swap(out_give, "seq", 1))

    lses_lent = lent(lse_row)
    two_pair = (two_keep, swap(two_give, "seq", 1))
    act, grad_gate, grad_up, norm_keep, norm_give, branch_keep, branch_give = mlp(
        bits, normed_two, out_grad, w_gate.T, w_up.T, w_down.T
    )
    own, other = head_sum_of(norm_give, norm_keep)
    w_down_grad = weight_grad(out_pair, act, "down", True)
    w_gate_grad = weight_grad(two_pair, grad_gate, "gate", True)
    w_up_grad = weight_grad(two_pair, grad_up, "up", True)

    grad_mid, gain_mlp_part, grad_attn_branch, mid_keep, mid_give = by_rows(
        back_kernel,
        bits,
        (mid, own, other, gain_two, out_grad),
        3,
        (F32, F32, BF16),
        "flip",
        "mid_back",
        part=1,
    )
    mid_pair = (mid_keep, swap(mid_give, "seq", 1))
    own, other = head_sum_of(branch_give, branch_keep)
    low_half = bits[1] == 0
    branch = jnp.concatenate(
        [jnp.where(low_half, own, other), jnp.where(low_half, other, own)], axis=1
    )
    block_out = (mid + branch.astype(F32)).astype(BF16)

    grad_att, delta, delta_row = out_back(valid_int, grad_attn_branch, w_out, attended)
    grad_atts = lent(grad_att)
    deltas_lent = lent(delta_row)
    grad_query_raw = attention_dq(low_col, tables, queries, grad_att, lse, delta, keys, values)
    grad_key_raw, grad_value_raw = attention_dkv(
        low_row, tables, keys, values, queries, grad_atts, lses_lent, deltas_lent
    )

    w_out_grad = weight_grad(mid_pair, attended, "wout")
    w_query_grad = weight_grad(one_pair, grad_query_raw, "query")
    w_key_grad = weight_grad(one_pair, grad_key_raw, "key")
    w_value_grad = weight_grad(one_pair, grad_value_raw, "value")
    own, other = head_sum(
        bits,
        (grad_query_raw, grad_key_raw, grad_value_raw),
        (w_query, w_key, w_value),
        "norm_one",
    )
    tokens_grad, gain_attn_part = by_rows(
        back_kernel,
        bits,
        (tokens, own, other, gain_one, grad_mid),
        3,
        (BF16, F32),
        False,
        "tokens_back",
        part=1,
    )
    gains = gain_sum(jnp.concatenate([gain_attn_part, gain_mlp_part], axis=0))
    gain_attn_grad, gain_mlp_grad = gains[0], gains[1]
    return (
        block_out,
        tokens_grad,
        gain_attn_grad,
        gain_mlp_grad,
        w_query_grad,
        w_key_grad,
        w_value_grad,
        w_out_grad,
        w_gate_grad,
        w_up_grad,
        w_down_grad,
    )


def solution(mesh):
    by_head = P(None, "head")
    both = P("seq", "head")
    placed = (P("seq", None), P(), P()) + (by_head,) * 9 + (P(), P("seq", None))
    return jax.shard_map(
        on_device,
        mesh=mesh,
        in_specs=placed,
        out_specs=(P("seq", None), P("seq", None), P("seq"), P("seq")) + (both,) * 7,
        check_vma=False,
    )
```

```python
import functools
import math

import jax
import jax.numpy as jnp
from jax import lax
from jax.experimental import pallas as pl
from jax.experimental.pallas import tpu as pltpu
from jax.sharding import PartitionSpec as P

HEAD_DIM = 128
WINDOW = 2048
PAD = 64
NSEQ = 4
EPS = 1e-06
MASKED = -1e30
LOG2E = 1.4426950408889634
BIG = 1 << 28
F32 = jnp.float32
BF16 = jnp.bfloat16


def swap(block, axis, bit):
    return lax.ppermute(block, axis, [(i, i ^ bit) for i in range(lax.axis_size(axis))])


def shifted(block, distance):
    n = lax.axis_size("seq")
    return lax.ppermute(
        block, "seq", [(i, i + distance) for i in range(n) if 0 <= i + distance < n]
    )


BIG_VMEM = pltpu.CompilerParams(vmem_limit_bytes=48 << 20)


def cost(flops, moved):
    return pl.CostEstimate(flops=int(flops), bytes_accessed=int(moved), transcendentals=0)


def dot_nt(left, right):
    return lax.dot_general(left, right, (((1,), (1,)), ((), ())), preferred_element_type=F32)


def row_blocks(width, step):
    return pl.BlockSpec((step, width), lambda i, bits: (i, 0))


def joined(bits_ref, own_ref, other_ref):
    low = bits_ref[1] == 0
    own, other = own_ref[...].astype(F32), other_ref[...].astype(F32)
    return jnp.concatenate([jnp.where(low, own, other), jnp.where(low, other, own)], axis=1)


def back_kernel(
    bits_ref, x_ref, own_ref, other_ref, gain_ref, add_ref, out_ref, part_ref
):
    x = x_ref[...].astype(F32)
    scale = lax.rsqrt(jnp.mean(x * x, axis=-1, keepdims=True) + EPS)
    grad = joined(bits_ref, own_ref, other_ref)
    unit = x * scale
    grad_unit = grad * gain_ref[...]
    total = add_ref[...].astype(F32) + scale * (
        grad_unit - unit * jnp.mean(grad_unit * unit, axis=-1, keepdims=True)
    )
    out_ref[...] = total.astype(out_ref.dtype)
    part = jnp.sum(grad * unit, axis=0, keepdims=True)

    @pl.when(pl.program_id(0) == 0)
    def _():
        part_ref[...] = part

    @pl.when(pl.program_id(0) > 0)
    def _():
        part_ref[...] += part


def by_rows(kernel, bits, arrays, gains_at, outs, name, part=None):
    rows, width = arrays[0].shape
    step = rows // 4
    in_specs = [
        pl.BlockSpec((1, width), lambda i, bits: (0, 0))
        if k == gains_at
        else row_blocks(a.shape[1], step)
        for k, a in enumerate(arrays)
    ]
    out_specs, out_shape = [], []
    for k, dtype in enumerate(outs):
        if k == part:
            out_specs.append(pl.BlockSpec((1, width), lambda i, bits: (0, 0)))
            out_shape.append(jax.ShapeDtypeStruct((1, width), F32))
        else:
            out_specs.append(row_blocks(width, step))
            out_shape.append(jax.ShapeDtypeStruct((rows, width), dtype))
    return pl.pallas_call(
        kernel,
        grid_spec=pltpu.PrefetchScalarGridSpec(
            num_scalar_prefetch=1, grid=(rows // step,), in_specs=in_specs, out_specs=out_specs
        ),
        out_shape=out_shape,
        compiler_params=BIG_VMEM,
        cost_estimate=cost(rows * width * 10, rows * width * 2 * (len(arrays) + len(out_shape))),
        name=name,
    )(bits, *arrays)


def half_kernel(pairs, flip, added, bits_ref, *refs):
    total = refs[2 * pairs][...].astype(F32) if added else None
    for k in range(pairs):
        term = dot_nt(refs[k][...], refs[pairs + k][...])
        total = term if total is None else total + term
    refs[-1][...] = total.astype(BF16)


def half_product(bits, lefts, rights, flip, added, name):
    rows = lefts[0].shape[0]
    width = rights[0].shape[0] // 2
    step = min(width, 512)
    steps = width // step

    def at(i, bits):
        return ((bits[1] ^ flip) * steps + i, 0)

    specs = [pl.BlockSpec(a.shape, lambda i, bits: (0, 0)) for a in lefts]
    specs += [pl.BlockSpec((step, a.shape[1]), at) for a in rights]
    extra = []
    if added is not None:
        extra = [added]
        specs.append(pl.BlockSpec((rows, step), lambda i, bits: (0, i)))
    depth = sum(a.shape[1] for a in lefts)
    return pl.pallas_call(
        functools.partial(half_kernel, len(lefts), flip, added is not None),
        grid_spec=pltpu.PrefetchScalarGridSpec(
            num_scalar_prefetch=1,
            grid=(steps,),
            in_specs=specs,
            out_specs=pl.BlockSpec((rows, step), lambda i, bits: (0, i)),
        ),
        out_shape=jax.ShapeDtypeStruct((rows, width), BF16),
        compiler_params=BIG_VMEM,
        cost_estimate=cost(2 * rows * depth * width, 2 * (rows + width) * depth),
        name=name,
    )(bits, *lefts, *rights, *extra)


def mlp_kernel(x_ref, g_ref, wg_ref, wu_ref, wd_ref, act_ref, gg_ref, gu_ref):
    x, g = x_ref[...], g_ref[...]
    gate = dot_nt(wg_ref[...], x)
    up = dot_nt(wu_ref[...], x)
    grad = dot_nt(wd_ref[...], g)
    sig = 1.0 / (1.0 + jnp.exp(-gate))
    silu = gate * sig
    act_ref[...] = (silu * up).astype(BF16)
    gg_ref[...] = (grad * up * sig * (1.0 + gate * (1.0 - sig))).astype(BF16)
    gu_ref[...] = (grad * silu).astype(BF16)


def mlp(x, grad, w_gate, w_up, w_down):
    rows, depth = x.shape
    width = w_gate.shape[0]
    step = -(-width // (4 * 32)) * 32
    whole = pl.BlockSpec((rows, depth), lambda i: (0, 0))
    block = pl.BlockSpec((step, depth), lambda i: (i, 0))
    return pl.pallas_call(
        mlp_kernel,
        grid=(pl.cdiv(width, step),),
        in_specs=[whole, whole, block, block, block],
        out_specs=[pl.BlockSpec((step, rows), lambda i: (i, 0))] * 3,
        out_shape=[jax.ShapeDtypeStruct((width, rows), BF16)] * 3,
        compiler_params=BIG_VMEM,
        cost_estimate=cost(6 * rows * depth * width, 6 * depth * width),
        name="mlp",
    )(x, grad, w_gate, w_up, w_down)


def back_products_kernel(bits_ref, gg_ref, gu_ref, wg_ref, wu_ref, out_ref, gg, gu):
    @pl.when(pl.program_id(0) == 0)
    def _():
        gg[...] = gg_ref[...].T
        gu[...] = gu_ref[...].T

    total = jnp.dot(gg[...], wg_ref[...], preferred_element_type=F32)
    total = total + jnp.dot(gu[...], wu_ref[...], preferred_element_type=F32)
    out_ref[0] = total.astype(BF16)


def back_products(bits, grad_gate, grad_up, w_gate, w_up):
    cols, rows = grad_gate.shape
    width = w_gate.shape[1]
    step = width // 4
    whole = pl.BlockSpec((cols, rows), lambda i, bits: (0, 0))
    column = pl.BlockSpec(
        (cols, step), lambda i, bits: (0, 2 * (bits[1] ^ 1 ^ (i // 2)) + i % 2)
    )
    return pl.pallas_call(
        back_products_kernel,
        grid_spec=pltpu.PrefetchScalarGridSpec(
            num_scalar_prefetch=1,
            grid=(4,),
            in_specs=[whole, whole, column, column],
            out_specs=pl.BlockSpec((1, rows, step), lambda i, bits: (i // 2, 0, i % 2)),
            scratch_shapes=[pltpu.VMEM((rows, cols), BF16)] * 2,
        ),
        out_shape=jax.ShapeDtypeStruct((2, rows, width // 2), BF16),
        compiler_params=BIG_VMEM,
        cost_estimate=cost(4 * rows * cols * width, 4 * cols * width),
        name="back_products",
    )(bits, grad_gate, grad_up, w_gate, w_up)


def blocks_kernel(order_ref, flip, xa_ref, xb_ref, ga_ref, gb_ref, *refs):
    if flip:
        total = jnp.dot(ga_ref[...], xa_ref[0], preferred_element_type=F32)
        total = total + jnp.dot(gb_ref[...], xb_ref[0], preferred_element_type=F32)
    else:
        total = jnp.dot(xa_ref[0], ga_ref[...], preferred_element_type=F32)
        total = total + jnp.dot(xb_ref[0], gb_ref[...], preferred_element_type=F32)
    if len(refs) == 2:
        total = total + refs[0][0].astype(F32)
    refs[-1][0] = total.astype(BF16)


def grad_blocks(order, x_own, x_got, g_own, g_got, added, flip, name):
    count = order.shape[0]
    if flip:
        _, rows, depth = x_own.shape
        cols = g_own.shape[0]
        shape = (cols, depth)
    else:
        _, depth, rows = x_own.shape
        cols = g_own.shape[1]
        shape = (depth, cols)
    x_spec = pl.BlockSpec((1,) + x_own.shape[1:], lambda i, order: (order[i], 0, 0))
    g_spec = pl.BlockSpec(g_own.shape, lambda i, order: (0, 0))
    out_spec = pl.BlockSpec((1,) + shape, lambda i, order: (i, 0, 0))
    extra = [] if added is None else [added]

    def kernel(order_ref, *refs):
        blocks_kernel(order_ref, flip, *refs)

    return pl.pallas_call(
        kernel,
        grid_spec=pltpu.PrefetchScalarGridSpec(
            num_scalar_prefetch=1,
            grid=(count,),
            in_specs=[x_spec, x_spec, g_spec, g_spec] + [out_spec] * len(extra),
            out_specs=out_spec,
        ),
        out_shape=jax.ShapeDtypeStruct((count,) + shape, BF16),
        compiler_params=BIG_VMEM,
        cost_estimate=cost(
            4 * count * depth * rows * cols, 2 * count * depth * cols + 4 * rows * cols
        ),
        name=name,
    )(order, x_own, x_got, g_own, g_got, *extra)


def shard_orders(first, n):
    bits = [1 << k for k in range(n.bit_length() - 1)]
    return [first] + [b for b in bits if b != first]


class Order:
    def __init__(self):
        self.last = None

    def after(self, operand):
        if self.last is None:
            return operand
        return lax.optimization_barrier((operand, self.last))[0]

    def ran(self, result):
        self.last = result
        return result


class WeightGrad:
    def __init__(self, order, x_pair, g_own, g_got, first, name, flip=False):
        n = lax.axis_size("seq")
        self.order, self.flip, self.name = order, flip, name
        self.operands = (*x_pair, g_own, g_got)
        self.bits = shard_orders(first, n)
        index = lax.axis_index("seq")
        shards = []
        for p in range(n // 2):
            apart = sum(
                b for k, b in enumerate(self.bits[1:]) if (p >> (len(self.bits) - 2 - k)) & 1
            )
            shard = index ^ apart
            shards.append(shard // (2 * first) * first + shard % first)
        self.shards = jnp.stack(shards).astype(jnp.int32)
        self.count = n // 4

    def blocks(self, shards, added, name):
        return self.order.ran(
            grad_blocks(
                self.order.after(shards), *self.operands, added, self.flip, self.name + name
            )
        )

    def give(self):
        give = self.blocks(self.shards[self.count :], None, "_give")
        self.got = swap(give, "seq", self.bits[1])

    def keep(self):
        self.part = self.blocks(self.shards[: self.count], self.got, "_keep")
        left = self.count // 2
        self.got = swap(self.part[left:], "seq", self.bits[2])

    def finish(self):
        left, part = self.count // 2, self.part
        total = part[:left].astype(F32) + self.got.astype(F32)
        for bit in self.bits[3:]:
            left //= 2
            part = total.astype(BF16)
            total = part[:left].astype(F32) + swap(part[left:], "seq", bit).astype(F32)
        return total[0].T if self.flip else total[0]


def gain_sum(part):
    n = lax.axis_size("seq")
    total = part
    bit = 1
    while bit < n:
        total = total + swap(total, "seq", bit)
        bit *= 2
    width = part.shape[-1] // n
    return lax.dynamic_slice_in_dim(total, lax.axis_index("seq") * width, width, total.ndim - 1)


def turned_back(grad, cosine, sine):
    return (grad * cosine - pltpu.roll(grad, HEAD_DIM // 2, 1) * sine).astype(BF16)


def place(devices, cores):
    s, h = lax.axis_index("seq"), lax.axis_index("head")
    odd, core = lax.rem(s, 2), lax.rem(h, 2)
    pair = s + 1 - 2 * odd
    mate = h + 1 - 2 * core
    across = lax.rem(h + cores // 2, cores)
    return s, h, odd, core, pair, mate, across


def remote(src, dst, send, recv, seq, head):
    return pltpu.make_async_remote_copy(
        src_ref=src,
        dst_ref=dst,
        send_sem=send,
        recv_sem=recv,
        device_id=(seq, head),
        device_id_type=pl.DeviceIdType.MESH,
    )


def greet(seq, head):
    pl.semaphore_signal(
        pltpu.get_barrier_semaphore(),
        inc=1,
        device_id=(seq, head),
        device_id_type=pl.DeviceIdType.MESH,
    )


def greet_all(devices, cores):
    s, h, odd, core, pair, mate, across = place(devices, cores)
    greet(pair, h)
    greet(s, mate)
    greet(s, across)

    @pl.when(s >= 2)
    def _():
        greet(s - 2, h)

    @pl.when(s < devices - 2)
    def _():
        greet(s + 2, h)


def all_greeted(devices):
    s = lax.axis_index("seq")
    inner = (s >= 2) & (s < devices - 2)

    @pl.when(inner)
    def _():
        pl.semaphore_wait(pltpu.get_barrier_semaphore(), 5)

    @pl.when(jnp.logical_not(inner))
    def _():
        pl.semaphore_wait(pltpu.get_barrier_semaphore(), 4)


class Chain:
    def __init__(self, devices, buf, send, recv, side):
        self.s, self.h = lax.axis_index("seq"), lax.axis_index("head")
        odd = lax.rem(self.s, 2)
        self.pair = self.s + 1 - 2 * odd
        self.buf, self.send, self.recv = buf, send, recv
        self.next = self.s + 2 * side
        left, right = self.s >= 2, self.s < devices - 2
        self.sends, self.gets = (right, left) if side > 0 else (left, right)
        self.early = odd == (0 if side > 0 else 1)
        self.late = odd == (1 if side > 0 else 0)

    def hop(self, slot, seq, src, dst):
        return remote(
            self.buf.at[src], self.buf.at[dst], self.send.at[slot], self.recv.at[slot], seq, self.h
        )

    def first(self):
        @pl.when(self.sends)
        def _():
            self.hop(0, self.next, 0, 2).start()

        @pl.when(self.early)
        def _():
            self.hop(2, self.pair, 0, 1).start()

    def second(self):
        @pl.when(self.gets)
        def _():
            self.hop(0, self.next, 0, 2).wait_recv()

        @pl.when(self.sends)
        def _():
            self.hop(1, self.next, 2, 4).start()

        @pl.when(self.early)
        def _():
            self.hop(3, self.pair, 2, 3).start()

        @pl.when(self.late)
        def _():
            self.hop(2, self.pair, 2, 1).start()

    def third(self):
        @pl.when(self.gets)
        def _():
            self.hop(1, self.next, 2, 4).wait_recv()

        @pl.when(self.late)
        def _():
            self.hop(3, self.pair, 4, 3).start()

    def arrived(self, slot):
        self.hop(slot, self.pair, 0, 1 if slot == 2 else 3).wait_recv()

    def all_sent(self):
        @pl.when(self.sends)
        def _():
            self.hop(0, self.next, 0, 2).wait_send()
            self.hop(1, self.next, 2, 4).wait_send()

        self.hop(2, self.pair, 0, 1).wait_send()
        self.hop(3, self.pair, 0, 3).wait_send()


def differing(s, bit):
    return s + bit - 2 * bit * lax.rem(s // bit, 2)


class Give:
    def __init__(self, devices, first, operands, bufs, send, recv):
        self.s, self.h = lax.axis_index("seq"), lax.axis_index("head")
        g_own, g_got, x_own, x_got = operands
        self.g, self.x, self.slot, self.got, sem = bufs
        self.send, self.recv = send, recv
        bits = shard_orders(first, devices)
        self.partner = differing(self.s, bits[1])
        self.count = devices // 4
        self.loads = [
            pltpu.make_async_copy(g_own, self.g.at[0], sem.at[0]),
            pltpu.make_async_copy(g_got, self.g.at[1], sem.at[1]),
        ]
        for j in range(self.count):
            shard = self.s
            for k, b in enumerate(bits[1:]):
                if ((j + self.count) >> (len(bits) - 2 - k)) & 1:
                    shard = differing(shard, b)
            at = shard // (2 * first) * first + lax.rem(shard, first)
            for k, x in enumerate((x_own, x_got)):
                self.loads.append(
                    pltpu.make_async_copy(x.at[at], self.x.at[k, j], sem.at[2 + 2 * j + k])
                )

    def load(self):
        for copy in self.loads:
            copy.start()

    def loaded(self):
        for copy in self.loads:
            copy.wait()

    def make(self, j):
        total = jnp.dot(self.g[0], self.x[0, j], preferred_element_type=F32)
        total = total + jnp.dot(self.g[1], self.x[1, j], preferred_element_type=F32)
        self.slot[j] = total.astype(BF16)

    def half(self, j, k):
        step = self.slot.shape[1] // 2
        at = pl.ds(k * step, step)
        return remote(
            self.slot.at[j, at, :],
            self.got.at[j, at, :],
            self.send.at[2 * j + k],
            self.recv.at[2 * j + k],
            self.partner,
            self.h,
        )

    def finish(self):
        for j in range(self.count):
            for k in range(2):
                self.half(j, k).wait()


class HeadSum:
    def __init__(self, devices, cores, core_got, chip, y_got, own, other, send, recv):
        self.s, self.h, _, self.core, _, self.mate, self.across = place(devices, cores)
        self.core_got, self.chip, self.y_got = core_got, chip, y_got
        self.own, self.other, self.send, self.recv = own, other, send, recv

    def to_mate(self, i, src=None):
        return remote(
            self.chip.at[i] if src is None else src,
            self.core_got.at[i],
            self.send.at[i],
            self.recv.at[i],
            self.s,
            self.mate,
        )

    def over(self, i):
        return remote(
            self.chip.at[i],
            self.y_got.at[i],
            self.send.at[4 + i],
            self.recv.at[4 + i],
            self.s,
            self.across,
        )

    def back(self, i):
        return remote(
            self.own.at[i],
            self.other.at[i],
            self.send.at[8 + i],
            self.recv.at[8 + i],
            self.s,
            self.mate,
        )

    def chip_sum(self, i, part):
        self.to_mate(i).wait_recv()
        self.chip[i] = (part + self.core_got[i].astype(F32)).astype(BF16)
        self.over(i).start()

    def total(self, i):
        self.over(i).wait_recv()
        self.own[i] = (self.chip[i].astype(F32) + self.y_got[i].astype(F32)).astype(BF16)
        self.back(i).start()

    def joined(self, i):
        self.back(i).wait_recv()
        own, other = self.own[i].astype(F32), self.other[i].astype(F32)
        low = self.core == 0
        return jnp.concatenate([jnp.where(low, own, other), jnp.where(low, other, own)], axis=1)

    def all_sent(self):
        for i in range(4):
            self.to_mate(i).wait_send()
            self.over(i).wait_send()
            self.back(i).wait_send()


def forward_kernel(
    devices,
    cores,
    lengths_ref,
    x_ref,
    gain_one_ref,
    gain_two_ref,
    og_hbm,
    wk_hbm,
    wv_hbm,
    wq_hbm,
    wo_hbm,
    prev_k_hbm,
    prev_v_hbm,
    k_out,
    v_out,
    q_out,
    one_keep_out,
    one_give_out,
    mid_out,
    two_out,
    two_keep_out,
    two_got_out,
    og_keep_out,
    og_give_out,
    att_got,
    att_out,
    lse_out,
    row_out,
    cos_ref,
    sin_ref,
    lo_ref,
    lo_row_ref,
    valid_ref,
    kx,
    vx,
    qx,
    wk,
    wv,
    wq,
    wo,
    normed,
    flipped,
    tops,
    totals,
    acc,
    core_send,
    core_got,
    chip,
    y_got,
    own_half,
    other_half,
    mid,
    two_blocks,
    two_got,
    og,
    load_sem,
    store_sem,
    k_send,
    k_recv,
    v_send,
    v_recv,
    q_send,
    q_recv,
    sum_send,
    sum_recv,
    two_send,
    two_recv,
):
    rows, width = x_ref.shape
    heads = kx.shape[2] // HEAD_DIM
    s, h, odd, core, pair, mate, across = place(devices, cores)
    has_left, has_right = s >= 2, s < devices - 2
    scale = HEAD_DIM ** (-0.5) * LOG2E
    k_chain = Chain(devices, kx, k_send, k_recv, 1)
    v_chain = Chain(devices, vx, v_send, v_recv, 1)
    q_chain = Chain(devices, qx, q_send, q_recv, -1)
    head_sum = HeadSum(
        devices, cores, core_got, chip, y_got, own_half, other_half, sum_send, sum_recv
    )

    loads = [
        pltpu.make_async_copy(src, dst, load_sem.at[i])
        for i, (src, dst) in enumerate(
            ((wk_hbm, wk), (wv_hbm, wv), (wq_hbm, wq), (wo_hbm, wo), (og_hbm, og))
        )
    ]
    for load in loads:
        load.start()

    greet_all(devices, cores)
    step = rows // 4

    def normalize(i, _):
        at = pl.ds(pl.multiple_of(i * step, step), step)
        x = x_ref[at, :].astype(F32)
        root = lax.rsqrt(jnp.mean(x * x, axis=-1, keepdims=True) + EPS)
        normed[at, :] = (x * root * gain_one_ref[...]).astype(BF16)
        return 0

    lax.fori_loop(0, 4, normalize, 0)

    starts, padded = [0], 0
    for r in range(NSEQ - 1):
        padded = padded + (lengths_ref[r] + PAD - 1) // PAD * PAD
        starts.append(padded)

    def sequence_of(at):
        start = jnp.zeros_like(at)
        low = jnp.full_like(at, -BIG)
        length = jnp.zeros_like(at) + lengths_ref[0]
        for r in range(1, NSEQ):
            inside = at >= starts[r]
            start = jnp.where(inside, starts[r], start)
            low = jnp.where(inside, starts[r], low)
            length = jnp.where(inside, lengths_ref[r], length)
        valid = at - start < length
        low = jnp.where(valid, jnp.maximum(low, at - (WINDOW - 1)), at)
        return at - start, valid, jnp.where(at < devices * rows, low, BIG) - s * rows

    at = lax.broadcasted_iota(jnp.int32, (rows, HEAD_DIM), 0) + s * rows
    position, valid, low = sequence_of(at)
    valid_ref[...] = valid[:, 0:1].astype(jnp.int32)
    lo_ref[...] = low[:, 0:1]
    lane = lax.broadcasted_iota(jnp.int32, (1, HEAD_DIM), 1)
    half_dim = HEAD_DIM // 2
    pair_of = lax.rem(lane, half_dim).astype(F32)
    freq = jnp.exp(-math.log(10000.0) * (2.0 * pair_of / HEAD_DIM))
    angle = position.astype(F32) * freq
    cos_ref[...] = jnp.cos(angle)
    sin_ref[...] = jnp.sin(angle) * jnp.where(lane < half_dim, -1.0, 1.0)
    lo_row_ref[...] = sequence_of(lax.broadcasted_iota(jnp.int32, lo_row_ref.shape, 1) + s * rows)[2]

    def turn_into(weight, out):
        raw = jnp.dot(normed[...], weight[...], preferred_element_type=F32)
        for k in range(heads):
            u = raw[:, k * HEAD_DIM : (k + 1) * HEAD_DIM]
            u = u * cos_ref[...] + pltpu.roll(u, HEAD_DIM // 2, 1) * sin_ref[...]
            out[0, :, k * HEAD_DIM : (k + 1) * HEAD_DIM] = u.astype(BF16)

    loads[0].wait()
    turn_into(wk, kx)

    all_greeted(devices)
    k_chain.first()
    loads[1].wait()
    vx[0] = jnp.dot(normed[...], wv[...], preferred_element_type=F32).astype(BF16)
    v_chain.first()

    @pl.when(jnp.logical_not(has_left))
    def _():
        copies = []
        for i, (src, dst) in enumerate(((prev_k_hbm, kx), (prev_v_hbm, vx))):
            for j, d in enumerate((2, 4)):
                at = pl.multiple_of((s - d) * rows + WINDOW, rows)
                copies.append(
                    pltpu.make_async_copy(
                        src.at[pl.ds(at, rows), :], dst.at[d], load_sem.at[5 + 2 * i + j]
                    )
                )
        for copy in copies:
            copy.start()
        for copy in copies:
            copy.wait()

    @pl.when(jnp.logical_not(has_right))
    def _():
        qx[2] = jnp.zeros_like(qx[2])
        qx[4] = jnp.zeros_like(qx[4])

    loads[2].wait()
    turn_into(wq, qx)
    q_chain.first()

    for i in range(4):
        flip_at = slice(i * step, (i + 1) * step)
        flipped[:, :, flip_at] = normed[flip_at, :].T.reshape(devices, width // devices, step)
    split = flipped.reshape(devices // 2, 2, width // devices, rows)
    stores = [
        pltpu.make_async_copy(split.at[:, odd], one_keep_out, store_sem.at[0]),
        pltpu.make_async_copy(split.at[:, 1 - odd], one_give_out, store_sem.at[1]),
    ]
    stores[0].start()
    stores[1].start()

    depth = width // devices
    loads[4].wait()
    for j in range(devices):
        two_blocks[j] = og[:, j * depth : (j + 1) * depth]
    near = lax.rem(s // 2, 2)
    split = two_blocks.reshape(devices // 4, 2, 2, rows, depth)
    og_stores = [
        pltpu.make_async_copy(split.at[:, near], og_keep_out, store_sem.at[4]),
        pltpu.make_async_copy(split.at[:, 1 - near], og_give_out, store_sem.at[5]),
    ]
    og_stores[0].start()
    og_stores[1].start()
    sub = rows // 2

    def attend(d):
        def body(i, _):
            k = i // 2
            at = pl.ds(pl.multiple_of((i % 2) * sub, sub), sub)
            lanes = pl.ds(pl.multiple_of(k * HEAD_DIM, HEAD_DIM), HEAD_DIM)
            scores = dot_nt(qx[0, at, lanes], kx[d, :, lanes])
            u = lax.broadcasted_iota(jnp.int32, scores.shape, 1) - d * rows
            seen = u >= lo_ref[at, :]
            if d == 0:
                t = lax.broadcasted_iota(jnp.int32, scores.shape, 0) + (i % 2) * sub
                seen = seen & (u <= t)
            scores = jnp.where(seen, scores * scale, MASKED)
            top = jnp.max(scores, axis=1, keepdims=True)
            if d > 0:
                old = tops[k, at, :]
                top = jnp.maximum(top, old)
            p = jnp.exp2(scores - top)
            total = jnp.sum(p, axis=1, keepdims=True)
            mixed = jnp.dot(p.astype(BF16), vx[d, :, lanes], preferred_element_type=F32)
            if d > 0:
                fade = jnp.exp2(old - top)
                total = total + totals[k, at, :] * fade
                mixed = mixed + acc[at, lanes] * fade
            tops[k, at, :] = top
            totals[k, at, :] = total
            acc[at, lanes] = mixed
            return 0

        lax.fori_loop(0, 2 * heads, body, 0)

    attend(0)
    k_chain.second()
    v_chain.second()
    attend(2)
    k_chain.arrived(2)
    v_chain.arrived(2)
    attend(1)
    k_chain.third()
    v_chain.third()
    attend(4)
    q_chain.second()
    k_chain.arrived(3)
    v_chain.arrived(3)
    attend(3)
    stores.append(pltpu.make_async_copy(kx, k_out, store_sem.at[2]))
    stores.append(pltpu.make_async_copy(vx, v_out, store_sem.at[3]))
    stores[2].start()
    stores[3].start()

    for k in range(heads):
        lanes = slice(k * HEAD_DIM, (k + 1) * HEAD_DIM)
        out = jnp.where(valid_ref[...] > 0, acc[:, lanes] / totals[k], 0.0)
        att_out[:, lanes] = out.astype(BF16)
        lse = tops[k] + jnp.log2(totals[k])
        lse_out[k] = lse
        row_out[k] = jnp.broadcast_to(lse, (rows, HEAD_DIM)).T[0:1, :]

    att_swap = remote(att_out, att_got, two_send.at[4], two_recv.at[4], pair, h)
    att_swap.start()

    og_stores[0].wait()
    og_stores[1].wait()
    blocks = two_blocks.reshape(devices // 2, 2, rows, depth)

    def to_pair(i):
        at = pl.ds(i * step, step)
        return remote(
            blocks.at[:, 1 - odd, at, :], two_got.at[:, at, :], two_send.at[i], two_recv.at[i], pair, h
        )

    half = width // 2
    loads[3].wait()
    mine = pl.ds(pl.multiple_of(core * half, half), half)
    theirs = pl.ds(pl.multiple_of((1 - core) * half, half), half)

    for i in range(4):
        part = dot_nt(att_out[i * step : (i + 1) * step, :], wo[theirs, :])
        core_send[i] = part.astype(BF16)
        head_sum.to_mate(i, core_send.at[i]).start()
    for i in range(4):
        part = dot_nt(att_out[i * step : (i + 1) * step, :], wo[mine, :])
        head_sum.chip_sum(i, part)
    q_chain.third()

    def finish(i):
        at = slice(i * step, (i + 1) * step)
        total = x_ref[at, :].astype(F32) + head_sum.joined(i)
        mid[at, :] = total
        root = lax.rsqrt(jnp.mean(total * total, axis=-1, keepdims=True) + EPS)
        two = (total * root * gain_two_ref[...]).astype(BF16)
        normed[at, :] = two
        for j in range(devices):
            two_blocks[j, at, :] = two[:, j * depth : (j + 1) * depth]
        to_pair(i).start()

    for i in range(4):
        head_sum.total(i)
        if i > 0:
            finish(i - 1)
    finish(3)
    for src, dst in (
        (mid, mid_out),
        (normed, two_out),
        (blocks.at[:, odd], two_keep_out),
    ):
        stores.append(pltpu.make_async_copy(src, dst, store_sem.at[2 + len(stores)]))
        stores[-1].start()
    q_chain.arrived(2)
    q_chain.arrived(3)
    stores.append(pltpu.make_async_copy(qx, q_out, store_sem.at[2 + len(stores)]))
    stores[-1].start()
    for i in range(4):
        to_pair(i).wait_recv()
    stores.append(pltpu.make_async_copy(two_got, two_got_out, store_sem.at[2 + len(stores)]))
    stores[-1].start()
    att_swap.wait()
    for i in range(4):
        to_pair(i).wait_send()
    for chain in (k_chain, v_chain, q_chain):
        chain.all_sent()
    head_sum.all_sent()
    for store in stores:
        store.wait()


def forward(devices, cores, lengths, x, gains, grad, weights, w_out, prevs):
    rows, width = x.shape
    cols = weights[0].shape[1]
    heads = cols // HEAD_DIM
    depth = width // devices
    parts = WINDOW // rows + 1
    step = rows // 4
    vmem = pl.BlockSpec(memory_space=pltpu.VMEM)
    hbm = pl.BlockSpec(memory_space=pl.ANY)

    def shape(*dims, dtype=BF16):
        return jax.ShapeDtypeStruct(dims, dtype)

    blocks = pltpu.VMEM((4, step, width // 2), BF16)
    dma = pltpu.SemaphoreType.DMA
    return pl.pallas_call(
        functools.partial(forward_kernel, devices, cores),
        in_specs=[pl.BlockSpec(memory_space=pltpu.SMEM)] + [vmem] * 3 + [hbm] * 7,
        out_specs=[hbm] * 11 + [vmem] * 9,
        out_shape=[
            shape(parts, rows, cols),
            shape(parts, rows, cols),
            shape(parts, rows, cols),
            shape(devices // 2, depth, rows),
            shape(devices // 2, depth, rows),
            shape(rows, width, dtype=F32),
            shape(rows, width),
            shape(devices // 2, rows, depth),
            shape(devices // 2, rows, depth),
            shape(devices // 4, 2, rows, depth),
            shape(devices // 4, 2, rows, depth),
            shape(rows, cols),
            shape(rows, cols),
            shape(heads, rows, 1, dtype=F32),
            shape(heads, 1, rows, dtype=F32),
            shape(rows, HEAD_DIM, dtype=F32),
            shape(rows, HEAD_DIM, dtype=F32),
            shape(rows, 1, dtype=jnp.int32),
            shape(1, parts * rows, dtype=jnp.int32),
            shape(rows, 1, dtype=jnp.int32),
        ],
        scratch_shapes=[pltpu.VMEM((parts, rows, cols), BF16)] * 3
        + [pltpu.VMEM((width, cols), BF16)] * 4
        + [
            pltpu.VMEM((rows, width), BF16),
            pltpu.VMEM((devices, depth, rows), BF16),
            pltpu.VMEM((heads, rows, 1), F32),
            pltpu.VMEM((heads, rows, 1), F32),
            pltpu.VMEM((rows, cols), F32),
        ]
        + [blocks] * 6
        + [
            pltpu.VMEM((rows, width), F32),
            pltpu.VMEM((devices, rows, depth), BF16),
            pltpu.VMEM((devices // 2, rows, depth), BF16),
            pltpu.VMEM((rows, width), BF16),
            dma((9,)),
            dma((12,)),
        ]
        + [dma((4,))] * 6
        + [dma((12,))] * 2
        + [dma((5,))] * 2,
        compiler_params=pltpu.CompilerParams(
            collective_id=0, has_side_effects=True, vmem_limit_bytes=56 << 20
        ),
        cost_estimate=cost(10 * rows * width * cols, 40 << 20),
        name="forward",
    )(lengths, x, *gains, grad, *weights, w_out, *prevs)


def norm_two_kernel(
    devices,
    cores,
    parts_ref,
    mid_ref,
    gain_ref,
    og_ref,
    wo_ref,
    att_ref,
    valid_ref,
    lse_row_ref,
    act_ref,
    wd_hbm,
    branch_out,
    gm_out,
    keep_out,
    give_out,
    part_out,
    do_out,
    delta_out,
    stat_out,
    core_got,
    chip,
    y_got,
    own_half,
    other_half,
    flipped,
    wd,
    act,
    store_sem,
    sum_send,
    sum_recv,
):
    rows, width = mid_ref.shape
    heads = att_ref.shape[1] // HEAD_DIM
    step = rows // 4
    s, h, odd, core, pair, mate, across = place(devices, cores)
    head_sum = HeadSum(
        devices, cores, core_got, chip, y_got, own_half, other_half, sum_send, sum_recv
    )
    load = pltpu.make_async_copy(wd_hbm, wd, store_sem.at[2])
    load.start()
    greet(s, mate)
    greet(s, across)
    pl.semaphore_wait(pltpu.get_barrier_semaphore(), 2)
    for i in range(4):
        head_sum.to_mate(i, parts_ref.at[0, pl.ds(i * step, step), :]).start()
    for i in range(4):
        head_sum.chip_sum(i, parts_ref[1, i * step : (i + 1) * step, :].astype(F32))

    half = width // 2
    act[...] = act_ref[...].T
    load.wait()

    def product(i, _):
        start = lax.rem(i // 2 + 1 + core, 2) * half + lax.rem(i, 2) * (half // 2)
        lanes = pl.ds(pl.multiple_of(start, half // 2), half // 2)
        to = pl.ds(pl.multiple_of(lax.rem(i, 2) * (half // 2), half // 2), half // 2)
        branch_out[i // 2, :, to] = jnp.dot(
            act[...], wd[:, lanes], preferred_element_type=F32
        ).astype(BF16)
        return 0

    lax.fori_loop(0, 4, product, 0)

    def finish(i):
        at = slice(i * step, (i + 1) * step)
        x = mid_ref[at, :]
        root = lax.rsqrt(jnp.mean(x * x, axis=-1, keepdims=True) + EPS)
        grad = head_sum.joined(i)
        unit = x * root
        part = jnp.sum(grad * unit, axis=0, keepdims=True)
        part_out[...] = part if i == 0 else part_out[...] + part
        grad = grad * gain_ref[...]
        total = og_ref[at, :].astype(F32) + root * (
            grad - unit * jnp.mean(grad * unit, axis=-1, keepdims=True)
        )
        gm_out[at, :] = total
        low = total.astype(BF16)
        flipped[:, :, at] = low.T.reshape(devices, width // devices, step)
        do = jnp.dot(low, wo_ref[...], preferred_element_type=F32).astype(BF16).astype(F32)
        do = jnp.where(valid_ref[at, :] > 0, do, 0.0)
        do_out[at, :] = do.astype(BF16)
        product = do * att_ref[at, :].astype(F32)
        for k in range(heads):
            delta = jnp.sum(product[:, k * HEAD_DIM : (k + 1) * HEAD_DIM], axis=1, keepdims=True)
            delta_out[k, at, :] = delta
            stat_out[k, 0:1, at] = lse_row_ref[k, :, at]
            stat_out[k, 1:2, at] = jnp.broadcast_to(delta, (step, HEAD_DIM)).T[0:1, :]

    for i in range(4):
        head_sum.total(i)
        if i > 0:
            finish(i - 1)
    finish(3)
    split = flipped.reshape(devices // 2, 2, width // devices, rows)
    stores = [
        pltpu.make_async_copy(split.at[:, odd], keep_out, store_sem.at[0]),
        pltpu.make_async_copy(split.at[:, 1 - odd], give_out, store_sem.at[1]),
    ]
    stores[0].start()
    stores[1].start()
    head_sum.all_sent()
    stores[0].wait()
    stores[1].wait()


def sum_scratch(rows, width):
    return [pltpu.VMEM((4, rows // 4, width // 2), BF16)] * 5


def norm_two_back(
    devices, cores, parts, mid, gain, grad, w_out, attended, valid, lse_row, act, w_down
):
    rows, width = mid.shape
    cols = attended.shape[1]
    heads = cols // HEAD_DIM
    depth = width // devices
    vmem = pl.BlockSpec(memory_space=pltpu.VMEM)
    hbm = pl.BlockSpec(memory_space=pl.ANY)
    dma = pltpu.SemaphoreType.DMA
    return pl.pallas_call(
        functools.partial(norm_two_kernel, devices, cores),
        in_specs=[vmem] * 9 + [hbm],
        out_specs=[vmem, vmem, hbm, hbm] + [vmem] * 4,
        out_shape=[
            jax.ShapeDtypeStruct((2, rows, width // 2), BF16),
            jax.ShapeDtypeStruct((rows, width), F32),
            jax.ShapeDtypeStruct((devices // 2, depth, rows), BF16),
            jax.ShapeDtypeStruct((devices // 2, depth, rows), BF16),
            jax.ShapeDtypeStruct((1, width), F32),
            jax.ShapeDtypeStruct((rows, cols), BF16),
            jax.ShapeDtypeStruct((heads, rows, 1), F32),
            jax.ShapeDtypeStruct((heads, 2, rows), F32),
        ],
        scratch_shapes=sum_scratch(rows, width)
        + [
            pltpu.VMEM((devices, depth, rows), BF16),
            pltpu.VMEM(w_down.shape, BF16),
            pltpu.VMEM(act.shape[::-1], BF16),
            dma((3,)),
            dma((12,)),
            dma((12,)),
        ],
        compiler_params=pltpu.CompilerParams(
            collective_id=1, has_side_effects=True, vmem_limit_bytes=52 << 20
        ),
        cost_estimate=cost(4 * rows * width * cols, 60 << 20),
        name="norm_two_back",
    )(parts, mid, gain, grad, w_out, attended, valid, lse_row, act, w_down)


def attention_back_kernel(
    devices,
    cores,
    do_hbm,
    stat_hbm,
    gg_hbm,
    gg_got_hbm,
    two_hbm,
    two_got_hbm,
    act_hbm,
    act_got_hbm,
    og_hbm,
    og_got_hbm,
    parts_ref,
    mid_ref,
    lo_ref,
    lo_row_ref,
    cos_ref,
    sin_ref,
    kx,
    vx,
    qx,
    lse_ref,
    delta_ref,
    block_out,
    gq_out,
    gk_out,
    gv_out,
    gate_got,
    down_got,
    dx,
    sx,
    dk_acc,
    dv_acc,
    core_got,
    chip,
    y_got,
    own_half,
    other_half,
    gate_g,
    gate_x,
    gate_slot,
    gate_sem,
    gate_send,
    gate_recv,
    down_g,
    down_x,
    down_slot,
    down_sem,
    down_send,
    down_recv,
    load_sem,
    d_send,
    d_recv,
    s_send,
    s_recv,
    sum_send,
    sum_recv,
):
    parts, rows, cols = kx.shape
    heads = cols // HEAD_DIM
    step = rows // 4
    sub = rows // 2
    s, h, odd, core, pair, mate, across = place(devices, cores)
    scale = HEAD_DIM ** (-0.5) * LOG2E
    d_chain = Chain(devices, dx, d_send, d_recv, -1)
    s_chain = Chain(devices, sx, s_send, s_recv, -1)
    head_sum = HeadSum(
        devices, cores, core_got, chip, y_got, own_half, other_half, sum_send, sum_recv
    )
    gate = Give(
        devices,
        1,
        (gg_hbm, gg_got_hbm, two_hbm, two_got_hbm),
        (gate_g, gate_x, gate_slot, gate_got, gate_sem),
        gate_send,
        gate_recv,
    )
    down = Give(
        devices,
        2,
        (act_hbm, act_got_hbm, og_hbm, og_got_hbm),
        (down_g, down_x, down_slot, down_got, down_sem),
        down_send,
        down_recv,
    )
    greet_all(devices, cores)
    loads = [
        pltpu.make_async_copy(do_hbm, dx.at[0], load_sem.at[0]),
        pltpu.make_async_copy(stat_hbm, sx.at[0], load_sem.at[1]),
    ]
    loads[0].start()
    loads[1].start()
    gate.load()
    down.load()

    @pl.when(s >= devices - 2)
    def _():
        for d in (2, 4):
            dx[d] = jnp.zeros_like(dx[d])
            sx[d] = jnp.zeros_like(sx[d])

    loads[0].wait()
    loads[1].wait()
    all_greeted(devices)
    d_chain.first()
    s_chain.first()
    for i in range(4):
        head_sum.to_mate(i, parts_ref.at[0, pl.ds(i * step, step), :]).start()

    def queries_back(start, count):
        def body(i, _):
            k = start + i // 2
            at = pl.ds(pl.multiple_of((i % 2) * sub, sub), sub)
            lanes = pl.ds(pl.multiple_of(k * HEAD_DIM, HEAD_DIM), HEAD_DIM)
            q, do, lo = qx[0, at, lanes], dx[0, at, lanes], lo_ref[at, :]
            lse, delta = lse_ref[k, at, :], delta_ref[k, at, :]
            total = jnp.zeros((sub, HEAD_DIM), F32)
            for d in range(parts):
                key = kx[d, :, lanes]
                scores = dot_nt(q, key)
                u = lax.broadcasted_iota(jnp.int32, scores.shape, 1) - d * rows
                seen = u >= lo
                if d == 0:
                    t = lax.broadcasted_iota(jnp.int32, scores.shape, 0) + (i % 2) * sub
                    seen = seen & (u <= t)
                p = jnp.exp2(jnp.where(seen, scores * scale, MASKED) - lse)
                ds = (p * (dot_nt(do, vx[d, :, lanes]) - delta)).astype(BF16)
                total = total + jnp.dot(ds, key, preferred_element_type=F32)
            gq_out[at, lanes] = turned_back(
                total * HEAD_DIM ** (-0.5), cos_ref[at, :], sin_ref[at, :]
            )
            return 0

        lax.fori_loop(0, 2 * count, body, 0)

    def keys_back(d):
        def body(i, _):
            k = i // 2
            at = pl.ds(pl.multiple_of((i % 2) * sub, sub), sub)
            lanes = pl.ds(pl.multiple_of(k * HEAD_DIM, HEAD_DIM), HEAD_DIM)
            key, value = kx[0, at, lanes], vx[0, at, lanes]
            q, do = qx[d, :, lanes], dx[d, :, lanes]
            scores = dot_nt(key, q)
            u = lax.broadcasted_iota(jnp.int32, scores.shape, 0) + (i % 2) * sub
            seen = u >= lo_row_ref[:, d * rows : (d + 1) * rows]
            if d == 0:
                seen = seen & (u <= lax.broadcasted_iota(jnp.int32, scores.shape, 1))
            lse, delta = sx[d, k, 0:1, :], sx[d, k, 1:2, :]
            p = jnp.exp2(jnp.where(seen, scores * scale - lse, MASKED))
            dv = jnp.dot(p.astype(BF16), do, preferred_element_type=F32)
            ds = (p * (dot_nt(value, do) - delta)).astype(BF16)
            dk = jnp.dot(ds, q, preferred_element_type=F32)
            if d > 0:
                dv = dv + dv_acc[at, lanes]
                dk = dk + dk_acc[at, lanes]
            dv_acc[at, lanes] = dv
            dk_acc[at, lanes] = dk
            return 0

        lax.fori_loop(0, 2 * heads, body, 0)

    gate.loaded()
    gate.make(0)
    gate.half(0, 0).start()
    down.loaded()
    down.make(0)
    down.half(0, 0).start()
    queries_back(0, heads // 4)
    for i in range(4):
        head_sum.chip_sum(i, parts_ref[1, i * step : (i + 1) * step, :].astype(F32))
    s_chain.second()
    d_chain.second()
    gate.half(0, 1).start()
    for j in range(1, gate.count):
        gate.make(j)
        gate.half(j, 0).start()
        gate.half(j, 1).start()
    queries_back(heads // 4, heads // 2)
    down.half(0, 1).start()
    keys_back(0)
    keys_back(2)
    s_chain.third()
    d_chain.third()
    for j in range(1, down.count):
        down.make(j)
        down.half(j, 0).start()
        down.half(j, 1).start()
    queries_back(heads // 4 + heads // 2, heads - heads // 4 - heads // 2)
    for i in range(4):
        head_sum.total(i)
    s_chain.arrived(2)
    d_chain.arrived(2)
    keys_back(1)
    keys_back(4)
    for i in range(4):
        at = slice(i * step, (i + 1) * step)
        block_out[at, :] = (mid_ref[at, :] + head_sum.joined(i)).astype(BF16)
    s_chain.arrived(3)
    d_chain.arrived(3)
    keys_back(3)
    for k in range(heads):
        lanes = slice(k * HEAD_DIM, (k + 1) * HEAD_DIM)
        gk_out[:, lanes] = turned_back(
            dk_acc[:, lanes] * HEAD_DIM ** (-0.5), cos_ref[...], sin_ref[...]
        )
        gv_out[:, lanes] = dv_acc[:, lanes].astype(BF16)
    d_chain.all_sent()
    s_chain.all_sent()
    head_sum.all_sent()
    gate.finish()
    down.finish()


def attention_back(
    devices, cores, do, stat, gate, down, branch, mid, low_col, low_row, tables, keys, values, queries, lse, delta
):
    rows, width = mid.shape
    parts, _, cols = keys.shape
    heads = cols // HEAD_DIM
    units = gate[0].shape[0]
    count, depth = devices // 4, width // devices
    vmem = pl.BlockSpec(memory_space=pltpu.VMEM)
    hbm = pl.BlockSpec(memory_space=pl.ANY)
    dma = pltpu.SemaphoreType.DMA
    give = [
        pltpu.VMEM((2, units, rows), BF16),
        pltpu.VMEM((2, count, rows, depth), BF16),
        pltpu.VMEM((count, units, depth), BF16),
        dma((2 + 2 * count,)),
        dma((2 * count,)),
        dma((2 * count,)),
    ]
    flops = 14 * rows * rows * parts * cols
    return pl.pallas_call(
        functools.partial(attention_back_kernel, devices, cores),
        in_specs=[hbm] * 10 + [vmem] * 11,
        out_specs=[vmem] * 6,
        out_shape=[jax.ShapeDtypeStruct((rows, width), BF16)]
        + [jax.ShapeDtypeStruct((rows, cols), BF16)] * 3
        + [jax.ShapeDtypeStruct((count, units, depth), BF16)] * 2,
        scratch_shapes=[
            pltpu.VMEM((parts, rows, cols), BF16),
            pltpu.VMEM((parts, heads, 2, rows), F32),
            pltpu.VMEM((rows, cols), F32),
            pltpu.VMEM((rows, cols), F32),
        ]
        + sum_scratch(rows, width)
        + give
        + give
        + [dma((2,))]
        + [dma((4,))] * 4
        + [dma((12,))] * 2,
        compiler_params=pltpu.CompilerParams(
            collective_id=2, has_side_effects=True, vmem_limit_bytes=58 << 20
        ),
        cost_estimate=cost(flops, 80 << 20),
        name="attention_back",
    )(do, stat, *gate, *down, branch, mid, low_col, low_row, *tables, keys, values, queries, lse, delta)


def on_device(
    tokens,
    gain_attn,
    gain_mlp,
    w_query,
    w_key,
    w_value,
    w_out,
    w_gate,
    w_up,
    w_down,
    prev_keys,
    prev_values,
    lengths,
    out_grad,
):
    rows = tokens.shape[0]
    width = w_query.shape[1]
    devices, cores = lax.axis_size("seq"), lax.axis_size("head")
    index = lax.axis_index("seq")
    bits = jnp.stack([index & 1, lax.axis_index("head") & 1]).astype(jnp.int32)
    gain_one, gain_two = gain_attn[None, :], gain_mlp[None, :]

    (
        keys,
        values,
        queries,
        one_keep,
        one_give,
        mid,
        normed_two,
        two_keep,
        two_got,
        out_keep,
        out_give,
        attended_got,
        attended,
        lse,
        lse_row,
        cosine,
        sine,
        low_col,
        low_row,
        valid,
    ) = forward(
        devices,
        cores,
        lengths,
        tokens,
        (gain_one, gain_two),
        out_grad,
        (w_key, w_value, w_query),
        w_out,
        (prev_keys, prev_values),
    )
    order = Order()
    out_keep, out_give = (a.reshape(devices // 2, rows, -1) for a in (out_keep, out_give))
    out_pair = (out_keep, swap(out_give, "seq", 2))
    one_pair = (one_keep, swap(one_give, "seq", 1))
    two_pair = (two_keep, two_got)
    w_gate, w_up, w_down = w_gate.T, w_up.T, w_down.T
    act, grad_gate, grad_up = mlp(normed_two, out_grad, w_gate, w_up, w_down)
    act_got = swap(act, "seq", 2)
    gate_got = swap(grad_gate, "seq", 1)
    up_got = swap(grad_up, "seq", 1)
    norm_parts = back_products(bits, grad_gate, grad_up, w_gate, w_up)
    (
        branch_parts,
        grad_mid,
        mid_keep,
        mid_give,
        gain_mlp_part,
        grad_att,
        delta,
        stat,
    ) = norm_two_back(
        devices,
        cores,
        norm_parts,
        mid,
        gain_two,
        out_grad,
        w_out,
        attended,
        valid,
        lse_row,
        act,
        w_down,
    )
    order.ran(delta)
    gate = WeightGrad(order, two_pair, grad_gate, gate_got, 1, "gate", True)
    up = WeightGrad(order, two_pair, grad_up, up_got, 1, "up", True)
    down = WeightGrad(order, out_pair, act, act_got, 2, "down", True)
    block_out, grad_query_raw, grad_key_raw, grad_value_raw, gate.got, down.got = attention_back(
        devices,
        cores,
        order.after(grad_att),
        stat,
        (grad_gate, gate_got, *two_pair),
        (act, act_got, *out_pair),
        branch_parts,
        mid,
        low_col,
        low_row,
        (cosine, sine),
        keys,
        values,
        queries,
        lse,
        delta,
    )
    order.ran(grad_query_raw)
    query_got = swap(grad_query_raw, "seq", 1)
    key_got = swap(grad_key_raw, "seq", 1)
    value_got = swap(grad_value_raw, "seq", 1)
    mid_pair = (mid_keep, swap(order.after(mid_give), "seq", 1))
    gate.keep()
    up.give()
    down.keep()
    lefts = (grad_query_raw, grad_key_raw, grad_value_raw)
    rights = (w_query, w_key, w_value)
    give = order.ran(half_product(order.after(bits), lefts, rights, 1, None, "norm_one_give"))
    give = swap(give, "head", 1)
    query = WeightGrad(order, one_pair, grad_query_raw, query_got, 1, "query")
    key = WeightGrad(order, one_pair, grad_key_raw, key_got, 1, "key")
    value = WeightGrad(order, one_pair, grad_value_raw, value_got, 1, "value")
    wout = WeightGrad(order, mid_pair, attended, attended_got, 1, "wout")
    query.give()
    chip = order.ran(half_product(order.after(bits), lefts, rights, 0, give, "norm_one_keep"))
    chip_got = swap(chip, "head", 2)
    key.give()
    value.give()
    up.keep()
    wout.give()
    own = (chip.astype(F32) + chip_got.astype(F32)).astype(BF16)
    other = swap(own, "head", 1)
    query.keep()
    key.keep()
    tokens_grad, gain_attn_part = by_rows(
        back_kernel,
        order.after(bits),
        (tokens, own, other, gain_one, grad_mid),
        3,
        (BF16, F32),
        "tokens_back",
        part=1,
    )
    order.ran(gain_attn_part)
    value.keep()
    wout.keep()
    gains = gain_sum(jnp.concatenate([gain_attn_part, gain_mlp_part], axis=0))
    gain_attn_grad, gain_mlp_grad = gains[0], gains[1]
    w_gate_grad, w_up_grad, w_down_grad = gate.finish(), up.finish(), down.finish()
    w_out_grad = wout.finish()
    w_query_grad, w_key_grad, w_value_grad = query.finish(), key.finish(), value.finish()
    return (
        block_out,
        tokens_grad,
        gain_attn_grad,
        gain_mlp_grad,
        w_query_grad,
        w_key_grad,
        w_value_grad,
        w_out_grad,
        w_gate_grad,
        w_up_grad,
        w_down_grad,
    )


def solution(mesh):
    by_head = P(None, "head")
    both = P("seq", "head")
    placed = (P("seq", None), P(), P()) + (by_head,) * 9 + (P(), P("seq", None))
    return jax.shard_map(
        on_device,
        mesh=mesh,
        in_specs=placed,
        out_specs=(P("seq", None), P("seq", None), P("seq"), P("seq")) + (both,) * 7,
        check_vma=False,
    )
```

```python
import functools
import math

import jax
import jax.numpy as jnp
from jax import lax
from jax.experimental import pallas as pl
from jax.experimental.pallas import tpu as pltpu
from jax.sharding import PartitionSpec as P

HEAD_DIM = 128
WINDOW = 2048
PAD = 64
NSEQ = 4
EPS = 1e-06
MASKED = -1e30
LOG2E = 1.4426950408889634
BIG = 1 << 28
F32 = jnp.float32
BF16 = jnp.bfloat16


def swap(block, axis, bit):
    return lax.ppermute(block, axis, [(i, i ^ bit) for i in range(lax.axis_size(axis))])


def shifted(block, distance):
    n = lax.axis_size("seq")
    return lax.ppermute(
        block, "seq", [(i, i + distance) for i in range(n) if 0 <= i + distance < n]
    )


BIG_VMEM = pltpu.CompilerParams(vmem_limit_bytes=48 << 20)


def cost(flops, moved):
    return pl.CostEstimate(flops=int(flops), bytes_accessed=int(moved), transcendentals=0)


def dot_nt(left, right):
    return lax.dot_general(left, right, (((1,), (1,)), ((), ())), preferred_element_type=F32)


def row_blocks(width, step):
    return pl.BlockSpec((step, width), lambda i, bits: (i, 0))


def joined(bits_ref, own_ref, other_ref):
    low = bits_ref[1] == 0
    own, other = own_ref[...].astype(F32), other_ref[...].astype(F32)
    return jnp.concatenate([jnp.where(low, own, other), jnp.where(low, other, own)], axis=1)


def back_kernel(
    bits_ref, x_ref, own_ref, other_ref, gain_ref, add_ref, out_ref, part_ref
):
    x = x_ref[...].astype(F32)
    scale = lax.rsqrt(jnp.mean(x * x, axis=-1, keepdims=True) + EPS)
    grad = joined(bits_ref, own_ref, other_ref)
    unit = x * scale
    grad_unit = grad * gain_ref[...]
    total = add_ref[...].astype(F32) + scale * (
        grad_unit - unit * jnp.mean(grad_unit * unit, axis=-1, keepdims=True)
    )
    out_ref[...] = total.astype(out_ref.dtype)
    part = jnp.sum(grad * unit, axis=0, keepdims=True)

    @pl.when(pl.program_id(0) == 0)
    def _():
        part_ref[...] = part

    @pl.when(pl.program_id(0) > 0)
    def _():
        part_ref[...] += part


def by_rows(kernel, bits, arrays, gains_at, outs, name, part=None):
    rows, width = arrays[0].shape
    step = rows // 4
    in_specs = [
        pl.BlockSpec((1, width), lambda i, bits: (0, 0))
        if k == gains_at
        else row_blocks(a.shape[1], step)
        for k, a in enumerate(arrays)
    ]
    out_specs, out_shape = [], []
    for k, dtype in enumerate(outs):
        if k == part:
            out_specs.append(pl.BlockSpec((1, width), lambda i, bits: (0, 0)))
            out_shape.append(jax.ShapeDtypeStruct((1, width), F32))
        else:
            out_specs.append(row_blocks(width, step))
            out_shape.append(jax.ShapeDtypeStruct((rows, width), dtype))
    return pl.pallas_call(
        kernel,
        grid_spec=pltpu.PrefetchScalarGridSpec(
            num_scalar_prefetch=1, grid=(rows // step,), in_specs=in_specs, out_specs=out_specs
        ),
        out_shape=out_shape,
        compiler_params=BIG_VMEM,
        cost_estimate=cost(rows * width * 10, rows * width * 2 * (len(arrays) + len(out_shape))),
        name=name,
    )(bits, *arrays)


def half_kernel(pairs, flip, added, bits_ref, *refs):
    total = refs[2 * pairs][...].astype(F32) if added else None
    for k in range(pairs):
        term = dot_nt(refs[k][...], refs[pairs + k][...])
        total = term if total is None else total + term
    refs[-1][...] = total.astype(BF16)


def half_product(bits, lefts, rights, flip, added, name):
    rows = lefts[0].shape[0]
    width = rights[0].shape[0] // 2
    step = min(width, 512)
    steps = width // step

    def at(i, bits):
        return ((bits[1] ^ flip) * steps + i, 0)

    specs = [pl.BlockSpec(a.shape, lambda i, bits: (0, 0)) for a in lefts]
    specs += [pl.BlockSpec((step, a.shape[1]), at) for a in rights]
    extra = []
    if added is not None:
        extra = [added]
        specs.append(pl.BlockSpec((rows, step), lambda i, bits: (0, i)))
    depth = sum(a.shape[1] for a in lefts)
    return pl.pallas_call(
        functools.partial(half_kernel, len(lefts), flip, added is not None),
        grid_spec=pltpu.PrefetchScalarGridSpec(
            num_scalar_prefetch=1,
            grid=(steps,),
            in_specs=specs,
            out_specs=pl.BlockSpec((rows, step), lambda i, bits: (0, i)),
        ),
        out_shape=jax.ShapeDtypeStruct((rows, width), BF16),
        compiler_params=BIG_VMEM,
        cost_estimate=cost(2 * rows * depth * width, 2 * (rows + width) * depth),
        name=name,
    )(bits, *lefts, *rights, *extra)


def mlp_kernel(x_ref, g_ref, wg_ref, wu_ref, wd_ref, act_ref, gg_ref, gu_ref):
    x, g = x_ref[...], g_ref[...]
    gate = dot_nt(wg_ref[...], x)
    up = dot_nt(wu_ref[...], x)
    grad = dot_nt(wd_ref[...], g)
    sig = 1.0 / (1.0 + jnp.exp(-gate))
    silu = gate * sig
    act_ref[...] = (silu * up).astype(BF16)
    gg_ref[...] = (grad * up * sig * (1.0 + gate * (1.0 - sig))).astype(BF16)
    gu_ref[...] = (grad * silu).astype(BF16)


def mlp(x, grad, w_gate, w_up, w_down):
    rows, depth = x.shape
    width = w_gate.shape[0]
    step = -(-width // (4 * 32)) * 32
    whole = pl.BlockSpec((rows, depth), lambda i: (0, 0))
    block = pl.BlockSpec((step, depth), lambda i: (i, 0))
    return pl.pallas_call(
        mlp_kernel,
        grid=(pl.cdiv(width, step),),
        in_specs=[whole, whole, block, block, block],
        out_specs=[pl.BlockSpec((step, rows), lambda i: (i, 0))] * 3,
        out_shape=[jax.ShapeDtypeStruct((width, rows), BF16)] * 3,
        compiler_params=BIG_VMEM,
        cost_estimate=cost(6 * rows * depth * width, 6 * depth * width),
        name="mlp",
    )(x, grad, w_gate, w_up, w_down)


def back_products_kernel(bits_ref, gg_ref, gu_ref, wg_ref, wu_ref, out_ref, gg, gu):
    @pl.when(pl.program_id(0) == 0)
    def _():
        gg[...] = gg_ref[...].T
        gu[...] = gu_ref[...].T

    total = jnp.dot(gg[...], wg_ref[...], preferred_element_type=F32)
    total = total + jnp.dot(gu[...], wu_ref[...], preferred_element_type=F32)
    out_ref[0] = total.astype(BF16)


def back_products(bits, grad_gate, grad_up, w_gate, w_up):
    cols, rows = grad_gate.shape
    width = w_gate.shape[1]
    step = width // 4
    whole = pl.BlockSpec((cols, rows), lambda i, bits: (0, 0))
    column = pl.BlockSpec(
        (cols, step), lambda i, bits: (0, 2 * (bits[1] ^ 1 ^ (i // 2)) + i % 2)
    )
    return pl.pallas_call(
        back_products_kernel,
        grid_spec=pltpu.PrefetchScalarGridSpec(
            num_scalar_prefetch=1,
            grid=(4,),
            in_specs=[whole, whole, column, column],
            out_specs=pl.BlockSpec((1, rows, step), lambda i, bits: (i // 2, 0, i % 2)),
            scratch_shapes=[pltpu.VMEM((rows, cols), BF16)] * 2,
        ),
        out_shape=jax.ShapeDtypeStruct((2, rows, width // 2), BF16),
        compiler_params=BIG_VMEM,
        cost_estimate=cost(4 * rows * cols * width, 4 * cols * width),
        name="back_products",
    )(bits, grad_gate, grad_up, w_gate, w_up)


def blocks_kernel(order_ref, flip, xa_ref, xb_ref, ga_ref, gb_ref, *refs):
    if flip:
        total = jnp.dot(ga_ref[...], xa_ref[0], preferred_element_type=F32)
        total = total + jnp.dot(gb_ref[...], xb_ref[0], preferred_element_type=F32)
    else:
        total = jnp.dot(xa_ref[0], ga_ref[...], preferred_element_type=F32)
        total = total + jnp.dot(xb_ref[0], gb_ref[...], preferred_element_type=F32)
    if len(refs) == 2:
        total = total + refs[0][0].astype(F32)
    refs[-1][0] = total.astype(BF16)


def grad_blocks(order, x_own, x_got, g_own, g_got, added, flip, name):
    count = order.shape[0]
    if flip:
        _, rows, depth = x_own.shape
        cols = g_own.shape[0]
        shape = (cols, depth)
    else:
        _, depth, rows = x_own.shape
        cols = g_own.shape[1]
        shape = (depth, cols)
    x_spec = pl.BlockSpec((1,) + x_own.shape[1:], lambda i, order: (order[i], 0, 0))
    g_spec = pl.BlockSpec(g_own.shape, lambda i, order: (0, 0))
    out_spec = pl.BlockSpec((1,) + shape, lambda i, order: (i, 0, 0))
    extra = [] if added is None else [added]

    def kernel(order_ref, *refs):
        blocks_kernel(order_ref, flip, *refs)

    return pl.pallas_call(
        kernel,
        grid_spec=pltpu.PrefetchScalarGridSpec(
            num_scalar_prefetch=1,
            grid=(count,),
            in_specs=[x_spec, x_spec, g_spec, g_spec] + [out_spec] * len(extra),
            out_specs=out_spec,
        ),
        out_shape=jax.ShapeDtypeStruct((count,) + shape, BF16),
        compiler_params=BIG_VMEM,
        cost_estimate=cost(
            4 * count * depth * rows * cols, 2 * count * depth * cols + 4 * rows * cols
        ),
        name=name,
    )(order, x_own, x_got, g_own, g_got, *extra)


def shard_orders(first, n):
    bits = [1 << k for k in range(n.bit_length() - 1)]
    return [first] + [b for b in bits if b != first]


class Order:
    def __init__(self):
        self.last = None

    def after(self, operand):
        if self.last is None:
            return operand
        return lax.optimization_barrier((operand, self.last))[0]

    def ran(self, result):
        self.last = result
        return result


class WeightGrad:
    def __init__(self, order, x_pair, g_own, g_got, first, name, flip=False):
        n = lax.axis_size("seq")
        self.order, self.flip, self.name = order, flip, name
        self.operands = (*x_pair, g_own, g_got)
        self.bits = shard_orders(first, n)
        index = lax.axis_index("seq")
        shards = []
        for p in range(n // 2):
            apart = sum(
                b for k, b in enumerate(self.bits[1:]) if (p >> (len(self.bits) - 2 - k)) & 1
            )
            shard = index ^ apart
            shards.append(shard // (2 * first) * first + shard % first)
        self.shards = jnp.stack(shards).astype(jnp.int32)
        self.count = n // 4

    def blocks(self, shards, added, name):
        return self.order.ran(
            grad_blocks(
                self.order.after(shards), *self.operands, added, self.flip, self.name + name
            )
        )

    def give(self):
        give = self.blocks(self.shards[self.count :], None, "_give")
        self.got = swap(give, "seq", self.bits[1])

    def keep(self):
        self.part = self.blocks(self.shards[: self.count], self.got, "_keep")
        left = self.count // 2
        self.got = swap(self.part[left:], "seq", self.bits[2])

    def finish(self):
        left, part = self.count // 2, self.part
        total = part[:left].astype(F32) + self.got.astype(F32)
        for bit in self.bits[3:]:
            left //= 2
            part = total.astype(BF16)
            total = part[:left].astype(F32) + swap(part[left:], "seq", bit).astype(F32)
        return total[0].T if self.flip else total[0]


def gain_sum(part):
    n = lax.axis_size("seq")
    total = part
    bit = 1
    while bit < n:
        total = total + swap(total, "seq", bit)
        bit *= 2
    width = part.shape[-1] // n
    return lax.dynamic_slice_in_dim(total, lax.axis_index("seq") * width, width, total.ndim - 1)


def turned_back(grad, cosine, sine):
    return (grad * cosine - pltpu.roll(grad, HEAD_DIM // 2, 1) * sine).astype(BF16)


def place(devices, cores):
    s, h = lax.axis_index("seq"), lax.axis_index("head")
    odd, core = lax.rem(s, 2), lax.rem(h, 2)
    pair = s + 1 - 2 * odd
    mate = h + 1 - 2 * core
    across = lax.rem(h + cores // 2, cores)
    return s, h, odd, core, pair, mate, across


def remote(src, dst, send, recv, seq, head):
    return pltpu.make_async_remote_copy(
        src_ref=src,
        dst_ref=dst,
        send_sem=send,
        recv_sem=recv,
        device_id=(seq, head),
        device_id_type=pl.DeviceIdType.MESH,
    )


def greet(seq, head):
    pl.semaphore_signal(
        pltpu.get_barrier_semaphore(),
        inc=1,
        device_id=(seq, head),
        device_id_type=pl.DeviceIdType.MESH,
    )


def greet_all(devices, cores):
    s, h, odd, core, pair, mate, across = place(devices, cores)
    greet(pair, h)
    greet(s, mate)
    greet(s, across)

    @pl.when(s >= 2)
    def _():
        greet(s - 2, h)

    @pl.when(s < devices - 2)
    def _():
        greet(s + 2, h)


def all_greeted(devices):
    s = lax.axis_index("seq")
    inner = (s >= 2) & (s < devices - 2)

    @pl.when(inner)
    def _():
        pl.semaphore_wait(pltpu.get_barrier_semaphore(), 5)

    @pl.when(jnp.logical_not(inner))
    def _():
        pl.semaphore_wait(pltpu.get_barrier_semaphore(), 4)


class Chain:
    def __init__(self, devices, buf, send, recv, side):
        self.s, self.h = lax.axis_index("seq"), lax.axis_index("head")
        odd = lax.rem(self.s, 2)
        self.pair = self.s + 1 - 2 * odd
        self.buf, self.send, self.recv = buf, send, recv
        self.next = self.s + 2 * side
        left, right = self.s >= 2, self.s < devices - 2
        self.sends, self.gets = (right, left) if side > 0 else (left, right)
        self.early = odd == (0 if side > 0 else 1)
        self.late = odd == (1 if side > 0 else 0)

    def hop(self, slot, seq, src, dst):
        return remote(
            self.buf.at[src], self.buf.at[dst], self.send.at[slot], self.recv.at[slot], seq, self.h
        )

    def first(self):
        @pl.when(self.sends)
        def _():
            self.hop(0, self.next, 0, 2).start()

        @pl.when(self.early)
        def _():
            self.hop(2, self.pair, 0, 1).start()

    def second(self):
        @pl.when(self.gets)
        def _():
            self.hop(0, self.next, 0, 2).wait_recv()

        @pl.when(self.sends)
        def _():
            self.hop(1, self.next, 2, 4).start()

        @pl.when(self.early)
        def _():
            self.hop(3, self.pair, 2, 3).start()

        @pl.when(self.late)
        def _():
            self.hop(2, self.pair, 2, 1).start()

    def third(self):
        @pl.when(self.gets)
        def _():
            self.hop(1, self.next, 2, 4).wait_recv()

        @pl.when(self.late)
        def _():
            self.hop(3, self.pair, 4, 3).start()

    def arrived(self, slot):
        self.hop(slot, self.pair, 0, 1 if slot == 2 else 3).wait_recv()

    def all_sent(self):
        @pl.when(self.sends)
        def _():
            self.hop(0, self.next, 0, 2).wait_send()
            self.hop(1, self.next, 2, 4).wait_send()

        self.hop(2, self.pair, 0, 1).wait_send()
        self.hop(3, self.pair, 0, 3).wait_send()


def differing(s, bit):
    return s + bit - 2 * bit * lax.rem(s // bit, 2)


class Give:
    def __init__(self, devices, first, operands, bufs, send, recv):
        self.s, self.h = lax.axis_index("seq"), lax.axis_index("head")
        g_own, g_got, x_own, x_got = operands
        self.g, self.x, self.slot, self.got, sem = bufs
        self.send, self.recv = send, recv
        bits = shard_orders(first, devices)
        self.partner = differing(self.s, bits[1])
        self.count = devices // 4
        self.loads = [
            pltpu.make_async_copy(g_own, self.g.at[0], sem.at[0]),
            pltpu.make_async_copy(g_got, self.g.at[1], sem.at[1]),
        ]
        for j in range(self.count):
            shard = self.s
            for k, b in enumerate(bits[1:]):
                if ((j + self.count) >> (len(bits) - 2 - k)) & 1:
                    shard = differing(shard, b)
            at = shard // (2 * first) * first + lax.rem(shard, first)
            for k, x in enumerate((x_own, x_got)):
                self.loads.append(
                    pltpu.make_async_copy(x.at[at], self.x.at[k, j], sem.at[2 + 2 * j + k])
                )

    def load(self):
        for copy in self.loads:
            copy.start()

    def loaded(self):
        for copy in self.loads:
            copy.wait()

    def make(self, j):
        total = jnp.dot(self.g[0], self.x[0, j], preferred_element_type=F32)
        total = total + jnp.dot(self.g[1], self.x[1, j], preferred_element_type=F32)
        self.slot[j] = total.astype(BF16)

    def half(self, j, k):
        step = self.slot.shape[1] // 2
        at = pl.ds(k * step, step)
        return remote(
            self.slot.at[j, at, :],
            self.got.at[j, at, :],
            self.send.at[2 * j + k],
            self.recv.at[2 * j + k],
            self.partner,
            self.h,
        )

    def finish(self):
        for j in range(self.count):
            for k in range(2):
                self.half(j, k).wait()


class HeadSum:
    def __init__(self, devices, cores, core_got, chip, y_got, own, other, send, recv):
        self.s, self.h, _, self.core, _, self.mate, self.across = place(devices, cores)
        self.core_got, self.chip, self.y_got = core_got, chip, y_got
        self.own, self.other, self.send, self.recv = own, other, send, recv

    def to_mate(self, i, src=None):
        return remote(
            self.chip.at[i] if src is None else src,
            self.core_got.at[i],
            self.send.at[i],
            self.recv.at[i],
            self.s,
            self.mate,
        )

    def over(self, i):
        return remote(
            self.chip.at[i],
            self.y_got.at[i],
            self.send.at[4 + i],
            self.recv.at[4 + i],
            self.s,
            self.across,
        )

    def back(self, i):
        return remote(
            self.own.at[i],
            self.other.at[i],
            self.send.at[8 + i],
            self.recv.at[8 + i],
            self.s,
            self.mate,
        )

    def chip_sum(self, i, part):
        self.to_mate(i).wait_recv()
        self.chip[i] = (part + self.core_got[i].astype(F32)).astype(BF16)
        self.over(i).start()

    def total(self, i):
        self.over(i).wait_recv()
        self.own[i] = (self.chip[i].astype(F32) + self.y_got[i].astype(F32)).astype(BF16)
        self.back(i).start()

    def joined(self, i):
        self.back(i).wait_recv()
        own, other = self.own[i].astype(F32), self.other[i].astype(F32)
        low = self.core == 0
        return jnp.concatenate([jnp.where(low, own, other), jnp.where(low, other, own)], axis=1)

    def all_sent(self):
        for i in range(4):
            self.to_mate(i).wait_send()
            self.over(i).wait_send()
            self.back(i).wait_send()


def forward_kernel(
    devices,
    cores,
    lengths_ref,
    x_ref,
    gain_one_ref,
    gain_two_ref,
    og_hbm,
    wk_hbm,
    wv_hbm,
    wq_hbm,
    wo_hbm,
    prev_k_hbm,
    prev_v_hbm,
    k_out,
    v_out,
    q_out,
    one_keep_out,
    one_got_out,
    mid_out,
    two_out,
    two_keep_out,
    two_got_out,
    og_keep_out,
    og_give_out,
    att_got,
    att_out,
    lse_out,
    row_out,
    cos_ref,
    sin_ref,
    lo_ref,
    lo_row_ref,
    valid_ref,
    kx,
    vx,
    qx,
    wk,
    wv,
    wq,
    wo,
    normed,
    flipped,
    tops,
    totals,
    acc,
    core_send,
    core_got,
    chip,
    y_got,
    own_half,
    other_half,
    mid,
    two_blocks,
    two_got,
    one_got,
    og,
    load_sem,
    store_sem,
    k_send,
    k_recv,
    v_send,
    v_recv,
    q_send,
    q_recv,
    sum_send,
    sum_recv,
    two_send,
    two_recv,
):
    rows, width = x_ref.shape
    heads = kx.shape[2] // HEAD_DIM
    s, h, odd, core, pair, mate, across = place(devices, cores)
    has_left, has_right = s >= 2, s < devices - 2
    scale = HEAD_DIM ** (-0.5) * LOG2E
    k_chain = Chain(devices, kx, k_send, k_recv, 1)
    v_chain = Chain(devices, vx, v_send, v_recv, 1)
    q_chain = Chain(devices, qx, q_send, q_recv, -1)
    head_sum = HeadSum(
        devices, cores, core_got, chip, y_got, own_half, other_half, sum_send, sum_recv
    )

    loads = [
        pltpu.make_async_copy(src, dst, load_sem.at[i])
        for i, (src, dst) in enumerate(
            ((wk_hbm, wk), (wv_hbm, wv), (wq_hbm, wq), (wo_hbm, wo), (og_hbm, og))
        )
    ]
    for load in loads:
        load.start()

    greet_all(devices, cores)
    step = rows // 4

    def normalize(i, _):
        at = pl.ds(pl.multiple_of(i * step, step), step)
        x = x_ref[at, :].astype(F32)
        root = lax.rsqrt(jnp.mean(x * x, axis=-1, keepdims=True) + EPS)
        normed[at, :] = (x * root * gain_one_ref[...]).astype(BF16)
        return 0

    lax.fori_loop(0, 4, normalize, 0)

    starts, padded = [0], 0
    for r in range(NSEQ - 1):
        padded = padded + (lengths_ref[r] + PAD - 1) // PAD * PAD
        starts.append(padded)

    def sequence_of(at):
        start = jnp.zeros_like(at)
        low = jnp.full_like(at, -BIG)
        length = jnp.zeros_like(at) + lengths_ref[0]
        for r in range(1, NSEQ):
            inside = at >= starts[r]
            start = jnp.where(inside, starts[r], start)
            low = jnp.where(inside, starts[r], low)
            length = jnp.where(inside, lengths_ref[r], length)
        valid = at - start < length
        low = jnp.where(valid, jnp.maximum(low, at - (WINDOW - 1)), at)
        return at - start, valid, jnp.where(at < devices * rows, low, BIG) - s * rows

    at = lax.broadcasted_iota(jnp.int32, (rows, HEAD_DIM), 0) + s * rows
    position, valid, low = sequence_of(at)
    valid_ref[...] = valid[:, 0:1].astype(jnp.int32)
    lo_ref[...] = low[:, 0:1]
    lane = lax.broadcasted_iota(jnp.int32, (1, HEAD_DIM), 1)
    half_dim = HEAD_DIM // 2
    pair_of = lax.rem(lane, half_dim).astype(F32)
    freq = jnp.exp(-math.log(10000.0) * (2.0 * pair_of / HEAD_DIM))
    angle = position.astype(F32) * freq
    cos_ref[...] = jnp.cos(angle)
    sin_ref[...] = jnp.sin(angle) * jnp.where(lane < half_dim, -1.0, 1.0)
    lo_row_ref[...] = sequence_of(lax.broadcasted_iota(jnp.int32, lo_row_ref.shape, 1) + s * rows)[2]

    def turn_into(weight, out):
        raw = jnp.dot(normed[...], weight[...], preferred_element_type=F32)
        for k in range(heads):
            u = raw[:, k * HEAD_DIM : (k + 1) * HEAD_DIM]
            u = u * cos_ref[...] + pltpu.roll(u, HEAD_DIM // 2, 1) * sin_ref[...]
            out[0, :, k * HEAD_DIM : (k + 1) * HEAD_DIM] = u.astype(BF16)

    loads[0].wait()
    turn_into(wk, kx)

    all_greeted(devices)
    k_chain.first()
    loads[1].wait()
    vx[0] = jnp.dot(normed[...], wv[...], preferred_element_type=F32).astype(BF16)
    v_chain.first()

    @pl.when(jnp.logical_not(has_left))
    def _():
        copies = []
        for i, (src, dst) in enumerate(((prev_k_hbm, kx), (prev_v_hbm, vx))):
            for j, d in enumerate((2, 4)):
                at = pl.multiple_of((s - d) * rows + WINDOW, rows)
                copies.append(
                    pltpu.make_async_copy(
                        src.at[pl.ds(at, rows), :], dst.at[d], load_sem.at[5 + 2 * i + j]
                    )
                )
        for copy in copies:
            copy.start()
        for copy in copies:
            copy.wait()

    @pl.when(jnp.logical_not(has_right))
    def _():
        qx[2] = jnp.zeros_like(qx[2])
        qx[4] = jnp.zeros_like(qx[4])

    loads[2].wait()
    turn_into(wq, qx)
    q_chain.first()

    for i in range(4):
        flip_at = slice(i * step, (i + 1) * step)
        flipped[:, :, flip_at] = normed[flip_at, :].T.reshape(devices, width // devices, step)
    turned = flipped.reshape(devices // 2, 2, width // devices, rows)
    stores = [pltpu.make_async_copy(turned.at[:, odd], one_keep_out, store_sem.at[0])]
    stores[0].start()

    depth = width // devices
    loads[4].wait()
    for j in range(devices):
        two_blocks[j] = og[:, j * depth : (j + 1) * depth]
    near = lax.rem(s // 2, 2)
    split = two_blocks.reshape(devices // 4, 2, 2, rows, depth)
    og_stores = [
        pltpu.make_async_copy(split.at[:, near], og_keep_out, store_sem.at[4]),
        pltpu.make_async_copy(split.at[:, 1 - near], og_give_out, store_sem.at[5]),
    ]
    og_stores[0].start()
    og_stores[1].start()
    sub = rows // 2

    def attend(d):
        def body(i, _):
            k = i // 2
            at = pl.ds(pl.multiple_of((i % 2) * sub, sub), sub)
            lanes = pl.ds(pl.multiple_of(k * HEAD_DIM, HEAD_DIM), HEAD_DIM)
            scores = dot_nt(qx[0, at, lanes], kx[d, :, lanes])
            u = lax.broadcasted_iota(jnp.int32, scores.shape, 1) - d * rows
            seen = u >= lo_ref[at, :]
            if d == 0:
                t = lax.broadcasted_iota(jnp.int32, scores.shape, 0) + (i % 2) * sub
                seen = seen & (u <= t)
            scores = jnp.where(seen, scores * scale, MASKED)
            top = jnp.max(scores, axis=1, keepdims=True)
            if d > 0:
                old = tops[k, at, :]
                top = jnp.maximum(top, old)
            p = jnp.exp2(scores - top)
            total = jnp.sum(p, axis=1, keepdims=True)
            mixed = jnp.dot(p.astype(BF16), vx[d, :, lanes], preferred_element_type=F32)
            if d > 0:
                fade = jnp.exp2(old - top)
                total = total + totals[k, at, :] * fade
                mixed = mixed + acc[at, lanes] * fade
            tops[k, at, :] = top
            totals[k, at, :] = total
            acc[at, lanes] = mixed
            return 0

        lax.fori_loop(0, 2 * heads, body, 0)

    attend(0)
    k_chain.second()
    v_chain.second()
    attend(2)
    k_chain.arrived(2)
    v_chain.arrived(2)
    attend(1)
    k_chain.third()
    v_chain.third()
    attend(4)
    q_chain.second()
    k_chain.arrived(3)
    v_chain.arrived(3)
    attend(3)
    stores.append(pltpu.make_async_copy(kx, k_out, store_sem.at[2]))
    stores.append(pltpu.make_async_copy(vx, v_out, store_sem.at[3]))
    stores[1].start()
    stores[2].start()

    for k in range(heads):
        lanes = slice(k * HEAD_DIM, (k + 1) * HEAD_DIM)
        out = jnp.where(valid_ref[...] > 0, acc[:, lanes] / totals[k], 0.0)
        att_out[:, lanes] = out.astype(BF16)
        lse = tops[k] + jnp.log2(totals[k])
        lse_out[k] = lse
        row_out[k] = jnp.broadcast_to(lse, (rows, HEAD_DIM)).T[0:1, :]

    att_swap = remote(att_out, att_got, two_send.at[4], two_recv.at[4], pair, h)
    att_swap.start()
    share = devices // 4
    here = pl.ds(core * share, share)
    one_swap = remote(
        turned.at[here, 1 - odd], one_got.at[here], two_send.at[5], two_recv.at[5], pair, h
    )
    one_pass = remote(
        one_got.at[here], one_got.at[here], two_send.at[6], two_recv.at[6], s, mate
    )
    two_pass = remote(
        two_got.at[here], two_got.at[here], two_send.at[7], two_recv.at[7], s, mate
    )
    one_swap.start()

    og_stores[0].wait()
    og_stores[1].wait()
    blocks = two_blocks.reshape(devices // 2, 2, rows, depth)

    def to_pair(i):
        at = pl.ds(i * step, step)
        return remote(
            blocks.at[here, 1 - odd, at, :],
            two_got.at[here, at, :],
            two_send.at[i],
            two_recv.at[i],
            pair,
            h,
        )

    half = width // 2
    loads[3].wait()
    mine = pl.ds(pl.multiple_of(core * half, half), half)
    theirs = pl.ds(pl.multiple_of((1 - core) * half, half), half)

    for i in range(4):
        part = dot_nt(att_out[i * step : (i + 1) * step, :], wo[theirs, :])
        core_send[i] = part.astype(BF16)
        head_sum.to_mate(i, core_send.at[i]).start()
    for i in range(4):
        part = dot_nt(att_out[i * step : (i + 1) * step, :], wo[mine, :])
        head_sum.chip_sum(i, part)
    q_chain.third()

    def finish(i):
        at = slice(i * step, (i + 1) * step)
        total = x_ref[at, :].astype(F32) + head_sum.joined(i)
        mid[at, :] = total
        root = lax.rsqrt(jnp.mean(total * total, axis=-1, keepdims=True) + EPS)
        two = (total * root * gain_two_ref[...]).astype(BF16)
        normed[at, :] = two
        for j in range(devices):
            two_blocks[j, at, :] = two[:, j * depth : (j + 1) * depth]
        to_pair(i).start()

    for i in range(4):
        head_sum.total(i)
        if i > 0:
            finish(i - 1)
    finish(3)
    for src, dst in (
        (mid, mid_out),
        (normed, two_out),
        (blocks.at[:, odd], two_keep_out),
    ):
        stores.append(pltpu.make_async_copy(src, dst, store_sem.at[2 + len(stores)]))
        stores[-1].start()
    q_chain.arrived(2)
    q_chain.arrived(3)
    stores.append(pltpu.make_async_copy(qx, q_out, store_sem.at[2 + len(stores)]))
    stores[-1].start()
    one_swap.wait_recv()
    one_pass.start()
    for i in range(4):
        to_pair(i).wait_recv()
    two_pass.start()
    one_pass.wait_recv()
    stores.append(pltpu.make_async_copy(one_got, one_got_out, store_sem.at[2 + len(stores)]))
    stores[-1].start()
    two_pass.wait_recv()
    stores.append(pltpu.make_async_copy(two_got, two_got_out, store_sem.at[2 + len(stores)]))
    stores[-1].start()
    att_swap.wait()
    one_swap.wait_send()
    one_pass.wait_send()
    two_pass.wait_send()
    for i in range(4):
        to_pair(i).wait_send()
    for chain in (k_chain, v_chain, q_chain):
        chain.all_sent()
    head_sum.all_sent()
    for store in stores:
        store.wait()


def forward(devices, cores, lengths, x, gains, grad, weights, w_out, prevs):
    rows, width = x.shape
    cols = weights[0].shape[1]
    heads = cols // HEAD_DIM
    depth = width // devices
    parts = WINDOW // rows + 1
    step = rows // 4
    vmem = pl.BlockSpec(memory_space=pltpu.VMEM)
    hbm = pl.BlockSpec(memory_space=pl.ANY)

    def shape(*dims, dtype=BF16):
        return jax.ShapeDtypeStruct(dims, dtype)

    blocks = pltpu.VMEM((4, step, width // 2), BF16)
    dma = pltpu.SemaphoreType.DMA
    return pl.pallas_call(
        functools.partial(forward_kernel, devices, cores),
        in_specs=[pl.BlockSpec(memory_space=pltpu.SMEM)] + [vmem] * 3 + [hbm] * 7,
        out_specs=[hbm] * 11 + [vmem] * 9,
        out_shape=[
            shape(parts, rows, cols),
            shape(parts, rows, cols),
            shape(parts, rows, cols),
            shape(devices // 2, depth, rows),
            shape(devices // 2, depth, rows),
            shape(rows, width, dtype=F32),
            shape(rows, width),
            shape(devices // 2, rows, depth),
            shape(devices // 2, rows, depth),
            shape(devices // 4, 2, rows, depth),
            shape(devices // 4, 2, rows, depth),
            shape(rows, cols),
            shape(rows, cols),
            shape(heads, rows, 1, dtype=F32),
            shape(heads, 1, rows, dtype=F32),
            shape(rows, HEAD_DIM, dtype=F32),
            shape(rows, HEAD_DIM, dtype=F32),
            shape(rows, 1, dtype=jnp.int32),
            shape(1, parts * rows, dtype=jnp.int32),
            shape(rows, 1, dtype=jnp.int32),
        ],
        scratch_shapes=[pltpu.VMEM((parts, rows, cols), BF16)] * 3
        + [pltpu.VMEM((width, cols), BF16)] * 4
        + [
            pltpu.VMEM((rows, width), BF16),
            pltpu.VMEM((devices, depth, rows), BF16),
            pltpu.VMEM((heads, rows, 1), F32),
            pltpu.VMEM((heads, rows, 1), F32),
            pltpu.VMEM((rows, cols), F32),
        ]
        + [blocks] * 6
        + [
            pltpu.VMEM((rows, width), F32),
            pltpu.VMEM((devices, rows, depth), BF16),
            pltpu.VMEM((devices // 2, rows, depth), BF16),
            pltpu.VMEM((devices // 2, depth, rows), BF16),
            pltpu.VMEM((rows, width), BF16),
            dma((9,)),
            dma((12,)),
        ]
        + [dma((4,))] * 6
        + [dma((12,))] * 2
        + [dma((8,))] * 2,
        compiler_params=pltpu.CompilerParams(
            collective_id=0, has_side_effects=True, vmem_limit_bytes=56 << 20
        ),
        cost_estimate=cost(10 * rows * width * cols, 40 << 20),
        name="forward",
    )(lengths, x, *gains, grad, *weights, w_out, *prevs)


def norm_two_kernel(
    devices,
    cores,
    parts_ref,
    mid_ref,
    gain_ref,
    og_ref,
    wo_ref,
    att_ref,
    valid_ref,
    lse_row_ref,
    act_ref,
    wd_hbm,
    branch_out,
    gm_out,
    keep_out,
    give_out,
    part_out,
    do_out,
    delta_out,
    stat_out,
    core_got,
    chip,
    y_got,
    own_half,
    other_half,
    flipped,
    wd,
    act,
    store_sem,
    sum_send,
    sum_recv,
):
    rows, width = mid_ref.shape
    heads = att_ref.shape[1] // HEAD_DIM
    step = rows // 4
    s, h, odd, core, pair, mate, across = place(devices, cores)
    head_sum = HeadSum(
        devices, cores, core_got, chip, y_got, own_half, other_half, sum_send, sum_recv
    )
    load = pltpu.make_async_copy(wd_hbm, wd, store_sem.at[2])
    load.start()
    greet(s, mate)
    greet(s, across)
    pl.semaphore_wait(pltpu.get_barrier_semaphore(), 2)
    for i in range(4):
        head_sum.to_mate(i, parts_ref.at[0, pl.ds(i * step, step), :]).start()
    for i in range(4):
        head_sum.chip_sum(i, parts_ref[1, i * step : (i + 1) * step, :].astype(F32))

    half = width // 2
    act[...] = act_ref[...].T
    load.wait()

    def product(i, _):
        start = lax.rem(i // 2 + 1 + core, 2) * half + lax.rem(i, 2) * (half // 2)
        lanes = pl.ds(pl.multiple_of(start, half // 2), half // 2)
        to = pl.ds(pl.multiple_of(lax.rem(i, 2) * (half // 2), half // 2), half // 2)
        branch_out[i // 2, :, to] = jnp.dot(
            act[...], wd[:, lanes], preferred_element_type=F32
        ).astype(BF16)
        return 0

    lax.fori_loop(0, 4, product, 0)

    def finish(i):
        at = slice(i * step, (i + 1) * step)
        x = mid_ref[at, :]
        root = lax.rsqrt(jnp.mean(x * x, axis=-1, keepdims=True) + EPS)
        grad = head_sum.joined(i)
        unit = x * root
        part = jnp.sum(grad * unit, axis=0, keepdims=True)
        part_out[...] = part if i == 0 else part_out[...] + part
        grad = grad * gain_ref[...]
        total = og_ref[at, :].astype(F32) + root * (
            grad - unit * jnp.mean(grad * unit, axis=-1, keepdims=True)
        )
        gm_out[at, :] = total
        low = total.astype(BF16)
        flipped[:, :, at] = low.T.reshape(devices, width // devices, step)
        do = jnp.dot(low, wo_ref[...], preferred_element_type=F32).astype(BF16).astype(F32)
        do = jnp.where(valid_ref[at, :] > 0, do, 0.0)
        do_out[at, :] = do.astype(BF16)
        product = do * att_ref[at, :].astype(F32)
        for k in range(heads):
            delta = jnp.sum(product[:, k * HEAD_DIM : (k + 1) * HEAD_DIM], axis=1, keepdims=True)
            delta_out[k, at, :] = delta
            stat_out[k, 0:1, at] = lse_row_ref[k, :, at]
            stat_out[k, 1:2, at] = jnp.broadcast_to(delta, (step, HEAD_DIM)).T[0:1, :]

    for i in range(4):
        head_sum.total(i)
        if i > 0:
            finish(i - 1)
    finish(3)
    split = flipped.reshape(devices // 2, 2, width // devices, rows)
    stores = [
        pltpu.make_async_copy(split.at[:, odd], keep_out, store_sem.at[0]),
        pltpu.make_async_copy(split.at[:, 1 - odd], give_out, store_sem.at[1]),
    ]
    stores[0].start()
    stores[1].start()
    head_sum.all_sent()
    stores[0].wait()
    stores[1].wait()


def sum_scratch(rows, width):
    return [pltpu.VMEM((4, rows // 4, width // 2), BF16)] * 5


def norm_two_back(
    devices, cores, parts, mid, gain, grad, w_out, attended, valid, lse_row, act, w_down
):
    rows, width = mid.shape
    cols = attended.shape[1]
    heads = cols // HEAD_DIM
    depth = width // devices
    vmem = pl.BlockSpec(memory_space=pltpu.VMEM)
    hbm = pl.BlockSpec(memory_space=pl.ANY)
    dma = pltpu.SemaphoreType.DMA
    return pl.pallas_call(
        functools.partial(norm_two_kernel, devices, cores),
        in_specs=[vmem] * 9 + [hbm],
        out_specs=[vmem, vmem, hbm, hbm] + [vmem] * 4,
        out_shape=[
            jax.ShapeDtypeStruct((2, rows, width // 2), BF16),
            jax.ShapeDtypeStruct((rows, width), F32),
            jax.ShapeDtypeStruct((devices // 2, depth, rows), BF16),
            jax.ShapeDtypeStruct((devices // 2, depth, rows), BF16),
            jax.ShapeDtypeStruct((1, width), F32),
            jax.ShapeDtypeStruct((rows, cols), BF16),
            jax.ShapeDtypeStruct((heads, rows, 1), F32),
            jax.ShapeDtypeStruct((heads, 2, rows), F32),
        ],
        scratch_shapes=sum_scratch(rows, width)
        + [
            pltpu.VMEM((devices, depth, rows), BF16),
            pltpu.VMEM(w_down.shape, BF16),
            pltpu.VMEM(act.shape[::-1], BF16),
            dma((3,)),
            dma((12,)),
            dma((12,)),
        ],
        compiler_params=pltpu.CompilerParams(
            collective_id=1, has_side_effects=True, vmem_limit_bytes=52 << 20
        ),
        cost_estimate=cost(4 * rows * width * cols, 60 << 20),
        name="norm_two_back",
    )(parts, mid, gain, grad, w_out, attended, valid, lse_row, act, w_down)


def attention_back_kernel(
    devices,
    cores,
    do_hbm,
    stat_hbm,
    gg_hbm,
    gg_got_hbm,
    two_hbm,
    two_got_hbm,
    parts_ref,
    mid_ref,
    lo_ref,
    lo_row_ref,
    cos_ref,
    sin_ref,
    kx,
    vx,
    qx,
    lse_ref,
    delta_ref,
    block_out,
    gq_out,
    gk_out,
    gv_out,
    gate_got,
    dx,
    sx,
    dk_acc,
    dv_acc,
    core_got,
    chip,
    y_got,
    own_half,
    other_half,
    gate_g,
    gate_x,
    gate_slot,
    gate_sem,
    gate_send,
    gate_recv,
    load_sem,
    d_send,
    d_recv,
    s_send,
    s_recv,
    sum_send,
    sum_recv,
):
    parts, rows, cols = kx.shape
    heads = cols // HEAD_DIM
    step = rows // 4
    sub = rows // 2
    s, h, odd, core, pair, mate, across = place(devices, cores)
    scale = HEAD_DIM ** (-0.5) * LOG2E
    d_chain = Chain(devices, dx, d_send, d_recv, -1)
    s_chain = Chain(devices, sx, s_send, s_recv, -1)
    head_sum = HeadSum(
        devices, cores, core_got, chip, y_got, own_half, other_half, sum_send, sum_recv
    )
    gate = Give(
        devices,
        1,
        (gg_hbm, gg_got_hbm, two_hbm, two_got_hbm),
        (gate_g, gate_x, gate_slot, gate_got, gate_sem),
        gate_send,
        gate_recv,
    )
    greet_all(devices, cores)
    loads = [
        pltpu.make_async_copy(do_hbm, dx.at[0], load_sem.at[0]),
        pltpu.make_async_copy(stat_hbm, sx.at[0], load_sem.at[1]),
    ]
    loads[0].start()
    loads[1].start()
    gate.load()

    @pl.when(s >= devices - 2)
    def _():
        for d in (2, 4):
            dx[d] = jnp.zeros_like(dx[d])
            sx[d] = jnp.zeros_like(sx[d])

    loads[0].wait()
    loads[1].wait()
    all_greeted(devices)
    d_chain.first()
    s_chain.first()
    for i in range(4):
        head_sum.to_mate(i, parts_ref.at[0, pl.ds(i * step, step), :]).start()

    def queries_back(start, count):
        def body(i, _):
            k = start + i // 2
            at = pl.ds(pl.multiple_of((i % 2) * sub, sub), sub)
            lanes = pl.ds(pl.multiple_of(k * HEAD_DIM, HEAD_DIM), HEAD_DIM)
            q, do, lo = qx[0, at, lanes], dx[0, at, lanes], lo_ref[at, :]
            lse, delta = lse_ref[k, at, :], delta_ref[k, at, :]
            total = jnp.zeros((sub, HEAD_DIM), F32)
            for d in range(parts):
                key = kx[d, :, lanes]
                scores = dot_nt(q, key)
                u = lax.broadcasted_iota(jnp.int32, scores.shape, 1) - d * rows
                seen = u >= lo
                if d == 0:
                    t = lax.broadcasted_iota(jnp.int32, scores.shape, 0) + (i % 2) * sub
                    seen = seen & (u <= t)
                p = jnp.exp2(jnp.where(seen, scores * scale, MASKED) - lse)
                ds = (p * (dot_nt(do, vx[d, :, lanes]) - delta)).astype(BF16)
                total = total + jnp.dot(ds, key, preferred_element_type=F32)
            gq_out[at, lanes] = turned_back(
                total * HEAD_DIM ** (-0.5), cos_ref[at, :], sin_ref[at, :]
            )
            return 0

        lax.fori_loop(0, 2 * count, body, 0)

    def keys_back(d):
        def body(i, _):
            k = i // 2
            at = pl.ds(pl.multiple_of((i % 2) * sub, sub), sub)
            lanes = pl.ds(pl.multiple_of(k * HEAD_DIM, HEAD_DIM), HEAD_DIM)
            key, value = kx[0, at, lanes], vx[0, at, lanes]
            q, do = qx[d, :, lanes], dx[d, :, lanes]
            scores = dot_nt(key, q)
            u = lax.broadcasted_iota(jnp.int32, scores.shape, 0) + (i % 2) * sub
            seen = u >= lo_row_ref[:, d * rows : (d + 1) * rows]
            if d == 0:
                seen = seen & (u <= lax.broadcasted_iota(jnp.int32, scores.shape, 1))
            lse, delta = sx[d, k, 0:1, :], sx[d, k, 1:2, :]
            p = jnp.exp2(jnp.where(seen, scores * scale - lse, MASKED))
            dv = jnp.dot(p.astype(BF16), do, preferred_element_type=F32)
            ds = (p * (dot_nt(value, do) - delta)).astype(BF16)
            dk = jnp.dot(ds, q, preferred_element_type=F32)
            if d > 0:
                dv = dv + dv_acc[at, lanes]
                dk = dk + dk_acc[at, lanes]
            dv_acc[at, lanes] = dv
            dk_acc[at, lanes] = dk
            return 0

        lax.fori_loop(0, 2 * heads, body, 0)

    gate.loaded()
    gate.make(0)
    gate.half(0, 0).start()
    queries_back(0, heads // 4)
    for i in range(4):
        head_sum.chip_sum(i, parts_ref[1, i * step : (i + 1) * step, :].astype(F32))
    s_chain.second()
    d_chain.second()
    gate.half(0, 1).start()
    for j in range(1, gate.count):
        gate.make(j)
        gate.half(j, 0).start()
        gate.half(j, 1).start()
    queries_back(heads // 4, heads // 2)
    keys_back(0)
    keys_back(2)
    s_chain.third()
    d_chain.third()
    queries_back(heads // 4 + heads // 2, heads - heads // 4 - heads // 2)
    for i in range(4):
        head_sum.total(i)
    s_chain.arrived(2)
    d_chain.arrived(2)
    keys_back(1)
    keys_back(4)
    for i in range(4):
        at = slice(i * step, (i + 1) * step)
        block_out[at, :] = (mid_ref[at, :] + head_sum.joined(i)).astype(BF16)
    s_chain.arrived(3)
    d_chain.arrived(3)
    keys_back(3)
    for k in range(heads):
        lanes = slice(k * HEAD_DIM, (k + 1) * HEAD_DIM)
        gk_out[:, lanes] = turned_back(
            dk_acc[:, lanes] * HEAD_DIM ** (-0.5), cos_ref[...], sin_ref[...]
        )
        gv_out[:, lanes] = dv_acc[:, lanes].astype(BF16)
    d_chain.all_sent()
    s_chain.all_sent()
    head_sum.all_sent()
    gate.finish()


def attention_back(
    devices, cores, do, stat, gate, branch, mid, low_col, low_row, tables, keys, values, queries, lse, delta
):
    rows, width = mid.shape
    parts, _, cols = keys.shape
    heads = cols // HEAD_DIM
    units = gate[0].shape[0]
    count, depth = devices // 4, width // devices
    vmem = pl.BlockSpec(memory_space=pltpu.VMEM)
    hbm = pl.BlockSpec(memory_space=pl.ANY)
    dma = pltpu.SemaphoreType.DMA
    give = [
        pltpu.VMEM((2, units, rows), BF16),
        pltpu.VMEM((2, count, rows, depth), BF16),
        pltpu.VMEM((count, units, depth), BF16),
        dma((2 + 2 * count,)),
        dma((2 * count,)),
        dma((2 * count,)),
    ]
    flops = 14 * rows * rows * parts * cols
    return pl.pallas_call(
        functools.partial(attention_back_kernel, devices, cores),
        in_specs=[hbm] * 6 + [vmem] * 11,
        out_specs=[vmem] * 5,
        out_shape=[jax.ShapeDtypeStruct((rows, width), BF16)]
        + [jax.ShapeDtypeStruct((rows, cols), BF16)] * 3
        + [jax.ShapeDtypeStruct((count, units, depth), BF16)],
        scratch_shapes=[
            pltpu.VMEM((parts, rows, cols), BF16),
            pltpu.VMEM((parts, heads, 2, rows), F32),
            pltpu.VMEM((rows, cols), F32),
            pltpu.VMEM((rows, cols), F32),
        ]
        + sum_scratch(rows, width)
        + give
        + [dma((2,))]
        + [dma((4,))] * 4
        + [dma((12,))] * 2,
        compiler_params=pltpu.CompilerParams(
            collective_id=2, has_side_effects=True, vmem_limit_bytes=58 << 20
        ),
        cost_estimate=cost(flops, 80 << 20),
        name="attention_back",
    )(do, stat, *gate, branch, mid, low_col, low_row, *tables, keys, values, queries, lse, delta)


class Reduce:
    def __init__(self, block, near, far, slot, got, keep, last, send, recv):
        self.h = lax.axis_index("head")
        self.block, self.near_seq, self.far_seq = block, near, far
        self.slot, self.got, self.keep, self.last = slot, got, keep, last
        self.send, self.recv = send, recv

    def near(self, j):
        return remote(
            self.slot.at[j], self.got.at[j], self.send.at[j], self.recv.at[j], self.near_seq, self.h
        )

    def far(self):
        return remote(
            self.keep.at[1], self.last, self.send.at[2], self.recv.at[2], self.far_seq, self.h
        )

    def give(self):
        for j in range(2):
            self.slot[j] = self.block(2 + j).astype(BF16)
            self.near(j).start()

    def combine(self, received=None):
        for j in (1, 0):
            total = self.block(j)
            if received is None:
                self.near(j).wait_recv()
            total = total + self.got[j].astype(F32)
            self.keep[j] = total.astype(BF16)
            if j == 1:
                self.far().start()

    def result(self):
        self.far().wait_recv()
        return (self.keep[0].astype(F32) + self.last[...].astype(F32)).astype(BF16)

    def all_sent(self, gave):
        if gave:
            self.near(0).wait_send()
            self.near(1).wait_send()
        self.far().wait_send()


def weights_kernel(
    devices,
    cores,
    gate_hbm,
    gate_other_hbm,
    up_hbm,
    up_other_hbm,
    down_hbm,
    down_other_hbm,
    two_hbm,
    two_other_hbm,
    og_hbm,
    og_other_hbm,
    gate_got_hbm,
    mid_give_hbm,
    wq_hbm,
    wk_hbm,
    wv_hbm,
    gm_hbm,
    x_ref,
    gain_ref,
    mlp_part_ref,
    gq,
    gk,
    gv,
    att,
    att_other,
    one,
    one_other,
    mid_x,
    gate_out,
    up_out,
    down_out,
    wq_out,
    wk_out,
    wv_out,
    wo_out,
    tokens_out,
    gains_out,
    g_a,
    g_b,
    x_a,
    x_b,
    up_slot,
    down_slot,
    got_mlp,
    keep_mlp,
    last_mlp,
    gq_other,
    gk_other,
    gv_other,
    mid_other,
    slot_att,
    got_att,
    keep_att,
    last_att,
    wq,
    wk,
    wv,
    gm,
    core_send,
    core_got,
    chip,
    y_got,
    own_half,
    other_half,
    gains_got,
    load_sem,
    gm_sem,
    x_send,
    x_recv,
    job_send,
    job_recv,
    sum_send,
    sum_recv,
    gain_send,
    gain_recv,
):
    rows, width = x_ref.shape
    half = width // 2
    step = rows // 4
    s, h, odd, core, pair, mate, across = place(devices, cores)
    near, far = differing(s, 2), differing(s, 4)
    head_sum = HeadSum(
        devices, cores, core_got, chip, y_got, own_half, other_half, sum_send, sum_recv
    )
    greet(pair, h)
    greet(near, h)
    greet(far, h)
    greet(s, mate)
    greet(s, across)

    def position(first, p):
        bits = shard_orders(first, devices)
        shard = s
        for k, b in enumerate(bits[1:]):
            if (p >> (len(bits) - 2 - k)) & 1:
                shard = differing(shard, b)
        return shard // (2 * first) * first + lax.rem(shard, first)

    count = [0]

    def load(src, dst):
        copy = pltpu.make_async_copy(src, dst, load_sem.at[count[0]])
        count[0] += 1
        copy.start()
        return copy

    def load_job(g_own, g_other, x_own, x_other, g, x, first, blocks):
        copies = [load(g_own, g.at[0]), load(g_other, g.at[1])]
        for p in blocks:
            at = position(first, p)
            copies += [load(x_own.at[at], x.at[0, p]), load(x_other.at[at], x.at[1, p])]
        return copies

    def wait(copies):
        for copy in copies:
            copy.wait()

    gate_loads = load_job(gate_hbm, gate_other_hbm, two_hbm, two_other_hbm, g_a, x_a, 1, (0, 1))
    gate_loads.append(load(gate_got_hbm, got_mlp.at[0]))
    up_loads = load_job(up_hbm, up_other_hbm, two_hbm, two_other_hbm, g_b, x_b, 1, (0, 1, 2, 3))
    w_loads = [load(wq_hbm, wq), load(wk_hbm, wk), load(wv_hbm, wv)]

    def gm_load(i):
        return pltpu.make_async_copy(
            gm_hbm.at[pl.ds(i * step, step), :], gm.at[i % 2], gm_sem.at[i % 2]
        )

    gm_load(0).start()
    gm_load(1).start()

    def mlp_block(g, x):
        def block(p):
            total = jnp.dot(g[0], x[0, p], preferred_element_type=F32)
            return total + jnp.dot(g[1], x[1, p], preferred_element_type=F32)

        return block

    def att_block(x_own, x_other, g_own, g_other):
        def block(p):
            at = position(1, p)
            total = jnp.dot(x_own[at], g_own[...], preferred_element_type=F32)
            return total + jnp.dot(x_other[at], g_other[...], preferred_element_type=F32)

        return block

    def job(k, block, first_seq, slot, got, keep, last):
        return Reduce(block, first_seq, far, slot, got, keep, last, job_send.at[k], job_recv.at[k])

    gate = job(0, mlp_block(g_a, x_a), near, None, got_mlp.at[0], keep_mlp.at[0], last_mlp.at[0])
    up = job(1, mlp_block(g_b, x_b), near, up_slot, got_mlp.at[1], keep_mlp.at[1], last_mlp.at[1])
    down = job(2, mlp_block(g_a, x_a), pair, down_slot, got_mlp.at[2], keep_mlp.at[2], last_mlp.at[2])
    attention = []
    for k, operands in enumerate(
        (
            (one, one_other, gq, gq_other),
            (one, one_other, gk, gk_other),
            (one, one_other, gv, gv_other),
            (mid_x, mid_other, att, att_other),
        )
    ):
        attention.append(
            job(
                3 + k,
                att_block(*operands),
                near,
                slot_att.at[k],
                got_att.at[k],
                keep_att.at[k],
                last_att.at[k],
            )
        )

    pl.semaphore_wait(pltpu.get_barrier_semaphore(), 5)
    swaps = [
        remote(src, dst, x_send.at[i], x_recv.at[i], pair, h)
        for i, (src, dst) in enumerate(
            ((gq, gq_other), (gk, gk_other), (gv, gv_other), (mid_give_hbm, mid_other))
        )
    ]
    for copy in swaps[:3]:
        copy.start()

    wait(gate_loads)
    gate.combine(True)
    down_loads = load_job(down_hbm, down_other_hbm, og_hbm, og_other_hbm, g_a, x_a, 2, (0, 1, 2, 3))
    wait(up_loads)
    up.give()
    wait(down_loads)
    down.give()
    swaps[3].start()

    wait(w_loads)
    mine, theirs = (pl.multiple_of(c * half, half) for c in (core, 1 - core))

    def product(i, start):
        at = slice(i * step, (i + 1) * step)
        total = None
        for g, w in ((gq, wq), (gk, wk), (gv, wv)):
            term = dot_nt(g[at, :], w[pl.ds(start, half), :])
            total = term if total is None else total + term
        return total

    for i in range(4):
        core_send[i] = product(i, theirs).astype(BF16)
        head_sum.to_mate(i, core_send.at[i]).start()
    for i in range(4):
        head_sum.chip_sum(i, product(i, mine))
    for k in range(3):
        swaps[k].wait_recv()
        attention[k].give()

    def finish(i):
        at = slice(i * step, (i + 1) * step)
        gm_load(i).wait()
        x = x_ref[at, :].astype(F32)
        root = lax.rsqrt(jnp.mean(x * x, axis=-1, keepdims=True) + EPS)
        grad = head_sum.joined(i)
        unit = x * root
        part = jnp.sum(grad * unit, axis=0, keepdims=True)
        gains_out[0:1, :] = part if i == 0 else gains_out[0:1, :] + part
        grad = grad * gain_ref[...]
        total = gm[i % 2] + root * (grad - unit * jnp.mean(grad * unit, axis=-1, keepdims=True))
        tokens_out[at, :] = total.astype(BF16)
        if i < 2:
            gm_load(i + 2).start()

    up.combine()
    for i in range(4):
        head_sum.total(i)
        if i > 0:
            finish(i - 1)
    finish(3)
    gains_out[1:2, :] = mlp_part_ref[...]

    def gain_swap(k, seq):
        return remote(gains_out, gains_got.at[k], gain_send.at[k], gain_recv.at[k], seq, h)

    def gain_step(k, seq):
        gain_swap(k, seq).wait()
        gains_out[...] = gains_out[...] + gains_got[k]

    gain_swap(0, pair).start()
    attention[0].combine()
    attention[1].combine()
    gain_step(0, pair)
    gain_swap(1, near).start()
    down.combine()
    swaps[3].wait_recv()
    attention[3].give()
    attention[2].combine()
    gain_step(1, near)
    gain_swap(2, far).start()
    attention[3].combine()
    gate_out[...] = gate.result()
    down_out[...] = down.result()
    up_out[...] = up.result()
    gain_step(2, far)
    for k, out in enumerate((wq_out, wk_out, wv_out, wo_out)):
        out[...] = attention[k].result()
    gate.all_sent(False)
    down.all_sent(True)
    up.all_sent(True)
    for k in range(4):
        attention[k].all_sent(True)
        swaps[k].wait_send()
    head_sum.all_sent()


def weight_gradients(
    devices, cores, mlp_operands, others, weights, grad_mid, x, gain, mlp_part, attention_operands
):
    rows, width = x.shape
    units = mlp_operands[0].shape[0]
    cols = weights[0].shape[1]
    depth = width // devices
    vmem = pl.BlockSpec(memory_space=pltpu.VMEM)
    hbm = pl.BlockSpec(memory_space=pl.ANY)
    dma = pltpu.SemaphoreType.DMA
    operands = (*mlp_operands, *others, *weights, grad_mid)
    kept = (x, gain, mlp_part, *attention_operands)
    return pl.pallas_call(
        functools.partial(weights_kernel, devices, cores),
        in_specs=[hbm] * len(operands) + [vmem] * len(kept),
        out_specs=[vmem] * 9,
        out_shape=[jax.ShapeDtypeStruct((units, depth), BF16)] * 3
        + [jax.ShapeDtypeStruct((depth, cols), BF16)] * 4
        + [jax.ShapeDtypeStruct((rows, width), BF16), jax.ShapeDtypeStruct((2, width), F32)],
        scratch_shapes=[
            pltpu.VMEM((2, units, rows), BF16),
            pltpu.VMEM((2, units, rows), BF16),
            pltpu.VMEM((2, 4, rows, depth), BF16),
            pltpu.VMEM((2, 4, rows, depth), BF16),
            pltpu.VMEM((2, units, depth), BF16),
            pltpu.VMEM((2, units, depth), BF16),
            pltpu.VMEM((3, 2, units, depth), BF16),
            pltpu.VMEM((3, 2, units, depth), BF16),
            pltpu.VMEM((3, units, depth), BF16),
        ]
        + [pltpu.VMEM((rows, cols), BF16)] * 3
        + [
            pltpu.VMEM((devices // 2, depth, rows), BF16),
            pltpu.VMEM((4, 2, depth, cols), BF16),
            pltpu.VMEM((4, 2, depth, cols), BF16),
            pltpu.VMEM((4, 2, depth, cols), BF16),
            pltpu.VMEM((4, depth, cols), BF16),
        ]
        + [pltpu.VMEM((width, cols), BF16)] * 3
        + [pltpu.VMEM((2, rows // 4, width), F32)]
        + [pltpu.VMEM((4, rows // 4, width // 2), BF16)]
        + sum_scratch(rows, width)
        + [pltpu.VMEM((3, 2, width), F32)]
        + [dma((32,)), dma((2,)), dma((4,)), dma((4,)), dma((7, 3)), dma((7, 3))]
        + [dma((12,)), dma((12,)), dma((3,)), dma((3,))],
        compiler_params=pltpu.CompilerParams(
            collective_id=3, has_side_effects=True, vmem_limit_bytes=62 << 20
        ),
        cost_estimate=cost(20 * rows * width * cols, 60 << 20),
        name="weight_gradients",
    )(*operands, *kept)


def on_device(
    tokens,
    gain_attn,
    gain_mlp,
    w_query,
    w_key,
    w_value,
    w_out,
    w_gate,
    w_up,
    w_down,
    prev_keys,
    prev_values,
    lengths,
    out_grad,
):
    rows = tokens.shape[0]
    width = w_query.shape[1]
    devices, cores = lax.axis_size("seq"), lax.axis_size("head")
    index = lax.axis_index("seq")
    bits = jnp.stack([index & 1, lax.axis_index("head") & 1]).astype(jnp.int32)
    gain_one, gain_two = gain_attn[None, :], gain_mlp[None, :]

    (
        keys,
        values,
        queries,
        one_keep,
        one_got,
        mid,
        normed_two,
        two_keep,
        two_got,
        out_keep,
        out_give,
        attended_got,
        attended,
        lse,
        lse_row,
        cosine,
        sine,
        low_col,
        low_row,
        valid,
    ) = forward(
        devices,
        cores,
        lengths,
        tokens,
        (gain_one, gain_two),
        out_grad,
        (w_key, w_value, w_query),
        w_out,
        (prev_keys, prev_values),
    )
    order = Order()
    out_keep, out_give = (a.reshape(devices // 2, rows, -1) for a in (out_keep, out_give))
    out_pair = (out_keep, swap(out_give, "seq", 2))
    one_pair = (one_keep, one_got)
    two_pair = (two_keep, two_got)
    w_gate, w_up, w_down = w_gate.T, w_up.T, w_down.T
    act, grad_gate, grad_up = mlp(normed_two, out_grad, w_gate, w_up, w_down)
    act_got = swap(act, "seq", 2)
    gate_got = swap(grad_gate, "seq", 1)
    up_got = swap(grad_up, "seq", 1)
    norm_parts = back_products(bits, grad_gate, grad_up, w_gate, w_up)
    (
        branch_parts,
        grad_mid,
        mid_keep,
        mid_give,
        gain_mlp_part,
        grad_att,
        delta,
        stat,
    ) = norm_two_back(
        devices,
        cores,
        norm_parts,
        mid,
        gain_two,
        out_grad,
        w_out,
        attended,
        valid,
        lse_row,
        act,
        w_down,
    )
    order.ran(delta)
    gate = WeightGrad(order, two_pair, grad_gate, gate_got, 1, "gate", True)
    up = WeightGrad(order, two_pair, grad_up, up_got, 1, "up", True)
    down = WeightGrad(order, out_pair, act, act_got, 2, "down", True)
    block_out, grad_query_raw, grad_key_raw, grad_value_raw, gate.got = attention_back(
        devices,
        cores,
        order.after(grad_att),
        stat,
        (grad_gate, gate_got, *two_pair),
        branch_parts,
        mid,
        low_col,
        low_row,
        (cosine, sine),
        keys,
        values,
        queries,
        lse,
        delta,
    )
    if devices == 8:
        sums = weight_gradients(
            devices,
            cores,
            (grad_gate, gate_got, grad_up, up_got, act, act_got),
            (*two_pair, *out_pair, gate.got, mid_give),
            (w_query, w_key, w_value),
            grad_mid,
            tokens,
            gain_one,
            gain_mlp_part,
            (
                grad_query_raw,
                grad_key_raw,
                grad_value_raw,
                attended,
                attended_got,
                *one_pair,
                mid_keep,
            ),
        )
        gate_grad, up_grad, down_grad = (a.astype(F32).T for a in sums[:3])
        gains = lax.dynamic_slice_in_dim(sums[8], index * sums[8].shape[1] // devices, sums[8].shape[1] // devices, 1)
        return (
            block_out,
            sums[7],
            gains[0],
            gains[1],
            *(a.astype(F32) for a in sums[3:7]),
            gate_grad,
            up_grad,
            down_grad,
        )
    order.ran(grad_query_raw)
    query_got = swap(grad_query_raw, "seq", 1)
    key_got = swap(grad_key_raw, "seq", 1)
    value_got = swap(grad_value_raw, "seq", 1)
    mid_pair = (mid_keep, swap(order.after(mid_give), "seq", 1))
    gate.keep()
    up.give()
    down.give()
    lefts = (grad_query_raw, grad_key_raw, grad_value_raw)
    rights = (w_query, w_key, w_value)
    give = order.ran(half_product(order.after(bits), lefts, rights, 1, None, "norm_one_give"))
    give = swap(give, "head", 1)
    query = WeightGrad(order, one_pair, grad_query_raw, query_got, 1, "query")
    key = WeightGrad(order, one_pair, grad_key_raw, key_got, 1, "key")
    value = WeightGrad(order, one_pair, grad_value_raw, value_got, 1, "value")
    wout = WeightGrad(order, mid_pair, attended, attended_got, 1, "wout")
    query.give()
    chip = order.ran(half_product(order.after(bits), lefts, rights, 0, give, "norm_one_keep"))
    chip_got = swap(chip, "head", 2)
    key.give()
    value.give()
    up.keep()
    down.keep()
    wout.give()
    own = (chip.astype(F32) + chip_got.astype(F32)).astype(BF16)
    other = swap(own, "head", 1)
    query.keep()
    key.keep()
    tokens_grad, gain_attn_part = by_rows(
        back_kernel,
        order.after(bits),
        (tokens, own, other, gain_one, grad_mid),
        3,
        (BF16, F32),
        "tokens_back",
        part=1,
    )
    order.ran(gain_attn_part)
    value.keep()
    wout.keep()
    gains = gain_sum(jnp.concatenate([gain_attn_part, gain_mlp_part], axis=0))
    gain_attn_grad, gain_mlp_grad = gains[0], gains[1]
    w_gate_grad, w_up_grad, w_down_grad = gate.finish(), up.finish(), down.finish()
    w_out_grad = wout.finish()
    w_query_grad, w_key_grad, w_value_grad = query.finish(), key.finish(), value.finish()
    return (
        block_out,
        tokens_grad,
        gain_attn_grad,
        gain_mlp_grad,
        w_query_grad,
        w_key_grad,
        w_value_grad,
        w_out_grad,
        w_gate_grad,
        w_up_grad,
        w_down_grad,
    )


def solution(mesh):
    by_head = P(None, "head")
    both = P("seq", "head")
    placed = (P("seq", None), P(), P()) + (by_head,) * 9 + (P(), P("seq", None))
    return jax.shard_map(
        on_device,
        mesh=mesh,
        in_specs=placed,
        out_specs=(P("seq", None), P("seq", None), P("seq"), P("seq")) + (both,) * 7,
        check_vma=False,
    )
```

```python
import functools
import math

import jax
import jax.numpy as jnp
from jax import lax
from jax.experimental import pallas as pl
from jax.experimental.pallas import tpu as pltpu
from jax.sharding import PartitionSpec as P

HEAD_DIM = 128
WINDOW = 2048
PAD = 64
NSEQ = 4
EPS = 1e-06
MASKED = -1e30
LOG2E = 1.4426950408889634
BIG = 1 << 28
F32 = jnp.float32
BF16 = jnp.bfloat16


def swap(block, axis, bit):
    return lax.ppermute(block, axis, [(i, i ^ bit) for i in range(lax.axis_size(axis))])


def shifted(block, distance):
    n = lax.axis_size("seq")
    return lax.ppermute(
        block, "seq", [(i, i + distance) for i in range(n) if 0 <= i + distance < n]
    )


BIG_VMEM = pltpu.CompilerParams(vmem_limit_bytes=48 << 20)


def cost(flops, moved):
    return pl.CostEstimate(flops=int(flops), bytes_accessed=int(moved), transcendentals=0)


def dot_nt(left, right):
    return lax.dot_general(left, right, (((1,), (1,)), ((), ())), preferred_element_type=F32)


def row_blocks(width, step):
    return pl.BlockSpec((step, width), lambda i, bits: (i, 0))


def joined(bits_ref, own_ref, other_ref):
    low = bits_ref[1] == 0
    own, other = own_ref[...].astype(F32), other_ref[...].astype(F32)
    return jnp.concatenate([jnp.where(low, own, other), jnp.where(low, other, own)], axis=1)


def back_kernel(
    bits_ref, x_ref, own_ref, other_ref, gain_ref, add_ref, out_ref, part_ref
):
    x = x_ref[...].astype(F32)
    scale = lax.rsqrt(jnp.mean(x * x, axis=-1, keepdims=True) + EPS)
    grad = joined(bits_ref, own_ref, other_ref)
    unit = x * scale
    grad_unit = grad * gain_ref[...]
    total = add_ref[...].astype(F32) + scale * (
        grad_unit - unit * jnp.mean(grad_unit * unit, axis=-1, keepdims=True)
    )
    out_ref[...] = total.astype(out_ref.dtype)
    part = jnp.sum(grad * unit, axis=0, keepdims=True)

    @pl.when(pl.program_id(0) == 0)
    def _():
        part_ref[...] = part

    @pl.when(pl.program_id(0) > 0)
    def _():
        part_ref[...] += part


def by_rows(kernel, bits, arrays, gains_at, outs, name, part=None):
    rows, width = arrays[0].shape
    step = rows // 4
    in_specs = [
        pl.BlockSpec((1, width), lambda i, bits: (0, 0))
        if k == gains_at
        else row_blocks(a.shape[1], step)
        for k, a in enumerate(arrays)
    ]
    out_specs, out_shape = [], []
    for k, dtype in enumerate(outs):
        if k == part:
            out_specs.append(pl.BlockSpec((1, width), lambda i, bits: (0, 0)))
            out_shape.append(jax.ShapeDtypeStruct((1, width), F32))
        else:
            out_specs.append(row_blocks(width, step))
            out_shape.append(jax.ShapeDtypeStruct((rows, width), dtype))
    return pl.pallas_call(
        kernel,
        grid_spec=pltpu.PrefetchScalarGridSpec(
            num_scalar_prefetch=1, grid=(rows // step,), in_specs=in_specs, out_specs=out_specs
        ),
        out_shape=out_shape,
        compiler_params=BIG_VMEM,
        cost_estimate=cost(rows * width * 10, rows * width * 2 * (len(arrays) + len(out_shape))),
        name=name,
    )(bits, *arrays)


def half_kernel(pairs, flip, added, bits_ref, *refs):
    total = refs[2 * pairs][...].astype(F32) if added else None
    for k in range(pairs):
        term = dot_nt(refs[k][...], refs[pairs + k][...])
        total = term if total is None else total + term
    refs[-1][...] = total.astype(BF16)


def half_product(bits, lefts, rights, flip, added, name):
    rows = lefts[0].shape[0]
    width = rights[0].shape[0] // 2
    step = min(width, 512)
    steps = width // step

    def at(i, bits):
        return ((bits[1] ^ flip) * steps + i, 0)

    specs = [pl.BlockSpec(a.shape, lambda i, bits: (0, 0)) for a in lefts]
    specs += [pl.BlockSpec((step, a.shape[1]), at) for a in rights]
    extra = []
    if added is not None:
        extra = [added]
        specs.append(pl.BlockSpec((rows, step), lambda i, bits: (0, i)))
    depth = sum(a.shape[1] for a in lefts)
    return pl.pallas_call(
        functools.partial(half_kernel, len(lefts), flip, added is not None),
        grid_spec=pltpu.PrefetchScalarGridSpec(
            num_scalar_prefetch=1,
            grid=(steps,),
            in_specs=specs,
            out_specs=pl.BlockSpec((rows, step), lambda i, bits: (0, i)),
        ),
        out_shape=jax.ShapeDtypeStruct((rows, width), BF16),
        compiler_params=BIG_VMEM,
        cost_estimate=cost(2 * rows * depth * width, 2 * (rows + width) * depth),
        name=name,
    )(bits, *lefts, *rights, *extra)


def blocks_kernel(order_ref, flip, xa_ref, xb_ref, ga_ref, gb_ref, *refs):
    if flip:
        total = jnp.dot(ga_ref[...], xa_ref[0], preferred_element_type=F32)
        total = total + jnp.dot(gb_ref[...], xb_ref[0], preferred_element_type=F32)
    else:
        total = jnp.dot(xa_ref[0], ga_ref[...], preferred_element_type=F32)
        total = total + jnp.dot(xb_ref[0], gb_ref[...], preferred_element_type=F32)
    if len(refs) == 2:
        total = total + refs[0][0].astype(F32)
    refs[-1][0] = total.astype(BF16)


def grad_blocks(order, x_own, x_got, g_own, g_got, added, flip, name):
    count = order.shape[0]
    if flip:
        _, rows, depth = x_own.shape
        cols = g_own.shape[0]
        shape = (cols, depth)
    else:
        _, depth, rows = x_own.shape
        cols = g_own.shape[1]
        shape = (depth, cols)
    x_spec = pl.BlockSpec((1,) + x_own.shape[1:], lambda i, order: (order[i], 0, 0))
    g_spec = pl.BlockSpec(g_own.shape, lambda i, order: (0, 0))
    out_spec = pl.BlockSpec((1,) + shape, lambda i, order: (i, 0, 0))
    extra = [] if added is None else [added]

    def kernel(order_ref, *refs):
        blocks_kernel(order_ref, flip, *refs)

    return pl.pallas_call(
        kernel,
        grid_spec=pltpu.PrefetchScalarGridSpec(
            num_scalar_prefetch=1,
            grid=(count,),
            in_specs=[x_spec, x_spec, g_spec, g_spec] + [out_spec] * len(extra),
            out_specs=out_spec,
        ),
        out_shape=jax.ShapeDtypeStruct((count,) + shape, BF16),
        compiler_params=BIG_VMEM,
        cost_estimate=cost(
            4 * count * depth * rows * cols, 2 * count * depth * cols + 4 * rows * cols
        ),
        name=name,
    )(order, x_own, x_got, g_own, g_got, *extra)


def shard_orders(first, n):
    bits = [1 << k for k in range(n.bit_length() - 1)]
    return [first] + [b for b in bits if b != first]


class Order:
    def __init__(self):
        self.last = None

    def after(self, operand):
        if self.last is None:
            return operand
        return lax.optimization_barrier((operand, self.last))[0]

    def ran(self, result):
        self.last = result
        return result


class WeightGrad:
    def __init__(self, order, x_pair, g_own, g_got, first, name, flip=False):
        n = lax.axis_size("seq")
        self.order, self.flip, self.name = order, flip, name
        self.operands = (*x_pair, g_own, g_got)
        self.bits = shard_orders(first, n)
        index = lax.axis_index("seq")
        shards = []
        for p in range(n // 2):
            apart = sum(
                b for k, b in enumerate(self.bits[1:]) if (p >> (len(self.bits) - 2 - k)) & 1
            )
            shard = index ^ apart
            shards.append(shard // (2 * first) * first + shard % first)
        self.shards = jnp.stack(shards).astype(jnp.int32)
        self.count = n // 4

    def blocks(self, shards, added, name):
        return self.order.ran(
            grad_blocks(
                self.order.after(shards), *self.operands, added, self.flip, self.name + name
            )
        )

    def give(self):
        give = self.blocks(self.shards[self.count :], None, "_give")
        self.got = swap(give, "seq", self.bits[1])

    def keep(self):
        self.part = self.blocks(self.shards[: self.count], self.got, "_keep")
        left = self.count // 2
        self.got = swap(self.part[left:], "seq", self.bits[2])

    def finish(self):
        left, part = self.count // 2, self.part
        total = part[:left].astype(F32) + self.got.astype(F32)
        for bit in self.bits[3:]:
            left //= 2
            part = total.astype(BF16)
            total = part[:left].astype(F32) + swap(part[left:], "seq", bit).astype(F32)
        return total[0].T if self.flip else total[0]


def gain_sum(part):
    n = lax.axis_size("seq")
    total = part
    bit = 1
    while bit < n:
        total = total + swap(total, "seq", bit)
        bit *= 2
    width = part.shape[-1] // n
    return lax.dynamic_slice_in_dim(total, lax.axis_index("seq") * width, width, total.ndim - 1)


def turned_back(grad, cosine, sine):
    return (grad * cosine - pltpu.roll(grad, HEAD_DIM // 2, 1) * sine).astype(BF16)


def place(devices, cores):
    s, h = lax.axis_index("seq"), lax.axis_index("head")
    odd, core = lax.rem(s, 2), lax.rem(h, 2)
    pair = s + 1 - 2 * odd
    mate = h + 1 - 2 * core
    across = lax.rem(h + cores // 2, cores)
    return s, h, odd, core, pair, mate, across


def remote(src, dst, send, recv, seq, head):
    return pltpu.make_async_remote_copy(
        src_ref=src,
        dst_ref=dst,
        send_sem=send,
        recv_sem=recv,
        device_id=(seq, head),
        device_id_type=pl.DeviceIdType.MESH,
    )


def greet(seq, head):
    pl.semaphore_signal(
        pltpu.get_barrier_semaphore(),
        inc=1,
        device_id=(seq, head),
        device_id_type=pl.DeviceIdType.MESH,
    )


def greet_all(devices, cores):
    s, h, odd, core, pair, mate, across = place(devices, cores)
    greet(pair, h)
    greet(s, mate)
    greet(s, across)

    @pl.when(s >= 2)
    def _():
        greet(s - 2, h)

    @pl.when(s < devices - 2)
    def _():
        greet(s + 2, h)


def all_greeted(devices):
    s = lax.axis_index("seq")
    inner = (s >= 2) & (s < devices - 2)

    @pl.when(inner)
    def _():
        pl.semaphore_wait(pltpu.get_barrier_semaphore(), 5)

    @pl.when(jnp.logical_not(inner))
    def _():
        pl.semaphore_wait(pltpu.get_barrier_semaphore(), 4)


class Chain:
    def __init__(self, devices, buf, send, recv, side):
        self.s, self.h = lax.axis_index("seq"), lax.axis_index("head")
        odd = lax.rem(self.s, 2)
        self.pair = self.s + 1 - 2 * odd
        self.buf, self.send, self.recv = buf, send, recv
        self.next = self.s + 2 * side
        left, right = self.s >= 2, self.s < devices - 2
        self.sends, self.gets = (right, left) if side > 0 else (left, right)
        self.early = odd == (0 if side > 0 else 1)
        self.late = odd == (1 if side > 0 else 0)

    def hop(self, slot, seq, src, dst):
        return remote(
            self.buf.at[src], self.buf.at[dst], self.send.at[slot], self.recv.at[slot], seq, self.h
        )

    def first(self):
        @pl.when(self.sends)
        def _():
            self.hop(0, self.next, 0, 2).start()

        @pl.when(self.early)
        def _():
            self.hop(2, self.pair, 0, 1).start()

    def second(self):
        @pl.when(self.gets)
        def _():
            self.hop(0, self.next, 0, 2).wait_recv()

        @pl.when(self.sends)
        def _():
            self.hop(1, self.next, 2, 4).start()

        @pl.when(self.early)
        def _():
            self.hop(3, self.pair, 2, 3).start()

        @pl.when(self.late)
        def _():
            self.hop(2, self.pair, 2, 1).start()

    def third(self):
        @pl.when(self.gets)
        def _():
            self.hop(1, self.next, 2, 4).wait_recv()

        @pl.when(self.late)
        def _():
            self.hop(3, self.pair, 4, 3).start()

    def arrived(self, slot):
        self.hop(slot, self.pair, 0, 1 if slot == 2 else 3).wait_recv()

    def all_sent(self):
        @pl.when(self.sends)
        def _():
            self.hop(0, self.next, 0, 2).wait_send()
            self.hop(1, self.next, 2, 4).wait_send()

        self.hop(2, self.pair, 0, 1).wait_send()
        self.hop(3, self.pair, 0, 3).wait_send()


def differing(s, bit):
    return s + bit - 2 * bit * lax.rem(s // bit, 2)


class Give:
    def __init__(self, devices, first, operands, bufs, send, recv):
        self.s, self.h = lax.axis_index("seq"), lax.axis_index("head")
        g_own, g_got, x_own, x_got = operands
        self.g, self.x, self.slot, self.got, sem = bufs
        self.send, self.recv = send, recv
        bits = shard_orders(first, devices)
        self.partner = differing(self.s, bits[1])
        self.count = devices // 4
        self.loads = [
            pltpu.make_async_copy(g_own, self.g.at[0], sem.at[0]),
            pltpu.make_async_copy(g_got, self.g.at[1], sem.at[1]),
        ]
        for j in range(self.count):
            shard = self.s
            for k, b in enumerate(bits[1:]):
                if ((j + self.count) >> (len(bits) - 2 - k)) & 1:
                    shard = differing(shard, b)
            at = shard // (2 * first) * first + lax.rem(shard, first)
            for k, x in enumerate((x_own, x_got)):
                self.loads.append(
                    pltpu.make_async_copy(x.at[at], self.x.at[k, j], sem.at[2 + 2 * j + k])
                )

    def load(self):
        for copy in self.loads:
            copy.start()

    def loaded(self):
        for copy in self.loads:
            copy.wait()

    def make(self, j):
        total = jnp.dot(self.g[0], self.x[0, j], preferred_element_type=F32)
        total = total + jnp.dot(self.g[1], self.x[1, j], preferred_element_type=F32)
        self.slot[j] = total.astype(BF16)

    def half(self, j, k):
        step = self.slot.shape[1] // 2
        at = pl.ds(k * step, step)
        return remote(
            self.slot.at[j, at, :],
            self.got.at[j, at, :],
            self.send.at[2 * j + k],
            self.recv.at[2 * j + k],
            self.partner,
            self.h,
        )

    def finish(self):
        for j in range(self.count):
            for k in range(2):
                self.half(j, k).wait()


class HeadSum:
    def __init__(self, devices, cores, core_got, chip, y_got, own, other, send, recv):
        self.s, self.h, _, self.core, _, self.mate, self.across = place(devices, cores)
        self.core_got, self.chip, self.y_got = core_got, chip, y_got
        self.own, self.other, self.send, self.recv = own, other, send, recv

    def to_mate(self, i, src=None):
        return remote(
            self.chip.at[i] if src is None else src,
            self.core_got.at[i],
            self.send.at[i],
            self.recv.at[i],
            self.s,
            self.mate,
        )

    def over(self, i):
        return remote(
            self.chip.at[i],
            self.y_got.at[i],
            self.send.at[4 + i],
            self.recv.at[4 + i],
            self.s,
            self.across,
        )

    def back(self, i):
        return remote(
            self.own.at[i],
            self.other.at[i],
            self.send.at[8 + i],
            self.recv.at[8 + i],
            self.s,
            self.mate,
        )

    def chip_sum(self, i, part):
        self.to_mate(i).wait_recv()
        self.chip[i] = (part + self.core_got[i].astype(F32)).astype(BF16)
        self.over(i).start()

    def total(self, i):
        self.over(i).wait_recv()
        self.own[i] = (self.chip[i].astype(F32) + self.y_got[i].astype(F32)).astype(BF16)
        self.back(i).start()

    def joined(self, i):
        self.back(i).wait_recv()
        own, other = self.own[i].astype(F32), self.other[i].astype(F32)
        low = self.core == 0
        return jnp.concatenate([jnp.where(low, own, other), jnp.where(low, other, own)], axis=1)

    def all_sent(self):
        for i in range(4):
            self.to_mate(i).wait_send()
            self.over(i).wait_send()
            self.back(i).wait_send()


def forward_kernel(
    devices,
    cores,
    lengths_ref,
    x_ref,
    gain_one_ref,
    gain_two_ref,
    og_hbm,
    wk_hbm,
    wv_hbm,
    wq_hbm,
    wo_hbm,
    prev_k_hbm,
    prev_v_hbm,
    k_out,
    v_out,
    q_out,
    one_keep_out,
    one_give_out,
    mid_out,
    two_out,
    two_keep_out,
    two_got_out,
    og_keep_out,
    og_give_out,
    og_got_out,
    att_out,
    lse_out,
    row_out,
    cos_ref,
    sin_ref,
    lo_ref,
    lo_row_ref,
    valid_ref,
    kx,
    vx,
    qx,
    wk,
    wv,
    wq,
    wo,
    normed,
    flipped,
    tops,
    totals,
    acc,
    core_send,
    core_got,
    chip,
    y_got,
    own_half,
    other_half,
    mid,
    two_blocks,
    two_got,
    og,
    load_sem,
    store_sem,
    k_send,
    k_recv,
    v_send,
    v_recv,
    q_send,
    q_recv,
    sum_send,
    sum_recv,
    two_send,
    two_recv,
):
    rows, width = x_ref.shape
    heads = kx.shape[2] // HEAD_DIM
    s, h, odd, core, pair, mate, across = place(devices, cores)
    has_left, has_right = s >= 2, s < devices - 2
    scale = HEAD_DIM ** (-0.5) * LOG2E
    k_chain = Chain(devices, kx, k_send, k_recv, 1)
    v_chain = Chain(devices, vx, v_send, v_recv, 1)
    chains = [v_chain, k_chain]
    q_chain = Chain(devices, qx, q_send, q_recv, -1)
    head_sum = HeadSum(
        devices, cores, core_got, chip, y_got, own_half, other_half, sum_send, sum_recv
    )

    loads = [
        pltpu.make_async_copy(src, dst, load_sem.at[i])
        for i, (src, dst) in enumerate(
            ((wk_hbm, wk), (wv_hbm, wv), (wq_hbm, wq), (wo_hbm, wo), (og_hbm, og))
        )
    ]
    for load in loads:
        load.start()

    greet_all(devices, cores)
    step = rows // 4

    def normalize(i, _):
        at = pl.ds(pl.multiple_of(i * step, step), step)
        x = x_ref[at, :].astype(F32)
        root = lax.rsqrt(jnp.mean(x * x, axis=-1, keepdims=True) + EPS)
        normed[at, :] = (x * root * gain_one_ref[...]).astype(BF16)
        return 0

    lax.fori_loop(0, 4, normalize, 0)

    starts, padded = [0], 0
    for r in range(NSEQ - 1):
        padded = padded + (lengths_ref[r] + PAD - 1) // PAD * PAD
        starts.append(padded)

    def sequence_of(at):
        start = jnp.zeros_like(at)
        low = jnp.full_like(at, -BIG)
        length = jnp.zeros_like(at) + lengths_ref[0]
        for r in range(1, NSEQ):
            inside = at >= starts[r]
            start = jnp.where(inside, starts[r], start)
            low = jnp.where(inside, starts[r], low)
            length = jnp.where(inside, lengths_ref[r], length)
        valid = at - start < length
        low = jnp.where(valid, jnp.maximum(low, at - (WINDOW - 1)), at)
        return at - start, valid, jnp.where(at < devices * rows, low, BIG) - s * rows

    def turn_into(weight, out):
        raw = jnp.dot(normed[...], weight[...], preferred_element_type=F32)
        for k in range(heads):
            u = raw[:, k * HEAD_DIM : (k + 1) * HEAD_DIM]
            u = u * cos_ref[...] + pltpu.roll(u, HEAD_DIM // 2, 1) * sin_ref[...]
            out[0, :, k * HEAD_DIM : (k + 1) * HEAD_DIM] = u.astype(BF16)

    loads[1].wait()
    vx[0] = jnp.dot(normed[...], wv[...], preferred_element_type=F32).astype(BF16)
    all_greeted(devices)
    v_chain.first()
    at = lax.broadcasted_iota(jnp.int32, (rows, HEAD_DIM), 0) + s * rows
    position, valid, low = sequence_of(at)
    valid_ref[...] = valid[:, 0:1].astype(jnp.int32)
    lo_ref[...] = low[:, 0:1]
    lane = lax.broadcasted_iota(jnp.int32, (1, HEAD_DIM), 1)
    half_dim = HEAD_DIM // 2
    pair_of = lax.rem(lane, half_dim).astype(F32)
    freq = jnp.exp(-math.log(10000.0) * (2.0 * pair_of / HEAD_DIM))
    angle = position.astype(F32) * freq
    cos_ref[...] = jnp.cos(angle)
    sin_ref[...] = jnp.sin(angle) * jnp.where(lane < half_dim, -1.0, 1.0)
    lo_row_ref[...] = sequence_of(lax.broadcasted_iota(jnp.int32, lo_row_ref.shape, 1) + s * rows)[2]
    loads[0].wait()
    turn_into(wk, kx)
    k_chain.first()

    @pl.when(jnp.logical_not(has_left))
    def _():
        copies = []
        for i, (src, dst) in enumerate(((prev_k_hbm, kx), (prev_v_hbm, vx))):
            for j, d in enumerate((2, 4)):
                at = pl.multiple_of((s - d) * rows + WINDOW, rows)
                copies.append(
                    pltpu.make_async_copy(
                        src.at[pl.ds(at, rows), :], dst.at[d], load_sem.at[5 + 2 * i + j]
                    )
                )
        for copy in copies:
            copy.start()
        for copy in copies:
            copy.wait()

    @pl.when(jnp.logical_not(has_right))
    def _():
        qx[2] = jnp.zeros_like(qx[2])
        qx[4] = jnp.zeros_like(qx[4])

    loads[2].wait()
    turn_into(wq, qx)
    q_chain.first()

    for i in range(4):
        flip_at = slice(i * step, (i + 1) * step)
        flipped[:, :, flip_at] = normed[flip_at, :].T.reshape(devices, width // devices, step)
    turned = flipped.reshape(devices // 2, 2, width // devices, rows)
    stores = [
        pltpu.make_async_copy(turned.at[:, odd], one_keep_out, store_sem.at[0]),
        pltpu.make_async_copy(turned.at[:, 1 - odd], one_give_out, store_sem.at[1]),
    ]
    stores[0].start()
    stores[1].start()

    depth = width // devices
    loads[4].wait()
    for j in range(devices):
        two_blocks[j] = og[:, j * depth : (j + 1) * depth]
    near = lax.rem(s // 2, 2)
    split = two_blocks.reshape(devices // 4, 2, 2, rows, depth)
    og_stores = [
        pltpu.make_async_copy(split.at[:, near], og_keep_out, store_sem.at[4]),
        pltpu.make_async_copy(split.at[:, 1 - near], og_give_out, store_sem.at[5]),
    ]
    og_stores[0].start()
    og_stores[1].start()
    sub = rows // 2

    def attend(d, only=None):
        def body(i, _):
            if only is None:
                k, part = i // 2, lax.rem(i, 2)
            else:
                k, part = i, only
            at = pl.ds(pl.multiple_of(part * sub, sub), sub)
            lanes = pl.ds(pl.multiple_of(k * HEAD_DIM, HEAD_DIM), HEAD_DIM)
            scores = dot_nt(qx[0, at, lanes], kx[d, :, lanes])
            u = lax.broadcasted_iota(jnp.int32, scores.shape, 1) - d * rows
            seen = u >= lo_ref[at, :]
            if d == 0:
                t = lax.broadcasted_iota(jnp.int32, scores.shape, 0) + part * sub
                seen = seen & (u <= t)
            scores = jnp.where(seen, scores * scale, MASKED)
            top = jnp.max(scores, axis=1, keepdims=True)
            if d > 0:
                old = tops[k, at, :]
                top = jnp.maximum(top, old)
            p = jnp.exp2(scores - top)
            total = jnp.sum(p, axis=1, keepdims=True)
            mixed = jnp.dot(p.astype(BF16), vx[d, :, lanes], preferred_element_type=F32)
            if d > 0:
                fade = jnp.exp2(old - top)
                total = total + totals[k, at, :] * fade
                mixed = mixed + acc[at, lanes] * fade
            tops[k, at, :] = top
            totals[k, at, :] = total
            acc[at, lanes] = mixed
            return 0

        lax.fori_loop(0, 2 * heads if only is None else heads, body, 0)

    attend(0)
    for chain in chains:
        chain.second()
    attend(2)
    for chain in chains:
        chain.arrived(2)
    attend(1)
    for chain in chains:
        chain.third()
    attend(4)
    q_chain.second()
    for chain in chains:
        chain.arrived(3)
    stores.append(pltpu.make_async_copy(kx, k_out, store_sem.at[2]))
    stores.append(pltpu.make_async_copy(vx, v_out, store_sem.at[3]))
    stores[2].start()
    stores[3].start()

    og_stores[0].wait()
    og_stores[1].wait()
    blocks = two_blocks.reshape(devices // 2, 2, rows, depth)

    def to_pair(i):
        at = pl.ds(i * step, step)
        return remote(
            blocks.at[here, 1 - odd, at, :],
            two_got.at[here, at, :],
            two_send.at[i],
            two_recv.at[i],
            pair,
            h,
        )

    half = width // 2
    loads[3].wait()
    mine = pl.ds(pl.multiple_of(core * half, half), half)
    theirs = pl.ds(pl.multiple_of((1 - core) * half, half), half)

    for t in range(2):
        attend(3, t)
        at = slice(t * sub, (t + 1) * sub)
        for k in range(heads):
            columns = slice(k * HEAD_DIM, (k + 1) * HEAD_DIM)
            out = jnp.where(valid_ref[at, :] > 0, acc[at, columns] / totals[k, at, :], 0.0)
            att_out[at, columns] = out.astype(BF16)
        total = dot_nt(att_out[at, :], wo[theirs, :]).astype(BF16)
        for j in range(2):
            core_send[2 * t + j] = total[j * step : (j + 1) * step, :]
            head_sum.to_mate(2 * t + j, core_send.at[2 * t + j]).start()
        total = dot_nt(att_out[at, :], wo[mine, :])
        for j in range(2):
            head_sum.chip_sum(2 * t + j, total[j * step : (j + 1) * step, :])
    for k in range(heads):
        lse = tops[k] + jnp.log2(totals[k])
        lse_out[k] = lse
        row_out[k] = jnp.broadcast_to(lse, (rows, HEAD_DIM)).T[0:1, :]
    share = devices // 4
    here = pl.ds(core * share, share)
    two_pass = remote(
        two_got.at[here], two_got.at[here], two_send.at[7], two_recv.at[7], s, mate
    )
    og_here = pl.ds(core * (devices // 8), devices // 8)
    og_swap = remote(
        og_give_out.at[og_here],
        og_got_out.at[og_here],
        two_send.at[8],
        two_recv.at[8],
        differing(s, 2),
        h,
    )
    og_pass = remote(
        og_got_out.at[og_here], og_got_out.at[og_here], two_send.at[9], two_recv.at[9], s, mate
    )
    og_swap.start()

    q_chain.third()

    def finish(i):
        at = slice(i * step, (i + 1) * step)
        total = x_ref[at, :].astype(F32) + head_sum.joined(i)
        mid[at, :] = total
        root = lax.rsqrt(jnp.mean(total * total, axis=-1, keepdims=True) + EPS)
        two = (total * root * gain_two_ref[...]).astype(BF16)
        normed[at, :] = two
        for j in range(devices):
            two_blocks[j, at, :] = two[:, j * depth : (j + 1) * depth]
        to_pair(i).start()

    for i in range(4):
        head_sum.total(i)
        if i > 0:
            finish(i - 1)
    finish(3)
    for src, dst in (
        (mid, mid_out),
        (normed, two_out),
        (blocks.at[:, odd], two_keep_out),
    ):
        stores.append(pltpu.make_async_copy(src, dst, store_sem.at[2 + len(stores)]))
        stores[-1].start()
    q_chain.arrived(2)
    q_chain.arrived(3)
    stores.append(pltpu.make_async_copy(qx, q_out, store_sem.at[2 + len(stores)]))
    stores[-1].start()
    og_swap.wait_recv()
    og_pass.start()
    for i in range(4):
        to_pair(i).wait_recv()
    two_pass.start()
    two_pass.wait_recv()
    stores.append(pltpu.make_async_copy(two_got, two_got_out, store_sem.at[2 + len(stores)]))
    stores[-1].start()
    og_swap.wait_send()
    og_pass.wait()
    two_pass.wait_send()
    for i in range(4):
        to_pair(i).wait_send()
    for chain in (*chains, q_chain):
        chain.all_sent()
    head_sum.all_sent()
    for store in stores:
        store.wait()


def forward(devices, cores, lengths, x, gains, grad, weights, w_out, prevs):
    rows, width = x.shape
    cols = weights[0].shape[1]
    heads = cols // HEAD_DIM
    depth = width // devices
    parts = WINDOW // rows + 1
    step = rows // 4
    vmem = pl.BlockSpec(memory_space=pltpu.VMEM)
    hbm = pl.BlockSpec(memory_space=pl.ANY)

    def shape(*dims, dtype=BF16):
        return jax.ShapeDtypeStruct(dims, dtype)

    blocks = pltpu.VMEM((4, step, width // 2), BF16)
    dma = pltpu.SemaphoreType.DMA
    return pl.pallas_call(
        functools.partial(forward_kernel, devices, cores),
        in_specs=[pl.BlockSpec(memory_space=pltpu.SMEM)] + [vmem] * 3 + [hbm] * 7,
        out_specs=[hbm] * 12 + [vmem] * 8,
        out_shape=[
            shape(parts, rows, cols),
            shape(parts, rows, cols),
            shape(parts, rows, cols),
            shape(devices // 2, depth, rows),
            shape(devices // 2, depth, rows),
            shape(rows, width, dtype=F32),
            shape(rows, width),
            shape(devices // 2, rows, depth),
            shape(devices // 2, rows, depth),
            shape(devices // 4, 2, rows, depth),
            shape(devices // 4, 2, rows, depth),
            shape(devices // 4, 2, rows, depth),
            shape(rows, cols),
            shape(heads, rows, 1, dtype=F32),
            shape(heads, 1, rows, dtype=F32),
            shape(rows, HEAD_DIM, dtype=F32),
            shape(rows, HEAD_DIM, dtype=F32),
            shape(rows, 1, dtype=jnp.int32),
            shape(1, parts * rows, dtype=jnp.int32),
            shape(rows, 1, dtype=jnp.int32),
        ],
        scratch_shapes=[pltpu.VMEM((parts, rows, cols), BF16)] * 3
        + [pltpu.VMEM((width, cols), BF16)] * 4
        + [
            pltpu.VMEM((rows, width), BF16),
            pltpu.VMEM((devices, depth, rows), BF16),
            pltpu.VMEM((heads, rows, 1), F32),
            pltpu.VMEM((heads, rows, 1), F32),
            pltpu.VMEM((rows, cols), F32),
        ]
        + [blocks] * 6
        + [
            pltpu.VMEM((rows, width), F32),
            pltpu.VMEM((devices, rows, depth), BF16),
            pltpu.VMEM((devices // 2, rows, depth), BF16),
            pltpu.VMEM((rows, width), BF16),
            dma((9,)),
            dma((12,)),
        ]
        + [dma((4,))] * 6
        + [dma((12,))] * 2
        + [dma((10,))] * 2,
        compiler_params=pltpu.CompilerParams(
            collective_id=0, has_side_effects=True, vmem_limit_bytes=56 << 20
        ),
        cost_estimate=cost(10 * rows * width * cols, 40 << 20),
        name="forward",
    )(lengths, x, *gains, grad, *weights, w_out, *prevs)


def pieces_of(extent, step):
    return [(start, min(step, extent - start)) for start in range(0, extent, step)]


def middle_kernel(
    devices,
    cores,
    two_ref,
    og_ref,
    gain_ref,
    valid_ref,
    lse_row_ref,
    wg_hbm,
    wu_hbm,
    wd_hbm,
    mid_hbm,
    wo_hbm,
    att_hbm,
    branch_out,
    gm_out,
    part_out,
    do_out,
    delta_out,
    stat_out,
    act_out,
    gg_out,
    gu_out,
    act_got,
    gg_got,
    keep_out,
    give_out,
    wg,
    wu,
    wd,
    act_t,
    gg_t,
    gu_t,
    act,
    gg,
    gu,
    mid,
    wo,
    att,
    core_send,
    core_got,
    chip,
    y_got,
    own_half,
    other_half,
    flipped,
    load_sem,
    store_sem,
    far_send,
    far_recv,
    sum_send,
    sum_recv,
):
    rows, width = mid.shape
    units = wg.shape[0]
    heads = att.shape[1] // HEAD_DIM
    step = rows // 4
    half = width // 2
    s, h, odd, core, pair, mate, across = place(devices, cores)
    near = differing(s, 2)
    head_sum = HeadSum(
        devices, cores, core_got, chip, y_got, own_half, other_half, sum_send, sum_recv
    )
    greet(pair, h)
    greet(near, h)
    greet(s, mate)
    greet(s, across)
    pieces = pieces_of(units, 3 * HEAD_DIM)
    loads = []
    for c, (start, size) in enumerate(pieces):
        at = pl.ds(start, size)
        loads.append(
            [
                pltpu.make_async_copy(src.at[at, :], dst.at[at, :], load_sem.at[3 * c + k])
                for k, (src, dst) in enumerate(((wg_hbm, wg), (wu_hbm, wu), (wd_hbm, wd)))
            ]
        )
        for copy in loads[-1]:
            copy.start()
    first = 3 * len(pieces)
    later = [
        pltpu.make_async_copy(src, dst, load_sem.at[first + k])
        for k, (src, dst) in enumerate(((mid_hbm, mid), (wo_hbm, wo), (att_hbm, att)))
    ]
    for copy in later:
        copy.start()
    pl.semaphore_wait(pltpu.get_barrier_semaphore(), 4)

    mine, theirs = (pl.ds(pl.multiple_of(c * half, half), half) for c in (core, 1 - core))
    swaps = []

    def product(tokens, columns):
        total = jnp.dot(gg[tokens, :], wg[:, columns], preferred_element_type=F32)
        return total + jnp.dot(gu[tokens, :], wu[:, columns], preferred_element_type=F32)

    for t in range(2):
        tokens = slice(2 * t * step, 2 * (t + 1) * step)
        for c, (start, size) in enumerate(pieces):
            at = slice(start, start + size)
            if t == 0:
                for copy in loads[c]:
                    copy.wait()
            gate = dot_nt(wg[at, :], two_ref[tokens, :])
            up = dot_nt(wu[at, :], two_ref[tokens, :])
            grad = dot_nt(wd[at, :], og_ref[tokens, :])
            sig = 1.0 / (1.0 + jnp.exp(-gate))
            silu = gate * sig
            value = (silu * up).astype(BF16)
            grad_gate = (grad * up * sig * (1.0 + gate * (1.0 - sig))).astype(BF16)
            grad_up = (grad * silu).astype(BF16)
            act_t[at, tokens] = value
            gg_t[at, tokens] = grad_gate
            gu_t[at, tokens] = grad_up
            act[tokens, at] = value.T
            gg[tokens, at] = grad_gate.T
            gu[tokens, at] = grad_up.T
        part = pl.ds(2 * t * step, 2 * step)
        for k, (src, dst, seq) in enumerate(((gg_t, gg_got, pair), (act_t, act_got, near))):
            i = 2 * t + k
            swaps.append(
                remote(src.at[:, part], dst.at[:, part], far_send.at[i], far_recv.at[i], seq, h)
            )
            swaps[-1].start()
        total = product(tokens, theirs).astype(BF16)
        for j in range(2):
            core_send[2 * t + j] = total[j * step : (j + 1) * step, :]
            head_sum.to_mate(2 * t + j, core_send.at[2 * t + j]).start()
        total = product(tokens, mine)
        for j in range(2):
            head_sum.chip_sum(2 * t + j, total[j * step : (j + 1) * step, :])
    stores = [
        pltpu.make_async_copy(src, dst, store_sem.at[k])
        for k, (src, dst) in enumerate(((act_t, act_out), (gg_t, gg_out), (gu_t, gu_out)))
    ]
    for store in stores:
        store.start()

    for k, columns in enumerate((theirs, mine)):
        branch_out[k] = jnp.dot(act[...], wd[:, columns], preferred_element_type=F32).astype(BF16)
    for copy in later:
        copy.wait()

    def finish(i):
        at = slice(i * step, (i + 1) * step)
        x = mid[at, :]
        root = lax.rsqrt(jnp.mean(x * x, axis=-1, keepdims=True) + EPS)
        grad = head_sum.joined(i)
        unit = x * root
        part = jnp.sum(grad * unit, axis=0, keepdims=True)
        part_out[...] = part if i == 0 else part_out[...] + part
        grad = grad * gain_ref[...]
        total = og_ref[at, :].astype(F32) + root * (
            grad - unit * jnp.mean(grad * unit, axis=-1, keepdims=True)
        )
        gm_out[at, :] = total
        low = total.astype(BF16)
        flipped[:, :, at] = low.T.reshape(devices, width // devices, step)
        do = jnp.dot(low, wo[...], preferred_element_type=F32).astype(BF16).astype(F32)
        do = jnp.where(valid_ref[at, :] > 0, do, 0.0)
        do_out[at, :] = do.astype(BF16)
        product = do * att[at, :].astype(F32)
        for k in range(heads):
            delta = jnp.sum(product[:, k * HEAD_DIM : (k + 1) * HEAD_DIM], axis=1, keepdims=True)
            delta_out[k, at, :] = delta
            stat_out[k, 0:1, at] = lse_row_ref[k, :, at]
            stat_out[k, 1:2, at] = jnp.broadcast_to(delta, (step, HEAD_DIM)).T[0:1, :]

    for i in range(4):
        head_sum.total(i)
        if i > 0:
            finish(i - 1)
    finish(3)
    split = flipped.reshape(devices // 2, 2, width // devices, rows)
    stores += [
        pltpu.make_async_copy(split.at[:, odd], keep_out, store_sem.at[3]),
        pltpu.make_async_copy(split.at[:, 1 - odd], give_out, store_sem.at[4]),
    ]
    stores[3].start()
    stores[4].start()
    for copy in swaps:
        copy.wait()
    head_sum.all_sent()
    for store in stores:
        store.wait()


def sum_scratch(rows, width):
    return [pltpu.VMEM((4, rows // 4, width // 2), BF16)] * 5


def middle(
    devices, cores, two, grad, gain, valid, lse_row, weights, mid, w_out, attended
):
    rows, width = mid.shape
    units = weights[0].shape[0]
    cols = attended.shape[1]
    heads = cols // HEAD_DIM
    depth = width // devices
    count = len(pieces_of(units, 3 * HEAD_DIM))
    vmem = pl.BlockSpec(memory_space=pltpu.VMEM)
    hbm = pl.BlockSpec(memory_space=pl.ANY)
    dma = pltpu.SemaphoreType.DMA

    def shape(*dims, dtype=BF16):
        return jax.ShapeDtypeStruct(dims, dtype)

    return pl.pallas_call(
        functools.partial(middle_kernel, devices, cores),
        in_specs=[vmem] * 5 + [hbm] * 6,
        out_specs=[vmem] * 6 + [hbm] * 7,
        out_shape=[
            shape(2, rows, width // 2),
            shape(rows, width, dtype=F32),
            shape(1, width, dtype=F32),
            shape(rows, cols),
            shape(heads, rows, 1, dtype=F32),
            shape(heads, 2, rows, dtype=F32),
        ]
        + [shape(units, rows)] * 5
        + [shape(devices // 2, depth, rows)] * 2,
        scratch_shapes=[pltpu.VMEM((units, width), BF16)] * 3
        + [pltpu.VMEM((units, rows), BF16)] * 3
        + [pltpu.VMEM((rows, units), BF16)] * 3
        + [
            pltpu.VMEM((rows, width), F32),
            pltpu.VMEM((width, cols), BF16),
            pltpu.VMEM((rows, cols), BF16),
            pltpu.VMEM((4, rows // 4, width // 2), BF16),
        ]
        + sum_scratch(rows, width)
        + [
            pltpu.VMEM((devices, depth, rows), BF16),
            dma((3 * count + 3,)),
            dma((5,)),
            dma((4,)),
            dma((4,)),
            dma((12,)),
            dma((12,)),
        ],
        compiler_params=pltpu.CompilerParams(
            collective_id=1, has_side_effects=True, vmem_limit_bytes=62 << 20
        ),
        cost_estimate=cost(12 * rows * width * units, 60 << 20),
        name="middle",
    )(two, grad, gain, valid, lse_row, *weights, mid, w_out, attended)


def attention_back_kernel(
    devices,
    cores,
    do_hbm,
    stat_hbm,
    gg_hbm,
    gg_got_hbm,
    two_hbm,
    two_got_hbm,
    gu_hbm,
    parts_ref,
    mid_ref,
    lo_ref,
    lo_row_ref,
    cos_ref,
    sin_ref,
    kx,
    vx,
    qx,
    lse_ref,
    delta_ref,
    block_out,
    gq_out,
    gk_out,
    gv_out,
    gate_got,
    gu_got,
    dx,
    sx,
    dk_acc,
    dv_acc,
    core_got,
    chip,
    y_got,
    own_half,
    other_half,
    gate_g,
    gate_x,
    gate_slot,
    gate_sem,
    gate_send,
    gate_recv,
    up_send,
    up_recv,
    load_sem,
    d_send,
    d_recv,
    s_send,
    s_recv,
    sum_send,
    sum_recv,
):
    parts, rows, cols = kx.shape
    heads = cols // HEAD_DIM
    step = rows // 4
    sub = rows // 2
    s, h, odd, core, pair, mate, across = place(devices, cores)
    scale = HEAD_DIM ** (-0.5) * LOG2E
    d_chain = Chain(devices, dx, d_send, d_recv, -1)
    s_chain = Chain(devices, sx, s_send, s_recv, -1)
    head_sum = HeadSum(
        devices, cores, core_got, chip, y_got, own_half, other_half, sum_send, sum_recv
    )
    gate = Give(
        devices,
        1,
        (gg_hbm, gg_got_hbm, two_hbm, two_got_hbm),
        (gate_g, gate_x, gate_slot, gate_got, gate_sem),
        gate_send,
        gate_recv,
    )
    greet_all(devices, cores)
    loads = [
        pltpu.make_async_copy(do_hbm, dx.at[0], load_sem.at[0]),
        pltpu.make_async_copy(stat_hbm, sx.at[0], load_sem.at[1]),
    ]
    loads[0].start()
    loads[1].start()
    gate.load()

    @pl.when(s >= devices - 2)
    def _():
        for d in (2, 4):
            dx[d] = jnp.zeros_like(dx[d])
            sx[d] = jnp.zeros_like(sx[d])

    loads[0].wait()
    loads[1].wait()
    all_greeted(devices)
    d_chain.first()
    s_chain.first()
    for i in range(4):
        head_sum.to_mate(i, parts_ref.at[0, pl.ds(i * step, step), :]).start()

    def queries_back(start, count):
        def body(i, _):
            k = start + i // 2
            at = pl.ds(pl.multiple_of((i % 2) * sub, sub), sub)
            lanes = pl.ds(pl.multiple_of(k * HEAD_DIM, HEAD_DIM), HEAD_DIM)
            q, do, lo = qx[0, at, lanes], dx[0, at, lanes], lo_ref[at, :]
            lse, delta = lse_ref[k, at, :], delta_ref[k, at, :]
            total = jnp.zeros((sub, HEAD_DIM), F32)
            for d in range(parts):
                key = kx[d, :, lanes]
                scores = dot_nt(q, key)
                u = lax.broadcasted_iota(jnp.int32, scores.shape, 1) - d * rows
                seen = u >= lo
                if d == 0:
                    t = lax.broadcasted_iota(jnp.int32, scores.shape, 0) + (i % 2) * sub
                    seen = seen & (u <= t)
                p = jnp.exp2(jnp.where(seen, scores * scale, MASKED) - lse)
                ds = (p * (dot_nt(do, vx[d, :, lanes]) - delta)).astype(BF16)
                total = total + jnp.dot(ds, key, preferred_element_type=F32)
            gq_out[at, lanes] = turned_back(
                total * HEAD_DIM ** (-0.5), cos_ref[at, :], sin_ref[at, :]
            )
            return 0

        lax.fori_loop(0, 2 * count, body, 0)

    def keys_back(d):
        def body(i, _):
            k = i // 2
            at = pl.ds(pl.multiple_of((i % 2) * sub, sub), sub)
            lanes = pl.ds(pl.multiple_of(k * HEAD_DIM, HEAD_DIM), HEAD_DIM)
            key, value = kx[0, at, lanes], vx[0, at, lanes]
            q, do = qx[d, :, lanes], dx[d, :, lanes]
            scores = dot_nt(key, q)
            u = lax.broadcasted_iota(jnp.int32, scores.shape, 0) + (i % 2) * sub
            seen = u >= lo_row_ref[:, d * rows : (d + 1) * rows]
            if d == 0:
                seen = seen & (u <= lax.broadcasted_iota(jnp.int32, scores.shape, 1))
            lse, delta = sx[d, k, 0:1, :], sx[d, k, 1:2, :]
            p = jnp.exp2(jnp.where(seen, scores * scale - lse, MASKED))
            dv = jnp.dot(p.astype(BF16), do, preferred_element_type=F32)
            ds = (p * (dot_nt(value, do) - delta)).astype(BF16)
            dk = jnp.dot(ds, q, preferred_element_type=F32)
            if d > 0:
                dv = dv + dv_acc[at, lanes]
                dk = dk + dk_acc[at, lanes]
            dv_acc[at, lanes] = dv
            dk_acc[at, lanes] = dk
            return 0

        lax.fori_loop(0, 2 * heads, body, 0)

    ups = [
        remote(
            gu_hbm.at[pl.ds(start, size), :],
            gu_got.at[pl.ds(start, size), :],
            up_send.at[i],
            up_recv.at[i],
            pair,
            h,
        )
        for i, (start, size) in enumerate(pieces_of(gu_hbm.shape[0], 3 * HEAD_DIM))
    ]
    ups[0].start()
    gate.loaded()
    gate.make(0)
    gate.half(0, 0).start()
    queries_back(0, heads // 4)
    for i in range(4):
        head_sum.chip_sum(i, parts_ref[1, i * step : (i + 1) * step, :].astype(F32))
    s_chain.second()
    d_chain.second()
    ups[1].start()
    gate.half(0, 1).start()
    for j in range(1, gate.count):
        gate.make(j)
        gate.half(j, 0).start()
        gate.half(j, 1).start()
    queries_back(heads // 4, heads // 2)
    keys_back(0)
    keys_back(2)
    s_chain.third()
    d_chain.third()
    for copy in ups[2:]:
        copy.start()
    queries_back(heads // 4 + heads // 2, heads - heads // 4 - heads // 2)
    for i in range(4):
        head_sum.total(i)
    s_chain.arrived(2)
    d_chain.arrived(2)
    keys_back(1)
    keys_back(4)
    for i in range(4):
        at = slice(i * step, (i + 1) * step)
        block_out[at, :] = (mid_ref[at, :] + head_sum.joined(i)).astype(BF16)
    s_chain.arrived(3)
    d_chain.arrived(3)
    keys_back(3)
    for k in range(heads):
        lanes = slice(k * HEAD_DIM, (k + 1) * HEAD_DIM)
        gk_out[:, lanes] = turned_back(
            dk_acc[:, lanes] * HEAD_DIM ** (-0.5), cos_ref[...], sin_ref[...]
        )
        gv_out[:, lanes] = dv_acc[:, lanes].astype(BF16)
    d_chain.all_sent()
    s_chain.all_sent()
    head_sum.all_sent()
    gate.finish()
    for copy in ups:
        copy.wait()


def attention_back(
    devices, cores, do, stat, gate, grad_up, branch, mid, low_col, low_row, tables, keys, values, queries, lse, delta
):
    rows, width = mid.shape
    parts, _, cols = keys.shape
    heads = cols // HEAD_DIM
    units = gate[0].shape[0]
    count, depth = devices // 4, width // devices
    vmem = pl.BlockSpec(memory_space=pltpu.VMEM)
    hbm = pl.BlockSpec(memory_space=pl.ANY)
    dma = pltpu.SemaphoreType.DMA
    give = [
        pltpu.VMEM((2, units, rows), BF16),
        pltpu.VMEM((2, count, rows, depth), BF16),
        pltpu.VMEM((count, units, depth), BF16),
        dma((2 + 2 * count,)),
        dma((2 * count,)),
        dma((2 * count,)),
    ]
    flops = 14 * rows * rows * parts * cols
    return pl.pallas_call(
        functools.partial(attention_back_kernel, devices, cores),
        in_specs=[hbm] * 7 + [vmem] * 11,
        out_specs=[vmem] * 5 + [hbm],
        out_shape=[jax.ShapeDtypeStruct((rows, width), BF16)]
        + [jax.ShapeDtypeStruct((rows, cols), BF16)] * 3
        + [jax.ShapeDtypeStruct((count, units, depth), BF16)]
        + [jax.ShapeDtypeStruct((units, rows), BF16)],
        scratch_shapes=[
            pltpu.VMEM((parts, rows, cols), BF16),
            pltpu.VMEM((parts, heads, 2, rows), F32),
            pltpu.VMEM((rows, cols), F32),
            pltpu.VMEM((rows, cols), F32),
        ]
        + sum_scratch(rows, width)
        + give
        + [dma((len(pieces_of(units, 3 * HEAD_DIM)),))] * 2
        + [dma((2,))]
        + [dma((4,))] * 4
        + [dma((12,))] * 2,
        compiler_params=pltpu.CompilerParams(
            collective_id=2, has_side_effects=True, vmem_limit_bytes=58 << 20
        ),
        cost_estimate=cost(flops, 80 << 20),
        name="attention_back",
    )(do, stat, *gate, grad_up, branch, mid, low_col, low_row, *tables, keys, values, queries, lse, delta)


class Reduce:
    def __init__(self, block, near, far, slot, got, keep, last, send, recv):
        self.h = lax.axis_index("head")
        self.block, self.near_seq, self.far_seq = block, near, far
        self.slot, self.got, self.keep, self.last = slot, got, keep, last
        self.send, self.recv = send, recv

    def near(self, j):
        return remote(
            self.slot.at[j], self.got.at[j], self.send.at[j], self.recv.at[j], self.near_seq, self.h
        )

    def far(self):
        return remote(
            self.keep.at[1], self.last, self.send.at[2], self.recv.at[2], self.far_seq, self.h
        )

    def give(self):
        for j in range(2):
            self.slot[j] = self.block(2 + j).astype(BF16)
            self.near(j).start()

    def combine(self, received=None):
        for j in (1, 0):
            total = self.block(j)
            if received is None:
                self.near(j).wait_recv()
            total = total + self.got[j].astype(F32)
            self.keep[j] = total.astype(BF16)
            if j == 1:
                self.far().start()

    def result(self):
        self.far().wait_recv()
        return (self.keep[0].astype(F32) + self.last[...].astype(F32)).astype(BF16)

    def all_sent(self, gave):
        if gave:
            self.near(0).wait_send()
            self.near(1).wait_send()
        self.far().wait_send()


def weights_kernel(
    devices,
    cores,
    gate_hbm,
    gate_other_hbm,
    up_hbm,
    up_other_hbm,
    down_hbm,
    down_other_hbm,
    two_hbm,
    two_other_hbm,
    og_hbm,
    og_other_hbm,
    gate_got_hbm,
    mid_give_hbm,
    one_give_hbm,
    wq_hbm,
    wk_hbm,
    wv_hbm,
    gm_hbm,
    x_ref,
    gain_ref,
    mlp_part_ref,
    gq,
    gk,
    gv,
    att,
    one,
    mid_x,
    gate_out,
    up_out,
    down_out,
    wq_out,
    wk_out,
    wv_out,
    wo_out,
    tokens_out,
    gains_out,
    g_a,
    g_b,
    x_a,
    x_b,
    up_slot,
    down_slot,
    got_mlp,
    keep_mlp,
    last_mlp,
    gq_other,
    gk_other,
    gv_other,
    mid_other,
    one_other,
    att_other,
    slot_att,
    got_att,
    keep_att,
    last_att,
    wq,
    wk,
    wv,
    gm,
    core_send,
    core_got,
    chip,
    y_got,
    own_half,
    other_half,
    gains_got,
    load_sem,
    gm_sem,
    x_send,
    x_recv,
    job_send,
    job_recv,
    sum_send,
    sum_recv,
    gain_send,
    gain_recv,
):
    rows, width = x_ref.shape
    half = width // 2
    step = rows // 4
    s, h, odd, core, pair, mate, across = place(devices, cores)
    near, far = differing(s, 2), differing(s, 4)
    head_sum = HeadSum(
        devices, cores, core_got, chip, y_got, own_half, other_half, sum_send, sum_recv
    )
    greet(pair, h)
    greet(near, h)
    greet(far, h)
    greet(s, mate)
    greet(s, across)

    def position(first, p):
        bits = shard_orders(first, devices)
        shard = s
        for k, b in enumerate(bits[1:]):
            if (p >> (len(bits) - 2 - k)) & 1:
                shard = differing(shard, b)
        return shard // (2 * first) * first + lax.rem(shard, first)

    count = [0]

    def load(src, dst):
        copy = pltpu.make_async_copy(src, dst, load_sem.at[count[0]])
        count[0] += 1
        copy.start()
        return copy

    def load_job(g_own, g_other, x_own, x_other, g, x, first, blocks):
        copies = [load(g_own, g.at[0]), load(g_other, g.at[1])]
        for p in blocks:
            at = position(first, p)
            copies += [load(x_own.at[at], x.at[0, p]), load(x_other.at[at], x.at[1, p])]
        return copies

    def wait(copies):
        for copy in copies:
            copy.wait()

    gate_loads = load_job(gate_hbm, gate_other_hbm, two_hbm, two_other_hbm, g_a, x_a, 1, (0, 1))
    gate_loads.append(load(gate_got_hbm, got_mlp.at[0]))
    up_loads = load_job(up_hbm, up_other_hbm, two_hbm, two_other_hbm, g_b, x_b, 1, (0, 1, 2, 3))
    w_loads = [load(wq_hbm, wq), load(wk_hbm, wk), load(wv_hbm, wv)]

    def gm_load(i):
        return pltpu.make_async_copy(
            gm_hbm.at[pl.ds(i * step, step), :], gm.at[i % 2], gm_sem.at[i % 2]
        )

    gm_load(0).start()
    gm_load(1).start()

    def mlp_block(g, x):
        def block(p):
            total = jnp.dot(g[0], x[0, p], preferred_element_type=F32)
            return total + jnp.dot(g[1], x[1, p], preferred_element_type=F32)

        return block

    def att_block(x_own, x_other, g_own, g_other):
        def block(p):
            at = position(1, p)
            total = jnp.dot(x_own[at], g_own[...], preferred_element_type=F32)
            return total + jnp.dot(x_other[at], g_other[...], preferred_element_type=F32)

        return block

    def job(k, block, first_seq, slot, got, keep, last):
        return Reduce(block, first_seq, far, slot, got, keep, last, job_send.at[k], job_recv.at[k])

    gate = job(0, mlp_block(g_a, x_a), near, None, got_mlp.at[0], keep_mlp.at[0], last_mlp.at[0])
    up = job(1, mlp_block(g_b, x_b), near, up_slot, got_mlp.at[1], keep_mlp.at[1], last_mlp.at[1])
    down = job(2, mlp_block(g_a, x_a), pair, down_slot, got_mlp.at[2], keep_mlp.at[2], last_mlp.at[2])
    attention = []
    for k, operands in enumerate(
        (
            (one, one_other, gq, gq_other),
            (one, one_other, gk, gk_other),
            (one, one_other, gv, gv_other),
            (mid_x, mid_other, att, att_other),
        )
    ):
        attention.append(
            job(
                3 + k,
                att_block(*operands),
                near,
                slot_att.at[k],
                got_att.at[k],
                keep_att.at[k],
                last_att.at[k],
            )
        )

    pl.semaphore_wait(pltpu.get_barrier_semaphore(), 5)
    swaps = [
        remote(src, dst, x_send.at[i], x_recv.at[i], pair, h)
        for i, (src, dst) in enumerate(
            ((gq, gq_other), (gk, gk_other), (gv, gv_other), (mid_give_hbm, mid_other), (att, att_other))
        )
    ]
    share = devices // 4
    here = pl.ds(core * share, share)
    one_swap = remote(
        one_give_hbm.at[here], one_other.at[here], x_send.at[5], x_recv.at[5], pair, h
    )
    one_pass = remote(
        one_other.at[here], one_other.at[here], x_send.at[6], x_recv.at[6], s, mate
    )
    one_swap.start()
    for copy in swaps[:3]:
        copy.start()

    wait(gate_loads)
    gate.combine(True)
    down_loads = load_job(down_hbm, down_other_hbm, og_hbm, og_other_hbm, g_a, x_a, 2, (0, 1, 2, 3))
    wait(up_loads)
    up.give()
    wait(down_loads)
    down.give()
    swaps[3].start()
    swaps[4].start()

    wait(w_loads)
    mine, theirs = (pl.multiple_of(c * half, half) for c in (core, 1 - core))

    def product(i, start):
        at = slice(i * step, (i + 1) * step)
        total = None
        for g, w in ((gq, wq), (gk, wk), (gv, wv)):
            term = dot_nt(g[at, :], w[pl.ds(start, half), :])
            total = term if total is None else total + term
        return total

    for i in range(4):
        core_send[i] = product(i, theirs).astype(BF16)
        head_sum.to_mate(i, core_send.at[i]).start()
    for i in range(4):
        head_sum.chip_sum(i, product(i, mine))
    one_swap.wait_recv()
    one_pass.start()
    one_pass.wait_recv()
    for k in range(3):
        swaps[k].wait_recv()
        attention[k].give()

    def finish(i):
        at = slice(i * step, (i + 1) * step)
        gm_load(i).wait()
        x = x_ref[at, :].astype(F32)
        root = lax.rsqrt(jnp.mean(x * x, axis=-1, keepdims=True) + EPS)
        grad = head_sum.joined(i)
        unit = x * root
        part = jnp.sum(grad * unit, axis=0, keepdims=True)
        gains_out[0:1, :] = part if i == 0 else gains_out[0:1, :] + part
        grad = grad * gain_ref[...]
        total = gm[i % 2] + root * (grad - unit * jnp.mean(grad * unit, axis=-1, keepdims=True))
        tokens_out[at, :] = total.astype(BF16)
        if i < 2:
            gm_load(i + 2).start()

    up.combine()
    for i in range(4):
        head_sum.total(i)
        if i > 0:
            finish(i - 1)
    finish(3)
    gains_out[1:2, :] = mlp_part_ref[...]

    def gain_swap(k, seq):
        return remote(gains_out, gains_got.at[k], gain_send.at[k], gain_recv.at[k], seq, h)

    def gain_step(k, seq):
        gain_swap(k, seq).wait()
        gains_out[...] = gains_out[...] + gains_got[k]

    gain_swap(0, pair).start()
    attention[0].combine()
    attention[1].combine()
    gain_step(0, pair)
    gain_swap(1, near).start()
    down.combine()
    swaps[3].wait_recv()
    swaps[4].wait_recv()
    attention[3].give()
    attention[2].combine()
    gain_step(1, near)
    gain_swap(2, far).start()
    attention[3].combine()
    gate_out[...] = gate.result()
    down_out[...] = down.result()
    up_out[...] = up.result()
    gain_step(2, far)
    for k, out in enumerate((wq_out, wk_out, wv_out, wo_out)):
        out[...] = attention[k].result()
    gate.all_sent(False)
    down.all_sent(True)
    up.all_sent(True)
    for k in range(4):
        attention[k].all_sent(True)
    for copy in (*swaps, one_swap, one_pass):
        copy.wait_send()
    head_sum.all_sent()


def weight_gradients(
    devices, cores, mlp_operands, others, weights, grad_mid, x, gain, mlp_part, attention_operands
):
    rows, width = x.shape
    units = mlp_operands[0].shape[0]
    cols = weights[0].shape[1]
    depth = width // devices
    vmem = pl.BlockSpec(memory_space=pltpu.VMEM)
    hbm = pl.BlockSpec(memory_space=pl.ANY)
    dma = pltpu.SemaphoreType.DMA
    operands = (*mlp_operands, *others, *weights, grad_mid)
    kept = (x, gain, mlp_part, *attention_operands)
    return pl.pallas_call(
        functools.partial(weights_kernel, devices, cores),
        in_specs=[hbm] * len(operands) + [vmem] * len(kept),
        out_specs=[vmem] * 9,
        out_shape=[jax.ShapeDtypeStruct((units, depth), BF16)] * 3
        + [jax.ShapeDtypeStruct((depth, cols), BF16)] * 4
        + [jax.ShapeDtypeStruct((rows, width), BF16), jax.ShapeDtypeStruct((2, width), F32)],
        scratch_shapes=[
            pltpu.VMEM((2, units, rows), BF16),
            pltpu.VMEM((2, units, rows), BF16),
            pltpu.VMEM((2, 4, rows, depth), BF16),
            pltpu.VMEM((2, 4, rows, depth), BF16),
            pltpu.VMEM((2, units, depth), BF16),
            pltpu.VMEM((2, units, depth), BF16),
            pltpu.VMEM((3, 2, units, depth), BF16),
            pltpu.VMEM((3, 2, units, depth), BF16),
            pltpu.VMEM((3, units, depth), BF16),
        ]
        + [pltpu.VMEM((rows, cols), BF16)] * 3
        + [
            pltpu.VMEM((devices // 2, depth, rows), BF16),
            pltpu.VMEM((devices // 2, depth, rows), BF16),
            pltpu.VMEM((rows, cols), BF16),
            pltpu.VMEM((4, 2, depth, cols), BF16),
            pltpu.VMEM((4, 2, depth, cols), BF16),
            pltpu.VMEM((4, 2, depth, cols), BF16),
            pltpu.VMEM((4, depth, cols), BF16),
        ]
        + [pltpu.VMEM((width, cols), BF16)] * 3
        + [pltpu.VMEM((2, rows // 4, width), F32)]
        + [pltpu.VMEM((4, rows // 4, width // 2), BF16)]
        + sum_scratch(rows, width)
        + [pltpu.VMEM((3, 2, width), F32)]
        + [dma((32,)), dma((2,)), dma((7,)), dma((7,)), dma((7, 3)), dma((7, 3))]
        + [dma((12,)), dma((12,)), dma((3,)), dma((3,))],
        compiler_params=pltpu.CompilerParams(
            collective_id=3, has_side_effects=True, vmem_limit_bytes=62 << 20
        ),
        cost_estimate=cost(20 * rows * width * cols, 60 << 20),
        name="weight_gradients",
    )(*operands, *kept)


def on_device(
    tokens,
    gain_attn,
    gain_mlp,
    w_query,
    w_key,
    w_value,
    w_out,
    w_gate,
    w_up,
    w_down,
    prev_keys,
    prev_values,
    lengths,
    out_grad,
):
    rows = tokens.shape[0]
    width = w_query.shape[1]
    devices, cores = lax.axis_size("seq"), lax.axis_size("head")
    index = lax.axis_index("seq")
    bits = jnp.stack([index & 1, lax.axis_index("head") & 1]).astype(jnp.int32)
    gain_one, gain_two = gain_attn[None, :], gain_mlp[None, :]

    (
        keys,
        values,
        queries,
        one_keep,
        one_give,
        mid,
        normed_two,
        two_keep,
        two_got,
        out_keep,
        out_give,
        out_got,
        attended,
        lse,
        lse_row,
        cosine,
        sine,
        low_col,
        low_row,
        valid,
    ) = forward(
        devices,
        cores,
        lengths,
        tokens,
        (gain_one, gain_two),
        out_grad,
        (w_key, w_value, w_query),
        w_out,
        (prev_keys, prev_values),
    )
    order = Order()
    out_keep, out_got = (a.reshape(devices // 2, rows, -1) for a in (out_keep, out_got))
    two_pair = (two_keep, two_got)
    (
        branch_parts,
        grad_mid,
        gain_mlp_part,
        grad_att,
        delta,
        stat,
        act,
        grad_gate,
        grad_up,
        act_got,
        gate_got,
        mid_keep,
        mid_give,
    ) = middle(
        devices,
        cores,
        normed_two,
        out_grad,
        gain_two,
        valid,
        lse_row,
        (w_gate.T, w_up.T, w_down.T),
        mid,
        w_out,
        attended,
    )
    out_pair = (out_keep, out_got)
    order.ran(delta)
    block_out, grad_query_raw, grad_key_raw, grad_value_raw, gate_sums, up_got = attention_back(
        devices,
        cores,
        order.after(grad_att),
        stat,
        (grad_gate, gate_got, *two_pair),
        grad_up,
        branch_parts,
        mid,
        low_col,
        low_row,
        (cosine, sine),
        keys,
        values,
        queries,
        lse,
        delta,
    )
    if devices == 8:
        sums = weight_gradients(
            devices,
            cores,
            (grad_gate, gate_got, grad_up, up_got, act, act_got),
            (*two_pair, *out_pair, gate_sums, mid_give, one_give),
            (w_query, w_key, w_value),
            grad_mid,
            tokens,
            gain_one,
            gain_mlp_part,
            (
                grad_query_raw,
                grad_key_raw,
                grad_value_raw,
                attended,
                one_keep,
                mid_keep,
            ),
        )
        gate_grad, up_grad, down_grad = (a.astype(F32).T for a in sums[:3])
        gains = lax.dynamic_slice_in_dim(sums[8], index * sums[8].shape[1] // devices, sums[8].shape[1] // devices, 1)
        return (
            block_out,
            sums[7],
            gains[0],
            gains[1],
            *(a.astype(F32) for a in sums[3:7]),
            gate_grad,
            up_grad,
            down_grad,
        )
    order.ran(grad_query_raw)
    attended_got = swap(attended, "seq", 1)
    one_pair = (one_keep, swap(one_give, "seq", 1))
    gate = WeightGrad(order, two_pair, grad_gate, gate_got, 1, "gate", True)
    up = WeightGrad(order, two_pair, grad_up, up_got, 1, "up", True)
    down = WeightGrad(order, out_pair, act, act_got, 2, "down", True)
    gate.got = gate_sums
    query_got = swap(grad_query_raw, "seq", 1)
    key_got = swap(grad_key_raw, "seq", 1)
    value_got = swap(grad_value_raw, "seq", 1)
    mid_pair = (mid_keep, swap(order.after(mid_give), "seq", 1))
    gate.keep()
    up.give()
    down.give()
    lefts = (grad_query_raw, grad_key_raw, grad_value_raw)
    rights = (w_query, w_key, w_value)
    give = order.ran(half_product(order.after(bits), lefts, rights, 1, None, "norm_one_give"))
    give = swap(give, "head", 1)
    query = WeightGrad(order, one_pair, grad_query_raw, query_got, 1, "query")
    key = WeightGrad(order, one_pair, grad_key_raw, key_got, 1, "key")
    value = WeightGrad(order, one_pair, grad_value_raw, value_got, 1, "value")
    wout = WeightGrad(order, mid_pair, attended, attended_got, 1, "wout")
    query.give()
    chip = order.ran(half_product(order.after(bits), lefts, rights, 0, give, "norm_one_keep"))
    chip_got = swap(chip, "head", 2)
    key.give()
    value.give()
    up.keep()
    down.keep()
    wout.give()
    own = (chip.astype(F32) + chip_got.astype(F32)).astype(BF16)
    other = swap(own, "head", 1)
    query.keep()
    key.keep()
    tokens_grad, gain_attn_part = by_rows(
        back_kernel,
        order.after(bits),
        (tokens, own, other, gain_one, grad_mid),
        3,
        (BF16, F32),
        "tokens_back",
        part=1,
    )
    order.ran(gain_attn_part)
    value.keep()
    wout.keep()
    gains = gain_sum(jnp.concatenate([gain_attn_part, gain_mlp_part], axis=0))
    gain_attn_grad, gain_mlp_grad = gains[0], gains[1]
    w_gate_grad, w_up_grad, w_down_grad = gate.finish(), up.finish(), down.finish()
    w_out_grad = wout.finish()
    w_query_grad, w_key_grad, w_value_grad = query.finish(), key.finish(), value.finish()
    return (
        block_out,
        tokens_grad,
        gain_attn_grad,
        gain_mlp_grad,
        w_query_grad,
        w_key_grad,
        w_value_grad,
        w_out_grad,
        w_gate_grad,
        w_up_grad,
        w_down_grad,
    )


def solution(mesh):
    by_head = P(None, "head")
    both = P("seq", "head")
    placed = (P("seq", None), P(), P()) + (by_head,) * 9 + (P(), P("seq", None))
    return jax.shard_map(
        on_device,
        mesh=mesh,
        in_specs=placed,
        out_specs=(P("seq", None), P("seq", None), P("seq"), P("seq")) + (both,) * 7,
        check_vma=False,
    )
```

```python
import functools
import math

import jax
import jax.numpy as jnp
from jax import lax
from jax.experimental import pallas as pl
from jax.experimental.pallas import tpu as pltpu
from jax.sharding import PartitionSpec as P

HEAD_DIM = 128
WINDOW = 2048
PAD = 64
NSEQ = 4
EPS = 1e-06
MASKED = -1e30
LOG2E = 1.4426950408889634
BIG = 1 << 28
F32 = jnp.float32
BF16 = jnp.bfloat16


def swap(block, axis, bit):
    return lax.ppermute(block, axis, [(i, i ^ bit) for i in range(lax.axis_size(axis))])


def shifted(block, distance):
    n = lax.axis_size("seq")
    return lax.ppermute(
        block, "seq", [(i, i + distance) for i in range(n) if 0 <= i + distance < n]
    )


BIG_VMEM = pltpu.CompilerParams(vmem_limit_bytes=48 << 20)


def cost(flops, moved):
    return pl.CostEstimate(flops=int(flops), bytes_accessed=int(moved), transcendentals=0)


def dot_nt(left, right):
    return lax.dot_general(left, right, (((1,), (1,)), ((), ())), preferred_element_type=F32)


def row_blocks(width, step):
    return pl.BlockSpec((step, width), lambda i, bits: (i, 0))


def joined(bits_ref, own_ref, other_ref):
    low = bits_ref[1] == 0
    own, other = own_ref[...].astype(F32), other_ref[...].astype(F32)
    return jnp.concatenate([jnp.where(low, own, other), jnp.where(low, other, own)], axis=1)


def back_kernel(
    bits_ref, x_ref, own_ref, other_ref, gain_ref, add_ref, out_ref, part_ref
):
    x = x_ref[...].astype(F32)
    scale = lax.rsqrt(jnp.mean(x * x, axis=-1, keepdims=True) + EPS)
    grad = joined(bits_ref, own_ref, other_ref)
    unit = x * scale
    grad_unit = grad * gain_ref[...]
    total = add_ref[...].astype(F32) + scale * (
        grad_unit - unit * jnp.mean(grad_unit * unit, axis=-1, keepdims=True)
    )
    out_ref[...] = total.astype(out_ref.dtype)
    part = jnp.sum(grad * unit, axis=0, keepdims=True)

    @pl.when(pl.program_id(0) == 0)
    def _():
        part_ref[...] = part

    @pl.when(pl.program_id(0) > 0)
    def _():
        part_ref[...] += part


def by_rows(kernel, bits, arrays, gains_at, outs, name, part=None):
    rows, width = arrays[0].shape
    step = rows // 4
    in_specs = [
        pl.BlockSpec((1, width), lambda i, bits: (0, 0))
        if k == gains_at
        else row_blocks(a.shape[1], step)
        for k, a in enumerate(arrays)
    ]
    out_specs, out_shape = [], []
    for k, dtype in enumerate(outs):
        if k == part:
            out_specs.append(pl.BlockSpec((1, width), lambda i, bits: (0, 0)))
            out_shape.append(jax.ShapeDtypeStruct((1, width), F32))
        else:
            out_specs.append(row_blocks(width, step))
            out_shape.append(jax.ShapeDtypeStruct((rows, width), dtype))
    return pl.pallas_call(
        kernel,
        grid_spec=pltpu.PrefetchScalarGridSpec(
            num_scalar_prefetch=1, grid=(rows // step,), in_specs=in_specs, out_specs=out_specs
        ),
        out_shape=out_shape,
        compiler_params=BIG_VMEM,
        cost_estimate=cost(rows * width * 10, rows * width * 2 * (len(arrays) + len(out_shape))),
        name=name,
    )(bits, *arrays)


def half_kernel(pairs, flip, added, bits_ref, *refs):
    total = refs[2 * pairs][...].astype(F32) if added else None
    for k in range(pairs):
        term = dot_nt(refs[k][...], refs[pairs + k][...])
        total = term if total is None else total + term
    refs[-1][...] = total.astype(BF16)


def half_product(bits, lefts, rights, flip, added, name):
    rows = lefts[0].shape[0]
    width = rights[0].shape[0] // 2
    step = min(width, 512)
    steps = width // step

    def at(i, bits):
        return ((bits[1] ^ flip) * steps + i, 0)

    specs = [pl.BlockSpec(a.shape, lambda i, bits: (0, 0)) for a in lefts]
    specs += [pl.BlockSpec((step, a.shape[1]), at) for a in rights]
    extra = []
    if added is not None:
        extra = [added]
        specs.append(pl.BlockSpec((rows, step), lambda i, bits: (0, i)))
    depth = sum(a.shape[1] for a in lefts)
    return pl.pallas_call(
        functools.partial(half_kernel, len(lefts), flip, added is not None),
        grid_spec=pltpu.PrefetchScalarGridSpec(
            num_scalar_prefetch=1,
            grid=(steps,),
            in_specs=specs,
            out_specs=pl.BlockSpec((rows, step), lambda i, bits: (0, i)),
        ),
        out_shape=jax.ShapeDtypeStruct((rows, width), BF16),
        compiler_params=BIG_VMEM,
        cost_estimate=cost(2 * rows * depth * width, 2 * (rows + width) * depth),
        name=name,
    )(bits, *lefts, *rights, *extra)


def blocks_kernel(order_ref, flip, xa_ref, xb_ref, ga_ref, gb_ref, *refs):
    if flip:
        total = jnp.dot(ga_ref[...], xa_ref[0], preferred_element_type=F32)
        total = total + jnp.dot(gb_ref[...], xb_ref[0], preferred_element_type=F32)
    else:
        total = jnp.dot(xa_ref[0], ga_ref[...], preferred_element_type=F32)
        total = total + jnp.dot(xb_ref[0], gb_ref[...], preferred_element_type=F32)
    if len(refs) == 2:
        total = total + refs[0][0].astype(F32)
    refs[-1][0] = total.astype(BF16)


def grad_blocks(order, x_own, x_got, g_own, g_got, added, flip, name):
    count = order.shape[0]
    if flip:
        _, rows, depth = x_own.shape
        cols = g_own.shape[0]
        shape = (cols, depth)
    else:
        _, depth, rows = x_own.shape
        cols = g_own.shape[1]
        shape = (depth, cols)
    x_spec = pl.BlockSpec((1,) + x_own.shape[1:], lambda i, order: (order[i], 0, 0))
    g_spec = pl.BlockSpec(g_own.shape, lambda i, order: (0, 0))
    out_spec = pl.BlockSpec((1,) + shape, lambda i, order: (i, 0, 0))
    extra = [] if added is None else [added]

    def kernel(order_ref, *refs):
        blocks_kernel(order_ref, flip, *refs)

    return pl.pallas_call(
        kernel,
        grid_spec=pltpu.PrefetchScalarGridSpec(
            num_scalar_prefetch=1,
            grid=(count,),
            in_specs=[x_spec, x_spec, g_spec, g_spec] + [out_spec] * len(extra),
            out_specs=out_spec,
        ),
        out_shape=jax.ShapeDtypeStruct((count,) + shape, BF16),
        compiler_params=BIG_VMEM,
        cost_estimate=cost(
            4 * count * depth * rows * cols, 2 * count * depth * cols + 4 * rows * cols
        ),
        name=name,
    )(order, x_own, x_got, g_own, g_got, *extra)


def shard_orders(first, n):
    bits = [1 << k for k in range(n.bit_length() - 1)]
    return [first] + [b for b in bits if b != first]


class Order:
    def __init__(self):
        self.last = None

    def after(self, operand):
        if self.last is None:
            return operand
        return lax.optimization_barrier((operand, self.last))[0]

    def ran(self, result):
        self.last = result
        return result


class WeightGrad:
    def __init__(self, order, x_pair, g_own, g_got, first, name, flip=False):
        n = lax.axis_size("seq")
        self.order, self.flip, self.name = order, flip, name
        self.operands = (*x_pair, g_own, g_got)
        self.bits = shard_orders(first, n)
        index = lax.axis_index("seq")
        shards = []
        for p in range(n // 2):
            apart = sum(
                b for k, b in enumerate(self.bits[1:]) if (p >> (len(self.bits) - 2 - k)) & 1
            )
            shard = index ^ apart
            shards.append(shard // (2 * first) * first + shard % first)
        self.shards = jnp.stack(shards).astype(jnp.int32)
        self.count = n // 4

    def blocks(self, shards, added, name):
        return self.order.ran(
            grad_blocks(
                self.order.after(shards), *self.operands, added, self.flip, self.name + name
            )
        )

    def give(self):
        give = self.blocks(self.shards[self.count :], None, "_give")
        self.got = swap(give, "seq", self.bits[1])

    def keep(self):
        self.part = self.blocks(self.shards[: self.count], self.got, "_keep")
        left = self.count // 2
        self.got = swap(self.part[left:], "seq", self.bits[2])

    def finish(self):
        left, part = self.count // 2, self.part
        total = part[:left].astype(F32) + self.got.astype(F32)
        for bit in self.bits[3:]:
            left //= 2
            part = total.astype(BF16)
            total = part[:left].astype(F32) + swap(part[left:], "seq", bit).astype(F32)
        return total[0].T if self.flip else total[0]


def gain_sum(part):
    n = lax.axis_size("seq")
    total = part
    bit = 1
    while bit < n:
        total = total + swap(total, "seq", bit)
        bit *= 2
    width = part.shape[-1] // n
    return lax.dynamic_slice_in_dim(total, lax.axis_index("seq") * width, width, total.ndim - 1)


def turned_back(grad, cosine, sine):
    return (grad * cosine - pltpu.roll(grad, HEAD_DIM // 2, 1) * sine).astype(BF16)


def place(devices, cores):
    s, h = lax.axis_index("seq"), lax.axis_index("head")
    odd, core = lax.rem(s, 2), lax.rem(h, 2)
    pair = s + 1 - 2 * odd
    mate = h + 1 - 2 * core
    across = lax.rem(h + cores // 2, cores)
    return s, h, odd, core, pair, mate, across


def remote(src, dst, send, recv, seq, head):
    return pltpu.make_async_remote_copy(
        src_ref=src,
        dst_ref=dst,
        send_sem=send,
        recv_sem=recv,
        device_id=(seq, head),
        device_id_type=pl.DeviceIdType.MESH,
    )


def greet(seq, head):
    pl.semaphore_signal(
        pltpu.get_barrier_semaphore(),
        inc=1,
        device_id=(seq, head),
        device_id_type=pl.DeviceIdType.MESH,
    )


def greet_all(devices, cores):
    s, h, odd, core, pair, mate, across = place(devices, cores)
    greet(pair, h)
    greet(s, mate)
    greet(s, across)

    @pl.when(s >= 2)
    def _():
        greet(s - 2, h)

    @pl.when(s < devices - 2)
    def _():
        greet(s + 2, h)


def all_greeted(devices):
    s = lax.axis_index("seq")
    inner = (s >= 2) & (s < devices - 2)

    @pl.when(inner)
    def _():
        pl.semaphore_wait(pltpu.get_barrier_semaphore(), 5)

    @pl.when(jnp.logical_not(inner))
    def _():
        pl.semaphore_wait(pltpu.get_barrier_semaphore(), 4)


class Chain:
    def __init__(self, devices, buf, send, recv, side):
        self.s, self.h = lax.axis_index("seq"), lax.axis_index("head")
        odd = lax.rem(self.s, 2)
        self.pair = self.s + 1 - 2 * odd
        self.buf, self.send, self.recv = buf, send, recv
        self.next = self.s + 2 * side
        left, right = self.s >= 2, self.s < devices - 2
        self.sends, self.gets = (right, left) if side > 0 else (left, right)
        self.early = odd == (0 if side > 0 else 1)
        self.late = odd == (1 if side > 0 else 0)

    def hop(self, slot, seq, src, dst):
        return remote(
            self.buf.at[src], self.buf.at[dst], self.send.at[slot], self.recv.at[slot], seq, self.h
        )

    def first(self):
        @pl.when(self.sends)
        def _():
            self.hop(0, self.next, 0, 2).start()

        @pl.when(self.early)
        def _():
            self.hop(2, self.pair, 0, 1).start()

    def second(self):
        @pl.when(self.gets)
        def _():
            self.hop(0, self.next, 0, 2).wait_recv()

        @pl.when(self.sends)
        def _():
            self.hop(1, self.next, 2, 4).start()

        @pl.when(self.early)
        def _():
            self.hop(3, self.pair, 2, 3).start()

        @pl.when(self.late)
        def _():
            self.hop(2, self.pair, 2, 1).start()

    def third(self):
        @pl.when(self.gets)
        def _():
            self.hop(1, self.next, 2, 4).wait_recv()

        @pl.when(self.late)
        def _():
            self.hop(3, self.pair, 4, 3).start()

    def arrived(self, slot):
        self.hop(slot, self.pair, 0, 1 if slot == 2 else 3).wait_recv()

    def all_sent(self):
        @pl.when(self.sends)
        def _():
            self.hop(0, self.next, 0, 2).wait_send()
            self.hop(1, self.next, 2, 4).wait_send()

        self.hop(2, self.pair, 0, 1).wait_send()
        self.hop(3, self.pair, 0, 3).wait_send()


def differing(s, bit):
    return s + bit - 2 * bit * lax.rem(s // bit, 2)


class Give:
    def __init__(self, devices, first, operands, bufs, send, recv):
        self.s, self.h = lax.axis_index("seq"), lax.axis_index("head")
        g_own, g_got, x_own, x_got = operands
        self.g, self.x, self.slot, self.got, sem = bufs
        self.send, self.recv = send, recv
        bits = shard_orders(first, devices)
        self.partner = differing(self.s, bits[1])
        self.count = devices // 4
        self.loads = [
            pltpu.make_async_copy(g_own, self.g.at[0], sem.at[0]),
            pltpu.make_async_copy(g_got, self.g.at[1], sem.at[1]),
        ]
        for j in range(self.count):
            shard = self.s
            for k, b in enumerate(bits[1:]):
                if ((j + self.count) >> (len(bits) - 2 - k)) & 1:
                    shard = differing(shard, b)
            at = shard // (2 * first) * first + lax.rem(shard, first)
            for k, x in enumerate((x_own, x_got)):
                self.loads.append(
                    pltpu.make_async_copy(x.at[at], self.x.at[k, j], sem.at[2 + 2 * j + k])
                )

    def load(self):
        for copy in self.loads:
            copy.start()

    def loaded(self):
        for copy in self.loads:
            copy.wait()

    def make(self, j):
        total = jnp.dot(self.g[0], self.x[0, j], preferred_element_type=F32)
        total = total + jnp.dot(self.g[1], self.x[1, j], preferred_element_type=F32)
        self.slot[j] = total.astype(BF16)

    def half(self, j, k):
        step = self.slot.shape[1] // 2
        at = pl.ds(k * step, step)
        return remote(
            self.slot.at[j, at, :],
            self.got.at[j, at, :],
            self.send.at[2 * j + k],
            self.recv.at[2 * j + k],
            self.partner,
            self.h,
        )

    def finish(self):
        for j in range(self.count):
            for k in range(2):
                self.half(j, k).wait()


class HeadSum:
    def __init__(self, devices, cores, core_got, chip, y_got, own, other, send, recv):
        self.s, self.h, _, self.core, _, self.mate, self.across = place(devices, cores)
        self.core_got, self.chip, self.y_got = core_got, chip, y_got
        self.own, self.other, self.send, self.recv = own, other, send, recv

    def to_mate(self, i, src=None):
        return remote(
            self.chip.at[i] if src is None else src,
            self.core_got.at[i],
            self.send.at[i],
            self.recv.at[i],
            self.s,
            self.mate,
        )

    def over(self, i):
        return remote(
            self.chip.at[i],
            self.y_got.at[i],
            self.send.at[4 + i],
            self.recv.at[4 + i],
            self.s,
            self.across,
        )

    def back(self, i):
        return remote(
            self.own.at[i],
            self.other.at[i],
            self.send.at[8 + i],
            self.recv.at[8 + i],
            self.s,
            self.mate,
        )

    def chip_sum(self, i, part):
        self.to_mate(i).wait_recv()
        self.chip[i] = (part + self.core_got[i].astype(F32)).astype(BF16)
        self.over(i).start()

    def total(self, i):
        self.over(i).wait_recv()
        self.own[i] = (self.chip[i].astype(F32) + self.y_got[i].astype(F32)).astype(BF16)
        self.back(i).start()

    def joined(self, i):
        self.back(i).wait_recv()
        own, other = self.own[i].astype(F32), self.other[i].astype(F32)
        low = self.core == 0
        return jnp.concatenate([jnp.where(low, own, other), jnp.where(low, other, own)], axis=1)

    def all_sent(self):
        for i in range(4):
            self.to_mate(i).wait_send()
            self.over(i).wait_send()
            self.back(i).wait_send()


def forward_kernel(
    devices,
    cores,
    lengths_ref,
    x_ref,
    gain_one_ref,
    gain_two_ref,
    og_hbm,
    wk_hbm,
    wv_hbm,
    wq_hbm,
    wo_hbm,
    prev_k_hbm,
    prev_v_hbm,
    k_out,
    v_out,
    q_out,
    one_keep_out,
    one_give_out,
    mid_out,
    two_out,
    two_keep_out,
    two_give_out,
    og_keep_out,
    og_give_out,
    og_got_out,
    att_out,
    lse_out,
    row_out,
    cos_ref,
    sin_ref,
    lo_ref,
    lo_row_ref,
    valid_ref,
    kx,
    vx,
    qx,
    wk,
    wv,
    wq,
    wo,
    normed,
    flipped,
    tops,
    totals,
    acc,
    core_send,
    core_got,
    chip,
    y_got,
    own_half,
    other_half,
    mid,
    two_blocks,
    og,
    load_sem,
    store_sem,
    k_send,
    k_recv,
    v_send,
    v_recv,
    q_send,
    q_recv,
    sum_send,
    sum_recv,
    two_send,
    two_recv,
):
    rows, width = x_ref.shape
    heads = kx.shape[2] // HEAD_DIM
    s, h, odd, core, pair, mate, across = place(devices, cores)
    has_left, has_right = s >= 2, s < devices - 2
    scale = HEAD_DIM ** (-0.5) * LOG2E
    k_chain = Chain(devices, kx, k_send, k_recv, 1)
    v_chain = Chain(devices, vx, v_send, v_recv, 1)
    chains = [v_chain, k_chain]
    q_chain = Chain(devices, qx, q_send, q_recv, -1)
    head_sum = HeadSum(
        devices, cores, core_got, chip, y_got, own_half, other_half, sum_send, sum_recv
    )

    loads = [
        pltpu.make_async_copy(src, dst, load_sem.at[i])
        for i, (src, dst) in enumerate(
            ((wk_hbm, wk), (wv_hbm, wv), (wq_hbm, wq), (wo_hbm, wo), (og_hbm, og))
        )
    ]
    for load in loads:
        load.start()

    greet_all(devices, cores)
    step = rows // 4

    def normalize(i, _):
        at = pl.ds(pl.multiple_of(i * step, step), step)
        x = x_ref[at, :].astype(F32)
        root = lax.rsqrt(jnp.mean(x * x, axis=-1, keepdims=True) + EPS)
        normed[at, :] = (x * root * gain_one_ref[...]).astype(BF16)
        return 0

    lax.fori_loop(0, 4, normalize, 0)

    starts, padded = [0], 0
    for r in range(NSEQ - 1):
        padded = padded + (lengths_ref[r] + PAD - 1) // PAD * PAD
        starts.append(padded)

    def sequence_of(at):
        start = jnp.zeros_like(at)
        low = jnp.full_like(at, -BIG)
        length = jnp.zeros_like(at) + lengths_ref[0]
        for r in range(1, NSEQ):
            inside = at >= starts[r]
            start = jnp.where(inside, starts[r], start)
            low = jnp.where(inside, starts[r], low)
            length = jnp.where(inside, lengths_ref[r], length)
        valid = at - start < length
        low = jnp.where(valid, jnp.maximum(low, at - (WINDOW - 1)), at)
        return at - start, valid, jnp.where(at < devices * rows, low, BIG) - s * rows

    def turn_into(weight, out):
        raw = jnp.dot(normed[...], weight[...], preferred_element_type=F32)
        for k in range(heads):
            u = raw[:, k * HEAD_DIM : (k + 1) * HEAD_DIM]
            u = u * cos_ref[...] + pltpu.roll(u, HEAD_DIM // 2, 1) * sin_ref[...]
            out[0, :, k * HEAD_DIM : (k + 1) * HEAD_DIM] = u.astype(BF16)

    loads[1].wait()
    vx[0] = jnp.dot(normed[...], wv[...], preferred_element_type=F32).astype(BF16)
    all_greeted(devices)
    v_chain.first()
    at = lax.broadcasted_iota(jnp.int32, (rows, HEAD_DIM), 0) + s * rows
    position, valid, low = sequence_of(at)
    valid_ref[...] = valid[:, 0:1].astype(jnp.int32)
    lo_ref[...] = low[:, 0:1]
    lane = lax.broadcasted_iota(jnp.int32, (1, HEAD_DIM), 1)
    half_dim = HEAD_DIM // 2
    pair_of = lax.rem(lane, half_dim).astype(F32)
    freq = jnp.exp(-math.log(10000.0) * (2.0 * pair_of / HEAD_DIM))
    angle = position.astype(F32) * freq
    cos_ref[...] = jnp.cos(angle)
    sin_ref[...] = jnp.sin(angle) * jnp.where(lane < half_dim, -1.0, 1.0)
    lo_row_ref[...] = sequence_of(lax.broadcasted_iota(jnp.int32, lo_row_ref.shape, 1) + s * rows)[2]
    loads[0].wait()
    turn_into(wk, kx)
    k_chain.first()

    @pl.when(jnp.logical_not(has_left))
    def _():
        copies = []
        for i, (src, dst) in enumerate(((prev_k_hbm, kx), (prev_v_hbm, vx))):
            for j, d in enumerate((2, 4)):
                at = pl.multiple_of((s - d) * rows + WINDOW, rows)
                copies.append(
                    pltpu.make_async_copy(
                        src.at[pl.ds(at, rows), :], dst.at[d], load_sem.at[5 + 2 * i + j]
                    )
                )
        for copy in copies:
            copy.start()
        for copy in copies:
            copy.wait()

    @pl.when(jnp.logical_not(has_right))
    def _():
        qx[2] = jnp.zeros_like(qx[2])
        qx[4] = jnp.zeros_like(qx[4])

    loads[2].wait()
    turn_into(wq, qx)
    q_chain.first()

    for i in range(4):
        flip_at = slice(i * step, (i + 1) * step)
        flipped[:, :, flip_at] = normed[flip_at, :].T.reshape(devices, width // devices, step)
    turned = flipped.reshape(devices // 2, 2, width // devices, rows)
    stores = [
        pltpu.make_async_copy(turned.at[:, odd], one_keep_out, store_sem.at[0]),
        pltpu.make_async_copy(turned.at[:, 1 - odd], one_give_out, store_sem.at[1]),
    ]
    stores[0].start()
    stores[1].start()

    depth = width // devices
    loads[4].wait()
    for j in range(devices):
        two_blocks[j] = og[:, j * depth : (j + 1) * depth]
    near = lax.rem(s // 2, 2)
    split = two_blocks.reshape(devices // 4, 2, 2, rows, depth)
    og_stores = [
        pltpu.make_async_copy(split.at[:, near], og_keep_out, store_sem.at[4]),
        pltpu.make_async_copy(split.at[:, 1 - near], og_give_out, store_sem.at[5]),
    ]
    og_stores[0].start()
    og_stores[1].start()
    sub = rows // 2

    def attend(d, only=None):
        def body(i, _):
            if only is None:
                k, part = i // 2, lax.rem(i, 2)
            else:
                k, part = i, only
            at = pl.ds(pl.multiple_of(part * sub, sub), sub)
            lanes = pl.ds(pl.multiple_of(k * HEAD_DIM, HEAD_DIM), HEAD_DIM)
            scores = dot_nt(qx[0, at, lanes], kx[d, :, lanes])
            u = lax.broadcasted_iota(jnp.int32, scores.shape, 1) - d * rows
            seen = u >= lo_ref[at, :]
            if d == 0:
                t = lax.broadcasted_iota(jnp.int32, scores.shape, 0) + part * sub
                seen = seen & (u <= t)
            scores = jnp.where(seen, scores * scale, MASKED)
            top = jnp.max(scores, axis=1, keepdims=True)
            if d > 0:
                old = tops[k, at, :]
                top = jnp.maximum(top, old)
            p = jnp.exp2(scores - top)
            total = jnp.sum(p, axis=1, keepdims=True)
            mixed = jnp.dot(p.astype(BF16), vx[d, :, lanes], preferred_element_type=F32)
            if d > 0:
                fade = jnp.exp2(old - top)
                total = total + totals[k, at, :] * fade
                mixed = mixed + acc[at, lanes] * fade
            tops[k, at, :] = top
            totals[k, at, :] = total
            acc[at, lanes] = mixed
            return 0

        lax.fori_loop(0, 2 * heads if only is None else heads, body, 0)

    attend(0)
    for chain in chains:
        chain.second()
    attend(2)
    for chain in chains:
        chain.arrived(2)
    attend(1)
    for chain in chains:
        chain.third()
    attend(4)
    q_chain.second()
    for chain in chains:
        chain.arrived(3)
    stores.append(pltpu.make_async_copy(kx, k_out, store_sem.at[2]))
    stores.append(pltpu.make_async_copy(vx, v_out, store_sem.at[3]))
    stores[2].start()
    stores[3].start()

    og_stores[0].wait()
    og_stores[1].wait()
    blocks = two_blocks.reshape(devices // 2, 2, rows, depth)

    half = width // 2
    loads[3].wait()
    mine = pl.ds(pl.multiple_of(core * half, half), half)
    theirs = pl.ds(pl.multiple_of((1 - core) * half, half), half)

    for t in range(2):
        attend(3, t)
        at = slice(t * sub, (t + 1) * sub)
        for k in range(heads):
            columns = slice(k * HEAD_DIM, (k + 1) * HEAD_DIM)
            out = jnp.where(valid_ref[at, :] > 0, acc[at, columns] / totals[k, at, :], 0.0)
            att_out[at, columns] = out.astype(BF16)
        total = dot_nt(att_out[at, :], wo[theirs, :]).astype(BF16)
        for j in range(2):
            core_send[2 * t + j] = total[j * step : (j + 1) * step, :]
            head_sum.to_mate(2 * t + j, core_send.at[2 * t + j]).start()
        total = dot_nt(att_out[at, :], wo[mine, :])
        for j in range(2):
            head_sum.chip_sum(2 * t + j, total[j * step : (j + 1) * step, :])
    for k in range(heads):
        lse = tops[k] + jnp.log2(totals[k])
        lse_out[k] = lse
        row_out[k] = jnp.broadcast_to(lse, (rows, HEAD_DIM)).T[0:1, :]
    og_here = pl.ds(core * (devices // 8), devices // 8)
    og_swap = remote(
        og_give_out.at[og_here],
        og_got_out.at[og_here],
        two_send.at[8],
        two_recv.at[8],
        differing(s, 2),
        h,
    )
    og_pass = remote(
        og_got_out.at[og_here], og_got_out.at[og_here], two_send.at[9], two_recv.at[9], s, mate
    )
    og_swap.start()

    q_chain.third()

    def finish(i):
        at = slice(i * step, (i + 1) * step)
        total = x_ref[at, :].astype(F32) + head_sum.joined(i)
        mid[at, :] = total
        root = lax.rsqrt(jnp.mean(total * total, axis=-1, keepdims=True) + EPS)
        two = (total * root * gain_two_ref[...]).astype(BF16)
        normed[at, :] = two
        for j in range(devices):
            two_blocks[j, at, :] = two[:, j * depth : (j + 1) * depth]

    for i in range(4):
        head_sum.total(i)
        if i > 0:
            finish(i - 1)
    finish(3)
    for src, dst in (
        (mid, mid_out),
        (normed, two_out),
        (blocks.at[:, odd], two_keep_out),
        (blocks.at[:, 1 - odd], two_give_out),
    ):
        stores.append(pltpu.make_async_copy(src, dst, store_sem.at[2 + len(stores)]))
        stores[-1].start()
    q_chain.arrived(2)
    q_chain.arrived(3)
    stores.append(pltpu.make_async_copy(qx, q_out, store_sem.at[2 + len(stores)]))
    stores[-1].start()
    og_swap.wait_recv()
    og_pass.start()
    og_swap.wait_send()
    og_pass.wait()
    for chain in (*chains, q_chain):
        chain.all_sent()
    head_sum.all_sent()
    for store in stores:
        store.wait()


def forward(devices, cores, lengths, x, gains, grad, weights, w_out, prevs):
    rows, width = x.shape
    cols = weights[0].shape[1]
    heads = cols // HEAD_DIM
    depth = width // devices
    parts = WINDOW // rows + 1
    step = rows // 4
    vmem = pl.BlockSpec(memory_space=pltpu.VMEM)
    hbm = pl.BlockSpec(memory_space=pl.ANY)

    def shape(*dims, dtype=BF16):
        return jax.ShapeDtypeStruct(dims, dtype)

    blocks = pltpu.VMEM((4, step, width // 2), BF16)
    dma = pltpu.SemaphoreType.DMA
    return pl.pallas_call(
        functools.partial(forward_kernel, devices, cores),
        in_specs=[pl.BlockSpec(memory_space=pltpu.SMEM)] + [vmem] * 3 + [hbm] * 7,
        out_specs=[hbm] * 12 + [vmem] * 8,
        out_shape=[
            shape(parts, rows, cols),
            shape(parts, rows, cols),
            shape(parts, rows, cols),
            shape(devices // 2, depth, rows),
            shape(devices // 2, depth, rows),
            shape(rows, width, dtype=F32),
            shape(rows, width),
            shape(devices // 2, rows, depth),
            shape(devices // 2, rows, depth),
            shape(devices // 4, 2, rows, depth),
            shape(devices // 4, 2, rows, depth),
            shape(devices // 4, 2, rows, depth),
            shape(rows, cols),
            shape(heads, rows, 1, dtype=F32),
            shape(heads, 1, rows, dtype=F32),
            shape(rows, HEAD_DIM, dtype=F32),
            shape(rows, HEAD_DIM, dtype=F32),
            shape(rows, 1, dtype=jnp.int32),
            shape(1, parts * rows, dtype=jnp.int32),
            shape(rows, 1, dtype=jnp.int32),
        ],
        scratch_shapes=[pltpu.VMEM((parts, rows, cols), BF16)] * 3
        + [pltpu.VMEM((width, cols), BF16)] * 4
        + [
            pltpu.VMEM((rows, width), BF16),
            pltpu.VMEM((devices, depth, rows), BF16),
            pltpu.VMEM((heads, rows, 1), F32),
            pltpu.VMEM((heads, rows, 1), F32),
            pltpu.VMEM((rows, cols), F32),
        ]
        + [blocks] * 6
        + [
            pltpu.VMEM((rows, width), F32),
            pltpu.VMEM((devices, rows, depth), BF16),
            pltpu.VMEM((rows, width), BF16),
            dma((9,)),
            dma((12,)),
        ]
        + [dma((4,))] * 6
        + [dma((12,))] * 2
        + [dma((10,))] * 2,
        compiler_params=pltpu.CompilerParams(
            collective_id=0, has_side_effects=True, vmem_limit_bytes=56 << 20
        ),
        cost_estimate=cost(10 * rows * width * cols, 40 << 20),
        name="forward",
    )(lengths, x, *gains, grad, *weights, w_out, *prevs)


def pieces_of(extent, step):
    return [(start, min(step, extent - start)) for start in range(0, extent, step)]


def middle_kernel(
    devices,
    cores,
    two_ref,
    og_ref,
    gain_ref,
    valid_ref,
    lse_row_ref,
    wg_hbm,
    wu_hbm,
    wd_hbm,
    mid_hbm,
    wo_hbm,
    att_hbm,
    two_give_hbm,
    branch_out,
    gm_out,
    part_out,
    do_out,
    delta_out,
    stat_out,
    act_out,
    gg_out,
    gu_out,
    act_got,
    gg_got,
    two_got,
    keep_out,
    give_out,
    wg,
    wu,
    wd,
    act_t,
    gg_t,
    gu_t,
    act,
    gg,
    gu,
    mid,
    wo,
    att,
    core_send,
    core_got,
    chip,
    y_got,
    own_half,
    other_half,
    flipped,
    load_sem,
    store_sem,
    far_send,
    far_recv,
    sum_send,
    sum_recv,
):
    rows, width = mid.shape
    units = wg.shape[0]
    heads = att.shape[1] // HEAD_DIM
    step = rows // 4
    half = width // 2
    s, h, odd, core, pair, mate, across = place(devices, cores)
    near = differing(s, 2)
    head_sum = HeadSum(
        devices, cores, core_got, chip, y_got, own_half, other_half, sum_send, sum_recv
    )
    greet(pair, h)
    greet(near, h)
    greet(s, mate)
    greet(s, across)
    pieces = pieces_of(units, 3 * HEAD_DIM)
    loads = []
    for c, (start, size) in enumerate(pieces):
        at = pl.ds(start, size)
        loads.append(
            [
                pltpu.make_async_copy(src.at[at, :], dst.at[at, :], load_sem.at[3 * c + k])
                for k, (src, dst) in enumerate(((wg_hbm, wg), (wu_hbm, wu), (wd_hbm, wd)))
            ]
        )
        for copy in loads[-1]:
            copy.start()
    first = 3 * len(pieces)
    later = [
        pltpu.make_async_copy(src, dst, load_sem.at[first + k])
        for k, (src, dst) in enumerate(((mid_hbm, mid), (wo_hbm, wo), (att_hbm, att)))
    ]
    for copy in later:
        copy.start()
    pl.semaphore_wait(pltpu.get_barrier_semaphore(), 4)

    share = devices // 4
    here = pl.ds(core * share, share)
    two_swap = remote(
        two_give_hbm.at[here], two_got.at[here], far_send.at[4], far_recv.at[4], pair, h
    )
    two_pass = remote(
        two_got.at[here], two_got.at[here], far_send.at[5], far_recv.at[5], s, mate
    )
    two_swap.start()
    mine, theirs = (pl.ds(pl.multiple_of(c * half, half), half) for c in (core, 1 - core))
    swaps = []

    def product(tokens, columns):
        total = jnp.dot(gg[tokens, :], wg[:, columns], preferred_element_type=F32)
        return total + jnp.dot(gu[tokens, :], wu[:, columns], preferred_element_type=F32)

    for t in range(2):
        tokens = slice(2 * t * step, 2 * (t + 1) * step)
        for c, (start, size) in enumerate(pieces):
            at = slice(start, start + size)
            if t == 0:
                for copy in loads[c]:
                    copy.wait()
            gate = dot_nt(wg[at, :], two_ref[tokens, :])
            up = dot_nt(wu[at, :], two_ref[tokens, :])
            grad = dot_nt(wd[at, :], og_ref[tokens, :])
            sig = 1.0 / (1.0 + jnp.exp(-gate))
            silu = gate * sig
            value = (silu * up).astype(BF16)
            grad_gate = (grad * up * sig * (1.0 + gate * (1.0 - sig))).astype(BF16)
            grad_up = (grad * silu).astype(BF16)
            act_t[at, tokens] = value
            gg_t[at, tokens] = grad_gate
            gu_t[at, tokens] = grad_up
            act[tokens, at] = value.T
            gg[tokens, at] = grad_gate.T
            gu[tokens, at] = grad_up.T
        part = pl.ds(2 * t * step, 2 * step)
        for k, (src, dst, seq) in enumerate(((gg_t, gg_got, pair), (act_t, act_got, near))):
            i = 2 * t + k
            swaps.append(
                remote(src.at[:, part], dst.at[:, part], far_send.at[i], far_recv.at[i], seq, h)
            )
            swaps[-1].start()
        total = product(tokens, theirs).astype(BF16)
        for j in range(2):
            core_send[2 * t + j] = total[j * step : (j + 1) * step, :]
            head_sum.to_mate(2 * t + j, core_send.at[2 * t + j]).start()
        total = product(tokens, mine)
        for j in range(2):
            head_sum.chip_sum(2 * t + j, total[j * step : (j + 1) * step, :])
    stores = [
        pltpu.make_async_copy(src, dst, store_sem.at[k])
        for k, (src, dst) in enumerate(((act_t, act_out), (gg_t, gg_out), (gu_t, gu_out)))
    ]
    for store in stores:
        store.start()

    for k, columns in enumerate((theirs, mine)):
        branch_out[k] = jnp.dot(act[...], wd[:, columns], preferred_element_type=F32).astype(BF16)
    for copy in later:
        copy.wait()
    two_swap.wait_recv()
    two_pass.start()

    def finish(i):
        at = slice(i * step, (i + 1) * step)
        x = mid[at, :]
        root = lax.rsqrt(jnp.mean(x * x, axis=-1, keepdims=True) + EPS)
        grad = head_sum.joined(i)
        unit = x * root
        part = jnp.sum(grad * unit, axis=0, keepdims=True)
        part_out[...] = part if i == 0 else part_out[...] + part
        grad = grad * gain_ref[...]
        total = og_ref[at, :].astype(F32) + root * (
            grad - unit * jnp.mean(grad * unit, axis=-1, keepdims=True)
        )
        gm_out[at, :] = total
        low = total.astype(BF16)
        flipped[:, :, at] = low.T.reshape(devices, width // devices, step)
        do = jnp.dot(low, wo[...], preferred_element_type=F32).astype(BF16).astype(F32)
        do = jnp.where(valid_ref[at, :] > 0, do, 0.0)
        do_out[at, :] = do.astype(BF16)
        product = do * att[at, :].astype(F32)
        for k in range(heads):
            delta = jnp.sum(product[:, k * HEAD_DIM : (k + 1) * HEAD_DIM], axis=1, keepdims=True)
            delta_out[k, at, :] = delta
            stat_out[k, 0:1, at] = lse_row_ref[k, :, at]
            stat_out[k, 1:2, at] = jnp.broadcast_to(delta, (step, HEAD_DIM)).T[0:1, :]

    for i in range(4):
        head_sum.total(i)
        if i > 0:
            finish(i - 1)
    finish(3)
    split = flipped.reshape(devices // 2, 2, width // devices, rows)
    stores += [
        pltpu.make_async_copy(split.at[:, odd], keep_out, store_sem.at[3]),
        pltpu.make_async_copy(split.at[:, 1 - odd], give_out, store_sem.at[4]),
    ]
    stores[3].start()
    stores[4].start()
    for copy in swaps:
        copy.wait()
    two_swap.wait_send()
    two_pass.wait()
    head_sum.all_sent()
    for store in stores:
        store.wait()


def sum_scratch(rows, width):
    return [pltpu.VMEM((4, rows // 4, width // 2), BF16)] * 5


def middle(
    devices, cores, two, grad, gain, valid, lse_row, weights, mid, w_out, attended, two_give
):
    rows, width = mid.shape
    units = weights[0].shape[0]
    cols = attended.shape[1]
    heads = cols // HEAD_DIM
    depth = width // devices
    count = len(pieces_of(units, 3 * HEAD_DIM))
    vmem = pl.BlockSpec(memory_space=pltpu.VMEM)
    hbm = pl.BlockSpec(memory_space=pl.ANY)
    dma = pltpu.SemaphoreType.DMA

    def shape(*dims, dtype=BF16):
        return jax.ShapeDtypeStruct(dims, dtype)

    return pl.pallas_call(
        functools.partial(middle_kernel, devices, cores),
        in_specs=[vmem] * 5 + [hbm] * 7,
        out_specs=[vmem] * 6 + [hbm] * 8,
        out_shape=[
            shape(2, rows, width // 2),
            shape(rows, width, dtype=F32),
            shape(1, width, dtype=F32),
            shape(rows, cols),
            shape(heads, rows, 1, dtype=F32),
            shape(heads, 2, rows, dtype=F32),
        ]
        + [shape(units, rows)] * 5
        + [shape(devices // 2, rows, depth)]
        + [shape(devices // 2, depth, rows)] * 2,
        scratch_shapes=[pltpu.VMEM((units, width), BF16)] * 3
        + [pltpu.VMEM((units, rows), BF16)] * 3
        + [pltpu.VMEM((rows, units), BF16)] * 3
        + [
            pltpu.VMEM((rows, width), F32),
            pltpu.VMEM((width, cols), BF16),
            pltpu.VMEM((rows, cols), BF16),
            pltpu.VMEM((4, rows // 4, width // 2), BF16),
        ]
        + sum_scratch(rows, width)
        + [
            pltpu.VMEM((devices, depth, rows), BF16),
            dma((3 * count + 3,)),
            dma((5,)),
            dma((6,)),
            dma((6,)),
            dma((12,)),
            dma((12,)),
        ],
        compiler_params=pltpu.CompilerParams(
            collective_id=1, has_side_effects=True, vmem_limit_bytes=62 << 20
        ),
        cost_estimate=cost(12 * rows * width * units, 60 << 20),
        name="middle",
    )(two, grad, gain, valid, lse_row, *weights, mid, w_out, attended, two_give)


def attention_back_kernel(
    devices,
    cores,
    do_hbm,
    stat_hbm,
    gg_hbm,
    gg_got_hbm,
    two_hbm,
    two_got_hbm,
    gu_hbm,
    parts_ref,
    mid_ref,
    lo_ref,
    lo_row_ref,
    cos_ref,
    sin_ref,
    kx,
    vx,
    qx,
    lse_ref,
    delta_ref,
    block_out,
    gq_out,
    gk_out,
    gv_out,
    gate_got,
    gu_got,
    dx,
    sx,
    dk_acc,
    dv_acc,
    core_got,
    chip,
    y_got,
    own_half,
    other_half,
    gate_g,
    gate_x,
    gate_slot,
    gate_sem,
    gate_send,
    gate_recv,
    up_send,
    up_recv,
    load_sem,
    d_send,
    d_recv,
    s_send,
    s_recv,
    sum_send,
    sum_recv,
):
    parts, rows, cols = kx.shape
    heads = cols // HEAD_DIM
    step = rows // 4
    sub = rows // 2
    s, h, odd, core, pair, mate, across = place(devices, cores)
    scale = HEAD_DIM ** (-0.5) * LOG2E
    d_chain = Chain(devices, dx, d_send, d_recv, -1)
    s_chain = Chain(devices, sx, s_send, s_recv, -1)
    head_sum = HeadSum(
        devices, cores, core_got, chip, y_got, own_half, other_half, sum_send, sum_recv
    )
    gate = Give(
        devices,
        1,
        (gg_hbm, gg_got_hbm, two_hbm, two_got_hbm),
        (gate_g, gate_x, gate_slot, gate_got, gate_sem),
        gate_send,
        gate_recv,
    )
    greet_all(devices, cores)
    loads = [
        pltpu.make_async_copy(do_hbm, dx.at[0], load_sem.at[0]),
        pltpu.make_async_copy(stat_hbm, sx.at[0], load_sem.at[1]),
    ]
    loads[0].start()
    loads[1].start()
    gate.load()

    @pl.when(s >= devices - 2)
    def _():
        for d in (2, 4):
            dx[d] = jnp.zeros_like(dx[d])
            sx[d] = jnp.zeros_like(sx[d])

    loads[0].wait()
    loads[1].wait()
    all_greeted(devices)
    d_chain.first()
    s_chain.first()
    for i in range(4):
        head_sum.to_mate(i, parts_ref.at[0, pl.ds(i * step, step), :]).start()

    def queries_back(start, count):
        def body(i, _):
            k = start + i // 2
            at = pl.ds(pl.multiple_of((i % 2) * sub, sub), sub)
            lanes = pl.ds(pl.multiple_of(k * HEAD_DIM, HEAD_DIM), HEAD_DIM)
            q, do, lo = qx[0, at, lanes], dx[0, at, lanes], lo_ref[at, :]
            lse, delta = lse_ref[k, at, :], delta_ref[k, at, :]
            total = jnp.zeros((sub, HEAD_DIM), F32)
            for d in range(parts):
                key = kx[d, :, lanes]
                scores = dot_nt(q, key)
                u = lax.broadcasted_iota(jnp.int32, scores.shape, 1) - d * rows
                seen = u >= lo
                if d == 0:
                    t = lax.broadcasted_iota(jnp.int32, scores.shape, 0) + (i % 2) * sub
                    seen = seen & (u <= t)
                p = jnp.exp2(jnp.where(seen, scores * scale, MASKED) - lse)
                ds = (p * (dot_nt(do, vx[d, :, lanes]) - delta)).astype(BF16)
                total = total + jnp.dot(ds, key, preferred_element_type=F32)
            gq_out[at, lanes] = turned_back(
                total * HEAD_DIM ** (-0.5), cos_ref[at, :], sin_ref[at, :]
            )
            return 0

        lax.fori_loop(0, 2 * count, body, 0)

    def keys_back(d):
        def body(i, _):
            k = i // 2
            at = pl.ds(pl.multiple_of((i % 2) * sub, sub), sub)
            lanes = pl.ds(pl.multiple_of(k * HEAD_DIM, HEAD_DIM), HEAD_DIM)
            key, value = kx[0, at, lanes], vx[0, at, lanes]
            q, do = qx[d, :, lanes], dx[d, :, lanes]
            scores = dot_nt(key, q)
            u = lax.broadcasted_iota(jnp.int32, scores.shape, 0) + (i % 2) * sub
            seen = u >= lo_row_ref[:, d * rows : (d + 1) * rows]
            if d == 0:
                seen = seen & (u <= lax.broadcasted_iota(jnp.int32, scores.shape, 1))
            lse, delta = sx[d, k, 0:1, :], sx[d, k, 1:2, :]
            p = jnp.exp2(jnp.where(seen, scores * scale - lse, MASKED))
            dv = jnp.dot(p.astype(BF16), do, preferred_element_type=F32)
            ds = (p * (dot_nt(value, do) - delta)).astype(BF16)
            dk = jnp.dot(ds, q, preferred_element_type=F32)
            if d > 0:
                dv = dv + dv_acc[at, lanes]
                dk = dk + dk_acc[at, lanes]
            dv_acc[at, lanes] = dv
            dk_acc[at, lanes] = dk
            return 0

        lax.fori_loop(0, 2 * heads, body, 0)

    ups = [
        remote(
            gu_hbm.at[pl.ds(start, size), :],
            gu_got.at[pl.ds(start, size), :],
            up_send.at[i],
            up_recv.at[i],
            pair,
            h,
        )
        for i, (start, size) in enumerate(pieces_of(gu_hbm.shape[0], 3 * HEAD_DIM))
    ]
    ups[0].start()
    ups[1].start()
    gate.loaded()
    gate.make(0)
    gate.half(0, 0).start()
    queries_back(0, heads // 4)
    for i in range(4):
        head_sum.chip_sum(i, parts_ref[1, i * step : (i + 1) * step, :].astype(F32))
    s_chain.second()
    d_chain.second()
    ups[2].start()
    gate.half(0, 1).start()
    for j in range(1, gate.count):
        gate.make(j)
        gate.half(j, 0).start()
        gate.half(j, 1).start()
    queries_back(heads // 4, heads // 2)
    keys_back(0)
    keys_back(2)
    s_chain.third()
    d_chain.third()
    for copy in ups[3:]:
        copy.start()
    queries_back(heads // 4 + heads // 2, heads - heads // 4 - heads // 2)
    for i in range(4):
        head_sum.total(i)
    s_chain.arrived(2)
    d_chain.arrived(2)
    keys_back(1)
    keys_back(4)
    for i in range(4):
        at = slice(i * step, (i + 1) * step)
        block_out[at, :] = (mid_ref[at, :] + head_sum.joined(i)).astype(BF16)
    s_chain.arrived(3)
    d_chain.arrived(3)
    keys_back(3)
    for k in range(heads):
        lanes = slice(k * HEAD_DIM, (k + 1) * HEAD_DIM)
        gk_out[:, lanes] = turned_back(
            dk_acc[:, lanes] * HEAD_DIM ** (-0.5), cos_ref[...], sin_ref[...]
        )
        gv_out[:, lanes] = dv_acc[:, lanes].astype(BF16)
    d_chain.all_sent()
    s_chain.all_sent()
    head_sum.all_sent()
    gate.finish()
    for copy in ups:
        copy.wait()


def attention_back(
    devices, cores, do, stat, gate, grad_up, branch, mid, low_col, low_row, tables, keys, values, queries, lse, delta
):
    rows, width = mid.shape
    parts, _, cols = keys.shape
    heads = cols // HEAD_DIM
    units = gate[0].shape[0]
    count, depth = devices // 4, width // devices
    vmem = pl.BlockSpec(memory_space=pltpu.VMEM)
    hbm = pl.BlockSpec(memory_space=pl.ANY)
    dma = pltpu.SemaphoreType.DMA
    give = [
        pltpu.VMEM((2, units, rows), BF16),
        pltpu.VMEM((2, count, rows, depth), BF16),
        pltpu.VMEM((count, units, depth), BF16),
        dma((2 + 2 * count,)),
        dma((2 * count,)),
        dma((2 * count,)),
    ]
    flops = 14 * rows * rows * parts * cols
    return pl.pallas_call(
        functools.partial(attention_back_kernel, devices, cores),
        in_specs=[hbm] * 7 + [vmem] * 11,
        out_specs=[vmem] * 5 + [hbm],
        out_shape=[jax.ShapeDtypeStruct((rows, width), BF16)]
        + [jax.ShapeDtypeStruct((rows, cols), BF16)] * 3
        + [jax.ShapeDtypeStruct((count, units, depth), BF16)]
        + [jax.ShapeDtypeStruct((units, rows), BF16)],
        scratch_shapes=[
            pltpu.VMEM((parts, rows, cols), BF16),
            pltpu.VMEM((parts, heads, 2, rows), F32),
            pltpu.VMEM((rows, cols), F32),
            pltpu.VMEM((rows, cols), F32),
        ]
        + sum_scratch(rows, width)
        + give
        + [dma((len(pieces_of(units, 3 * HEAD_DIM)),))] * 2
        + [dma((2,))]
        + [dma((4,))] * 4
        + [dma((12,))] * 2,
        compiler_params=pltpu.CompilerParams(
            collective_id=2, has_side_effects=True, vmem_limit_bytes=58 << 20
        ),
        cost_estimate=cost(flops, 80 << 20),
        name="attention_back",
    )(do, stat, *gate, grad_up, branch, mid, low_col, low_row, *tables, keys, values, queries, lse, delta)


class Reduce:
    def __init__(self, block, near, far, slot, got, keep, last, send, recv):
        self.h = lax.axis_index("head")
        self.block, self.near_seq, self.far_seq = block, near, far
        self.slot, self.got, self.keep, self.last = slot, got, keep, last
        self.send, self.recv = send, recv

    def near(self, j):
        return remote(
            self.slot.at[j], self.got.at[j], self.send.at[j], self.recv.at[j], self.near_seq, self.h
        )

    def far(self):
        return remote(
            self.keep.at[1], self.last, self.send.at[2], self.recv.at[2], self.far_seq, self.h
        )

    def give(self):
        for j in range(2):
            self.slot[j] = self.block(2 + j).astype(BF16)
            self.near(j).start()

    def combine(self, received=None):
        for j in (1, 0):
            total = self.block(j)
            if received is None:
                self.near(j).wait_recv()
            total = total + self.got[j].astype(F32)
            self.keep[j] = total.astype(BF16)
            if j == 1:
                self.far().start()

    def result(self):
        self.far().wait_recv()
        return (self.keep[0].astype(F32) + self.last[...].astype(F32)).astype(BF16)

    def all_sent(self, gave):
        if gave:
            self.near(0).wait_send()
            self.near(1).wait_send()
        self.far().wait_send()


def weights_kernel(
    devices,
    cores,
    gate_hbm,
    gate_other_hbm,
    up_hbm,
    up_other_hbm,
    down_hbm,
    down_other_hbm,
    two_hbm,
    two_other_hbm,
    og_hbm,
    og_other_hbm,
    gate_got_hbm,
    mid_give_hbm,
    one_give_hbm,
    wq_hbm,
    wk_hbm,
    wv_hbm,
    gm_hbm,
    x_ref,
    gain_ref,
    mlp_part_ref,
    gq,
    gk,
    gv,
    att,
    one,
    mid_x,
    gate_out,
    up_out,
    down_out,
    wq_out,
    wk_out,
    wv_out,
    wo_out,
    tokens_out,
    gains_out,
    g_a,
    g_b,
    x_a,
    x_b,
    up_slot,
    down_slot,
    got_mlp,
    keep_mlp,
    last_mlp,
    gq_other,
    gk_other,
    gv_other,
    mid_other,
    one_other,
    att_other,
    slot_att,
    got_att,
    keep_att,
    last_att,
    wq,
    wk,
    wv,
    gm,
    core_send,
    core_got,
    chip,
    y_got,
    own_half,
    other_half,
    gains_got,
    load_sem,
    gm_sem,
    x_send,
    x_recv,
    job_send,
    job_recv,
    sum_send,
    sum_recv,
    gain_send,
    gain_recv,
):
    rows, width = x_ref.shape
    half = width // 2
    step = rows // 4
    s, h, odd, core, pair, mate, across = place(devices, cores)
    near, far = differing(s, 2), differing(s, 4)
    head_sum = HeadSum(
        devices, cores, core_got, chip, y_got, own_half, other_half, sum_send, sum_recv
    )
    greet(pair, h)
    greet(near, h)
    greet(far, h)
    greet(s, mate)
    greet(s, across)

    def position(first, p):
        bits = shard_orders(first, devices)
        shard = s
        for k, b in enumerate(bits[1:]):
            if (p >> (len(bits) - 2 - k)) & 1:
                shard = differing(shard, b)
        return shard // (2 * first) * first + lax.rem(shard, first)

    count = [0]

    def load(src, dst):
        copy = pltpu.make_async_copy(src, dst, load_sem.at[count[0]])
        count[0] += 1
        copy.start()
        return copy

    def load_job(g_own, g_other, x_own, x_other, g, x, first, blocks):
        copies = [load(g_own, g.at[0]), load(g_other, g.at[1])]
        for p in blocks:
            at = position(first, p)
            copies += [load(x_own.at[at], x.at[0, p]), load(x_other.at[at], x.at[1, p])]
        return copies

    def wait(copies):
        for copy in copies:
            copy.wait()

    gate_loads = load_job(gate_hbm, gate_other_hbm, two_hbm, two_other_hbm, g_a, x_a, 1, (0, 1))
    gate_loads.append(load(gate_got_hbm, got_mlp.at[0]))
    up_loads = load_job(up_hbm, up_other_hbm, two_hbm, two_other_hbm, g_b, x_b, 1, (0, 1, 2, 3))
    w_loads = [load(wq_hbm, wq), load(wk_hbm, wk), load(wv_hbm, wv)]

    def gm_load(i):
        return pltpu.make_async_copy(
            gm_hbm.at[pl.ds(i * step, step), :], gm.at[i % 2], gm_sem.at[i % 2]
        )

    gm_load(0).start()
    gm_load(1).start()

    def mlp_block(g, x):
        def block(p):
            total = jnp.dot(g[0], x[0, p], preferred_element_type=F32)
            return total + jnp.dot(g[1], x[1, p], preferred_element_type=F32)

        return block

    def att_block(x_own, x_other, g_own, g_other):
        def block(p):
            at = position(1, p)
            total = jnp.dot(x_own[at], g_own[...], preferred_element_type=F32)
            return total + jnp.dot(x_other[at], g_other[...], preferred_element_type=F32)

        return block

    def job(k, block, first_seq, slot, got, keep, last):
        return Reduce(block, first_seq, far, slot, got, keep, last, job_send.at[k], job_recv.at[k])

    gate = job(0, mlp_block(g_a, x_a), near, None, got_mlp.at[0], keep_mlp.at[0], last_mlp.at[0])
    up = job(1, mlp_block(g_b, x_b), near, up_slot, got_mlp.at[1], keep_mlp.at[1], last_mlp.at[1])
    down = job(2, mlp_block(g_a, x_a), pair, down_slot, got_mlp.at[2], keep_mlp.at[2], last_mlp.at[2])
    attention = []
    for k, operands in enumerate(
        (
            (one, one_other, gq, gq_other),
            (one, one_other, gk, gk_other),
            (one, one_other, gv, gv_other),
            (mid_x, mid_other, att, att_other),
        )
    ):
        attention.append(
            job(
                3 + k,
                att_block(*operands),
                near,
                slot_att.at[k],
                got_att.at[k],
                keep_att.at[k],
                last_att.at[k],
            )
        )

    pl.semaphore_wait(pltpu.get_barrier_semaphore(), 5)
    swaps = [
        remote(src, dst, x_send.at[i], x_recv.at[i], pair, h)
        for i, (src, dst) in enumerate(
            ((gq, gq_other), (gk, gk_other), (gv, gv_other))
        )
    ]
    share = devices // 4
    here = pl.ds(core * share, share)
    one_swap = remote(
        one_give_hbm.at[here], one_other.at[here], x_send.at[5], x_recv.at[5], pair, h
    )
    one_pass = remote(
        one_other.at[here], one_other.at[here], x_send.at[6], x_recv.at[6], s, mate
    )
    mid_swap = remote(
        mid_give_hbm.at[here], mid_other.at[here], x_send.at[3], x_recv.at[3], pair, h
    )
    mid_pass = remote(
        mid_other.at[here], mid_other.at[here], x_send.at[7], x_recv.at[7], s, mate
    )
    one_swap.start()
    for copy in swaps[:3]:
        copy.start()

    wait(gate_loads)
    gate.combine(True)
    down_loads = load_job(down_hbm, down_other_hbm, og_hbm, og_other_hbm, g_a, x_a, 2, (0, 1, 2, 3))
    wait(up_loads)
    up.give()
    wait(down_loads)
    down.give()
    swaps.append(remote(att, att_other, x_send.at[4], x_recv.at[4], pair, h))
    mid_swap.start()
    swaps[3].start()

    wait(w_loads)
    mine, theirs = (pl.multiple_of(c * half, half) for c in (core, 1 - core))

    def product(i, start):
        at = slice(i * step, (i + 1) * step)
        total = None
        for g, w in ((gq, wq), (gk, wk), (gv, wv)):
            term = dot_nt(g[at, :], w[pl.ds(start, half), :])
            total = term if total is None else total + term
        return total

    for i in range(4):
        core_send[i] = product(i, theirs).astype(BF16)
        head_sum.to_mate(i, core_send.at[i]).start()
    for i in range(4):
        head_sum.chip_sum(i, product(i, mine))
    one_swap.wait_recv()
    one_pass.start()
    one_pass.wait_recv()
    for k in range(3):
        swaps[k].wait_recv()
        attention[k].give()

    def finish(i):
        at = slice(i * step, (i + 1) * step)
        gm_load(i).wait()
        x = x_ref[at, :].astype(F32)
        root = lax.rsqrt(jnp.mean(x * x, axis=-1, keepdims=True) + EPS)
        grad = head_sum.joined(i)
        unit = x * root
        part = jnp.sum(grad * unit, axis=0, keepdims=True)
        gains_out[0:1, :] = part if i == 0 else gains_out[0:1, :] + part
        grad = grad * gain_ref[...]
        total = gm[i % 2] + root * (grad - unit * jnp.mean(grad * unit, axis=-1, keepdims=True))
        tokens_out[at, :] = total.astype(BF16)
        if i < 2:
            gm_load(i + 2).start()

    up.combine()
    for i in range(4):
        head_sum.total(i)
        if i > 0:
            finish(i - 1)
    finish(3)
    gains_out[1:2, :] = mlp_part_ref[...]

    def gain_swap(k, seq):
        return remote(gains_out, gains_got.at[k], gain_send.at[k], gain_recv.at[k], seq, h)

    def gain_step(k, seq):
        gain_swap(k, seq).wait()
        gains_out[...] = gains_out[...] + gains_got[k]

    gain_swap(0, pair).start()
    attention[0].combine()
    attention[1].combine()
    gain_step(0, pair)
    gain_swap(1, near).start()
    down.combine()
    mid_swap.wait_recv()
    mid_pass.start()
    swaps[3].wait_recv()
    mid_pass.wait_recv()
    attention[3].give()
    attention[2].combine()
    gain_step(1, near)
    gain_swap(2, far).start()
    attention[3].combine()
    gate_out[...] = gate.result()
    down_out[...] = down.result()
    up_out[...] = up.result()
    gain_step(2, far)
    for k, out in enumerate((wq_out, wk_out, wv_out, wo_out)):
        out[...] = attention[k].result()
    gate.all_sent(False)
    down.all_sent(True)
    up.all_sent(True)
    for k in range(4):
        attention[k].all_sent(True)
    for copy in (*swaps, one_swap, one_pass, mid_swap, mid_pass):
        copy.wait_send()
    head_sum.all_sent()


def weight_gradients(
    devices, cores, mlp_operands, others, weights, grad_mid, x, gain, mlp_part, attention_operands
):
    rows, width = x.shape
    units = mlp_operands[0].shape[0]
    cols = weights[0].shape[1]
    depth = width // devices
    vmem = pl.BlockSpec(memory_space=pltpu.VMEM)
    hbm = pl.BlockSpec(memory_space=pl.ANY)
    dma = pltpu.SemaphoreType.DMA
    operands = (*mlp_operands, *others, *weights, grad_mid)
    kept = (x, gain, mlp_part, *attention_operands)
    return pl.pallas_call(
        functools.partial(weights_kernel, devices, cores),
        in_specs=[hbm] * len(operands) + [vmem] * len(kept),
        out_specs=[vmem] * 9,
        out_shape=[jax.ShapeDtypeStruct((units, depth), BF16)] * 3
        + [jax.ShapeDtypeStruct((depth, cols), BF16)] * 4
        + [jax.ShapeDtypeStruct((rows, width), BF16), jax.ShapeDtypeStruct((2, width), F32)],
        scratch_shapes=[
            pltpu.VMEM((2, units, rows), BF16),
            pltpu.VMEM((2, units, rows), BF16),
            pltpu.VMEM((2, 4, rows, depth), BF16),
            pltpu.VMEM((2, 4, rows, depth), BF16),
            pltpu.VMEM((2, units, depth), BF16),
            pltpu.VMEM((2, units, depth), BF16),
            pltpu.VMEM((3, 2, units, depth), BF16),
            pltpu.VMEM((3, 2, units, depth), BF16),
            pltpu.VMEM((3, units, depth), BF16),
        ]
        + [pltpu.VMEM((rows, cols), BF16)] * 3
        + [
            pltpu.VMEM((devices // 2, depth, rows), BF16),
            pltpu.VMEM((devices // 2, depth, rows), BF16),
            pltpu.VMEM((rows, cols), BF16),
            pltpu.VMEM((4, 2, depth, cols), BF16),
            pltpu.VMEM((4, 2, depth, cols), BF16),
            pltpu.VMEM((4, 2, depth, cols), BF16),
            pltpu.VMEM((4, depth, cols), BF16),
        ]
        + [pltpu.VMEM((width, cols), BF16)] * 3
        + [pltpu.VMEM((2, rows // 4, width), F32)]
        + [pltpu.VMEM((4, rows // 4, width // 2), BF16)]
        + sum_scratch(rows, width)
        + [pltpu.VMEM((3, 2, width), F32)]
        + [dma((32,)), dma((2,)), dma((8,)), dma((8,)), dma((7, 3)), dma((7, 3))]
        + [dma((12,)), dma((12,)), dma((3,)), dma((3,))],
        compiler_params=pltpu.CompilerParams(
            collective_id=3, has_side_effects=True, vmem_limit_bytes=62 << 20
        ),
        cost_estimate=cost(20 * rows * width * cols, 60 << 20),
        name="weight_gradients",
    )(*operands, *kept)


def on_device(
    tokens,
    gain_attn,
    gain_mlp,
    w_query,
    w_key,
    w_value,
    w_out,
    w_gate,
    w_up,
    w_down,
    prev_keys,
    prev_values,
    lengths,
    out_grad,
):
    rows = tokens.shape[0]
    width = w_query.shape[1]
    devices, cores = lax.axis_size("seq"), lax.axis_size("head")
    index = lax.axis_index("seq")
    bits = jnp.stack([index & 1, lax.axis_index("head") & 1]).astype(jnp.int32)
    gain_one, gain_two = gain_attn[None, :], gain_mlp[None, :]

    (
        keys,
        values,
        queries,
        one_keep,
        one_give,
        mid,
        normed_two,
        two_keep,
        two_give,
        out_keep,
        out_give,
        out_got,
        attended,
        lse,
        lse_row,
        cosine,
        sine,
        low_col,
        low_row,
        valid,
    ) = forward(
        devices,
        cores,
        lengths,
        tokens,
        (gain_one, gain_two),
        out_grad,
        (w_key, w_value, w_query),
        w_out,
        (prev_keys, prev_values),
    )
    order = Order()
    out_keep, out_got = (a.reshape(devices // 2, rows, -1) for a in (out_keep, out_got))
    (
        branch_parts,
        grad_mid,
        gain_mlp_part,
        grad_att,
        delta,
        stat,
        act,
        grad_gate,
        grad_up,
        act_got,
        gate_got,
        two_got,
        mid_keep,
        mid_give,
    ) = middle(
        devices,
        cores,
        normed_two,
        out_grad,
        gain_two,
        valid,
        lse_row,
        (w_gate.T, w_up.T, w_down.T),
        mid,
        w_out,
        attended,
        two_give,
    )
    out_pair = (out_keep, out_got)
    two_pair = (two_keep, two_got)
    order.ran(delta)
    block_out, grad_query_raw, grad_key_raw, grad_value_raw, gate_sums, up_got = attention_back(
        devices,
        cores,
        order.after(grad_att),
        stat,
        (grad_gate, gate_got, *two_pair),
        grad_up,
        branch_parts,
        mid,
        low_col,
        low_row,
        (cosine, sine),
        keys,
        values,
        queries,
        lse,
        delta,
    )
    if devices == 8:
        sums = weight_gradients(
            devices,
            cores,
            (grad_gate, gate_got, grad_up, up_got, act, act_got),
            (*two_pair, *out_pair, gate_sums, mid_give, one_give),
            (w_query, w_key, w_value),
            grad_mid,
            tokens,
            gain_one,
            gain_mlp_part,
            (
                grad_query_raw,
                grad_key_raw,
                grad_value_raw,
                attended,
                one_keep,
                mid_keep,
            ),
        )
        gate_grad, up_grad, down_grad = (a.astype(F32).T for a in sums[:3])
        gains = lax.dynamic_slice_in_dim(sums[8], index * sums[8].shape[1] // devices, sums[8].shape[1] // devices, 1)
        return (
            block_out,
            sums[7],
            gains[0],
            gains[1],
            *(a.astype(F32) for a in sums[3:7]),
            gate_grad,
            up_grad,
            down_grad,
        )
    order.ran(grad_query_raw)
    attended_got = swap(attended, "seq", 1)
    one_pair = (one_keep, swap(one_give, "seq", 1))
    gate = WeightGrad(order, two_pair, grad_gate, gate_got, 1, "gate", True)
    up = WeightGrad(order, two_pair, grad_up, up_got, 1, "up", True)
    down = WeightGrad(order, out_pair, act, act_got, 2, "down", True)
    gate.got = gate_sums
    query_got = swap(grad_query_raw, "seq", 1)
    key_got = swap(grad_key_raw, "seq", 1)
    value_got = swap(grad_value_raw, "seq", 1)
    mid_pair = (mid_keep, swap(order.after(mid_give), "seq", 1))
    gate.keep()
    up.give()
    down.give()
    lefts = (grad_query_raw, grad_key_raw, grad_value_raw)
    rights = (w_query, w_key, w_value)
    give = order.ran(half_product(order.after(bits), lefts, rights, 1, None, "norm_one_give"))
    give = swap(give, "head", 1)
    query = WeightGrad(order, one_pair, grad_query_raw, query_got, 1, "query")
    key = WeightGrad(order, one_pair, grad_key_raw, key_got, 1, "key")
    value = WeightGrad(order, one_pair, grad_value_raw, value_got, 1, "value")
    wout = WeightGrad(order, mid_pair, attended, attended_got, 1, "wout")
    query.give()
    chip = order.ran(half_product(order.after(bits), lefts, rights, 0, give, "norm_one_keep"))
    chip_got = swap(chip, "head", 2)
    key.give()
    value.give()
    up.keep()
    down.keep()
    wout.give()
    own = (chip.astype(F32) + chip_got.astype(F32)).astype(BF16)
    other = swap(own, "head", 1)
    query.keep()
    key.keep()
    tokens_grad, gain_attn_part = by_rows(
        back_kernel,
        order.after(bits),
        (tokens, own, other, gain_one, grad_mid),
        3,
        (BF16, F32),
        "tokens_back",
        part=1,
    )
    order.ran(gain_attn_part)
    value.keep()
    wout.keep()
    gains = gain_sum(jnp.concatenate([gain_attn_part, gain_mlp_part], axis=0))
    gain_attn_grad, gain_mlp_grad = gains[0], gains[1]
    w_gate_grad, w_up_grad, w_down_grad = gate.finish(), up.finish(), down.finish()
    w_out_grad = wout.finish()
    w_query_grad, w_key_grad, w_value_grad = query.finish(), key.finish(), value.finish()
    return (
        block_out,
        tokens_grad,
        gain_attn_grad,
        gain_mlp_grad,
        w_query_grad,
        w_key_grad,
        w_value_grad,
        w_out_grad,
        w_gate_grad,
        w_up_grad,
        w_down_grad,
    )


def solution(mesh):
    by_head = P(None, "head")
    both = P("seq", "head")
    placed = (P("seq", None), P(), P()) + (by_head,) * 9 + (P(), P("seq", None))
    return jax.shard_map(
        on_device,
        mesh=mesh,
        in_specs=placed,
        out_specs=(P("seq", None), P("seq", None), P("seq"), P("seq")) + (both,) * 7,
        check_vma=False,
    )
```

```python
import functools
import math

import jax
import jax.numpy as jnp
from jax import lax
from jax.experimental import pallas as pl
from jax.experimental.pallas import tpu as pltpu
from jax.sharding import PartitionSpec as P

HEAD_DIM = 128
WINDOW = 2048
PAD = 64
NSEQ = 4
EPS = 1e-06
MASKED = -1e30
LOG2E = 1.4426950408889634
BIG = 1 << 28
F32 = jnp.float32
BF16 = jnp.bfloat16


def swap(block, axis, bit):
    return lax.ppermute(block, axis, [(i, i ^ bit) for i in range(lax.axis_size(axis))])


def shifted(block, distance):
    n = lax.axis_size("seq")
    return lax.ppermute(
        block, "seq", [(i, i + distance) for i in range(n) if 0 <= i + distance < n]
    )


BIG_VMEM = pltpu.CompilerParams(vmem_limit_bytes=48 << 20)


def cost(flops, moved):
    return pl.CostEstimate(flops=int(flops), bytes_accessed=int(moved), transcendentals=0)


def dot_nt(left, right):
    return lax.dot_general(left, right, (((1,), (1,)), ((), ())), preferred_element_type=F32)


def row_blocks(width, step):
    return pl.BlockSpec((step, width), lambda i, bits: (i, 0))


def joined(bits_ref, own_ref, other_ref):
    low = bits_ref[1] == 0
    own, other = own_ref[...].astype(F32), other_ref[...].astype(F32)
    return jnp.concatenate([jnp.where(low, own, other), jnp.where(low, other, own)], axis=1)


def back_kernel(
    bits_ref, x_ref, own_ref, other_ref, gain_ref, add_ref, out_ref, part_ref
):
    x = x_ref[...].astype(F32)
    scale = lax.rsqrt(jnp.mean(x * x, axis=-1, keepdims=True) + EPS)
    grad = joined(bits_ref, own_ref, other_ref)
    unit = x * scale
    grad_unit = grad * gain_ref[...]
    total = add_ref[...].astype(F32) + scale * (
        grad_unit - unit * jnp.mean(grad_unit * unit, axis=-1, keepdims=True)
    )
    out_ref[...] = total.astype(out_ref.dtype)
    part = jnp.sum(grad * unit, axis=0, keepdims=True)

    @pl.when(pl.program_id(0) == 0)
    def _():
        part_ref[...] = part

    @pl.when(pl.program_id(0) > 0)
    def _():
        part_ref[...] += part


def by_rows(kernel, bits, arrays, gains_at, outs, name, part=None):
    rows, width = arrays[0].shape
    step = rows // 4
    in_specs = [
        pl.BlockSpec((1, width), lambda i, bits: (0, 0))
        if k == gains_at
        else row_blocks(a.shape[1], step)
        for k, a in enumerate(arrays)
    ]
    out_specs, out_shape = [], []
    for k, dtype in enumerate(outs):
        if k == part:
            out_specs.append(pl.BlockSpec((1, width), lambda i, bits: (0, 0)))
            out_shape.append(jax.ShapeDtypeStruct((1, width), F32))
        else:
            out_specs.append(row_blocks(width, step))
            out_shape.append(jax.ShapeDtypeStruct((rows, width), dtype))
    return pl.pallas_call(
        kernel,
        grid_spec=pltpu.PrefetchScalarGridSpec(
            num_scalar_prefetch=1, grid=(rows // step,), in_specs=in_specs, out_specs=out_specs
        ),
        out_shape=out_shape,
        compiler_params=BIG_VMEM,
        cost_estimate=cost(rows * width * 10, rows * width * 2 * (len(arrays) + len(out_shape))),
        name=name,
    )(bits, *arrays)


def half_kernel(pairs, flip, added, bits_ref, *refs):
    total = refs[2 * pairs][...].astype(F32) if added else None
    for k in range(pairs):
        term = dot_nt(refs[k][...], refs[pairs + k][...])
        total = term if total is None else total + term
    refs[-1][...] = total.astype(BF16)


def half_product(bits, lefts, rights, flip, added, name):
    rows = lefts[0].shape[0]
    width = rights[0].shape[0] // 2
    step = min(width, 512)
    steps = width // step

    def at(i, bits):
        return ((bits[1] ^ flip) * steps + i, 0)

    specs = [pl.BlockSpec(a.shape, lambda i, bits: (0, 0)) for a in lefts]
    specs += [pl.BlockSpec((step, a.shape[1]), at) for a in rights]
    extra = []
    if added is not None:
        extra = [added]
        specs.append(pl.BlockSpec((rows, step), lambda i, bits: (0, i)))
    depth = sum(a.shape[1] for a in lefts)
    return pl.pallas_call(
        functools.partial(half_kernel, len(lefts), flip, added is not None),
        grid_spec=pltpu.PrefetchScalarGridSpec(
            num_scalar_prefetch=1,
            grid=(steps,),
            in_specs=specs,
            out_specs=pl.BlockSpec((rows, step), lambda i, bits: (0, i)),
        ),
        out_shape=jax.ShapeDtypeStruct((rows, width), BF16),
        compiler_params=BIG_VMEM,
        cost_estimate=cost(2 * rows * depth * width, 2 * (rows + width) * depth),
        name=name,
    )(bits, *lefts, *rights, *extra)


def blocks_kernel(order_ref, flip, xa_ref, xb_ref, ga_ref, gb_ref, *refs):
    if flip:
        total = jnp.dot(ga_ref[...], xa_ref[0], preferred_element_type=F32)
        total = total + jnp.dot(gb_ref[...], xb_ref[0], preferred_element_type=F32)
    else:
        total = jnp.dot(xa_ref[0], ga_ref[...], preferred_element_type=F32)
        total = total + jnp.dot(xb_ref[0], gb_ref[...], preferred_element_type=F32)
    if len(refs) == 2:
        total = total + refs[0][0].astype(F32)
    refs[-1][0] = total.astype(BF16)


def grad_blocks(order, x_own, x_got, g_own, g_got, added, flip, name):
    count = order.shape[0]
    if flip:
        _, rows, depth = x_own.shape
        cols = g_own.shape[0]
        shape = (cols, depth)
    else:
        _, depth, rows = x_own.shape
        cols = g_own.shape[1]
        shape = (depth, cols)
    x_spec = pl.BlockSpec((1,) + x_own.shape[1:], lambda i, order: (order[i], 0, 0))
    g_spec = pl.BlockSpec(g_own.shape, lambda i, order: (0, 0))
    out_spec = pl.BlockSpec((1,) + shape, lambda i, order: (i, 0, 0))
    extra = [] if added is None else [added]

    def kernel(order_ref, *refs):
        blocks_kernel(order_ref, flip, *refs)

    return pl.pallas_call(
        kernel,
        grid_spec=pltpu.PrefetchScalarGridSpec(
            num_scalar_prefetch=1,
            grid=(count,),
            in_specs=[x_spec, x_spec, g_spec, g_spec] + [out_spec] * len(extra),
            out_specs=out_spec,
        ),
        out_shape=jax.ShapeDtypeStruct((count,) + shape, BF16),
        compiler_params=BIG_VMEM,
        cost_estimate=cost(
            4 * count * depth * rows * cols, 2 * count * depth * cols + 4 * rows * cols
        ),
        name=name,
    )(order, x_own, x_got, g_own, g_got, *extra)


def shard_orders(first, n):
    bits = [1 << k for k in range(n.bit_length() - 1)]
    return [first] + [b for b in bits if b != first]


class Order:
    def __init__(self):
        self.last = None

    def after(self, operand):
        if self.last is None:
            return operand
        return lax.optimization_barrier((operand, self.last))[0]

    def ran(self, result):
        self.last = result
        return result


class WeightGrad:
    def __init__(self, order, x_pair, g_own, g_got, first, name, flip=False):
        n = lax.axis_size("seq")
        self.order, self.flip, self.name = order, flip, name
        self.operands = (*x_pair, g_own, g_got)
        self.bits = shard_orders(first, n)
        index = lax.axis_index("seq")
        shards = []
        for p in range(n // 2):
            apart = sum(
                b for k, b in enumerate(self.bits[1:]) if (p >> (len(self.bits) - 2 - k)) & 1
            )
            shard = index ^ apart
            shards.append(shard // (2 * first) * first + shard % first)
        self.shards = jnp.stack(shards).astype(jnp.int32)
        self.count = n // 4

    def blocks(self, shards, added, name):
        return self.order.ran(
            grad_blocks(
                self.order.after(shards), *self.operands, added, self.flip, self.name + name
            )
        )

    def give(self):
        give = self.blocks(self.shards[self.count :], None, "_give")
        self.got = swap(give, "seq", self.bits[1])

    def keep(self):
        self.part = self.blocks(self.shards[: self.count], self.got, "_keep")
        left = self.count // 2
        self.got = swap(self.part[left:], "seq", self.bits[2])

    def finish(self):
        left, part = self.count // 2, self.part
        total = part[:left].astype(F32) + self.got.astype(F32)
        for bit in self.bits[3:]:
            left //= 2
            part = total.astype(BF16)
            total = part[:left].astype(F32) + swap(part[left:], "seq", bit).astype(F32)
        return total[0].T if self.flip else total[0]


def gain_sum(part):
    n = lax.axis_size("seq")
    total = part
    bit = 1
    while bit < n:
        total = total + swap(total, "seq", bit)
        bit *= 2
    width = part.shape[-1] // n
    return lax.dynamic_slice_in_dim(total, lax.axis_index("seq") * width, width, total.ndim - 1)


def turned_back(grad, cosine, sine):
    return (grad * cosine - pltpu.roll(grad, HEAD_DIM // 2, 1) * sine).astype(BF16)


def place(devices, cores):
    s, h = lax.axis_index("seq"), lax.axis_index("head")
    odd, core = lax.rem(s, 2), lax.rem(h, 2)
    pair = s + 1 - 2 * odd
    mate = h + 1 - 2 * core
    across = lax.rem(h + cores // 2, cores)
    return s, h, odd, core, pair, mate, across


def remote(src, dst, send, recv, seq, head):
    return pltpu.make_async_remote_copy(
        src_ref=src,
        dst_ref=dst,
        send_sem=send,
        recv_sem=recv,
        device_id=(seq, head),
        device_id_type=pl.DeviceIdType.MESH,
    )


def greet(seq, head):
    pl.semaphore_signal(
        pltpu.get_barrier_semaphore(),
        inc=1,
        device_id=(seq, head),
        device_id_type=pl.DeviceIdType.MESH,
    )


def greet_all(devices, cores):
    s, h, odd, core, pair, mate, across = place(devices, cores)
    greet(pair, h)
    greet(s, mate)
    greet(s, across)

    @pl.when(s >= 2)
    def _():
        greet(s - 2, h)

    @pl.when(s < devices - 2)
    def _():
        greet(s + 2, h)


def all_greeted(devices):
    s = lax.axis_index("seq")
    inner = (s >= 2) & (s < devices - 2)

    @pl.when(inner)
    def _():
        pl.semaphore_wait(pltpu.get_barrier_semaphore(), 5)

    @pl.when(jnp.logical_not(inner))
    def _():
        pl.semaphore_wait(pltpu.get_barrier_semaphore(), 4)


class Chain:
    def __init__(self, devices, buf, send, recv, side):
        self.s, self.h = lax.axis_index("seq"), lax.axis_index("head")
        odd = lax.rem(self.s, 2)
        self.pair = self.s + 1 - 2 * odd
        self.buf, self.send, self.recv = buf, send, recv
        self.next = self.s + 2 * side
        left, right = self.s >= 2, self.s < devices - 2
        self.sends, self.gets = (right, left) if side > 0 else (left, right)
        self.early = odd == (0 if side > 0 else 1)
        self.late = odd == (1 if side > 0 else 0)

    def hop(self, slot, seq, src, dst):
        return remote(
            self.buf.at[src], self.buf.at[dst], self.send.at[slot], self.recv.at[slot], seq, self.h
        )

    def first(self):
        @pl.when(self.sends)
        def _():
            self.hop(0, self.next, 0, 2).start()

        @pl.when(self.early)
        def _():
            self.hop(2, self.pair, 0, 1).start()

    def second(self):
        @pl.when(self.gets)
        def _():
            self.hop(0, self.next, 0, 2).wait_recv()

        @pl.when(self.sends)
        def _():
            self.hop(1, self.next, 2, 4).start()

        @pl.when(self.early)
        def _():
            self.hop(3, self.pair, 2, 3).start()

        @pl.when(self.late)
        def _():
            self.hop(2, self.pair, 2, 1).start()

    def third(self):
        @pl.when(self.gets)
        def _():
            self.hop(1, self.next, 2, 4).wait_recv()

        @pl.when(self.late)
        def _():
            self.hop(3, self.pair, 4, 3).start()

    def arrived(self, slot):
        self.hop(slot, self.pair, 0, 1 if slot == 2 else 3).wait_recv()

    def all_sent(self):
        @pl.when(self.sends)
        def _():
            self.hop(0, self.next, 0, 2).wait_send()
            self.hop(1, self.next, 2, 4).wait_send()

        self.hop(2, self.pair, 0, 1).wait_send()
        self.hop(3, self.pair, 0, 3).wait_send()


def differing(s, bit):
    return s + bit - 2 * bit * lax.rem(s // bit, 2)


class Give:
    def __init__(self, devices, first, operands, bufs, send, recv):
        self.s, self.h = lax.axis_index("seq"), lax.axis_index("head")
        g_own, g_got, x_own, x_got = operands
        self.g, self.x, self.slot, self.got, sem = bufs
        self.send, self.recv = send, recv
        bits = shard_orders(first, devices)
        self.partner = differing(self.s, bits[1])
        self.count = devices // 4
        self.loads = [
            pltpu.make_async_copy(g_own, self.g.at[0], sem.at[0]),
            pltpu.make_async_copy(g_got, self.g.at[1], sem.at[1]),
        ]
        for j in range(self.count):
            shard = self.s
            for k, b in enumerate(bits[1:]):
                if ((j + self.count) >> (len(bits) - 2 - k)) & 1:
                    shard = differing(shard, b)
            at = shard // (2 * first) * first + lax.rem(shard, first)
            for k, x in enumerate((x_own, x_got)):
                self.loads.append(
                    pltpu.make_async_copy(x.at[at], self.x.at[k, j], sem.at[2 + 2 * j + k])
                )

    def load(self):
        for copy in self.loads:
            copy.start()

    def loaded(self):
        for copy in self.loads:
            copy.wait()

    def make(self, j):
        total = jnp.dot(self.g[0], self.x[0, j], preferred_element_type=F32)
        total = total + jnp.dot(self.g[1], self.x[1, j], preferred_element_type=F32)
        self.slot[j] = total.astype(BF16)

    def half(self, j, k):
        step = self.slot.shape[1] // 2
        at = pl.ds(k * step, step)
        return remote(
            self.slot.at[j, at, :],
            self.got.at[j, at, :],
            self.send.at[2 * j + k],
            self.recv.at[2 * j + k],
            self.partner,
            self.h,
        )

    def finish(self):
        for j in range(self.count):
            for k in range(2):
                self.half(j, k).wait()


class HeadSum:
    def __init__(self, devices, cores, core_got, chip, y_got, own, other, send, recv):
        self.s, self.h, _, self.core, _, self.mate, self.across = place(devices, cores)
        self.core_got, self.chip, self.y_got = core_got, chip, y_got
        self.own, self.other, self.send, self.recv = own, other, send, recv

    def to_mate(self, i, src=None):
        return remote(
            self.chip.at[i] if src is None else src,
            self.core_got.at[i],
            self.send.at[i],
            self.recv.at[i],
            self.s,
            self.mate,
        )

    def over(self, i):
        return remote(
            self.chip.at[i],
            self.y_got.at[i],
            self.send.at[4 + i],
            self.recv.at[4 + i],
            self.s,
            self.across,
        )

    def back(self, i):
        return remote(
            self.own.at[i],
            self.other.at[i],
            self.send.at[8 + i],
            self.recv.at[8 + i],
            self.s,
            self.mate,
        )

    def chip_sum(self, i, part):
        self.to_mate(i).wait_recv()
        self.chip[i] = (part + self.core_got[i].astype(F32)).astype(BF16)
        self.over(i).start()

    def total(self, i):
        self.over(i).wait_recv()
        self.own[i] = (self.chip[i].astype(F32) + self.y_got[i].astype(F32)).astype(BF16)
        self.back(i).start()

    def joined(self, i):
        self.back(i).wait_recv()
        own, other = self.own[i].astype(F32), self.other[i].astype(F32)
        low = self.core == 0
        return jnp.concatenate([jnp.where(low, own, other), jnp.where(low, other, own)], axis=1)

    def all_sent(self):
        for i in range(4):
            self.to_mate(i).wait_send()
            self.over(i).wait_send()
            self.back(i).wait_send()


def forward_kernel(
    devices,
    cores,
    lengths_ref,
    x_ref,
    gain_one_ref,
    gain_two_ref,
    og_hbm,
    wk_hbm,
    wv_hbm,
    wq_hbm,
    wo_hbm,
    prev_k_hbm,
    prev_v_hbm,
    k_out,
    v_out,
    q_out,
    one_keep_out,
    one_give_out,
    mid_out,
    two_out,
    two_keep_out,
    two_give_out,
    og_keep_out,
    og_give_out,
    og_got_out,
    att_out,
    lse_out,
    row_out,
    cos_ref,
    sin_ref,
    lo_ref,
    lo_row_ref,
    valid_ref,
    kx,
    vx,
    qx,
    wk,
    wv,
    wq,
    wo,
    normed,
    flipped,
    tops,
    totals,
    acc,
    core_send,
    core_got,
    chip,
    y_got,
    own_half,
    other_half,
    mid,
    two_blocks,
    og,
    load_sem,
    store_sem,
    k_send,
    k_recv,
    v_send,
    v_recv,
    q_send,
    q_recv,
    sum_send,
    sum_recv,
    two_send,
    two_recv,
):
    rows, width = x_ref.shape
    heads = kx.shape[2] // HEAD_DIM
    s, h, odd, core, pair, mate, across = place(devices, cores)
    has_left, has_right = s >= 2, s < devices - 2
    scale = HEAD_DIM ** (-0.5) * LOG2E
    k_chain = Chain(devices, kx, k_send, k_recv, 1)
    v_chain = Chain(devices, vx, v_send, v_recv, 1)
    chains = [v_chain, k_chain]
    q_chain = Chain(devices, qx, q_send, q_recv, -1)
    head_sum = HeadSum(
        devices, cores, core_got, chip, y_got, own_half, other_half, sum_send, sum_recv
    )

    loads = [
        pltpu.make_async_copy(src, dst, load_sem.at[i])
        for i, (src, dst) in enumerate(
            ((wk_hbm, wk), (wv_hbm, wv), (wq_hbm, wq), (wo_hbm, wo), (og_hbm, og))
        )
    ]
    for load in loads:
        load.start()

    greet_all(devices, cores)
    step = rows // 4

    def normalize(i, _):
        at = pl.ds(pl.multiple_of(i * step, step), step)
        x = x_ref[at, :].astype(F32)
        root = lax.rsqrt(jnp.mean(x * x, axis=-1, keepdims=True) + EPS)
        normed[at, :] = (x * root * gain_one_ref[...]).astype(BF16)
        return 0

    lax.fori_loop(0, 4, normalize, 0)

    starts, padded = [0], 0
    for r in range(NSEQ - 1):
        padded = padded + (lengths_ref[r] + PAD - 1) // PAD * PAD
        starts.append(padded)

    def sequence_of(at):
        start = jnp.zeros_like(at)
        low = jnp.full_like(at, -BIG)
        length = jnp.zeros_like(at) + lengths_ref[0]
        for r in range(1, NSEQ):
            inside = at >= starts[r]
            start = jnp.where(inside, starts[r], start)
            low = jnp.where(inside, starts[r], low)
            length = jnp.where(inside, lengths_ref[r], length)
        valid = at - start < length
        low = jnp.where(valid, jnp.maximum(low, at - (WINDOW - 1)), at)
        return at - start, valid, jnp.where(at < devices * rows, low, BIG) - s * rows

    def turn_into(weight, out):
        raw = jnp.dot(normed[...], weight[...], preferred_element_type=F32)
        for k in range(heads):
            u = raw[:, k * HEAD_DIM : (k + 1) * HEAD_DIM]
            u = u * cos_ref[...] + pltpu.roll(u, HEAD_DIM // 2, 1) * sin_ref[...]
            out[0, :, k * HEAD_DIM : (k + 1) * HEAD_DIM] = u.astype(BF16)

    loads[1].wait()
    vx[0] = jnp.dot(normed[...], wv[...], preferred_element_type=F32).astype(BF16)
    all_greeted(devices)
    v_chain.first()
    at = lax.broadcasted_iota(jnp.int32, (rows, HEAD_DIM), 0) + s * rows
    position, valid, low = sequence_of(at)
    valid_ref[...] = valid[:, 0:1].astype(jnp.int32)
    lo_ref[...] = low[:, 0:1]
    lane = lax.broadcasted_iota(jnp.int32, (1, HEAD_DIM), 1)
    half_dim = HEAD_DIM // 2
    pair_of = lax.rem(lane, half_dim).astype(F32)
    freq = jnp.exp(-math.log(10000.0) * (2.0 * pair_of / HEAD_DIM))
    angle = position.astype(F32) * freq
    cos_ref[...] = jnp.cos(angle)
    sin_ref[...] = jnp.sin(angle) * jnp.where(lane < half_dim, -1.0, 1.0)
    lo_row_ref[...] = sequence_of(lax.broadcasted_iota(jnp.int32, lo_row_ref.shape, 1) + s * rows)[2]
    loads[0].wait()
    turn_into(wk, kx)
    k_chain.first()

    @pl.when(jnp.logical_not(has_left))
    def _():
        copies = []
        for i, (src, dst) in enumerate(((prev_k_hbm, kx), (prev_v_hbm, vx))):
            for j, d in enumerate((2, 4)):
                at = pl.multiple_of((s - d) * rows + WINDOW, rows)
                copies.append(
                    pltpu.make_async_copy(
                        src.at[pl.ds(at, rows), :], dst.at[d], load_sem.at[5 + 2 * i + j]
                    )
                )
        for copy in copies:
            copy.start()
        for copy in copies:
            copy.wait()

    @pl.when(jnp.logical_not(has_right))
    def _():
        qx[2] = jnp.zeros_like(qx[2])
        qx[4] = jnp.zeros_like(qx[4])

    loads[2].wait()
    turn_into(wq, qx)
    q_chain.first()

    for i in range(4):
        flip_at = slice(i * step, (i + 1) * step)
        flipped[:, :, flip_at] = normed[flip_at, :].T.reshape(devices, width // devices, step)
    turned = flipped.reshape(devices // 2, 2, width // devices, rows)
    stores = [
        pltpu.make_async_copy(turned.at[:, odd], one_keep_out, store_sem.at[0]),
        pltpu.make_async_copy(turned.at[:, 1 - odd], one_give_out, store_sem.at[1]),
    ]
    stores[0].start()
    stores[1].start()

    depth = width // devices
    loads[4].wait()
    for j in range(devices):
        two_blocks[j] = og[:, j * depth : (j + 1) * depth]
    near = lax.rem(s // 2, 2)
    split = two_blocks.reshape(devices // 4, 2, 2, rows, depth)
    og_stores = [
        pltpu.make_async_copy(split.at[:, near], og_keep_out, store_sem.at[4]),
        pltpu.make_async_copy(split.at[:, 1 - near], og_give_out, store_sem.at[5]),
    ]
    og_stores[0].start()
    og_stores[1].start()
    sub = rows // 2

    def attend(d, only=None):
        def body(i, _):
            if only is None:
                k, part = i // 2, lax.rem(i, 2)
            else:
                k, part = i, only
            at = pl.ds(pl.multiple_of(part * sub, sub), sub)
            lanes = pl.ds(pl.multiple_of(k * HEAD_DIM, HEAD_DIM), HEAD_DIM)
            scores = dot_nt(qx[0, at, lanes], kx[d, :, lanes])
            u = lax.broadcasted_iota(jnp.int32, scores.shape, 1) - d * rows
            seen = u >= lo_ref[at, :]
            if d == 0:
                t = lax.broadcasted_iota(jnp.int32, scores.shape, 0) + part * sub
                seen = seen & (u <= t)
            scores = jnp.where(seen, scores * scale, MASKED)
            top = jnp.max(scores, axis=1, keepdims=True)
            if d > 0:
                old = tops[k, at, :]
                top = jnp.maximum(top, old)
            p = jnp.exp2(scores - top)
            total = jnp.sum(p, axis=1, keepdims=True)
            mixed = jnp.dot(p.astype(BF16), vx[d, :, lanes], preferred_element_type=F32)
            if d > 0:
                fade = jnp.exp2(old - top)
                total = total + totals[k, at, :] * fade
                mixed = mixed + acc[at, lanes] * fade
            tops[k, at, :] = top
            totals[k, at, :] = total
            acc[at, lanes] = mixed
            return 0

        lax.fori_loop(0, 2 * heads if only is None else heads, body, 0)

    attend(0)
    for chain in chains:
        chain.second()
    attend(2)
    for chain in chains:
        chain.arrived(2)
    attend(1)
    for chain in chains:
        chain.third()
    attend(4)
    q_chain.second()
    for chain in chains:
        chain.arrived(3)
    stores.append(pltpu.make_async_copy(kx, k_out, store_sem.at[2]))
    stores.append(pltpu.make_async_copy(vx, v_out, store_sem.at[3]))
    stores[2].start()
    stores[3].start()

    og_stores[0].wait()
    og_stores[1].wait()
    blocks = two_blocks.reshape(devices // 2, 2, rows, depth)

    half = width // 2
    loads[3].wait()
    mine = pl.ds(pl.multiple_of(core * half, half), half)
    theirs = pl.ds(pl.multiple_of((1 - core) * half, half), half)

    for t in range(2):
        attend(3, t)
        at = slice(t * sub, (t + 1) * sub)
        for k in range(heads):
            columns = slice(k * HEAD_DIM, (k + 1) * HEAD_DIM)
            out = jnp.where(valid_ref[at, :] > 0, acc[at, columns] / totals[k, at, :], 0.0)
            att_out[at, columns] = out.astype(BF16)
        total = dot_nt(att_out[at, :], wo[theirs, :]).astype(BF16)
        for j in range(2):
            core_send[2 * t + j] = total[j * step : (j + 1) * step, :]
            head_sum.to_mate(2 * t + j, core_send.at[2 * t + j]).start()
        total = dot_nt(att_out[at, :], wo[mine, :])
        for j in range(2):
            head_sum.chip_sum(2 * t + j, total[j * step : (j + 1) * step, :])
    for k in range(heads):
        lse = tops[k] + jnp.log2(totals[k])
        lse_out[k] = lse
        row_out[k] = jnp.broadcast_to(lse, (rows, HEAD_DIM)).T[0:1, :]
    og_here = pl.ds(core * (devices // 8), devices // 8)
    og_swap = remote(
        og_give_out.at[og_here],
        og_got_out.at[og_here],
        two_send.at[8],
        two_recv.at[8],
        differing(s, 2),
        h,
    )
    og_pass = remote(
        og_got_out.at[og_here], og_got_out.at[og_here], two_send.at[9], two_recv.at[9], s, mate
    )
    og_swap.start()

    q_chain.third()

    def finish(i):
        at = slice(i * step, (i + 1) * step)
        total = x_ref[at, :].astype(F32) + head_sum.joined(i)
        mid[at, :] = total
        root = lax.rsqrt(jnp.mean(total * total, axis=-1, keepdims=True) + EPS)
        two = (total * root * gain_two_ref[...]).astype(BF16)
        normed[at, :] = two
        for j in range(devices):
            two_blocks[j, at, :] = two[:, j * depth : (j + 1) * depth]

    for i in range(4):
        head_sum.total(i)
        if i > 0:
            finish(i - 1)
    finish(3)
    for src, dst in (
        (mid, mid_out),
        (normed, two_out),
        (blocks.at[:, odd], two_keep_out),
        (blocks.at[:, 1 - odd], two_give_out),
    ):
        stores.append(pltpu.make_async_copy(src, dst, store_sem.at[2 + len(stores)]))
        stores[-1].start()
    q_chain.arrived(2)
    q_chain.arrived(3)
    stores.append(pltpu.make_async_copy(qx, q_out, store_sem.at[2 + len(stores)]))
    stores[-1].start()
    og_swap.wait_recv()
    og_pass.start()
    og_swap.wait_send()
    og_pass.wait()
    for chain in (*chains, q_chain):
        chain.all_sent()
    head_sum.all_sent()
    for store in stores:
        store.wait()


def forward(devices, cores, lengths, x, gains, grad, weights, w_out, prevs):
    rows, width = x.shape
    cols = weights[0].shape[1]
    heads = cols // HEAD_DIM
    depth = width // devices
    parts = WINDOW // rows + 1
    step = rows // 4
    vmem = pl.BlockSpec(memory_space=pltpu.VMEM)
    hbm = pl.BlockSpec(memory_space=pl.ANY)

    def shape(*dims, dtype=BF16):
        return jax.ShapeDtypeStruct(dims, dtype)

    blocks = pltpu.VMEM((4, step, width // 2), BF16)
    dma = pltpu.SemaphoreType.DMA
    return pl.pallas_call(
        functools.partial(forward_kernel, devices, cores),
        in_specs=[pl.BlockSpec(memory_space=pltpu.SMEM)] + [vmem] * 3 + [hbm] * 7,
        out_specs=[hbm] * 12 + [vmem] * 8,
        out_shape=[
            shape(parts, rows, cols),
            shape(parts, rows, cols),
            shape(parts, rows, cols),
            shape(devices // 2, depth, rows),
            shape(devices // 2, depth, rows),
            shape(rows, width, dtype=F32),
            shape(rows, width),
            shape(devices // 2, rows, depth),
            shape(devices // 2, rows, depth),
            shape(devices // 4, 2, rows, depth),
            shape(devices // 4, 2, rows, depth),
            shape(devices // 4, 2, rows, depth),
            shape(rows, cols),
            shape(heads, rows, 1, dtype=F32),
            shape(heads, 1, rows, dtype=F32),
            shape(rows, HEAD_DIM, dtype=F32),
            shape(rows, HEAD_DIM, dtype=F32),
            shape(rows, 1, dtype=jnp.int32),
            shape(1, parts * rows, dtype=jnp.int32),
            shape(rows, 1, dtype=jnp.int32),
        ],
        scratch_shapes=[pltpu.VMEM((parts, rows, cols), BF16)] * 3
        + [pltpu.VMEM((width, cols), BF16)] * 4
        + [
            pltpu.VMEM((rows, width), BF16),
            pltpu.VMEM((devices, depth, rows), BF16),
            pltpu.VMEM((heads, rows, 1), F32),
            pltpu.VMEM((heads, rows, 1), F32),
            pltpu.VMEM((rows, cols), F32),
        ]
        + [blocks] * 6
        + [
            pltpu.VMEM((rows, width), F32),
            pltpu.VMEM((devices, rows, depth), BF16),
            pltpu.VMEM((rows, width), BF16),
            dma((9,)),
            dma((12,)),
        ]
        + [dma((4,))] * 6
        + [dma((12,))] * 2
        + [dma((10,))] * 2,
        compiler_params=pltpu.CompilerParams(
            collective_id=0, has_side_effects=True, vmem_limit_bytes=56 << 20
        ),
        cost_estimate=cost(10 * rows * width * cols, 40 << 20),
        name="forward",
    )(lengths, x, *gains, grad, *weights, w_out, *prevs)


def pieces_of(extent, step):
    return [(start, min(step, extent - start)) for start in range(0, extent, step)]


def middle_kernel(
    devices,
    cores,
    two_ref,
    og_ref,
    gain_ref,
    valid_ref,
    lse_row_ref,
    wg_hbm,
    wu_hbm,
    wd_hbm,
    mid_hbm,
    wo_hbm,
    att_hbm,
    two_give_hbm,
    branch_out,
    gm_out,
    part_out,
    do_out,
    delta_out,
    stat_out,
    act_out,
    gg_out,
    gu_out,
    act_got,
    gg_got,
    two_got,
    keep_out,
    give_out,
    wg,
    wu,
    wd,
    act_t,
    gg_t,
    gu_t,
    act,
    gg,
    gu,
    mid,
    wo,
    att,
    core_send,
    core_got,
    chip,
    y_got,
    own_half,
    other_half,
    flipped,
    load_sem,
    store_sem,
    far_send,
    far_recv,
    sum_send,
    sum_recv,
):
    rows, width = mid.shape
    units = wg.shape[0]
    heads = att.shape[1] // HEAD_DIM
    step = rows // 4
    half = width // 2
    s, h, odd, core, pair, mate, across = place(devices, cores)
    near = differing(s, 2)
    head_sum = HeadSum(
        devices, cores, core_got, chip, y_got, own_half, other_half, sum_send, sum_recv
    )
    greet(pair, h)
    greet(near, h)
    greet(s, mate)
    greet(s, across)
    pieces = pieces_of(units, 3 * HEAD_DIM)
    loads = []
    for c, (start, size) in enumerate(pieces):
        at = pl.ds(start, size)
        loads.append(
            [
                pltpu.make_async_copy(src.at[at, :], dst.at[at, :], load_sem.at[3 * c + k])
                for k, (src, dst) in enumerate(((wg_hbm, wg), (wu_hbm, wu), (wd_hbm, wd)))
            ]
        )
        for copy in loads[-1]:
            copy.start()
    first = 3 * len(pieces)
    later = [
        pltpu.make_async_copy(src, dst, load_sem.at[first + k])
        for k, (src, dst) in enumerate(((mid_hbm, mid), (wo_hbm, wo), (att_hbm, att)))
    ]
    for copy in later:
        copy.start()
    pl.semaphore_wait(pltpu.get_barrier_semaphore(), 4)

    share = devices // 4
    here = pl.ds(core * share, share)
    two_swap = remote(
        two_give_hbm.at[here], two_got.at[here], far_send.at[4], far_recv.at[4], pair, h
    )
    two_pass = remote(
        two_got.at[here], two_got.at[here], far_send.at[5], far_recv.at[5], s, mate
    )
    two_swap.start()
    mine, theirs = (pl.ds(pl.multiple_of(c * half, half), half) for c in (core, 1 - core))
    swaps = []

    def product(tokens, columns):
        total = jnp.dot(gg[tokens, :], wg[:, columns], preferred_element_type=F32)
        return total + jnp.dot(gu[tokens, :], wu[:, columns], preferred_element_type=F32)

    for t in range(2):
        tokens = slice(2 * t * step, 2 * (t + 1) * step)
        for c, (start, size) in enumerate(pieces):
            at = slice(start, start + size)
            if t == 0:
                for copy in loads[c]:
                    copy.wait()
            gate = dot_nt(wg[at, :], two_ref[tokens, :])
            up = dot_nt(wu[at, :], two_ref[tokens, :])
            grad = dot_nt(wd[at, :], og_ref[tokens, :])
            sig = 1.0 / (1.0 + jnp.exp(-gate))
            silu = gate * sig
            value = (silu * up).astype(BF16)
            grad_gate = (grad * up * sig * (1.0 + gate * (1.0 - sig))).astype(BF16)
            grad_up = (grad * silu).astype(BF16)
            act_t[at, tokens] = value
            gg_t[at, tokens] = grad_gate
            gu_t[at, tokens] = grad_up
            act[tokens, at] = value.T
            gg[tokens, at] = grad_gate.T
            gu[tokens, at] = grad_up.T
        part = pl.ds(2 * t * step, 2 * step)
        for k, (src, dst, seq) in enumerate(((gg_t, gg_got, pair), (act_t, act_got, near))):
            i = 2 * t + k
            swaps.append(
                remote(src.at[:, part], dst.at[:, part], far_send.at[i], far_recv.at[i], seq, h)
            )
            swaps[-1].start()
        total = product(tokens, theirs).astype(BF16)
        for j in range(2):
            core_send[2 * t + j] = total[j * step : (j + 1) * step, :]
            head_sum.to_mate(2 * t + j, core_send.at[2 * t + j]).start()
        total = product(tokens, mine)
        for j in range(2):
            head_sum.chip_sum(2 * t + j, total[j * step : (j + 1) * step, :])
    stores = [
        pltpu.make_async_copy(src, dst, store_sem.at[k])
        for k, (src, dst) in enumerate(((act_t, act_out), (gg_t, gg_out), (gu_t, gu_out)))
    ]
    for store in stores:
        store.start()

    for k, columns in enumerate((theirs, mine)):
        branch_out[k] = jnp.dot(act[...], wd[:, columns], preferred_element_type=F32).astype(BF16)
    for copy in later:
        copy.wait()
    two_swap.wait_recv()
    two_pass.start()

    def finish(i):
        at = slice(i * step, (i + 1) * step)
        x = mid[at, :]
        root = lax.rsqrt(jnp.mean(x * x, axis=-1, keepdims=True) + EPS)
        grad = head_sum.joined(i)
        unit = x * root
        part = jnp.sum(grad * unit, axis=0, keepdims=True)
        part_out[...] = part if i == 0 else part_out[...] + part
        grad = grad * gain_ref[...]
        total = og_ref[at, :].astype(F32) + root * (
            grad - unit * jnp.mean(grad * unit, axis=-1, keepdims=True)
        )
        gm_out[at, :] = total
        low = total.astype(BF16)
        flipped[:, :, at] = low.T.reshape(devices, width // devices, step)
        do = jnp.dot(low, wo[...], preferred_element_type=F32).astype(BF16).astype(F32)
        do = jnp.where(valid_ref[at, :] > 0, do, 0.0)
        do_out[at, :] = do.astype(BF16)
        product = do * att[at, :].astype(F32)
        for k in range(heads):
            delta = jnp.sum(product[:, k * HEAD_DIM : (k + 1) * HEAD_DIM], axis=1, keepdims=True)
            delta_out[k, at, :] = delta
            stat_out[k, 0:1, at] = lse_row_ref[k, :, at]
            stat_out[k, 1:2, at] = jnp.broadcast_to(delta, (step, HEAD_DIM)).T[0:1, :]

    for i in range(4):
        head_sum.total(i)
        if i > 0:
            finish(i - 1)
    finish(3)
    split = flipped.reshape(devices // 2, 2, width // devices, rows)
    stores += [
        pltpu.make_async_copy(split.at[:, odd], keep_out, store_sem.at[3]),
        pltpu.make_async_copy(split.at[:, 1 - odd], give_out, store_sem.at[4]),
    ]
    stores[3].start()
    stores[4].start()
    for copy in swaps:
        copy.wait()
    two_swap.wait_send()
    two_pass.wait()
    head_sum.all_sent()
    for store in stores:
        store.wait()


def sum_scratch(rows, width):
    return [pltpu.VMEM((4, rows // 4, width // 2), BF16)] * 5


def middle(
    devices, cores, two, grad, gain, valid, lse_row, weights, mid, w_out, attended, two_give
):
    rows, width = mid.shape
    units = weights[0].shape[0]
    cols = attended.shape[1]
    heads = cols // HEAD_DIM
    depth = width // devices
    count = len(pieces_of(units, 3 * HEAD_DIM))
    vmem = pl.BlockSpec(memory_space=pltpu.VMEM)
    hbm = pl.BlockSpec(memory_space=pl.ANY)
    dma = pltpu.SemaphoreType.DMA

    def shape(*dims, dtype=BF16):
        return jax.ShapeDtypeStruct(dims, dtype)

    return pl.pallas_call(
        functools.partial(middle_kernel, devices, cores),
        in_specs=[vmem] * 5 + [hbm] * 7,
        out_specs=[vmem] * 6 + [hbm] * 8,
        out_shape=[
            shape(2, rows, width // 2),
            shape(rows, width, dtype=F32),
            shape(1, width, dtype=F32),
            shape(rows, cols),
            shape(heads, rows, 1, dtype=F32),
            shape(heads, 2, rows, dtype=F32),
        ]
        + [shape(units, rows)] * 5
        + [shape(devices // 2, rows, depth)]
        + [shape(devices // 2, depth, rows)] * 2,
        scratch_shapes=[pltpu.VMEM((units, width), BF16)] * 3
        + [pltpu.VMEM((units, rows), BF16)] * 3
        + [pltpu.VMEM((rows, units), BF16)] * 3
        + [
            pltpu.VMEM((rows, width), F32),
            pltpu.VMEM((width, cols), BF16),
            pltpu.VMEM((rows, cols), BF16),
            pltpu.VMEM((4, rows // 4, width // 2), BF16),
        ]
        + sum_scratch(rows, width)
        + [
            pltpu.VMEM((devices, depth, rows), BF16),
            dma((3 * count + 3,)),
            dma((5,)),
            dma((6,)),
            dma((6,)),
            dma((12,)),
            dma((12,)),
        ],
        compiler_params=pltpu.CompilerParams(
            collective_id=1, has_side_effects=True, vmem_limit_bytes=62 << 20
        ),
        cost_estimate=cost(12 * rows * width * units, 60 << 20),
        name="middle",
    )(two, grad, gain, valid, lse_row, *weights, mid, w_out, attended, two_give)


def attention_back_kernel(
    devices,
    cores,
    do_hbm,
    stat_hbm,
    gg_hbm,
    gg_got_hbm,
    two_hbm,
    two_got_hbm,
    gu_hbm,
    parts_hbm,
    mid_hbm,
    kx_hbm,
    vx_hbm,
    qx_hbm,
    lo_ref,
    lo_row_ref,
    cos_ref,
    sin_ref,
    lse_ref,
    delta_ref,
    block_out,
    gq_out,
    gk_out,
    gv_out,
    gate_got,
    gu_got,
    kx,
    vx,
    qx,
    mid_ref,
    parts_ref,
    dx,
    sx,
    dk_acc,
    dv_acc,
    core_got,
    chip,
    y_got,
    own_half,
    other_half,
    gate_g,
    gate_x,
    gate_slot,
    gate_sem,
    gate_send,
    gate_recv,
    up_send,
    up_recv,
    load_sem,
    d_send,
    d_recv,
    s_send,
    s_recv,
    sum_send,
    sum_recv,
):
    parts, rows, cols = kx.shape
    heads = cols // HEAD_DIM
    step = rows // 4
    sub = rows // 2
    s, h, odd, core, pair, mate, across = place(devices, cores)
    scale = HEAD_DIM ** (-0.5) * LOG2E
    d_chain = Chain(devices, dx, d_send, d_recv, -1)
    s_chain = Chain(devices, sx, s_send, s_recv, -1)
    head_sum = HeadSum(
        devices, cores, core_got, chip, y_got, own_half, other_half, sum_send, sum_recv
    )
    gate = Give(
        devices,
        1,
        (gg_hbm, gg_got_hbm, two_hbm, two_got_hbm),
        (gate_g, gate_x, gate_slot, gate_got, gate_sem),
        gate_send,
        gate_recv,
    )
    greet_all(devices, cores)
    loads = [
        pltpu.make_async_copy(do_hbm, dx.at[0], load_sem.at[0]),
        pltpu.make_async_copy(stat_hbm, sx.at[0], load_sem.at[1]),
    ]
    loads += [
        pltpu.make_async_copy(src, dst, load_sem.at[2 + i])
        for i, (src, dst) in enumerate(
            ((qx_hbm, qx), (kx_hbm, kx), (vx_hbm, vx), (parts_hbm, parts_ref), (mid_hbm, mid_ref))
        )
    ]
    loads[0].start()
    loads[1].start()
    gate.load()
    for copy in loads[2:]:
        copy.start()

    @pl.when(s >= devices - 2)
    def _():
        for d in (2, 4):
            dx[d] = jnp.zeros_like(dx[d])
            sx[d] = jnp.zeros_like(sx[d])

    loads[0].wait()
    loads[1].wait()
    all_greeted(devices)
    d_chain.first()
    s_chain.first()
    for i in range(4):
        head_sum.to_mate(i, parts_hbm.at[0, pl.ds(i * step, step), :]).start()

    def queries_back(start, count):
        def body(i, _):
            k = start + i // 2
            at = pl.ds(pl.multiple_of((i % 2) * sub, sub), sub)
            lanes = pl.ds(pl.multiple_of(k * HEAD_DIM, HEAD_DIM), HEAD_DIM)
            q, do, lo = qx[0, at, lanes], dx[0, at, lanes], lo_ref[at, :]
            lse, delta = lse_ref[k, at, :], delta_ref[k, at, :]
            total = jnp.zeros((sub, HEAD_DIM), F32)
            for d in range(parts):
                key = kx[d, :, lanes]
                scores = dot_nt(q, key)
                u = lax.broadcasted_iota(jnp.int32, scores.shape, 1) - d * rows
                seen = u >= lo
                if d == 0:
                    t = lax.broadcasted_iota(jnp.int32, scores.shape, 0) + (i % 2) * sub
                    seen = seen & (u <= t)
                p = jnp.exp2(jnp.where(seen, scores * scale, MASKED) - lse)
                ds = (p * (dot_nt(do, vx[d, :, lanes]) - delta)).astype(BF16)
                total = total + jnp.dot(ds, key, preferred_element_type=F32)
            gq_out[at, lanes] = turned_back(
                total * HEAD_DIM ** (-0.5), cos_ref[at, :], sin_ref[at, :]
            )
            return 0

        lax.fori_loop(0, 2 * count, body, 0)

    def keys_back(d):
        def body(i, _):
            k = i // 2
            at = pl.ds(pl.multiple_of((i % 2) * sub, sub), sub)
            lanes = pl.ds(pl.multiple_of(k * HEAD_DIM, HEAD_DIM), HEAD_DIM)
            key, value = kx[0, at, lanes], vx[0, at, lanes]
            q, do = qx[d, :, lanes], dx[d, :, lanes]
            scores = dot_nt(key, q)
            u = lax.broadcasted_iota(jnp.int32, scores.shape, 0) + (i % 2) * sub
            seen = u >= lo_row_ref[:, d * rows : (d + 1) * rows]
            if d == 0:
                seen = seen & (u <= lax.broadcasted_iota(jnp.int32, scores.shape, 1))
            lse, delta = sx[d, k, 0:1, :], sx[d, k, 1:2, :]
            p = jnp.exp2(jnp.where(seen, scores * scale - lse, MASKED))
            dv = jnp.dot(p.astype(BF16), do, preferred_element_type=F32)
            ds = (p * (dot_nt(value, do) - delta)).astype(BF16)
            dk = jnp.dot(ds, q, preferred_element_type=F32)
            if d > 0:
                dv = dv + dv_acc[at, lanes]
                dk = dk + dk_acc[at, lanes]
            dv_acc[at, lanes] = dv
            dk_acc[at, lanes] = dk
            return 0

        lax.fori_loop(0, 2 * heads, body, 0)

    ups = [
        remote(
            gu_hbm.at[pl.ds(start, size), :],
            gu_got.at[pl.ds(start, size), :],
            up_send.at[i],
            up_recv.at[i],
            pair,
            h,
        )
        for i, (start, size) in enumerate(pieces_of(gu_hbm.shape[0], 3 * HEAD_DIM))
    ]
    ups[0].start()
    ups[1].start()
    gate.loaded()
    gate.make(0)
    gate.half(0, 0).start()
    for copy in loads[2:6]:
        copy.wait()
    queries_back(0, heads // 4)
    for i in range(4):
        head_sum.chip_sum(i, parts_ref[1, i * step : (i + 1) * step, :].astype(F32))
    s_chain.second()
    d_chain.second()
    ups[2].start()
    gate.half(0, 1).start()
    for j in range(1, gate.count):
        gate.make(j)
        gate.half(j, 0).start()
        gate.half(j, 1).start()
    queries_back(heads // 4, heads // 2)
    keys_back(0)
    keys_back(2)
    s_chain.third()
    d_chain.third()
    for copy in ups[3:]:
        copy.start()
    queries_back(heads // 4 + heads // 2, heads - heads // 4 - heads // 2)
    for i in range(4):
        head_sum.total(i)
    s_chain.arrived(2)
    d_chain.arrived(2)
    keys_back(1)
    keys_back(4)
    for i in range(4):
        at = slice(i * step, (i + 1) * step)
        if i == 0:
            loads[6].wait()
        block_out[at, :] = (mid_ref[at, :] + head_sum.joined(i)).astype(BF16)
    s_chain.arrived(3)
    d_chain.arrived(3)
    keys_back(3)
    for k in range(heads):
        lanes = slice(k * HEAD_DIM, (k + 1) * HEAD_DIM)
        gk_out[:, lanes] = turned_back(
            dk_acc[:, lanes] * HEAD_DIM ** (-0.5), cos_ref[...], sin_ref[...]
        )
        gv_out[:, lanes] = dv_acc[:, lanes].astype(BF16)
    d_chain.all_sent()
    s_chain.all_sent()
    head_sum.all_sent()
    gate.finish()
    for copy in ups:
        copy.wait()


def attention_back(
    devices, cores, do, stat, gate, grad_up, branch, mid, low_col, low_row, tables, keys, values, queries, lse, delta
):
    rows, width = mid.shape
    parts, _, cols = keys.shape
    heads = cols // HEAD_DIM
    units = gate[0].shape[0]
    count, depth = devices // 4, width // devices
    vmem = pl.BlockSpec(memory_space=pltpu.VMEM)
    hbm = pl.BlockSpec(memory_space=pl.ANY)
    dma = pltpu.SemaphoreType.DMA
    give = [
        pltpu.VMEM((2, units, rows), BF16),
        pltpu.VMEM((2, count, rows, depth), BF16),
        pltpu.VMEM((count, units, depth), BF16),
        dma((2 + 2 * count,)),
        dma((2 * count,)),
        dma((2 * count,)),
    ]
    flops = 14 * rows * rows * parts * cols
    return pl.pallas_call(
        functools.partial(attention_back_kernel, devices, cores),
        in_specs=[hbm] * 12 + [vmem] * 6,
        out_specs=[vmem] * 5 + [hbm],
        out_shape=[jax.ShapeDtypeStruct((rows, width), BF16)]
        + [jax.ShapeDtypeStruct((rows, cols), BF16)] * 3
        + [jax.ShapeDtypeStruct((count, units, depth), BF16)]
        + [jax.ShapeDtypeStruct((units, rows), BF16)],
        scratch_shapes=[pltpu.VMEM((parts, rows, cols), BF16)] * 3
        + [
            pltpu.VMEM((rows, width), F32),
            pltpu.VMEM((2, rows, width // 2), BF16),
            pltpu.VMEM((parts, rows, cols), BF16),
            pltpu.VMEM((parts, heads, 2, rows), F32),
            pltpu.VMEM((rows, cols), F32),
            pltpu.VMEM((rows, cols), F32),
        ]
        + sum_scratch(rows, width)
        + give
        + [dma((len(pieces_of(units, 3 * HEAD_DIM)),))] * 2
        + [dma((7,))]
        + [dma((4,))] * 4
        + [dma((12,))] * 2,
        compiler_params=pltpu.CompilerParams(
            collective_id=2, has_side_effects=True, vmem_limit_bytes=58 << 20
        ),
        cost_estimate=cost(flops, 80 << 20),
        name="attention_back",
    )(
        do,
        stat,
        *gate,
        grad_up,
        branch,
        mid,
        keys,
        values,
        queries,
        low_col,
        low_row,
        *tables,
        lse,
        delta,
    )


class Reduce:
    def __init__(self, block, near, far, slot, got, keep, last, send, recv):
        self.h = lax.axis_index("head")
        self.block, self.near_seq, self.far_seq = block, near, far
        self.slot, self.got, self.keep, self.last = slot, got, keep, last
        self.send, self.recv = send, recv

    def near(self, j):
        return remote(
            self.slot.at[j], self.got.at[j], self.send.at[j], self.recv.at[j], self.near_seq, self.h
        )

    def far(self):
        return remote(
            self.keep.at[1], self.last, self.send.at[2], self.recv.at[2], self.far_seq, self.h
        )

    def give(self):
        for j in range(2):
            self.slot[j] = self.block(2 + j).astype(BF16)
            self.near(j).start()

    def combine(self, received=None):
        for j in (1, 0):
            total = self.block(j)
            if received is None:
                self.near(j).wait_recv()
            total = total + self.got[j].astype(F32)
            self.keep[j] = total.astype(BF16)
            if j == 1:
                self.far().start()

    def result(self):
        self.far().wait_recv()
        return (self.keep[0].astype(F32) + self.last[...].astype(F32)).astype(BF16)

    def all_sent(self, gave):
        if gave:
            self.near(0).wait_send()
            self.near(1).wait_send()
        self.far().wait_send()


def weights_kernel(
    devices,
    cores,
    gate_hbm,
    gate_other_hbm,
    up_hbm,
    up_other_hbm,
    down_hbm,
    down_other_hbm,
    two_hbm,
    two_other_hbm,
    og_hbm,
    og_other_hbm,
    gate_got_hbm,
    mid_give_hbm,
    one_give_hbm,
    wq_hbm,
    wk_hbm,
    wv_hbm,
    gm_hbm,
    x_ref,
    gain_ref,
    mlp_part_ref,
    gq,
    gk,
    gv,
    att,
    one,
    mid_x,
    gate_out,
    up_out,
    down_out,
    wq_out,
    wk_out,
    wv_out,
    wo_out,
    tokens_out,
    gains_out,
    g_a,
    g_b,
    x_a,
    x_b,
    up_slot,
    down_slot,
    got_mlp,
    keep_mlp,
    last_mlp,
    gq_other,
    gk_other,
    gv_other,
    mid_other,
    one_other,
    att_other,
    slot_att,
    got_att,
    keep_att,
    last_att,
    wq,
    wk,
    wv,
    gm,
    core_send,
    core_got,
    chip,
    y_got,
    own_half,
    other_half,
    gains_got,
    load_sem,
    gm_sem,
    x_send,
    x_recv,
    job_send,
    job_recv,
    sum_send,
    sum_recv,
    gain_send,
    gain_recv,
):
    rows, width = x_ref.shape
    half = width // 2
    step = rows // 4
    s, h, odd, core, pair, mate, across = place(devices, cores)
    near, far = differing(s, 2), differing(s, 4)
    head_sum = HeadSum(
        devices, cores, core_got, chip, y_got, own_half, other_half, sum_send, sum_recv
    )
    greet(pair, h)
    greet(near, h)
    greet(far, h)
    greet(s, mate)
    greet(s, across)

    def position(first, p):
        bits = shard_orders(first, devices)
        shard = s
        for k, b in enumerate(bits[1:]):
            if (p >> (len(bits) - 2 - k)) & 1:
                shard = differing(shard, b)
        return shard // (2 * first) * first + lax.rem(shard, first)

    count = [0]

    def load(src, dst):
        copy = pltpu.make_async_copy(src, dst, load_sem.at[count[0]])
        count[0] += 1
        copy.start()
        return copy

    def load_job(g_own, g_other, x_own, x_other, g, x, first, blocks):
        copies = [load(g_own, g.at[0]), load(g_other, g.at[1])]
        for p in blocks:
            at = position(first, p)
            copies += [load(x_own.at[at], x.at[0, p]), load(x_other.at[at], x.at[1, p])]
        return copies

    def wait(copies):
        for copy in copies:
            copy.wait()

    gate_loads = load_job(gate_hbm, gate_other_hbm, two_hbm, two_other_hbm, g_a, x_a, 1, (0, 1))
    gate_loads.append(load(gate_got_hbm, got_mlp.at[0]))
    up_loads = load_job(up_hbm, up_other_hbm, two_hbm, two_other_hbm, g_b, x_b, 1, (0, 1, 2, 3))
    w_loads = [load(wq_hbm, wq), load(wk_hbm, wk), load(wv_hbm, wv)]

    def gm_load(i):
        return pltpu.make_async_copy(
            gm_hbm.at[pl.ds(i * step, step), :], gm.at[i % 2], gm_sem.at[i % 2]
        )

    gm_load(0).start()
    gm_load(1).start()

    def mlp_block(g, x):
        def block(p):
            total = jnp.dot(g[0], x[0, p], preferred_element_type=F32)
            return total + jnp.dot(g[1], x[1, p], preferred_element_type=F32)

        return block

    def att_block(x_own, x_other, g_own, g_other):
        def block(p):
            at = position(1, p)
            total = jnp.dot(x_own[at], g_own[...], preferred_element_type=F32)
            return total + jnp.dot(x_other[at], g_other[...], preferred_element_type=F32)

        return block

    def job(k, block, first_seq, slot, got, keep, last):
        return Reduce(block, first_seq, far, slot, got, keep, last, job_send.at[k], job_recv.at[k])

    gate = job(0, mlp_block(g_a, x_a), near, None, got_mlp.at[0], keep_mlp.at[0], last_mlp.at[0])
    up = job(1, mlp_block(g_b, x_b), near, up_slot, got_mlp.at[1], keep_mlp.at[1], last_mlp.at[1])
    down = job(2, mlp_block(g_a, x_a), pair, down_slot, got_mlp.at[2], keep_mlp.at[2], last_mlp.at[2])
    attention = []
    for k, operands in enumerate(
        (
            (one, one_other, gq, gq_other),
            (one, one_other, gk, gk_other),
            (one, one_other, gv, gv_other),
            (mid_x, mid_other, att, att_other),
        )
    ):
        attention.append(
            job(
                3 + k,
                att_block(*operands),
                near,
                slot_att.at[k],
                got_att.at[k],
                keep_att.at[k],
                last_att.at[k],
            )
        )

    pl.semaphore_wait(pltpu.get_barrier_semaphore(), 5)
    swaps = [
        remote(src, dst, x_send.at[i], x_recv.at[i], pair, h)
        for i, (src, dst) in enumerate(
            ((gq, gq_other), (gk, gk_other), (gv, gv_other))
        )
    ]
    share = devices // 4
    here = pl.ds(core * share, share)
    one_swap = remote(
        one_give_hbm.at[here], one_other.at[here], x_send.at[5], x_recv.at[5], pair, h
    )
    one_pass = remote(
        one_other.at[here], one_other.at[here], x_send.at[6], x_recv.at[6], s, mate
    )
    mid_swap = remote(
        mid_give_hbm.at[here], mid_other.at[here], x_send.at[3], x_recv.at[3], pair, h
    )
    mid_pass = remote(
        mid_other.at[here], mid_other.at[here], x_send.at[7], x_recv.at[7], s, mate
    )
    one_swap.start()
    for copy in swaps[:3]:
        copy.start()

    wait(gate_loads)
    gate.combine(True)
    down_loads = load_job(down_hbm, down_other_hbm, og_hbm, og_other_hbm, g_a, x_a, 2, (0, 1, 2, 3))
    wait(up_loads)
    up.give()
    wait(down_loads)
    down.give()
    swaps.append(remote(att, att_other, x_send.at[4], x_recv.at[4], pair, h))
    mid_swap.start()
    swaps[3].start()

    wait(w_loads)
    mine, theirs = (pl.multiple_of(c * half, half) for c in (core, 1 - core))

    def product(i, start):
        at = slice(i * step, (i + 1) * step)
        total = None
        for g, w in ((gq, wq), (gk, wk), (gv, wv)):
            term = dot_nt(g[at, :], w[pl.ds(start, half), :])
            total = term if total is None else total + term
        return total

    for i in range(4):
        core_send[i] = product(i, theirs).astype(BF16)
        head_sum.to_mate(i, core_send.at[i]).start()
    for i in range(4):
        head_sum.chip_sum(i, product(i, mine))
    one_swap.wait_recv()
    one_pass.start()
    one_pass.wait_recv()
    for k in range(3):
        swaps[k].wait_recv()
        attention[k].give()

    def finish(i):
        at = slice(i * step, (i + 1) * step)
        gm_load(i).wait()
        x = x_ref[at, :].astype(F32)
        root = lax.rsqrt(jnp.mean(x * x, axis=-1, keepdims=True) + EPS)
        grad = head_sum.joined(i)
        unit = x * root
        part = jnp.sum(grad * unit, axis=0, keepdims=True)
        gains_out[0:1, :] = part if i == 0 else gains_out[0:1, :] + part
        grad = grad * gain_ref[...]
        total = gm[i % 2] + root * (grad - unit * jnp.mean(grad * unit, axis=-1, keepdims=True))
        tokens_out[at, :] = total.astype(BF16)
        if i < 2:
            gm_load(i + 2).start()

    up.combine()
    for i in range(4):
        head_sum.total(i)
        if i > 0:
            finish(i - 1)
    finish(3)
    gains_out[1:2, :] = mlp_part_ref[...]

    def gain_swap(k, seq):
        return remote(gains_out, gains_got.at[k], gain_send.at[k], gain_recv.at[k], seq, h)

    def gain_step(k, seq):
        gain_swap(k, seq).wait()
        gains_out[...] = gains_out[...] + gains_got[k]

    gain_swap(0, pair).start()
    attention[0].combine()
    attention[1].combine()
    gain_step(0, pair)
    gain_swap(1, near).start()
    down.combine()
    mid_swap.wait_recv()
    mid_pass.start()
    swaps[3].wait_recv()
    mid_pass.wait_recv()
    attention[3].give()
    attention[2].combine()
    gain_step(1, near)
    gain_swap(2, far).start()
    attention[3].combine()
    gate_out[...] = gate.result()
    down_out[...] = down.result()
    up_out[...] = up.result()
    gain_step(2, far)
    for k, out in enumerate((wq_out, wk_out, wv_out, wo_out)):
        out[...] = attention[k].result()
    gate.all_sent(False)
    down.all_sent(True)
    up.all_sent(True)
    for k in range(4):
        attention[k].all_sent(True)
    for copy in (*swaps, one_swap, one_pass, mid_swap, mid_pass):
        copy.wait_send()
    head_sum.all_sent()


def weight_gradients(
    devices, cores, mlp_operands, others, weights, grad_mid, x, gain, mlp_part, attention_operands
):
    rows, width = x.shape
    units = mlp_operands[0].shape[0]
    cols = weights[0].shape[1]
    depth = width // devices
    vmem = pl.BlockSpec(memory_space=pltpu.VMEM)
    hbm = pl.BlockSpec(memory_space=pl.ANY)
    dma = pltpu.SemaphoreType.DMA
    operands = (*mlp_operands, *others, *weights, grad_mid)
    kept = (x, gain, mlp_part, *attention_operands)
    return pl.pallas_call(
        functools.partial(weights_kernel, devices, cores),
        in_specs=[hbm] * len(operands) + [vmem] * len(kept),
        out_specs=[vmem] * 9,
        out_shape=[jax.ShapeDtypeStruct((units, depth), BF16)] * 3
        + [jax.ShapeDtypeStruct((depth, cols), BF16)] * 4
        + [jax.ShapeDtypeStruct((rows, width), BF16), jax.ShapeDtypeStruct((2, width), F32)],
        scratch_shapes=[
            pltpu.VMEM((2, units, rows), BF16),
            pltpu.VMEM((2, units, rows), BF16),
            pltpu.VMEM((2, 4, rows, depth), BF16),
            pltpu.VMEM((2, 4, rows, depth), BF16),
            pltpu.VMEM((2, units, depth), BF16),
            pltpu.VMEM((2, units, depth), BF16),
            pltpu.VMEM((3, 2, units, depth), BF16),
            pltpu.VMEM((3, 2, units, depth), BF16),
            pltpu.VMEM((3, units, depth), BF16),
        ]
        + [pltpu.VMEM((rows, cols), BF16)] * 3
        + [
            pltpu.VMEM((devices // 2, depth, rows), BF16),
            pltpu.VMEM((devices // 2, depth, rows), BF16),
            pltpu.VMEM((rows, cols), BF16),
            pltpu.VMEM((4, 2, depth, cols), BF16),
            pltpu.VMEM((4, 2, depth, cols), BF16),
            pltpu.VMEM((4, 2, depth, cols), BF16),
            pltpu.VMEM((4, depth, cols), BF16),
        ]
        + [pltpu.VMEM((width, cols), BF16)] * 3
        + [pltpu.VMEM((2, rows // 4, width), F32)]
        + [pltpu.VMEM((4, rows // 4, width // 2), BF16)]
        + sum_scratch(rows, width)
        + [pltpu.VMEM((3, 2, width), F32)]
        + [dma((32,)), dma((2,)), dma((8,)), dma((8,)), dma((7, 3)), dma((7, 3))]
        + [dma((12,)), dma((12,)), dma((3,)), dma((3,))],
        compiler_params=pltpu.CompilerParams(
            collective_id=3, has_side_effects=True, vmem_limit_bytes=62 << 20
        ),
        cost_estimate=cost(20 * rows * width * cols, 60 << 20),
        name="weight_gradients",
    )(*operands, *kept)


def on_device(
    tokens,
    gain_attn,
    gain_mlp,
    w_query,
    w_key,
    w_value,
    w_out,
    w_gate,
    w_up,
    w_down,
    prev_keys,
    prev_values,
    lengths,
    out_grad,
):
    rows = tokens.shape[0]
    width = w_query.shape[1]
    devices, cores = lax.axis_size("seq"), lax.axis_size("head")
    index = lax.axis_index("seq")
    bits = jnp.stack([index & 1, lax.axis_index("head") & 1]).astype(jnp.int32)
    gain_one, gain_two = gain_attn[None, :], gain_mlp[None, :]

    (
        keys,
        values,
        queries,
        one_keep,
        one_give,
        mid,
        normed_two,
        two_keep,
        two_give,
        out_keep,
        out_give,
        out_got,
        attended,
        lse,
        lse_row,
        cosine,
        sine,
        low_col,
        low_row,
        valid,
    ) = forward(
        devices,
        cores,
        lengths,
        tokens,
        (gain_one, gain_two),
        out_grad,
        (w_key, w_value, w_query),
        w_out,
        (prev_keys, prev_values),
    )
    order = Order()
    out_keep, out_got = (a.reshape(devices // 2, rows, -1) for a in (out_keep, out_got))
    (
        branch_parts,
        grad_mid,
        gain_mlp_part,
        grad_att,
        delta,
        stat,
        act,
        grad_gate,
        grad_up,
        act_got,
        gate_got,
        two_got,
        mid_keep,
        mid_give,
    ) = middle(
        devices,
        cores,
        normed_two,
        out_grad,
        gain_two,
        valid,
        lse_row,
        (w_gate.T, w_up.T, w_down.T),
        mid,
        w_out,
        attended,
        two_give,
    )
    out_pair = (out_keep, out_got)
    two_pair = (two_keep, two_got)
    order.ran(delta)
    block_out, grad_query_raw, grad_key_raw, grad_value_raw, gate_sums, up_got = attention_back(
        devices,
        cores,
        order.after(grad_att),
        stat,
        (grad_gate, gate_got, *two_pair),
        grad_up,
        branch_parts,
        mid,
        low_col,
        low_row,
        (cosine, sine),
        keys,
        values,
        queries,
        lse,
        delta,
    )
    if devices == 8:
        sums = weight_gradients(
            devices,
            cores,
            (grad_gate, gate_got, grad_up, up_got, act, act_got),
            (*two_pair, *out_pair, gate_sums, mid_give, one_give),
            (w_query, w_key, w_value),
            grad_mid,
            tokens,
            gain_one,
            gain_mlp_part,
            (
                grad_query_raw,
                grad_key_raw,
                grad_value_raw,
                attended,
                one_keep,
                mid_keep,
            ),
        )
        gate_grad, up_grad, down_grad = (a.astype(F32).T for a in sums[:3])
        gains = lax.dynamic_slice_in_dim(sums[8], index * sums[8].shape[1] // devices, sums[8].shape[1] // devices, 1)
        return (
            block_out,
            sums[7],
            gains[0],
            gains[1],
            *(a.astype(F32) for a in sums[3:7]),
            gate_grad,
            up_grad,
            down_grad,
        )
    order.ran(grad_query_raw)
    attended_got = swap(attended, "seq", 1)
    one_pair = (one_keep, swap(one_give, "seq", 1))
    gate = WeightGrad(order, two_pair, grad_gate, gate_got, 1, "gate", True)
    up = WeightGrad(order, two_pair, grad_up, up_got, 1, "up", True)
    down = WeightGrad(order, out_pair, act, act_got, 2, "down", True)
    gate.got = gate_sums
    query_got = swap(grad_query_raw, "seq", 1)
    key_got = swap(grad_key_raw, "seq", 1)
    value_got = swap(grad_value_raw, "seq", 1)
    mid_pair = (mid_keep, swap(order.after(mid_give), "seq", 1))
    gate.keep()
    up.give()
    down.give()
    lefts = (grad_query_raw, grad_key_raw, grad_value_raw)
    rights = (w_query, w_key, w_value)
    give = order.ran(half_product(order.after(bits), lefts, rights, 1, None, "norm_one_give"))
    give = swap(give, "head", 1)
    query = WeightGrad(order, one_pair, grad_query_raw, query_got, 1, "query")
    key = WeightGrad(order, one_pair, grad_key_raw, key_got, 1, "key")
    value = WeightGrad(order, one_pair, grad_value_raw, value_got, 1, "value")
    wout = WeightGrad(order, mid_pair, attended, attended_got, 1, "wout")
    query.give()
    chip = order.ran(half_product(order.after(bits), lefts, rights, 0, give, "norm_one_keep"))
    chip_got = swap(chip, "head", 2)
    key.give()
    value.give()
    up.keep()
    down.keep()
    wout.give()
    own = (chip.astype(F32) + chip_got.astype(F32)).astype(BF16)
    other = swap(own, "head", 1)
    query.keep()
    key.keep()
    tokens_grad, gain_attn_part = by_rows(
        back_kernel,
        order.after(bits),
        (tokens, own, other, gain_one, grad_mid),
        3,
        (BF16, F32),
        "tokens_back",
        part=1,
    )
    order.ran(gain_attn_part)
    value.keep()
    wout.keep()
    gains = gain_sum(jnp.concatenate([gain_attn_part, gain_mlp_part], axis=0))
    gain_attn_grad, gain_mlp_grad = gains[0], gains[1]
    w_gate_grad, w_up_grad, w_down_grad = gate.finish(), up.finish(), down.finish()
    w_out_grad = wout.finish()
    w_query_grad, w_key_grad, w_value_grad = query.finish(), key.finish(), value.finish()
    return (
        block_out,
        tokens_grad,
        gain_attn_grad,
        gain_mlp_grad,
        w_query_grad,
        w_key_grad,
        w_value_grad,
        w_out_grad,
        w_gate_grad,
        w_up_grad,
        w_down_grad,
    )


def solution(mesh):
    by_head = P(None, "head")
    both = P("seq", "head")
    placed = (P("seq", None), P(), P()) + (by_head,) * 9 + (P(), P("seq", None))
    return jax.shard_map(
        on_device,
        mesh=mesh,
        in_specs=placed,
        out_specs=(P("seq", None), P("seq", None), P("seq"), P("seq")) + (both,) * 7,
        check_vma=False,
    )
```
